32 devices in a mesh: ctx: 8 (over z, y), head: 4 (over x, core).
Axes of the slice: x: 2, y: 2, z: 4, core: 2. Of those that a mesh axis runs over, the one named last changes fastest.
Arguments:
- query_input: bfloat16 [2048, 4096], P('ctx', 'head'), may hold values from -6 to 6
- key_entries_raw: bfloat16 [2048, 1024], P('ctx', 'head'), may hold values from -6 to 6
- value_entries_raw: bfloat16 [2048, 1024], P('ctx', 'head'), may hold values from -6 to 6
- out_grad: bfloat16 [2048, 4096], P('ctx', 'head'), may hold values from -6 to 6
- attn_out: bfloat16 [2048, 4096], P('ctx', 'head'), may hold values from -3 to 3
- log_sum_exp: float32 [32, 2048], P('head', 'ctx'), may hold values from 4 to 6
- positions: int32 [3, 2048], P(None, ('ctx', 'head')), may hold values from 0 to 4095
- span_map: int32 [8], replicated, may hold values from 0 to 7, each once
Outputs:
- query_grad: bfloat16 [2048, 4096], P('ctx', 'head')
- key_gradient_raw: bfloat16 [2048, 1024], P('ctx', 'head')
- value_gradient_rows: bfloat16 [2048, 1024], P('ctx', 'head')
The draws below stay inside these ranges and needn't reach their ends.
Inputs may be any that keep to these rules, and one draw needn't show every extreme that they name: Block b of 256 rows holds span span_map[b] of the sequence in its first 128 rows and span 2 * 8 - 1 - span_map[b] in its last 128 rows; each number appears once.
All inputs are finite; a program needn't handle non-finite values.
Results may differ from the reference program's by a relative error of at most 0.019.
The reference program's roundings to bfloat16 on the way (of `rounded_weights` and `rounded_grad`) count: a program that leaves them out, or rounds other values in their place, can miss the bound.
Values may be sent and summed in bfloat16 or wider, within the bound.
No kernel may reach another device: no remote copies, remote signals or barrier semaphores. Data moves between devices by JAX's collectives and lax.ppermute only.
A program may use at most 64 MiB of HBM per device.

```python
import math
import jax
import jax.numpy as jnp
from jax import lax

HQ = 32
KEY_VALUE_HEADS = 8
HEAD_ENTRIES = 128
WIN = 4
TOKENS_PER_PART = 256
SEQUENCE_TOKENS = 2048
N_CTX = 8


def set_ends(entries, stream_key, least, high):
    shape = entries.shape
    index_at = [jax.random.randint(jax.random.fold_in(stream_key, axis), (), 0, shape[axis]) for axis in range(len(shape))]
    entries = entries.at[tuple(index_at)].set(least)
    longest = shape.index(max(shape))
    index_at[longest] = (index_at[longest] + 1) % shape[longest]
    return entries.at[tuple(index_at)].set(high)


def block_scale(rng, dims, cuts, low, top_value):
    level, own = 1.0, jax.random.fold_in(rng, 6)
    for position, blocks in cuts:
        heights = jnp.exp(jax.random.uniform(jax.random.fold_in(own, position), (blocks,), jnp.float32, low / len(cuts), top_value / len(cuts)))
        level = level * jnp.repeat(heights, dims[position] // blocks).reshape([-1 if axis == position else 1 for axis in range(len(dims))])
    return level


def noise(rng, shape, spread, bound, shards=(), held_as=jnp.bfloat16):
    array = jax.random.normal(rng, shape, jnp.float32) * spread
    if len(shards) > 0:
        array = block_scale(rng, shape, shards, -0.22, 0.18) * array
    return jnp.clip(array, min=-bound, max=bound).astype(held_as)


def setup_inputs(seed: int = 0) -> dict:
    arg_keys = jax.random.split(jax.random.key(seed), 9)
    return {
        "query_input": noise(arg_keys[0], (SEQUENCE_TOKENS, HQ * HEAD_ENTRIES), 1.0, 6.0, ((0, 8), (1, 4))),
        "key_entries_raw": noise(arg_keys[1], (SEQUENCE_TOKENS, KEY_VALUE_HEADS * HEAD_ENTRIES), 1.0, 6.0, ((0, 8), (1, 4))),
        "value_entries_raw": noise(arg_keys[2], (SEQUENCE_TOKENS, KEY_VALUE_HEADS * HEAD_ENTRIES), 1.0, 6.0, ((0, 8), (1, 4))),
        "out_grad": noise(arg_keys[3], (SEQUENCE_TOKENS, HQ * HEAD_ENTRIES), 1.0, 6.0, ((0, 8), (1, 4))),
        "attn_out": noise(arg_keys[4], (SEQUENCE_TOKENS, HQ * HEAD_ENTRIES), 0.5, 3.0, ((0, 8), (1, 4))),
        "log_sum_exp": jnp.clip(4.0 + 2.0 * jax.random.uniform(arg_keys[5], (HQ, SEQUENCE_TOKENS), jnp.float32) ** block_scale(arg_keys[5], (HQ, SEQUENCE_TOKENS), ((0, 4), (1, 8)), -0.2, 0.2), 4.0, 6.0),
        "positions": set_ends(jax.random.randint(arg_keys[6], (3, SEQUENCE_TOKENS), 0, 4096), jax.random.fold_in(arg_keys[6], 1), 0, 4095).astype(jnp.int32),
        "span_map": jax.random.permutation(arg_keys[7], N_CTX).astype(jnp.int32),
    }


ROPE_BASE = 1000000.0
YARN_FACTOR = 4.0
YARN_INITIAL = 32768.0
BETA_FAST = 32.0
BETA_SLOW = 1.0
YARN_MSCALE = 1.0 + 0.1 * math.log(4.0)

def rope_tables(positions, head_width):
    half_width = head_width // 2
    pair_index = jnp.arange(half_width, dtype=jnp.float32)
    inverse = jnp.exp(-2.0 * pair_index / head_width * math.log(ROPE_BASE))
    ratio_value = YARN_INITIAL * inverse / (2.0 * math.pi)
    ramp_value = jnp.clip((ratio_value - BETA_SLOW) / (BETA_FAST - BETA_SLOW), 0.0, 1.0)
    frequency = inverse * ((1.0 - ramp_value) / YARN_FACTOR + ramp_value)
    first_cut = head_width // 8
    second_cut = first_cut + 3 * head_width // 16
    spot_values = positions.astype(jnp.float32)
    chosen = jnp.where(pair_index < first_cut, spot_values[0][:, None], jnp.where(pair_index < second_cut, spot_values[1][:, None], spot_values[2][:, None]))
    angles = chosen * frequency
    return (jnp.cos(angles) * YARN_MSCALE, jnp.sin(angles) * YARN_MSCALE)

def apply_rotary(block_rows, cosine_lookup, sine_lookup):
    half_width = block_rows.shape[-1] // 2
    widened = block_rows.astype(jnp.float32)
    first_half = widened[..., :half_width]
    second_half = widened[..., half_width:]
    cosine_rows = cosine_lookup[:, None, :]
    sine_rows = sine_lookup[:, None, :]
    return jnp.concatenate([first_half * cosine_rows - second_half * sine_rows, second_half * cosine_rows + first_half * sine_rows], axis=-1)

def reverse_rotary(gradient, cosine_lookup, sine_lookup):
    half_width = gradient.shape[-1] // 2
    first_half = gradient[..., :half_width]
    second_half = gradient[..., half_width:]
    cosine_rows = cosine_lookup[:, None, :]
    sine_rows = sine_lookup[:, None, :]
    return jnp.concatenate([first_half * cosine_rows + second_half * sine_rows, second_half * cosine_rows - first_half * sine_rows], axis=-1)

def block_grads(query_side, key_side, query_order, key_order):
    query_rotated, grad_heads, norm_rows, delta_rows = query_side
    key_turned, value_head_split = key_side
    row_count = query_rotated.shape[0]
    key_heads = key_turned.shape[1]
    head_width = key_turned.shape[2]
    group_size = query_rotated.shape[1] // key_heads
    root_scale = 1.0 / math.sqrt(head_width)
    query_groups = query_rotated.reshape(row_count, key_heads, group_size, head_width).astype(jnp.float32)
    grad_groups = grad_heads.reshape(row_count, key_heads, group_size, head_width).astype(jnp.float32)
    key_wide = key_turned.astype(jnp.float32)
    value_wide = value_head_split.astype(jnp.float32)
    scores = jnp.einsum('qgjd,kgd->gjqk', query_groups, key_wide) * root_scale
    visible = key_order[None, :] <= query_order[:, None]
    norm_table = norm_rows.reshape(key_heads, group_size, row_count)[..., None]
    weights = jnp.where(visible, jnp.exp(scores - norm_table), 0.0)
    rounded_weights = lax.optimization_barrier(weights.astype(jnp.bfloat16)).astype(jnp.float32)
    value_part = jnp.einsum('gjqk,qgjd->kgd', rounded_weights, grad_groups)
    weight_grad = jnp.einsum('qgjd,kgd->gjqk', grad_groups, value_wide)
    score_grad = weights * (weight_grad - delta_rows.reshape(key_heads, group_size, row_count)[..., None])
    rounded_grad = lax.optimization_barrier(score_grad.astype(jnp.bfloat16)).astype(jnp.float32)
    key_part = jnp.einsum('gjqk,qgjd->kgd', rounded_grad, query_groups) * root_scale
    query_part = jnp.einsum('gjqk,kgd->qgjd', rounded_grad, key_wide).reshape(row_count, key_heads * group_size, head_width) * root_scale
    return (query_part, key_part, value_part)

def reference(query_input, key_entries_raw, value_entries_raw, out_grad, attn_out, log_sum_exp, positions, span_map):
    cosine_lookup, sine_lookup = rope_tables(positions, HEAD_ENTRIES)
    query_rotated = apply_rotary(query_input.reshape(SEQUENCE_TOKENS, HQ, HEAD_ENTRIES), cosine_lookup, sine_lookup).astype(jnp.bfloat16)
    key_turned = apply_rotary(key_entries_raw.reshape(SEQUENCE_TOKENS, KEY_VALUE_HEADS, HEAD_ENTRIES), cosine_lookup, sine_lookup).astype(jnp.bfloat16)
    grad_heads = out_grad.reshape(SEQUENCE_TOKENS, HQ, HEAD_ENTRIES)
    value_head_split = value_entries_raw.reshape(SEQUENCE_TOKENS, KEY_VALUE_HEADS, HEAD_ENTRIES)
    delta_rows = lax.optimization_barrier(jnp.sum(grad_heads.astype(jnp.float32) * attn_out.reshape(SEQUENCE_TOKENS, HQ, HEAD_ENTRIES).astype(jnp.float32), axis=2)).T
    span_len = TOKENS_PER_PART // 2
    offsets = jnp.arange(span_len, dtype=jnp.int32)
    early_span = span_map.astype(jnp.int32)
    late_span = 2 * N_CTX - 1 - early_span
    order = jnp.concatenate([early_span[:, None] * span_len + offsets[None, :], late_span[:, None] * span_len + offsets[None, :]], axis=1)
    query_slots = query_rotated.reshape(N_CTX, TOKENS_PER_PART, HQ, HEAD_ENTRIES)
    grad_slots = grad_heads.reshape(N_CTX, TOKENS_PER_PART, HQ, HEAD_ENTRIES)
    key_places = key_turned.reshape(N_CTX, TOKENS_PER_PART, KEY_VALUE_HEADS, HEAD_ENTRIES)
    value_places = value_head_split.reshape(N_CTX, TOKENS_PER_PART, KEY_VALUE_HEADS, HEAD_ENTRIES)
    norm_slots = log_sum_exp.reshape(HQ, N_CTX, TOKENS_PER_PART).transpose(1, 0, 2)
    delta_slots = delta_rows.reshape(HQ, N_CTX, TOKENS_PER_PART).transpose(1, 0, 2)
    query_total = jnp.zeros((N_CTX, TOKENS_PER_PART, HQ, HEAD_ENTRIES), jnp.float32)
    key_overall = jnp.zeros((N_CTX, TOKENS_PER_PART, KEY_VALUE_HEADS, HEAD_ENTRIES), jnp.float32)
    value_overall = jnp.zeros((N_CTX, TOKENS_PER_PART, KEY_VALUE_HEADS, HEAD_ENTRIES), jnp.float32)
    for hop_index in range(WIN):

        def per_slot(slot_index):
            key_slot = ((slot_index + hop_index) % N_CTX).astype(jnp.int32)
            return block_grads((query_slots[slot_index], grad_slots[slot_index], norm_slots[slot_index], delta_slots[slot_index]), (key_places[key_slot], value_places[key_slot]), order[slot_index], order[key_slot])
        query_part, key_part, value_part = lax.map(per_slot, jnp.arange(N_CTX, dtype=jnp.int32))
        query_total = query_total + query_part
        key_overall = key_overall + jnp.roll(key_part, hop_index, axis=0)
        value_overall = value_overall + jnp.roll(value_part, hop_index, axis=0)
    query_grad = reverse_rotary(query_total.reshape(SEQUENCE_TOKENS, HQ, HEAD_ENTRIES), cosine_lookup, sine_lookup).reshape(SEQUENCE_TOKENS, HQ * HEAD_ENTRIES).astype(jnp.bfloat16)
    key_gradient_raw = reverse_rotary(key_overall.reshape(SEQUENCE_TOKENS, KEY_VALUE_HEADS, HEAD_ENTRIES), cosine_lookup, sine_lookup).reshape(SEQUENCE_TOKENS, KEY_VALUE_HEADS * HEAD_ENTRIES).astype(jnp.bfloat16)
    value_gradient_rows = value_overall.reshape(SEQUENCE_TOKENS, KEY_VALUE_HEADS * HEAD_ENTRIES).astype(jnp.bfloat16)
    return (query_grad, key_gradient_raw, value_gradient_rows)
```

```python
import functools
import math

import jax
import jax.numpy as jnp
import numpy as np
from jax import lax
from jax.experimental import pallas as pl
from jax.experimental.pallas import tpu as pltpu
from jax.sharding import PartitionSpec as P

HEAD = 128
HALF = HEAD // 2
WIN = 4
ROPE_BASE = 1000000.0
YARN_FACTOR = 4.0
YARN_INITIAL = 32768.0
BETA_FAST = 32.0
BETA_SLOW = 1.0
YARN_MSCALE = 1.0 + 0.1 * math.log(4.0)
ROOT_SCALE = 1.0 / math.sqrt(HEAD)
LOG2E = math.log2(math.e)
VMEM_LIMIT = 24 * 1024 * 1024

F32 = jnp.float32
BF16 = jnp.bfloat16


def frequencies():
    pair = np.arange(HALF, dtype=np.float64)
    inverse = np.exp(-2.0 * pair / HEAD * math.log(ROPE_BASE))
    ratio = YARN_INITIAL * inverse / (2.0 * math.pi)
    ramp = np.clip((ratio - BETA_SLOW) / (BETA_FAST - BETA_SLOW), 0.0, 1.0)
    return (inverse * ((1.0 - ramp) / YARN_FACTOR + ramp)).astype(np.float32)


def sine_cosine(angle):
    turns = jnp.floor(angle * (2.0 / math.pi) + 0.5)
    r = angle - turns * 1.5703125
    r = r - turns * 4.837512969970703125e-4
    r = r - turns * 7.54978995489188e-8
    r2 = r * r
    s = r + r * r2 * (-1.6666654611e-1 + r2 * (8.3321608736e-3 - r2 * 1.9515295891e-4))
    c = (
        1.0
        - 0.5 * r2
        + r2
        * r2
        * (4.166664568298827e-2 + r2 * (-1.388731625493765e-3 + r2 * 2.443315711809948e-5))
    )
    quadrant = turns.astype(jnp.int32) & 3
    odd = (quadrant & 1) == 1
    sine = jnp.where(odd, c, s)
    cosine = jnp.where(odd, s, c)
    sine = jnp.where(quadrant >= 2, -sine, sine)
    cosine = jnp.where((quadrant == 1) | (quadrant == 2), -cosine, cosine)
    return sine, cosine


def tables_transposed(place, freq):
    place = place.astype(F32)
    pair = lax.broadcasted_iota(jnp.int32, freq.shape, 0)
    first = HEAD // 8
    second = first + 3 * HEAD // 16
    chosen = jnp.where(
        pair < first, place[0:1], jnp.where(pair < second, place[1:2], place[2:3])
    )
    sine, cosine = sine_cosine(chosen * freq)
    return cosine * YARN_MSCALE, sine * YARN_MSCALE


def row_tables(cosine_t, sine_t):
    wide = jnp.concatenate([cosine_t, cosine_t], axis=0).T
    signed = jnp.concatenate([-sine_t, sine_t], axis=0).T
    return wide, signed


def rotated(x, wide, signed):
    return x * wide + pltpu.roll(x, HALF, 1) * signed


def dot_nt(a, b):
    return lax.dot_general(a, b, (((1,), (1,)), ((), ())), preferred_element_type=F32)


def dot_nn(a, b):
    return lax.dot_general(a, b, (((1,), (0,)), ((), ())), preferred_element_type=F32)


def dot_tn(a, b):
    return lax.dot_general(a, b, (((0,), (0,)), ((), ())), preferred_element_type=F32)


def pair_part(key, value, query, grad, norm, delta, causal):
    scores = dot_nt(key, query)
    weights = jnp.exp2(scores * (ROOT_SCALE * LOG2E) - norm)
    if causal:
        at_key = lax.broadcasted_iota(jnp.int32, scores.shape, 0)
        at_query = lax.broadcasted_iota(jnp.int32, scores.shape, 1)
        weights = jnp.where(at_key <= at_query, weights, 0.0)
    value_part = dot_nn(weights.astype(BF16), grad)
    score_grad = (weights * (dot_nt(value, grad) - delta)).astype(BF16)
    key_part = dot_nn(score_grad, query)
    query_part = dot_tn(key, score_grad)
    return value_part, key_part, query_part


def first_kernel(
    slot_ref, pos_ref, freq_ref, q_ref, k_ref, v_ref, do_ref, at_ref, lse_ref,
    qr_ref, delta_ref, wide_ref, signed_ref, dqt_ref, dkv_ref,
):
    heads = q_ref.shape[1] // HEAD
    groups = k_ref.shape[1] // HEAD
    size = heads // groups
    cosine_t, sine_t = tables_transposed(pos_ref[slot_ref[0]], freq_ref[...])
    wide, signed = row_tables(cosine_t, sine_t)
    wide_ref[...] = wide
    signed_ref[...] = signed
    delta = jnp.zeros(delta_ref.shape, F32)
    which = lax.broadcasted_iota(jnp.int32, (heads, HEAD), 0)
    for h in range(heads):
        cols = pl.ds(h * HEAD, HEAD)
        qr_ref[:, cols] = rotated(q_ref[:, cols].astype(F32), wide, signed).astype(BF16)
        product = do_ref[:, cols].astype(F32) * at_ref[:, cols].astype(F32)
        high = product.astype(BF16)
        low = (product - high.astype(F32)).astype(BF16)
        chooser = jnp.where(which == h, 1.0, 0.0).astype(BF16)
        delta = delta + dot_nt(chooser, high) + dot_nt(chooser, low)
    delta_ref[...] = delta
    norm = lse_ref[...] * LOG2E
    for g in range(groups):
        cols = pl.ds(g * HEAD, HEAD)
        key = rotated(k_ref[:, cols].astype(F32), wide, signed).astype(BF16)
        value = v_ref[:, cols]
        dk = dv = None
        for h in range(g * size, (g + 1) * size):
            hc = pl.ds(h * HEAD, HEAD)
            v_part, k_part, q_part = pair_part(
                key, value, qr_ref[:, hc], do_ref[:, hc], norm[h : h + 1], delta[h : h + 1], True
            )
            dqt_ref[hc, :] = q_part
            dv = v_part if dv is None else dv + v_part
            dk = k_part if dk is None else dk + k_part
        dkv_ref[:, cols] = dk
        dkv_ref[:, pl.ds((groups + g) * HEAD, HEAD)] = dv


def hop_body(
    step, slot_ref, span_ref, pos_ref, freq_ref, kv_ref, qr_ref, do_ref, lse_ref, delta_ref,
    dqt_in, dqt_ref, dkv_ref, key_ref,
):
    rows = qr_ref.shape[0]
    half = rows // 2
    heads = qr_ref.shape[1] // HEAD
    groups = kv_ref.shape[1] // HEAD // 2
    size = heads // groups
    count = span_ref.shape[0]
    me = slot_ref[0]
    other = lax.rem(me + step, count)
    cosine_t, sine_t = tables_transposed(pos_ref[other], freq_ref[...])
    wide, signed = row_tables(cosine_t, sine_t)
    for g in range(groups):
        cols = pl.ds(g * HEAD, HEAD)
        key_ref[:, cols] = rotated(kv_ref[:, cols].astype(F32), wide, signed).astype(BF16)
    earlier = span_ref[other] < span_ref[me]
    norm = lse_ref[...] * LOG2E
    delta = delta_ref[...]

    def run(keys, queries):
        for g in range(groups):
            kc = pl.ds(g * HEAD, HEAD)
            vc = pl.ds((groups + g) * HEAD, HEAD)
            dk = dv = None
            for h in range(g * size, (g + 1) * size):
                hc = pl.ds(h * HEAD, HEAD)
                v_part, k_part, q_part = pair_part(
                    key_ref[keys, kc], kv_ref[keys, vc], qr_ref[queries, hc], do_ref[queries, hc],
                    norm[h : h + 1, queries.start :], delta[h : h + 1, queries.start :], False,
                )
                if queries.start:
                    dqt_ref[hc, : queries.start] = dqt_in[hc, : queries.start]
                dqt_ref[hc, queries] = dqt_in[hc, queries] + q_part
                dv = v_part if dv is None else dv + v_part
                dk = k_part if dk is None else dk + k_part
            dkv_ref[keys, kc] = dk.astype(BF16)
            dkv_ref[keys, vc] = dv.astype(BF16)
        if keys.stop < rows:
            dkv_ref[keys.stop :, :] = jnp.zeros((rows - keys.stop, dkv_ref.shape[1]), BF16)

    @pl.when(earlier)
    def _():
        run(slice(0, half), slice(0, rows))

    @pl.when(jnp.logical_not(earlier))
    def _():
        run(slice(0, rows), slice(half, rows))


def middle_kernel(step, *refs):
    hop_body(step, *refs)


def last_kernel(
    step, slot_ref, span_ref, pos_ref, freq_ref, kv_ref, qr_ref, do_ref, lse_ref, delta_ref,
    dqt_in, out_ref, dkv_ref, key_ref, dqt_ref,
):
    hop_body(
        step, slot_ref, span_ref, pos_ref, freq_ref, kv_ref, qr_ref, do_ref, lse_ref, delta_ref,
        dqt_in, dqt_ref, dkv_ref, key_ref,
    )
    cosine_t, sine_t = tables_transposed(pos_ref[slot_ref[0]], freq_ref[...])
    cosine_t = cosine_t * ROOT_SCALE
    sine_t = sine_t * ROOT_SCALE
    for h in range(qr_ref.shape[1] // HEAD):
        y1 = dqt_ref[pl.ds(h * HEAD, HALF), :]
        y2 = dqt_ref[pl.ds(h * HEAD + HALF, HALF), :]
        turned = jnp.concatenate(
            [y1 * cosine_t + y2 * sine_t, y2 * cosine_t - y1 * sine_t], axis=0
        )
        out_ref[:, pl.ds(h * HEAD, HEAD)] = turned.T.astype(BF16)


def final_kernel(wide_ref, signed_ref, own_ref, a_ref, b_ref, c_ref, dk_ref, dv_ref):
    width = dk_ref.shape[1]
    total = (
        own_ref[...] + a_ref[...].astype(F32) + b_ref[...].astype(F32) + c_ref[...].astype(F32)
    )
    wide = wide_ref[...] * ROOT_SCALE
    signed = signed_ref[...] * -ROOT_SCALE
    for g in range(width // HEAD):
        cols = pl.ds(g * HEAD, HEAD)
        dk_ref[:, cols] = rotated(total[:, g * HEAD : (g + 1) * HEAD], wide, signed).astype(BF16)
    dv_ref[...] = total[:, width:].astype(BF16)


def call(kernel, outs, in_smem, n_in, scratch=(), flops=0, bytes_accessed=0, aliases=None):
    vmem = pl.BlockSpec(memory_space=pltpu.VMEM)
    smem = pl.BlockSpec(memory_space=pltpu.SMEM)
    return pl.pallas_call(
        kernel,
        out_shape=[jax.ShapeDtypeStruct(shape, dtype) for shape, dtype in outs],
        in_specs=[smem] * in_smem + [vmem] * n_in,
        out_specs=[vmem] * len(outs),
        scratch_shapes=list(scratch),
        input_output_aliases=aliases or {},
        compiler_params=pltpu.CompilerParams(vmem_limit_bytes=VMEM_LIMIT),
        cost_estimate=pl.CostEstimate(
            flops=flops, bytes_accessed=bytes_accessed, transcendentals=0
        ),
    )


def shifted(value, steps):
    count = lax.axis_size("ctx")
    pairs = [(source, (source + steps) % count) for source in range(count)]
    return lax.ppermute(value, "ctx", pairs)


def shards(q, k, v, do, at, lse, positions, span_map):
    rows = q.shape[0]
    wide_q = q.shape[1]
    wide_k = k.shape[1]
    heads = wide_q // HEAD
    slots = lax.axis_size("ctx")
    slot = lax.axis_index("ctx").astype(jnp.int32).reshape(1)
    freq = jnp.asarray(np.broadcast_to(frequencies()[:, None], (HALF, rows)).copy())

    kv = jnp.concatenate([k, v], axis=1)
    kv1 = shifted(kv, -1)
    kv2 = shifted(kv, -2)
    gathered = lax.all_gather(positions, ("ctx", "head"), axis=0)
    pos = gathered.reshape(slots, -1, 3, positions.shape[1]).transpose(0, 2, 1, 3)
    pos = pos.reshape(slots, 3, rows)
    kv3 = shifted(kv1, -2)

    flops = 10 * rows * rows * wide_q
    qr, delta, wide, signed, dqt, dkv = call(
        first_kernel,
        [
            ((rows, wide_q), BF16),
            ((heads, rows), F32),
            ((rows, HEAD), F32),
            ((rows, HEAD), F32),
            ((wide_q, rows), F32),
            ((rows, 2 * wide_k), F32),
        ],
        1,
        8,
        flops=flops,
        bytes_accessed=5 << 20,
    )(slot, pos, freq, q, k, v, do, at, lse)

    backs = []
    for step, arrived in ((1, kv1), (2, kv2), (3, kv3)):
        last = step == WIN - 1
        scratch = [pltpu.VMEM((rows, wide_k), BF16)]
        if last:
            scratch.append(pltpu.VMEM((wide_q, rows), F32))
        dqt, part = call(
            functools.partial(last_kernel if last else middle_kernel, step),
            [
                ((rows, wide_q), BF16) if last else ((wide_q, rows), F32),
                ((rows, 2 * wide_k), BF16),
            ],
            2,
            8,
            scratch,
            flops=flops // 2,
            bytes_accessed=4 << 20,
        )(slot, span_map, pos, freq, arrived, qr, do, lse, delta, dqt)
        backs.append(shifted(part, step))

    dk, dv = call(
        final_kernel,
        [((rows, wide_k), BF16), ((rows, wide_k), BF16)],
        0,
        6,
        bytes_accessed=2 << 20,
    )(wide, signed, dkv, *backs)
    return dqt, dk, dv


def solution(mesh):
    placed = (
        P("ctx", "head"),
        P("ctx", "head"),
        P("ctx", "head"),
        P("ctx", "head"),
        P("ctx", "head"),
        P("head", "ctx"),
        P(None, ("ctx", "head")),
        P(),
    )
    return jax.shard_map(
        shards,
        mesh=mesh,
        in_specs=placed,
        out_specs=(P("ctx", "head"), P("ctx", "head"), P("ctx", "head")),
        check_vma=False,
    )
```

```python
import functools
import math

import jax
import jax.numpy as jnp
import numpy as np
from jax import lax
from jax.experimental import pallas as pl
from jax.experimental.pallas import tpu as pltpu
from jax.sharding import PartitionSpec as P

HEAD = 128
HALF = HEAD // 2
WIN = 4
ROPE_BASE = 1000000.0
YARN_FACTOR = 4.0
YARN_INITIAL = 32768.0
BETA_FAST = 32.0
BETA_SLOW = 1.0
YARN_MSCALE = 1.0 + 0.1 * math.log(4.0)
ROOT_SCALE = 1.0 / math.sqrt(HEAD)
LOG2E = math.log2(math.e)
VMEM_LIMIT = 24 * 1024 * 1024

F32 = jnp.float32
BF16 = jnp.bfloat16


def frequencies():
    pair = np.arange(HALF, dtype=np.float64)
    inverse = np.exp(-2.0 * pair / HEAD * math.log(ROPE_BASE))
    ratio = YARN_INITIAL * inverse / (2.0 * math.pi)
    ramp = np.clip((ratio - BETA_SLOW) / (BETA_FAST - BETA_SLOW), 0.0, 1.0)
    return (inverse * ((1.0 - ramp) / YARN_FACTOR + ramp)).astype(np.float32)


def sine_cosine(angle):
    turns = jnp.floor(angle * (2.0 / math.pi) + 0.5)
    r = angle - turns * 1.5703125
    r = r - turns * 4.837512969970703125e-4
    r = r - turns * 7.54978995489188e-8
    r2 = r * r
    s = r + r * r2 * (-1.6666654611e-1 + r2 * (8.3321608736e-3 - r2 * 1.9515295891e-4))
    c = (
        1.0
        - 0.5 * r2
        + r2
        * r2
        * (4.166664568298827e-2 + r2 * (-1.388731625493765e-3 + r2 * 2.443315711809948e-5))
    )
    quadrant = turns.astype(jnp.int32) & 3
    odd = (quadrant & 1) == 1
    sine = jnp.where(odd, c, s)
    cosine = jnp.where(odd, s, c)
    sine = jnp.where(quadrant >= 2, -sine, sine)
    cosine = jnp.where((quadrant == 1) | (quadrant == 2), -cosine, cosine)
    return sine, cosine


def tables_transposed(place, freq):
    place = place.astype(F32)
    pair = lax.broadcasted_iota(jnp.int32, freq.shape, 0)
    first = HEAD // 8
    second = first + 3 * HEAD // 16
    chosen = jnp.where(
        pair < first, place[0:1], jnp.where(pair < second, place[1:2], place[2:3])
    )
    sine, cosine = sine_cosine(chosen * freq)
    return cosine * YARN_MSCALE, sine * YARN_MSCALE


def row_tables(cosine_t, sine_t):
    wide = jnp.concatenate([cosine_t, cosine_t], axis=0).T
    signed = jnp.concatenate([-sine_t, sine_t], axis=0).T
    return wide, signed


def rotated(x, wide, signed):
    return x * wide + pltpu.roll(x, HALF, 1) * signed


def dot_nt(a, b):
    return lax.dot_general(a, b, (((1,), (1,)), ((), ())), preferred_element_type=F32)


def dot_nn(a, b):
    return lax.dot_general(a, b, (((1,), (0,)), ((), ())), preferred_element_type=F32)


def dot_tn(a, b):
    return lax.dot_general(a, b, (((0,), (0,)), ((), ())), preferred_element_type=F32)


def pair_part(key, value, query, grad, norm, delta, causal):
    scores = dot_nt(key, query)
    weights = jnp.exp2(scores * (ROOT_SCALE * LOG2E) - norm)
    if causal:
        at_key = lax.broadcasted_iota(jnp.int32, scores.shape, 0)
        at_query = lax.broadcasted_iota(jnp.int32, scores.shape, 1)
        weights = jnp.where(at_key <= at_query, weights, 0.0)
    value_part = dot_nn(weights.astype(BF16), grad)
    score_grad = (weights * (dot_nt(value, grad) - delta)).astype(BF16)
    key_part = dot_nn(score_grad, query)
    query_part = dot_tn(key, score_grad)
    return value_part, key_part, query_part


def key_kernel(pos_ref, freq_ref, k_ref, kr_ref, tables_ref):
    cosine_t, sine_t = tables_transposed(pos_ref[...], freq_ref[...])
    tables_ref[:HALF, :] = cosine_t
    tables_ref[HALF:, :] = sine_t
    wide, signed = row_tables(cosine_t, sine_t)
    for g in range(k_ref.shape[1] // HEAD):
        cols = pl.ds(g * HEAD, HEAD)
        kr_ref[:, cols] = rotated(k_ref[:, cols].astype(F32), wide, signed).astype(BF16)


def delta_kernel(do_hbm, at_hbm, delta_ref, do_ref, at_ref, sems):
    heads = do_ref.shape[1] // HEAD
    halves = 2
    width = do_ref.shape[1] // halves
    copies = []
    for part in range(halves):
        cols = pl.ds(part * width, width)
        for i, (source, target) in enumerate(((do_hbm, do_ref), (at_hbm, at_ref))):
            copy = pltpu.make_async_copy(
                source.at[:, cols], target.at[:, cols], sems.at[2 * part + i]
            )
            copy.start()
            copies.append(copy)
    delta = jnp.zeros(delta_ref.shape, F32)
    which = lax.broadcasted_iota(jnp.int32, (heads, HEAD), 0)
    for h in range(heads):
        if h % (heads // halves) == 0:
            part = h // (heads // halves)
            copies[2 * part].wait()
            copies[2 * part + 1].wait()
        cols = pl.ds(h * HEAD, HEAD)
        product = do_ref[:, cols].astype(F32) * at_ref[:, cols].astype(F32)
        high = product.astype(BF16)
        low = (product - high.astype(F32)).astype(BF16)
        chooser = jnp.where(which == h, 1.0, 0.0).astype(BF16)
        delta = delta + dot_nt(chooser, high) + dot_nt(chooser, low)
    delta_ref[...] = delta


def first_kernel(
    tables_ref, q_hbm, kr_ref, v_ref, do_ref, lse_ref, delta_ref,
    qr_ref, dqt_ref, dkv_ref, q_ref, sems,
):
    heads = qr_ref.shape[1] // HEAD
    groups = kr_ref.shape[1] // HEAD
    size = heads // groups
    copies = []
    for g in range(groups):
        cols = pl.ds(g * size * HEAD, size * HEAD)
        copy = pltpu.make_async_copy(q_hbm.at[:, cols], q_ref.at[:, cols], sems.at[g])
        copy.start()
        copies.append(copy)
    wide, signed = row_tables(tables_ref[:HALF, :], tables_ref[HALF:, :])
    norm = lse_ref[...] * LOG2E
    delta = delta_ref[...]
    for g in range(groups):
        cols = pl.ds(g * HEAD, HEAD)
        dk = dv = None
        copies[g].wait()
        for h in range(g * size, (g + 1) * size):
            hc = pl.ds(h * HEAD, HEAD)
            query = rotated(q_ref[:, hc].astype(F32), wide, signed).astype(BF16)
            qr_ref[:, hc] = query
            v_part, k_part, q_part = pair_part(
                kr_ref[:, cols], v_ref[:, cols], query, do_ref[:, hc],
                norm[h : h + 1], delta[h : h + 1], True,
            )
            dqt_ref[hc, :] = q_part
            dv = v_part if dv is None else dv + v_part
            dk = k_part if dk is None else dk + k_part
        dkv_ref[:, cols] = dk
        dkv_ref[:, pl.ds((groups + g) * HEAD, HEAD)] = dv


def hop_body(
    step, slot_ref, span_ref, k_ref, v_ref, qr_ref, do_ref, lse_ref, delta_ref,
    dqt_in, dqt_ref, dkv_ref,
):
    rows = qr_ref.shape[0]
    half = rows // 2
    heads = qr_ref.shape[1] // HEAD
    groups = k_ref.shape[1] // HEAD
    size = heads // groups
    me = slot_ref[0]
    other = lax.rem(me + step, span_ref.shape[0])
    earlier = span_ref[other] < span_ref[me]
    norm = lse_ref[...] * LOG2E
    delta = delta_ref[...]

    def run(keys, queries):
        for g in range(groups):
            kc = pl.ds(g * HEAD, HEAD)
            vc = pl.ds((groups + g) * HEAD, HEAD)
            dk = dv = None
            for h in range(g * size, (g + 1) * size):
                hc = pl.ds(h * HEAD, HEAD)
                v_part, k_part, q_part = pair_part(
                    k_ref[keys, kc], v_ref[keys, kc], qr_ref[queries, hc], do_ref[queries, hc],
                    norm[h : h + 1, queries.start :], delta[h : h + 1, queries.start :], False,
                )
                if queries.start:
                    dqt_ref[hc, : queries.start] = dqt_in[hc, : queries.start]
                dqt_ref[hc, queries] = dqt_in[hc, queries] + q_part
                dv = v_part if dv is None else dv + v_part
                dk = k_part if dk is None else dk + k_part
            dkv_ref[keys, kc] = dk.astype(BF16)
            dkv_ref[keys, vc] = dv.astype(BF16)
        if keys.stop < rows:
            dkv_ref[keys.stop :, :] = jnp.zeros((rows - keys.stop, dkv_ref.shape[1]), BF16)

    @pl.when(earlier)
    def _():
        run(slice(0, half), slice(0, rows))

    @pl.when(jnp.logical_not(earlier))
    def _():
        run(slice(0, rows), slice(half, rows))


def last_kernel(
    step, slot_ref, span_ref, k_ref, v_ref, qr_ref, do_ref, lse_ref, delta_ref, dqt_in, tables_ref,
    out_ref, dkv_ref, dqt_ref,
):
    hop_body(
        step, slot_ref, span_ref, k_ref, v_ref, qr_ref, do_ref, lse_ref, delta_ref,
        dqt_in, dqt_ref, dkv_ref,
    )
    cosine_t = tables_ref[:HALF, :] * ROOT_SCALE
    sine_t = tables_ref[HALF:, :] * ROOT_SCALE
    for h in range(qr_ref.shape[1] // HEAD):
        y1 = dqt_ref[pl.ds(h * HEAD, HALF), :]
        y2 = dqt_ref[pl.ds(h * HEAD + HALF, HALF), :]
        turned = jnp.concatenate(
            [y1 * cosine_t + y2 * sine_t, y2 * cosine_t - y1 * sine_t], axis=0
        )
        out_ref[:, pl.ds(h * HEAD, HEAD)] = turned.T.astype(BF16)


def final_kernel(tables_ref, own_ref, a_ref, b_ref, c_ref, dk_ref, dv_ref):
    width = dk_ref.shape[1]
    wide, signed = row_tables(tables_ref[:HALF, :], tables_ref[HALF:, :])
    wide = wide * ROOT_SCALE
    signed = signed * -ROOT_SCALE
    total = (
        own_ref[...] + a_ref[...].astype(F32) + b_ref[...].astype(F32) + c_ref[...].astype(F32)
    )
    for g in range(width // HEAD):
        cols = pl.ds(g * HEAD, HEAD)
        dk_ref[:, cols] = rotated(total[:, g * HEAD : (g + 1) * HEAD], wide, signed).astype(BF16)
    dv_ref[...] = total[:, width:].astype(BF16)


SMEM = pl.BlockSpec(memory_space=pltpu.SMEM)
VMEM = pl.BlockSpec(memory_space=pltpu.VMEM)
HBM = pl.BlockSpec(memory_space=pltpu.HBM)


def call(kernel, outs, specs, scratch=(), flops=0, bytes_accessed=0):
    return pl.pallas_call(
        kernel,
        out_shape=[jax.ShapeDtypeStruct(shape, dtype) for shape, dtype in outs],
        in_specs=specs,
        out_specs=[VMEM] * len(outs),
        scratch_shapes=list(scratch),
        compiler_params=pltpu.CompilerParams(vmem_limit_bytes=VMEM_LIMIT),
        cost_estimate=pl.CostEstimate(
            flops=flops, bytes_accessed=bytes_accessed, transcendentals=0
        ),
    )


def shifted(value, steps):
    count = lax.axis_size("ctx")
    pairs = [(source, (source + steps) % count) for source in range(count)]
    return lax.ppermute(value, "ctx", pairs)


def shards(q, k, v, do, at, lse, positions, span_map):
    rows = q.shape[0]
    wide_q = q.shape[1]
    wide_k = k.shape[1]
    heads = wide_q // HEAD
    slot = lax.axis_index("ctx").astype(jnp.int32).reshape(1)
    freq = jnp.asarray(np.broadcast_to(frequencies()[:, None], (HALF, rows)).copy())

    v1 = shifted(v, -1)
    v2 = shifted(v, -2)
    pos = lax.all_gather(positions, "head", axis=1, tiled=True)
    (delta,) = call(
        delta_kernel,
        [((heads, rows), F32)],
        [HBM, HBM],
        [
            pltpu.VMEM((rows, wide_q), BF16),
            pltpu.VMEM((rows, wide_q), BF16),
            pltpu.SemaphoreType.DMA((4,)),
        ],
        flops=4 * rows * wide_q,
        bytes_accessed=4 * rows * wide_q,
    )(do, at)
    kr, tables = call(
        key_kernel,
        [((rows, wide_k), BF16), ((HEAD, rows), F32)],
        [VMEM] * 3,
        flops=100 * rows * HEAD,
        bytes_accessed=4 * rows * wide_k,
    )(pos, freq, k)
    k1 = shifted(kr, -1)
    k2 = shifted(kr, -2)
    v3 = shifted(v1, -2)
    k3 = shifted(k1, -2)

    flops = rows * rows * wide_q
    qr, dqt, dkv = call(
        first_kernel,
        [((rows, wide_q), BF16), ((wide_q, rows), F32), ((rows, 2 * wide_k), F32)],
        [VMEM, HBM] + [VMEM] * 5,
        [pltpu.VMEM((rows, wide_q), BF16), pltpu.SemaphoreType.DMA((wide_k // HEAD,))],
        flops=flops,
        bytes_accessed=1 << 20,
    )(tables, q, kr, v, do, lse, delta)

    backs = []
    for step, key, value in ((1, k1, v1), (2, k2, v2), (3, k3, v3)):
        last = step == WIN - 1
        dqt, part = call(
            functools.partial(last_kernel if last else hop_body, step),
            [
                ((rows, wide_q), BF16) if last else ((wide_q, rows), F32),
                ((rows, 2 * wide_k), BF16),
            ],
            [SMEM, SMEM] + [VMEM] * (8 if last else 7),
            [pltpu.VMEM((wide_q, rows), F32)] if last else [],
            flops=flops // 2,
            bytes_accessed=1 << 18,
        )(slot, span_map, key, value, qr, do, lse, delta, dqt, *([tables] if last else []))
        backs.append(shifted(part, step))

    dk, dv = call(
        final_kernel,
        [((rows, wide_k), BF16), ((rows, wide_k), BF16)],
        [VMEM] * 5,
        bytes_accessed=2 << 20,
    )(tables, dkv, *backs)
    return dqt, dk, dv


def solution(mesh):
    placed = (
        P("ctx", "head"),
        P("ctx", "head"),
        P("ctx", "head"),
        P("ctx", "head"),
        P("ctx", "head"),
        P("head", "ctx"),
        P(None, ("ctx", "head")),
        P(),
    )
    return jax.shard_map(
        shards,
        mesh=mesh,
        in_specs=placed,
        out_specs=(P("ctx", "head"), P("ctx", "head"), P("ctx", "head")),
        check_vma=False,
    )
```

```python
import functools
import math

import jax
import jax.numpy as jnp
import numpy as np
from jax import lax
from jax.experimental import pallas as pl
from jax.experimental.pallas import tpu as pltpu
from jax.sharding import PartitionSpec as P

HEAD = 128
HALF = HEAD // 2
WIN = 4
ROPE_BASE = 1000000.0
YARN_FACTOR = 4.0
YARN_INITIAL = 32768.0
BETA_FAST = 32.0
BETA_SLOW = 1.0
YARN_MSCALE = 1.0 + 0.1 * math.log(4.0)
ROOT_SCALE = 1.0 / math.sqrt(HEAD)
LOG2E = math.log2(math.e)
VMEM_LIMIT = 24 * 1024 * 1024

F32 = jnp.float32
BF16 = jnp.bfloat16


def frequencies():
    pair = np.arange(HALF, dtype=np.float64)
    inverse = np.exp(-2.0 * pair / HEAD * math.log(ROPE_BASE))
    ratio = YARN_INITIAL * inverse / (2.0 * math.pi)
    ramp = np.clip((ratio - BETA_SLOW) / (BETA_FAST - BETA_SLOW), 0.0, 1.0)
    return inverse * ((1.0 - ramp) / YARN_FACTOR + ramp)


def frequency_rows(lanes):
    values = frequencies()
    row = lax.broadcasted_iota(jnp.int32, (8, lanes), 0)
    tiles = []
    for first in range(0, HALF, 8):
        tile = jnp.full((8, lanes), float(values[first]), F32)
        for j in range(1, 8):
            tile = jnp.where(row == j, float(values[first + j]), tile)
        tiles.append(tile)
    return jnp.concatenate(tiles, axis=0)


def sine_cosine(angle):
    turns = jnp.floor(angle * (2.0 / math.pi) + 0.5)
    r = angle - turns * 1.5703125
    r = r - turns * 4.837512969970703125e-4
    r = r - turns * 7.54978995489188e-8
    r2 = r * r
    s = r + r * r2 * (-1.6666654611e-1 + r2 * (8.3321608736e-3 - r2 * 1.9515295891e-4))
    c = (
        1.0
        - 0.5 * r2
        + r2
        * r2
        * (4.166664568298827e-2 + r2 * (-1.388731625493765e-3 + r2 * 2.443315711809948e-5))
    )
    quadrant = turns.astype(jnp.int32) & 3
    odd = (quadrant & 1) == 1
    sine = jnp.where(odd, c, s)
    cosine = jnp.where(odd, s, c)
    sine = jnp.where(quadrant >= 2, -sine, sine)
    cosine = jnp.where((quadrant == 1) | (quadrant == 2), -cosine, cosine)
    return sine, cosine


def tables_transposed(place):
    place = place.astype(F32)
    freq = frequency_rows(place.shape[1])
    pair = lax.broadcasted_iota(jnp.int32, freq.shape, 0)
    first = HEAD // 8
    second = first + 3 * HEAD // 16
    chosen = jnp.where(
        pair < first, place[0:1], jnp.where(pair < second, place[1:2], place[2:3])
    )
    sine, cosine = sine_cosine(chosen * freq)
    return cosine * YARN_MSCALE, sine * YARN_MSCALE


def row_tables(cosine_t, sine_t):
    wide = jnp.concatenate([cosine_t, cosine_t], axis=0).T
    signed = jnp.concatenate([-sine_t, sine_t], axis=0).T
    return wide, signed


def rotated(x, wide, signed):
    return x * wide + pltpu.roll(x, HALF, 1) * signed


def dot_nt(a, b):
    return lax.dot_general(a, b, (((1,), (1,)), ((), ())), preferred_element_type=F32)


def dot_nn(a, b):
    return lax.dot_general(a, b, (((1,), (0,)), ((), ())), preferred_element_type=F32)


def dot_tn(a, b):
    return lax.dot_general(a, b, (((0,), (0,)), ((), ())), preferred_element_type=F32)


def pair_part(key, value, query, grad, norm, delta, causal):
    scores = dot_nt(key, query)
    weights = jnp.exp2(scores * (ROOT_SCALE * LOG2E) - norm)
    if causal:
        at_key = lax.broadcasted_iota(jnp.int32, scores.shape, 0)
        at_query = lax.broadcasted_iota(jnp.int32, scores.shape, 1)
        weights = jnp.where(at_key <= at_query, weights, 0.0)
    value_part = dot_nn(weights.astype(BF16), grad)
    score_grad = (weights * (dot_nt(value, grad) - delta)).astype(BF16)
    key_part = dot_nn(score_grad, query)
    query_part = dot_tn(key, score_grad)
    return value_part, key_part, query_part


def key_kernel(slot_ref, own_ref, p1_ref, p2_ref, p3_ref, k_ref, kr_ref, tables_ref):
    pieces = (own_ref[...], p1_ref[...], p2_ref[...], p3_ref[...])
    count = len(pieces)
    head = slot_ref[1]
    parts = []
    for j in range(count):
        back = lax.rem(head - j + count, count)
        part = pieces[0]
        for r in range(1, count):
            part = jnp.where(back == r, pieces[r], part)
        parts.append(part)
    cosine_t, sine_t = tables_transposed(jnp.concatenate(parts, axis=1))
    tables_ref[:HALF, :] = cosine_t
    tables_ref[HALF:, :] = sine_t
    wide, signed = row_tables(cosine_t, sine_t)
    for g in range(k_ref.shape[1] // HEAD):
        cols = pl.ds(g * HEAD, HEAD)
        kr_ref[:, cols] = rotated(k_ref[:, cols].astype(F32), wide, signed).astype(BF16)


def first_kernel(
    tables_ref, kr_ref, v_ref, lse_ref, q_hbm, do_hbm, at_hbm,
    qr_ref, do_ref, norm_ref, delta_ref, dqt_ref, dkv_ref, kv_ref, q_ref, at_ref, sems,
):
    heads = qr_ref.shape[1] // HEAD
    groups = kr_ref.shape[1] // HEAD
    size = heads // groups
    copies = []
    for g in range(groups):
        cols = pl.ds(g * size * HEAD, size * HEAD)
        for i, (source, target) in enumerate(
            ((q_hbm, q_ref), (do_hbm, do_ref), (at_hbm, at_ref))
        ):
            copy = pltpu.make_async_copy(
                source.at[:, cols], target.at[:, cols], sems.at[3 * g + i]
            )
            copy.start()
            copies.append(copy)
    wide, signed = row_tables(tables_ref[:HALF, :], tables_ref[HALF:, :])
    norm = lse_ref[...] * LOG2E
    norm_ref[...] = norm
    kv_ref[:, : groups * HEAD] = kr_ref[...]
    kv_ref[:, groups * HEAD :] = v_ref[...]
    chooser = jnp.ones((8, HEAD), BF16)
    for g in range(groups):
        cols = pl.ds(g * HEAD, HEAD)
        dk = dv = None
        for copy in copies[3 * g : 3 * g + 3]:
            copy.wait()
        for h in range(g * size, (g + 1) * size):
            hc = pl.ds(h * HEAD, HEAD)
            grad = do_ref[:, hc]
            query = rotated(q_ref[:, hc].astype(F32), wide, signed).astype(BF16)
            qr_ref[:, hc] = query
            product = grad.astype(F32) * at_ref[:, hc].astype(F32)
            high = product.astype(BF16)
            low = (product - high.astype(F32)).astype(BF16)
            delta = (dot_nt(chooser, high) + dot_nt(chooser, low))[:1]
            delta_ref[h : h + 1, :] = delta
            v_part, k_part, q_part = pair_part(
                kr_ref[:, cols], v_ref[:, cols], query, grad, norm[h : h + 1], delta, True
            )
            dqt_ref[hc, :] = q_part
            dv = v_part if dv is None else dv + v_part
            dk = k_part if dk is None else dk + k_part
        dkv_ref[:, cols] = dk
        dkv_ref[:, pl.ds((groups + g) * HEAD, HEAD)] = dv


def hop_body(
    step, slot_ref, span_ref, k_ref, v_ref, qr_ref, do_ref, norm_ref, delta_ref,
    dqt_in, dqt_ref, dkv_ref,
):
    rows = qr_ref.shape[0]
    half = rows // 2
    heads = qr_ref.shape[1] // HEAD
    groups = k_ref.shape[1] // HEAD
    size = heads // groups
    me = slot_ref[0]
    other = lax.rem(me + step, span_ref.shape[0])
    earlier = span_ref[other] < span_ref[me]
    norm = norm_ref[...]
    delta = delta_ref[...]

    def run(keys, queries):
        for g in range(groups):
            kc = pl.ds(g * HEAD, HEAD)
            vc = pl.ds((groups + g) * HEAD, HEAD)
            dk = dv = None
            for h in range(g * size, (g + 1) * size):
                hc = pl.ds(h * HEAD, HEAD)
                v_part, k_part, q_part = pair_part(
                    k_ref[keys, kc], v_ref[keys, kc], qr_ref[queries, hc], do_ref[queries, hc],
                    norm[h : h + 1, queries.start :], delta[h : h + 1, queries.start :], False,
                )
                if queries.start:
                    dqt_ref[hc, : queries.start] = dqt_in[hc, : queries.start]
                dqt_ref[hc, queries] = dqt_in[hc, queries] + q_part
                dv = v_part if dv is None else dv + v_part
                dk = k_part if dk is None else dk + k_part
            dkv_ref[keys, kc] = dk.astype(BF16)
            dkv_ref[keys, vc] = dv.astype(BF16)
        if keys.stop < rows:
            dkv_ref[keys.stop :, :] = jnp.zeros((rows - keys.stop, dkv_ref.shape[1]), BF16)

    @pl.when(earlier)
    def _():
        run(slice(0, half), slice(0, rows))

    @pl.when(jnp.logical_not(earlier))
    def _():
        run(slice(0, rows), slice(half, rows))


def last_kernel(
    step, slot_ref, span_ref, kv_ref, qr_ref, do_ref, norm_ref, delta_ref, dqt_in, tables_ref,
    out_ref, dkv_ref, dqt_ref,
):
    width = kv_ref.shape[1] // 2
    hop_body(
        step, slot_ref, span_ref, kv_ref.at[:, :width], kv_ref.at[:, width:], qr_ref, do_ref,
        norm_ref, delta_ref, dqt_in, dqt_ref, dkv_ref,
    )
    cosine_t = tables_ref[:HALF, :] * ROOT_SCALE
    sine_t = tables_ref[HALF:, :] * ROOT_SCALE
    for h in range(qr_ref.shape[1] // HEAD):
        y1 = dqt_ref[pl.ds(h * HEAD, HALF), :]
        y2 = dqt_ref[pl.ds(h * HEAD + HALF, HALF), :]
        turned = jnp.concatenate(
            [y1 * cosine_t + y2 * sine_t, y2 * cosine_t - y1 * sine_t], axis=0
        )
        out_ref[:, pl.ds(h * HEAD, HEAD)] = turned.T.astype(BF16)


def add_kernel(a_ref, b_ref, sum_ref):
    sum_ref[...] = (a_ref[...].astype(F32) + b_ref[...].astype(F32)).astype(BF16)


def final_kernel(tables_ref, own_ref, a_ref, b_ref, dk_ref, dv_ref):
    width = dk_ref.shape[1]
    wide, signed = row_tables(tables_ref[:HALF, :], tables_ref[HALF:, :])
    wide = wide * ROOT_SCALE
    signed = signed * -ROOT_SCALE
    total = own_ref[...] + a_ref[...].astype(F32) + b_ref[...].astype(F32)
    for g in range(width // HEAD):
        cols = pl.ds(g * HEAD, HEAD)
        dk_ref[:, cols] = rotated(total[:, g * HEAD : (g + 1) * HEAD], wide, signed).astype(BF16)
    dv_ref[...] = total[:, width:].astype(BF16)


SMEM = pl.BlockSpec(memory_space=pltpu.SMEM)
VMEM = pl.BlockSpec(memory_space=pltpu.VMEM)
HBM = pl.BlockSpec(memory_space=pltpu.HBM)


def call(kernel, outs, specs, scratch=(), moved=1):
    return pl.pallas_call(
        kernel,
        out_shape=[jax.ShapeDtypeStruct(shape, dtype) for shape, dtype in outs],
        in_specs=specs,
        out_specs=[VMEM] * len(outs),
        scratch_shapes=list(scratch),
        compiler_params=pltpu.CompilerParams(vmem_limit_bytes=VMEM_LIMIT),
        cost_estimate=pl.CostEstimate(
            flops=1 << 20, bytes_accessed=moved << 20, transcendentals=0
        ),
    )


def shifted(value, steps, axis="ctx"):
    count = lax.axis_size(axis)
    pairs = [(source, (source + steps) % count) for source in range(count)]
    return lax.ppermute(value, axis, pairs)


def shards(q, k, v, do, at, lse, positions, span_map):
    rows = q.shape[0]
    wide_q = q.shape[1]
    wide_k = k.shape[1]
    heads = wide_q // HEAD
    slot = jnp.stack([lax.axis_index("ctx"), lax.axis_index("head")]).astype(jnp.int32)
    q, do, at, k_here, span_map, own = (
        pltpu.with_memory_space_constraint(x, pltpu.HBM)
        for x in (q, do, at, k, span_map, positions)
    )

    pieces = [own] + [shifted(positions, r, "head") for r in (1, 2, 3)]
    v1 = shifted(v, -1)
    kr, tables = call(
        key_kernel,
        [((rows, wide_k), BF16), ((HEAD, rows), F32)],
        [SMEM] + [VMEM] * 5,
        moved=16,
    )(slot, *pieces, k_here)
    k1 = shifted(kr, -1)
    v3 = shifted(v1, -2)
    qr, grad, norm, delta, dqt, dkv, kv = call(
        first_kernel,
        [
            ((rows, wide_q), BF16),
            ((rows, wide_q), BF16),
            ((heads, rows), F32),
            ((heads, rows), F32),
            ((wide_q, rows), F32),
            ((rows, 2 * wide_k), F32),
            ((rows, 2 * wide_k), BF16),
        ],
        [VMEM] * 4 + [HBM] * 3,
        [
            pltpu.VMEM((rows, wide_q), BF16),
            pltpu.VMEM((rows, wide_q), BF16),
            pltpu.SemaphoreType.DMA((3 * (wide_k // HEAD),)),
        ],
        moved=12,
    )(tables, kr, v, lse, q, do, at)
    held, _ = lax.optimization_barrier((k1, delta))
    k3 = shifted(held, -2)
    kv2 = shifted(kv, -2)

    parts = {}
    for step, key, value in ((1, k1, v1), (3, k3, v3)):
        dqt, parts[step] = call(
            functools.partial(hop_body, step),
            [((wide_q, rows), F32), ((rows, 2 * wide_k), BF16)],
            [SMEM, SMEM] + [VMEM] * 7,
            moved=8,
        )(slot, span_map, key, value, qr, grad, norm, delta, dqt)
    back3 = shifted(parts[3], 2)
    dq, part2 = call(
        functools.partial(last_kernel, 2),
        [((rows, wide_q), BF16), ((rows, 2 * wide_k), BF16)],
        [SMEM, SMEM] + [VMEM] * 7,
        [pltpu.VMEM((wide_q, rows), F32)],
        moved=8,
    )(slot, span_map, kv2, qr, grad, norm, delta, dqt, tables)
    back2 = shifted(part2, 2)
    (part13,) = call(add_kernel, [((rows, 2 * wide_k), BF16)], [VMEM] * 2)(parts[1], back3)
    back1 = shifted(part13, 1)

    dk, dv = call(
        final_kernel,
        [((rows, wide_k), BF16), ((rows, wide_k), BF16)],
        [VMEM] * 4,
    )(tables, dkv, back1, back2)
    return dq, dk, dv


def solution(mesh):
    placed = (
        P("ctx", "head"),
        P("ctx", "head"),
        P("ctx", "head"),
        P("ctx", "head"),
        P("ctx", "head"),
        P("head", "ctx"),
        P(None, ("ctx", "head")),
        P(),
    )
    return jax.shard_map(
        shards,
        mesh=mesh,
        in_specs=placed,
        out_specs=(P("ctx", "head"), P("ctx", "head"), P("ctx", "head")),
        check_vma=False,
    )
```

```python
import functools
import math

import jax
import jax.numpy as jnp
import numpy as np
from jax import lax
from jax.experimental import pallas as pl
from jax.experimental.pallas import tpu as pltpu
from jax.sharding import PartitionSpec as P

HEAD = 128
HALF = HEAD // 2
WIN = 4
ROPE_BASE = 1000000.0
YARN_FACTOR = 4.0
YARN_INITIAL = 32768.0
BETA_FAST = 32.0
BETA_SLOW = 1.0
YARN_MSCALE = 1.0 + 0.1 * math.log(4.0)
ROOT_SCALE = 1.0 / math.sqrt(HEAD)
LOG2E = math.log2(math.e)
VMEM_LIMIT = 24 * 1024 * 1024

F32 = jnp.float32
BF16 = jnp.bfloat16


def frequencies():
    pair = np.arange(HALF, dtype=np.float64)
    inverse = np.exp(-2.0 * pair / HEAD * math.log(ROPE_BASE))
    ratio = YARN_INITIAL * inverse / (2.0 * math.pi)
    ramp = np.clip((ratio - BETA_SLOW) / (BETA_FAST - BETA_SLOW), 0.0, 1.0)
    return inverse * ((1.0 - ramp) / YARN_FACTOR + ramp)


def frequency_rows(lanes):
    values = frequencies()
    row = lax.broadcasted_iota(jnp.int32, (8, lanes), 0)
    tiles = []
    for first in range(0, HALF, 8):
        tile = jnp.full((8, lanes), float(values[first]), F32)
        for j in range(1, 8):
            tile = jnp.where(row == j, float(values[first + j]), tile)
        tiles.append(tile)
    return jnp.concatenate(tiles, axis=0)


def sine_cosine(angle):
    turns = jnp.floor(angle * (2.0 / math.pi) + 0.5)
    r = angle - turns * 1.5703125
    r = r - turns * 4.837512969970703125e-4
    r = r - turns * 7.54978995489188e-8
    r2 = r * r
    s = r + r * r2 * (-1.6666654611e-1 + r2 * (8.3321608736e-3 - r2 * 1.9515295891e-4))
    c = (
        1.0
        - 0.5 * r2
        + r2
        * r2
        * (4.166664568298827e-2 + r2 * (-1.388731625493765e-3 + r2 * 2.443315711809948e-5))
    )
    quadrant = turns.astype(jnp.int32) & 3
    odd = (quadrant & 1) == 1
    sine = jnp.where(odd, c, s)
    cosine = jnp.where(odd, s, c)
    sine = jnp.where(quadrant >= 2, -sine, sine)
    cosine = jnp.where((quadrant == 1) | (quadrant == 2), -cosine, cosine)
    return sine, cosine


def tables_transposed(place):
    freq = frequency_rows(place.shape[1])
    pair = lax.broadcasted_iota(jnp.int32, freq.shape, 0)
    first = HEAD // 8
    second = first + 3 * HEAD // 16
    chosen = jnp.where(
        pair < first, place[0:1], jnp.where(pair < second, place[1:2], place[2:3])
    )
    sine, cosine = sine_cosine(chosen * freq)
    return cosine * YARN_MSCALE, sine * YARN_MSCALE


def row_tables(cosine_t, sine_t):
    wide = jnp.concatenate([cosine_t, cosine_t], axis=0).T
    signed = jnp.concatenate([-sine_t, sine_t], axis=0).T
    return wide, signed


def rotated(x, wide, signed):
    return x * wide + pltpu.roll(x, HALF, 1) * signed


def dot_nt(a, b):
    return lax.dot_general(a, b, (((1,), (1,)), ((), ())), preferred_element_type=F32)


def dot_nn(a, b):
    return lax.dot_general(a, b, (((1,), (0,)), ((), ())), preferred_element_type=F32)


def dot_tn(a, b):
    return lax.dot_general(a, b, (((0,), (0,)), ((), ())), preferred_element_type=F32)


def pair_part(key, value, query, grad, norm, delta, causal):
    scores = dot_nt(key, query)
    weights = jnp.exp2(scores * (ROOT_SCALE * LOG2E) - norm)
    if causal:
        at_key = lax.broadcasted_iota(jnp.int32, scores.shape, 0)
        at_query = lax.broadcasted_iota(jnp.int32, scores.shape, 1)
        weights = jnp.where(at_key <= at_query, weights, 0.0)
    value_part = dot_nn(weights.astype(BF16), grad)
    score_grad = (weights * (dot_nt(value, grad) - delta)).astype(BF16)
    key_part = dot_nn(score_grad, query)
    query_part = dot_tn(key, score_grad)
    return value_part, key_part, query_part


def key_kernel(
    slot_ref, own_ref, p1_ref, p2_ref, p3_ref, k_ref, v_ref, tables_ref, kv_ref, packed_ref
):
    pieces = (own_ref[...], p1_ref[...], p2_ref[...], p3_ref[...])
    count = len(pieces)
    head = slot_ref[1]
    parts = []
    for j in range(count):
        back = lax.rem(head - j + count, count)
        part = pieces[0]
        for r in range(1, count):
            part = jnp.where(back == r, pieces[r], part)
        parts.append(part)
    place = jnp.concatenate(parts, axis=1)
    rows, width = v_ref.shape
    packed_ref[:rows, :] = v_ref[...]
    kv_ref[:, width:] = v_ref[...]
    spare = jnp.zeros((packed_ref.shape[0] - rows - 6, place.shape[1]), F32)
    packed_ref[rows:, :] = jnp.concatenate(
        [(place >> 6).astype(F32), (place & 63).astype(F32), spare], axis=0
    ).astype(BF16)
    cosine_t, sine_t = tables_transposed(place.astype(F32))
    tables_ref[:HALF, :] = cosine_t
    tables_ref[HALF:, :] = sine_t
    wide, signed = row_tables(cosine_t, sine_t)
    for g in range(width // HEAD):
        cols = pl.ds(g * HEAD, HEAD)
        kv_ref[:, cols] = rotated(k_ref[:, cols].astype(F32), wide, signed).astype(BF16)


def first_kernel(
    tables_ref, kv_ref, lse_ref, q_hbm, do_hbm, at_hbm,
    qr_ref, do_ref, norm_ref, delta_ref, dqt_ref, dkv_ref, q_ref, at_ref, sems,
):
    heads = qr_ref.shape[1] // HEAD
    groups = kv_ref.shape[1] // HEAD // 2
    size = heads // groups
    copies = []
    for g in range(groups):
        cols = pl.ds(g * size * HEAD, size * HEAD)
        for i, (source, target) in enumerate(
            ((q_hbm, q_ref), (do_hbm, do_ref), (at_hbm, at_ref))
        ):
            copy = pltpu.make_async_copy(
                source.at[:, cols], target.at[:, cols], sems.at[3 * g + i]
            )
            copy.start()
            copies.append(copy)
    wide, signed = row_tables(tables_ref[:HALF, :], tables_ref[HALF:, :])
    norm = lse_ref[...] * LOG2E
    norm_ref[...] = norm
    chooser = jnp.ones((8, HEAD), BF16)
    for g in range(groups):
        cols = pl.ds(g * HEAD, HEAD)
        dk = dv = None
        for copy in copies[3 * g : 3 * g + 3]:
            copy.wait()
        for h in range(g * size, (g + 1) * size):
            hc = pl.ds(h * HEAD, HEAD)
            grad = do_ref[:, hc]
            query = rotated(q_ref[:, hc].astype(F32), wide, signed).astype(BF16)
            qr_ref[:, hc] = query
            product = grad.astype(F32) * at_ref[:, hc].astype(F32)
            high = product.astype(BF16)
            low = (product - high.astype(F32)).astype(BF16)
            delta = (dot_nt(chooser, high) + dot_nt(chooser, low))[:1]
            delta_ref[h : h + 1, :] = delta
            v_part, k_part, q_part = pair_part(
                kv_ref[:, cols], kv_ref[:, pl.ds((groups + g) * HEAD, HEAD)], query, grad,
                norm[h : h + 1], delta, True,
            )
            dqt_ref[hc, :] = q_part
            dv = v_part if dv is None else dv + v_part
            dk = k_part if dk is None else dk + k_part
        dkv_ref[:, cols] = dk
        dkv_ref[:, pl.ds((groups + g) * HEAD, HEAD)] = dv


def hop_body(
    step, slot_ref, span_ref, k_ref, v_ref, qr_ref, do_ref, norm_ref, delta_ref,
    dqt_in, dqt_ref, dkv_ref,
):
    rows = qr_ref.shape[0]
    half = rows // 2
    heads = qr_ref.shape[1] // HEAD
    groups = k_ref.shape[1] // HEAD
    size = heads // groups
    me = slot_ref[0]
    other = lax.rem(me + step, span_ref.shape[0])
    earlier = span_ref[other] < span_ref[me]
    norm = norm_ref[...]
    delta = delta_ref[...]

    def run(keys, queries):
        for g in range(groups):
            kc = pl.ds(g * HEAD, HEAD)
            vc = pl.ds((groups + g) * HEAD, HEAD)
            dk = dv = None
            for h in range(g * size, (g + 1) * size):
                hc = pl.ds(h * HEAD, HEAD)
                v_part, k_part, q_part = pair_part(
                    k_ref[keys, kc], v_ref[keys, kc], qr_ref[queries, hc], do_ref[queries, hc],
                    norm[h : h + 1, queries.start :], delta[h : h + 1, queries.start :], False,
                )
                if queries.start:
                    dqt_ref[hc, : queries.start] = dqt_in[hc, : queries.start]
                dqt_ref[hc, queries] = dqt_in[hc, queries] + q_part
                dv = v_part if dv is None else dv + v_part
                dk = k_part if dk is None else dk + k_part
            dkv_ref[keys, kc] = dk.astype(BF16)
            dkv_ref[keys, vc] = dv.astype(BF16)
        if keys.stop < rows:
            dkv_ref[keys.stop :, :] = jnp.zeros((rows - keys.stop, dkv_ref.shape[1]), BF16)

    @pl.when(earlier)
    def _():
        run(slice(0, half), slice(0, rows))

    @pl.when(jnp.logical_not(earlier))
    def _():
        run(slice(0, rows), slice(half, rows))


def rotate_arrived(k_ref, packed_ref, key_ref):
    rows = k_ref.shape[0]
    tail = packed_ref[rows:, :].astype(F32)
    wide, signed = row_tables(*tables_transposed(tail[0:3] * 64.0 + tail[3:6]))
    for g in range(k_ref.shape[1] // HEAD):
        cols = pl.ds(g * HEAD, HEAD)
        key_ref[:, cols] = rotated(k_ref[:, cols].astype(F32), wide, signed).astype(BF16)


def raw_kernel(
    step, slot_ref, span_ref, k_ref, packed_ref, qr_ref, do_ref, norm_ref, delta_ref, dqt_in,
    dqt_ref, dkv_ref, key_ref,
):
    rotate_arrived(k_ref, packed_ref, key_ref)
    hop_body(
        step, slot_ref, span_ref, key_ref, packed_ref, qr_ref, do_ref, norm_ref, delta_ref,
        dqt_in, dqt_ref, dkv_ref,
    )


def turned_kernel(
    step, slot_ref, span_ref, kv_ref, qr_ref, do_ref, norm_ref, delta_ref, dqt_in,
    dqt_ref, dkv_ref,
):
    width = kv_ref.shape[1] // 2
    hop_body(
        step, slot_ref, span_ref, kv_ref.at[:, :width], kv_ref.at[:, width:], qr_ref, do_ref,
        norm_ref, delta_ref, dqt_in, dqt_ref, dkv_ref,
    )


def query_kernel(tables_ref, dqt_ref, own_ref, back_ref, out_ref, sum_ref):
    sum_ref[...] = own_ref[...] + back_ref[...].astype(F32)
    cosine_t = tables_ref[:HALF, :] * ROOT_SCALE
    sine_t = tables_ref[HALF:, :] * ROOT_SCALE
    for h in range(out_ref.shape[1] // HEAD):
        y1 = dqt_ref[pl.ds(h * HEAD, HALF), :]
        y2 = dqt_ref[pl.ds(h * HEAD + HALF, HALF), :]
        turned = jnp.concatenate(
            [y1 * cosine_t + y2 * sine_t, y2 * cosine_t - y1 * sine_t], axis=0
        )
        out_ref[:, pl.ds(h * HEAD, HEAD)] = turned.T.astype(BF16)


def add_kernel(a_ref, b_ref, sum_ref):
    sum_ref[...] = (a_ref[...].astype(F32) + b_ref[...].astype(F32)).astype(BF16)


def final_kernel(tables_ref, own_ref, a_ref, dk_ref, dv_ref):
    width = dk_ref.shape[1]
    wide, signed = row_tables(tables_ref[:HALF, :], tables_ref[HALF:, :])
    wide = wide * ROOT_SCALE
    signed = signed * -ROOT_SCALE
    total = own_ref[...] + a_ref[...].astype(F32)
    for g in range(width // HEAD):
        cols = pl.ds(g * HEAD, HEAD)
        dk_ref[:, cols] = rotated(total[:, g * HEAD : (g + 1) * HEAD], wide, signed).astype(BF16)
    dv_ref[...] = total[:, width:].astype(BF16)


SMEM = pl.BlockSpec(memory_space=pltpu.SMEM)
VMEM = pl.BlockSpec(memory_space=pltpu.VMEM)
HBM = pl.BlockSpec(memory_space=pltpu.HBM)


def call(kernel, outs, specs, scratch=(), moved=1):
    return pl.pallas_call(
        kernel,
        out_shape=[jax.ShapeDtypeStruct(shape, dtype) for shape, dtype in outs],
        in_specs=specs,
        out_specs=[VMEM] * len(outs),
        scratch_shapes=list(scratch),
        compiler_params=pltpu.CompilerParams(vmem_limit_bytes=VMEM_LIMIT),
        cost_estimate=pl.CostEstimate(
            flops=1 << 20, bytes_accessed=moved << 20, transcendentals=0
        ),
    )


def shifted(value, steps, axis="ctx"):
    count = lax.axis_size(axis)
    pairs = [(source, (source + steps) % count) for source in range(count)]
    return lax.ppermute(value, axis, pairs)


def shards(q, k, v, do, at, lse, positions, span_map):
    rows = q.shape[0]
    wide_q = q.shape[1]
    wide_k = k.shape[1]
    heads = wide_q // HEAD
    slot = jnp.stack([lax.axis_index("ctx"), lax.axis_index("head")]).astype(jnp.int32)
    q, do, at, k_here, v_here, span_map, own = (
        pltpu.with_memory_space_constraint(x, pltpu.HBM)
        for x in (q, do, at, k, v, span_map, positions)
    )

    k1 = shifted(k, -1)
    pieces = [own] + [shifted(positions, r, "head") for r in (1, 2, 3)]
    k1, *pieces = lax.optimization_barrier((k1, *pieces))
    tables, kv, packed = call(
        key_kernel,
        [((HEAD, rows), F32), ((rows, 2 * wide_k), BF16), ((rows + 16, wide_k), BF16)],
        [SMEM] + [VMEM] * 6,
        moved=16,
    )(slot, *pieces, k_here, v_here)
    v1 = shifted(packed, -1)
    kv2 = shifted(kv, -2)
    k3 = shifted(k1, -2)
    qr, grad, norm, delta, dqt, dkv = call(
        first_kernel,
        [
            ((rows, wide_q), BF16),
            ((rows, wide_q), BF16),
            ((heads, rows), F32),
            ((heads, rows), F32),
            ((wide_q, rows), F32),
            ((rows, 2 * wide_k), F32),
        ],
        [VMEM] * 3 + [HBM] * 3,
        [
            pltpu.VMEM((rows, wide_q), BF16),
            pltpu.VMEM((rows, wide_q), BF16),
            pltpu.SemaphoreType.DMA((3 * (wide_k // HEAD),)),
        ],
        moved=12,
    )(tables, kv, lse, q, do, at)
    held, _ = lax.optimization_barrier((v1, delta))
    v3 = shifted(held, -2)

    outs = [((wide_q, rows), F32), ((rows, 2 * wide_k), BF16)]
    turned_key = pltpu.VMEM((rows, wide_k), BF16)
    dqt, part1 = call(
        functools.partial(raw_kernel, 1), outs, [SMEM] * 2 + [VMEM] * 7, [turned_key], moved=8
    )(slot, span_map, k1, v1, qr, grad, norm, delta, dqt)
    dqt, part2 = call(
        functools.partial(turned_kernel, 2), outs, [SMEM] * 2 + [VMEM] * 6, moved=8
    )(slot, span_map, kv2, qr, grad, norm, delta, dqt)
    back2 = shifted(part2, 2)
    dqt, part3 = call(
        functools.partial(raw_kernel, 3), outs, [SMEM] * 2 + [VMEM] * 7, [turned_key], moved=8
    )(slot, span_map, k3, v3, qr, grad, norm, delta, dqt)
    back3 = shifted(part3, 2)
    dq, dkv = call(
        query_kernel, [((rows, wide_q), BF16), ((rows, 2 * wide_k), F32)], [VMEM] * 4, moved=4
    )(tables, dqt, dkv, back2)
    part1, _ = lax.optimization_barrier((part1, dkv))
    (part13,) = call(add_kernel, [((rows, 2 * wide_k), BF16)], [VMEM] * 2)(part1, back3)
    back1 = shifted(part13, 1)

    dk, dv = call(
        final_kernel,
        [((rows, wide_k), BF16), ((rows, wide_k), BF16)],
        [VMEM] * 3,
    )(tables, dkv, back1)
    return dq, dk, dv


def solution(mesh):
    placed = (
        P("ctx", "head"),
        P("ctx", "head"),
        P("ctx", "head"),
        P("ctx", "head"),
        P("ctx", "head"),
        P("head", "ctx"),
        P(None, ("ctx", "head")),
        P(),
    )
    return jax.shard_map(
        shards,
        mesh=mesh,
        in_specs=placed,
        out_specs=(P("ctx", "head"), P("ctx", "head"), P("ctx", "head")),
        check_vma=False,
    )
```

```python
import functools
import math

import jax
import jax.numpy as jnp
import numpy as np
from jax import lax
from jax.experimental import pallas as pl
from jax.experimental.pallas import tpu as pltpu
from jax.sharding import PartitionSpec as P

HEAD = 128
HALF = HEAD // 2
WIN = 4
ROPE_BASE = 1000000.0
YARN_FACTOR = 4.0
YARN_INITIAL = 32768.0
BETA_FAST = 32.0
BETA_SLOW = 1.0
YARN_MSCALE = 1.0 + 0.1 * math.log(4.0)
ROOT_SCALE = 1.0 / math.sqrt(HEAD)
LOG2E = math.log2(math.e)
VMEM_LIMIT = 24 * 1024 * 1024

F32 = jnp.float32
BF16 = jnp.bfloat16


def frequencies():
    pair = np.arange(HALF, dtype=np.float64)
    inverse = np.exp(-2.0 * pair / HEAD * math.log(ROPE_BASE))
    ratio = YARN_INITIAL * inverse / (2.0 * math.pi)
    ramp = np.clip((ratio - BETA_SLOW) / (BETA_FAST - BETA_SLOW), 0.0, 1.0)
    return inverse * ((1.0 - ramp) / YARN_FACTOR + ramp)


def frequency_rows(lanes):
    values = frequencies()
    row = lax.broadcasted_iota(jnp.int32, (8, lanes), 0)
    tiles = []
    for first in range(0, HALF, 8):
        tile = jnp.full((8, lanes), float(values[first]), F32)
        for j in range(1, 8):
            tile = jnp.where(row == j, float(values[first + j]), tile)
        tiles.append(tile)
    return jnp.concatenate(tiles, axis=0)


def sine_cosine(angle):
    turns = jnp.floor(angle * (2.0 / math.pi) + 0.5)
    r = angle - turns * 1.5703125
    r = r - turns * 4.837512969970703125e-4
    r = r - turns * 7.54978995489188e-8
    r2 = r * r
    s = r + r * r2 * (-1.6666654611e-1 + r2 * (8.3321608736e-3 - r2 * 1.9515295891e-4))
    c = (
        1.0
        - 0.5 * r2
        + r2
        * r2
        * (4.166664568298827e-2 + r2 * (-1.388731625493765e-3 + r2 * 2.443315711809948e-5))
    )
    quadrant = turns.astype(jnp.int32) & 3
    odd = (quadrant & 1) == 1
    sine = jnp.where(odd, c, s)
    cosine = jnp.where(odd, s, c)
    sine = jnp.where(quadrant >= 2, -sine, sine)
    cosine = jnp.where((quadrant == 1) | (quadrant == 2), -cosine, cosine)
    return sine, cosine


def tables_transposed(place):
    freq = frequency_rows(place.shape[1])
    pair = lax.broadcasted_iota(jnp.int32, freq.shape, 0)
    first = HEAD // 8
    second = first + 3 * HEAD // 16
    chosen = jnp.where(
        pair < first, place[0:1], jnp.where(pair < second, place[1:2], place[2:3])
    )
    sine, cosine = sine_cosine(chosen * freq)
    return cosine * YARN_MSCALE, sine * YARN_MSCALE


def row_tables(cosine_t, sine_t):
    wide = jnp.concatenate([cosine_t, cosine_t], axis=0).T
    signed = jnp.concatenate([-sine_t, sine_t], axis=0).T
    return wide, signed


def rotated(x, wide, signed):
    return x * wide + pltpu.roll(x, HALF, 1) * signed


def dot_nt(a, b):
    return lax.dot_general(a, b, (((1,), (1,)), ((), ())), preferred_element_type=F32)


def dot_nn(a, b):
    return lax.dot_general(a, b, (((1,), (0,)), ((), ())), preferred_element_type=F32)


def dot_tn(a, b):
    return lax.dot_general(a, b, (((0,), (0,)), ((), ())), preferred_element_type=F32)


def pair_part(key, value, query, grad, norm, delta, causal):
    scores = dot_nt(key, query)
    weights = jnp.exp2(scores * (ROOT_SCALE * LOG2E) - norm)
    if causal:
        at_key = lax.broadcasted_iota(jnp.int32, scores.shape, 0)
        at_query = lax.broadcasted_iota(jnp.int32, scores.shape, 1)
        weights = jnp.where(at_key <= at_query, weights, 0.0)
    value_part = dot_nn(weights.astype(BF16), grad)
    score_grad = (weights * (dot_nt(value, grad) - delta)).astype(BF16)
    key_part = dot_nn(score_grad, query)
    query_part = dot_tn(key, score_grad)
    return value_part, key_part, query_part


def merge_kernel(k_hbm, v_hbm, kv_ref, sems):
    width = k_hbm.shape[1]
    copies = [
        pltpu.make_async_copy(k_hbm, kv_ref.at[:, :width], sems.at[0]),
        pltpu.make_async_copy(v_hbm, kv_ref.at[:, width:], sems.at[1]),
    ]
    for copy in copies:
        copy.start()
    for copy in copies:
        copy.wait()


def key_kernel(
    slot_ref, own_ref, p1_ref, p2_ref, p3_ref, raw_ref, tables_ref, kv_ref, packed_ref
):
    pieces = (own_ref[...], p1_ref[...], p2_ref[...], p3_ref[...])
    count = len(pieces)
    head = slot_ref[1]
    parts = []
    for j in range(count):
        back = lax.rem(head - j + count, count)
        part = pieces[0]
        for r in range(1, count):
            part = jnp.where(back == r, pieces[r], part)
        parts.append(part)
    place = jnp.concatenate(parts, axis=1)
    width = raw_ref.shape[1] // 2
    spare = jnp.zeros((packed_ref.shape[0] - 6, place.shape[1]), F32)
    packed_ref[...] = jnp.concatenate(
        [(place >> 6).astype(F32), (place & 63).astype(F32), spare], axis=0
    ).astype(BF16)
    cosine_t, sine_t = tables_transposed(place.astype(F32))
    tables_ref[:HALF, :] = cosine_t
    tables_ref[HALF:, :] = sine_t
    wide, signed = row_tables(cosine_t, sine_t)
    kv_ref[:, width:] = raw_ref[:, width:]
    for g in range(width // HEAD):
        cols = pl.ds(g * HEAD, HEAD)
        kv_ref[:, cols] = rotated(raw_ref[:, cols].astype(F32), wide, signed).astype(BF16)


def first_kernel(
    tables_ref, kv_ref, lse_hbm, q_hbm, do_hbm, at_hbm,
    qr_ref, do_ref, norm_ref, delta_ref, *rest,
):
    heads = qr_ref.shape[1] // HEAD
    groups = kv_ref.shape[1] // HEAD // 2
    dqt_refs, part_refs = rest[:groups], rest[groups : 2 * groups]
    q_ref, at_ref, lse_ref, sems = rest[2 * groups :]
    size = heads // groups
    copies = []
    lse_copy = pltpu.make_async_copy(lse_hbm, lse_ref, sems.at[3 * groups])
    lse_copy.start()
    for g in range(groups):
        cols = pl.ds(g * size * HEAD, size * HEAD)
        for i, (source, target) in enumerate(
            ((q_hbm, q_ref), (do_hbm, do_ref), (at_hbm, at_ref))
        ):
            copy = pltpu.make_async_copy(
                source.at[:, cols], target.at[:, cols], sems.at[3 * g + i]
            )
            copy.start()
            copies.append(copy)
    wide, signed = row_tables(tables_ref[:HALF, :], tables_ref[HALF:, :])
    lse_copy.wait()
    norm = lse_ref[...] * LOG2E
    norm_ref[...] = norm
    chooser = jnp.ones((8, HEAD), BF16)
    for g in range(groups):
        cols = pl.ds(g * HEAD, HEAD)
        dk = dv = None
        for copy in copies[3 * g : 3 * g + 3]:
            copy.wait()
        for h in range(g * size, (g + 1) * size):
            hc = pl.ds(h * HEAD, HEAD)
            grad = do_ref[:, hc]
            query = rotated(q_ref[:, hc].astype(F32), wide, signed).astype(BF16)
            qr_ref[:, hc] = query
            product = grad.astype(F32) * at_ref[:, hc].astype(F32)
            high = product.astype(BF16)
            low = (product - high.astype(F32)).astype(BF16)
            delta = (dot_nt(chooser, high) + dot_nt(chooser, low))[:1]
            delta_ref[h : h + 1, :] = delta
            v_part, k_part, q_part = pair_part(
                kv_ref[:, cols], kv_ref[:, pl.ds((groups + g) * HEAD, HEAD)], query, grad,
                norm[h : h + 1], delta, True,
            )
            dqt_refs[g][pl.ds((h - g * size) * HEAD, HEAD), :] = q_part
            dv = v_part if dv is None else dv + v_part
            dk = k_part if dk is None else dk + k_part
        part_refs[g][:, :HEAD] = dk
        part_refs[g][:, HEAD:] = dv


def hop_body(
    step, wanted, slot_ref, span_ref, k_ref, v_ref, qr_ref, do_ref, norm_ref, delta_ref,
    dqt_ins, dqt_refs, part_refs,
):
    rows = qr_ref.shape[0]
    half = rows // 2
    heads = qr_ref.shape[1] // HEAD
    groups = k_ref.shape[1] // HEAD
    size = heads // groups
    me = slot_ref[0]
    other = lax.rem(me + step, span_ref.shape[0])
    earlier = span_ref[other] < span_ref[me]
    norm = norm_ref[...]
    delta = delta_ref[...]

    def run(keys, queries):
        for g, dqt_in, dqt_ref, part_ref in zip(wanted, dqt_ins, dqt_refs, part_refs):
            kc = pl.ds(g * HEAD, HEAD)
            dk = dv = None
            for j in range(size):
                h = g * size + j
                hc = pl.ds(h * HEAD, HEAD)
                to = pl.ds(j * HEAD, HEAD)
                v_part, k_part, q_part = pair_part(
                    k_ref[keys, kc], v_ref[keys, kc], qr_ref[queries, hc], do_ref[queries, hc],
                    norm[h : h + 1, queries.start :], delta[h : h + 1, queries.start :], False,
                )
                if queries.start:
                    dqt_ref[to, : queries.start] = dqt_in[to, : queries.start]
                dqt_ref[to, queries] = dqt_in[to, queries] + q_part
                dv = v_part if dv is None else dv + v_part
                dk = k_part if dk is None else dk + k_part
            part_ref[keys, :HEAD] = dk.astype(BF16)
            part_ref[keys, HEAD:] = dv.astype(BF16)
            if keys.stop < rows:
                part_ref[keys.stop :, :] = jnp.zeros((rows - keys.stop, 2 * HEAD), BF16)

    @pl.when(earlier)
    def _():
        run(slice(0, half), slice(0, rows))

    @pl.when(jnp.logical_not(earlier))
    def _():
        run(slice(0, rows), slice(half, rows))


def spread(refs, wanted):
    count = len(wanted)
    dqt_ins, dqt_refs, part_refs = refs[:count], refs[count : 2 * count], refs[2 * count :]
    if len(part_refs) < count:
        (part_ref,) = part_refs
        part_refs = [part_ref.at[:, 2 * HEAD * i : 2 * HEAD * (i + 1)] for i in range(count)]
    return dqt_ins, dqt_refs, part_refs


def raw_kernel(
    step, wanted, slot_ref, span_ref, kv_ref, packed_ref, qr_ref, do_ref, norm_ref, delta_ref,
    *rest,
):
    key_ref = rest[-1]
    width = kv_ref.shape[1] // 2
    place = packed_ref[...].astype(F32)
    wide, signed = row_tables(*tables_transposed(place[0:3] * 64.0 + place[3:6]))
    for g in wanted:
        cols = pl.ds(g * HEAD, HEAD)
        key_ref[:, cols] = rotated(kv_ref[:, cols].astype(F32), wide, signed).astype(BF16)
    hop_body(
        step, wanted, slot_ref, span_ref, key_ref, kv_ref.at[:, width:], qr_ref, do_ref, norm_ref,
        delta_ref, *spread(rest[:-1], wanted),
    )


def turned_kernel(
    step, wanted, slot_ref, span_ref, kv_ref, qr_ref, do_ref, norm_ref, delta_ref, *rest
):
    width = kv_ref.shape[1] // 2
    hop_body(
        step, wanted, slot_ref, span_ref, kv_ref.at[:, :width], kv_ref.at[:, width:], qr_ref,
        do_ref, norm_ref, delta_ref, *spread(rest, wanted),
    )


def query_kernel(groups, tables_ref, *refs):
    dqt_refs, own_refs, back_ref = refs[:groups], refs[groups : 2 * groups], refs[2 * groups]
    out_ref, sum_refs = refs[2 * groups + 1], refs[2 * groups + 2 :]
    cosine_t = tables_ref[:HALF, :] * ROOT_SCALE
    sine_t = tables_ref[HALF:, :] * ROOT_SCALE
    size = dqt_refs[0].shape[0] // HEAD
    for g in range(groups):
        sum_refs[g][...] = own_refs[g][...] + back_ref[
            :, 2 * HEAD * g : 2 * HEAD * (g + 1)
        ].astype(F32)
        for j in range(size):
            y1 = dqt_refs[g][pl.ds(j * HEAD, HALF), :]
            y2 = dqt_refs[g][pl.ds(j * HEAD + HALF, HALF), :]
            turned = jnp.concatenate(
                [y1 * cosine_t + y2 * sine_t, y2 * cosine_t - y1 * sine_t], axis=0
            )
            out_ref[:, pl.ds((g * size + j) * HEAD, HEAD)] = turned.T.astype(BF16)


def add_kernel(a_ref, b_ref, sum_ref):
    sum_ref[...] = (a_ref[...].astype(F32) + b_ref[...].astype(F32)).astype(BF16)


def final_kernel(groups, tables_ref, *refs):
    own, back = refs[:groups], refs[groups : 2 * groups]
    dk_ref, dv_ref = refs[2 * groups :]
    wide, signed = row_tables(tables_ref[:HALF, :], tables_ref[HALF:, :])
    wide = wide * ROOT_SCALE
    signed = signed * -ROOT_SCALE
    for g in range(groups):
        cols = pl.ds(g * HEAD, HEAD)
        total = own[g][...] + back[g][...].astype(F32)
        dk_ref[:, cols] = rotated(total[:, :HEAD], wide, signed).astype(BF16)
        dv_ref[:, cols] = total[:, HEAD:].astype(BF16)


SMEM = pl.BlockSpec(memory_space=pltpu.SMEM)
VMEM = pl.BlockSpec(memory_space=pltpu.VMEM)
HBM = pl.BlockSpec(memory_space=pltpu.HBM)


def call(kernel, outs, specs, scratch=()):
    return pl.pallas_call(
        kernel,
        out_shape=[jax.ShapeDtypeStruct(shape, dtype) for shape, dtype in outs],
        in_specs=specs,
        out_specs=[VMEM] * len(outs),
        scratch_shapes=list(scratch),
        compiler_params=pltpu.CompilerParams(vmem_limit_bytes=VMEM_LIMIT),
        cost_estimate=pl.CostEstimate(
            flops=1 << 20, bytes_accessed=1 << 18, transcendentals=0
        ),
    )


def shifted(value, steps, axis="ctx"):
    count = lax.axis_size(axis)
    pairs = [(source, (source + steps) % count) for source in range(count)]
    return lax.ppermute(value, axis, pairs)


def shards(q, k, v, do, at, lse, positions, span_map):
    rows = q.shape[0]
    wide_q = q.shape[1]
    wide_k = k.shape[1]
    heads = wide_q // HEAD
    slot = jnp.stack([lax.axis_index("ctx"), lax.axis_index("head")]).astype(jnp.int32)
    groups = wide_k // HEAD
    size = heads // groups
    q, do, at, k, v, lse, span_map, own = (
        pltpu.with_memory_space_constraint(x, pltpu.HBM)
        for x in (q, do, at, k, v, lse, span_map, positions)
    )
    dq_out = ((size * HEAD, rows), F32)
    part_out = ((rows, 2 * HEAD), BF16)

    (raw,) = call(
        merge_kernel,
        [((rows, 2 * wide_k), BF16)],
        [HBM] * 2,
        [pltpu.SemaphoreType.DMA((2,))],
    )(k, v)
    raw1 = shifted(raw, -1)
    pieces = [own] + [shifted(positions, r, "head") for r in (1, 2, 3)]
    tables, kv, packed = call(
        key_kernel,
        [((HEAD, rows), F32), ((rows, 2 * wide_k), BF16), ((16, rows), BF16)],
        [SMEM] + [VMEM] * 5,
    )(slot, *pieces, raw)
    packed1 = shifted(packed, -1)
    raw1, _ = lax.optimization_barrier((raw1, tables))
    raw3 = shifted(raw1, -2)
    packed3 = shifted(packed, -3)

    qr, grad, norm, delta, *rest = call(
        first_kernel,
        [((rows, wide_q), BF16)] * 2
        + [((heads, rows), F32)] * 2
        + [dq_out] * groups
        + [((rows, 2 * HEAD), F32)] * groups,
        [VMEM] * 2 + [HBM] * 4,
        [
            pltpu.VMEM((rows, wide_q), BF16),
            pltpu.VMEM((rows, wide_q), BF16),
            pltpu.VMEM((heads, rows), F32),
            pltpu.SemaphoreType.DMA((3 * groups + 1,)),
        ],
    )(tables, kv, lse, q, do, at)
    dqs, owns = rest[:groups], rest[groups:]
    held, packed1, packed3, _ = lax.optimization_barrier((kv, packed1, packed3, delta))
    kv2 = shifted(held, -2)

    shared = (qr, grad, norm, delta)
    key = pltpu.VMEM((rows, wide_k), BF16)

    def hop(kernel, step, wanted, arrived, dqs, split, scratch=()):
        count = len(wanted)
        outs = [part_out] * count if split else [((rows, count * 2 * HEAD), BF16)]
        results = call(
            functools.partial(kernel, step, wanted),
            [dq_out] * count + outs,
            [SMEM] * 2 + [VMEM] * (4 + len(arrived) + count),
            scratch,
        )(slot, span_map, *arrived, *shared, *(dqs[g] for g in wanted))
        for i, g in enumerate(wanted):
            dqs[g] = results[i]
        return results[count:]

    every = tuple(range(groups))
    dqs = list(dqs)
    (part1,) = hop(raw_kernel, 1, every, (raw1, packed1), dqs, False, [key])
    back1 = shifted(part1, 1)
    backs3 = []
    for g in every:
        (part3,) = hop(raw_kernel, 3, (g,), (raw3, packed3), dqs, True, [key])
        backs3.append(shifted(part3, 1))
    parts2 = hop(turned_kernel, 2, every, (kv2,), dqs, True)
    dq, *owns = call(
        functools.partial(query_kernel, groups),
        [((rows, wide_q), BF16)] + [((rows, 2 * HEAD), F32)] * groups,
        [VMEM] * (2 + 2 * groups),
    )(tables, *dqs, *owns, back1)
    *parts2, _ = lax.optimization_barrier((*parts2, owns[0]))
    backs2 = []
    for part, back in zip(parts2, backs3):
        (total,) = call(add_kernel, [part_out], [VMEM] * 2)(part, back)
        backs2.append(shifted(total, 2))

    dk, dv = call(
        functools.partial(final_kernel, groups),
        [((rows, wide_k), BF16), ((rows, wide_k), BF16)],
        [VMEM] * (1 + 2 * groups),
    )(tables, *owns, *backs2)
    return dq, dk, dv


def solution(mesh):
    placed = (
        P("ctx", "head"),
        P("ctx", "head"),
        P("ctx", "head"),
        P("ctx", "head"),
        P("ctx", "head"),
        P("head", "ctx"),
        P(None, ("ctx", "head")),
        P(),
    )
    return jax.shard_map(
        shards,
        mesh=mesh,
        in_specs=placed,
        out_specs=(P("ctx", "head"), P("ctx", "head"), P("ctx", "head")),
        check_vma=False,
    )
```

```python
import functools
import math

import jax
import jax.numpy as jnp
import numpy as np
from jax import lax
from jax.experimental import pallas as pl
from jax.experimental.pallas import tpu as pltpu
from jax.sharding import PartitionSpec as P

HEAD = 128
HALF = HEAD // 2
WIN = 4
ROPE_BASE = 1000000.0
YARN_FACTOR = 4.0
YARN_INITIAL = 32768.0
BETA_FAST = 32.0
BETA_SLOW = 1.0
YARN_MSCALE = 1.0 + 0.1 * math.log(4.0)
ROOT_SCALE = 1.0 / math.sqrt(HEAD)
LOG2E = math.log2(math.e)
VMEM_LIMIT = 24 * 1024 * 1024

F32 = jnp.float32
BF16 = jnp.bfloat16


def frequencies():
    pair = np.arange(HALF, dtype=np.float64)
    inverse = np.exp(-2.0 * pair / HEAD * math.log(ROPE_BASE))
    ratio = YARN_INITIAL * inverse / (2.0 * math.pi)
    ramp = np.clip((ratio - BETA_SLOW) / (BETA_FAST - BETA_SLOW), 0.0, 1.0)
    return inverse * ((1.0 - ramp) / YARN_FACTOR + ramp)


def frequency_rows(lanes):
    values = frequencies()
    row = lax.broadcasted_iota(jnp.int32, (8, lanes), 0)
    tiles = []
    for first in range(0, HALF, 8):
        tile = jnp.full((8, lanes), float(values[first]), F32)
        for j in range(1, 8):
            tile = jnp.where(row == j, float(values[first + j]), tile)
        tiles.append(tile)
    return jnp.concatenate(tiles, axis=0)


def sine_cosine(angle):
    turns = jnp.floor(angle * (2.0 / math.pi) + 0.5)
    r = angle - turns * 1.5703125
    r = r - turns * 4.837512969970703125e-4
    r = r - turns * 7.54978995489188e-8
    r2 = r * r
    s = r + r * r2 * (-1.6666654611e-1 + r2 * (8.3321608736e-3 - r2 * 1.9515295891e-4))
    c = (
        1.0
        - 0.5 * r2
        + r2
        * r2
        * (4.166664568298827e-2 + r2 * (-1.388731625493765e-3 + r2 * 2.443315711809948e-5))
    )
    quadrant = turns.astype(jnp.int32) & 3
    odd = (quadrant & 1) == 1
    sine = jnp.where(odd, c, s)
    cosine = jnp.where(odd, s, c)
    sine = jnp.where(quadrant >= 2, -sine, sine)
    cosine = jnp.where((quadrant == 1) | (quadrant == 2), -cosine, cosine)
    return sine, cosine


def tables_transposed(place):
    place = place.astype(F32)
    freq = frequency_rows(place.shape[1])
    pair = lax.broadcasted_iota(jnp.int32, freq.shape, 0)
    first = HEAD // 8
    second = first + 3 * HEAD // 16
    chosen = jnp.where(
        pair < first, place[0:1], jnp.where(pair < second, place[1:2], place[2:3])
    )
    sine, cosine = sine_cosine(chosen * freq)
    return cosine * YARN_MSCALE, sine * YARN_MSCALE


def row_tables(cosine_t, sine_t):
    wide = jnp.concatenate([cosine_t, cosine_t], axis=0).T
    signed = jnp.concatenate([-sine_t, sine_t], axis=0).T
    return wide, signed


def rotated(x, wide, signed):
    return x * wide + pltpu.roll(x, HALF, 1) * signed


def dot_nt(a, b):
    return lax.dot_general(a, b, (((1,), (1,)), ((), ())), preferred_element_type=F32)


def dot_nn(a, b):
    return lax.dot_general(a, b, (((1,), (0,)), ((), ())), preferred_element_type=F32)


def dot_tn(a, b):
    return lax.dot_general(a, b, (((0,), (0,)), ((), ())), preferred_element_type=F32)


def pair_part(key, value, query, grad, norm, delta, causal):
    scores = dot_nt(key, query)
    weights = jnp.exp2(scores * (ROOT_SCALE * LOG2E) - norm)
    if causal:
        at_key = lax.broadcasted_iota(jnp.int32, scores.shape, 0)
        at_query = lax.broadcasted_iota(jnp.int32, scores.shape, 1)
        weights = jnp.where(at_key <= at_query, weights, 0.0)
    value_part = dot_nn(weights.astype(BF16), grad)
    score_grad = (weights * (dot_nt(value, grad) - delta)).astype(BF16)
    key_part = dot_nn(score_grad, query)
    query_part = dot_tn(key, score_grad)
    return value_part, key_part, query_part


def key_kernel(slot_ref, own_ref, p1_ref, p2_ref, p3_ref, k_ref, kr_ref, tables_ref):
    pieces = (own_ref[...], p1_ref[...], p2_ref[...], p3_ref[...])
    count = len(pieces)
    head = slot_ref[1]
    parts = []
    for j in range(count):
        back = lax.rem(head - j + count, count)
        part = pieces[0]
        for r in range(1, count):
            part = jnp.where(back == r, pieces[r], part)
        parts.append(part)
    cosine_t, sine_t = tables_transposed(jnp.concatenate(parts, axis=1))
    tables_ref[:HALF, :] = cosine_t
    tables_ref[HALF:, :] = sine_t
    wide, signed = row_tables(cosine_t, sine_t)
    for g in range(k_ref.shape[1] // HEAD):
        cols = pl.ds(g * HEAD, HEAD)
        kr_ref[:, cols] = rotated(k_ref[:, cols].astype(F32), wide, signed).astype(BF16)


def first_kernel(
    tables_ref, kr_ref, v_ref, lse_ref, q_hbm, do_hbm, at_hbm,
    qr_ref, do_ref, norm_ref, delta_ref, dqt_ref, dkv_ref, kv_ref, q_ref, at_ref, sems,
):
    heads = qr_ref.shape[1] // HEAD
    groups = kr_ref.shape[1] // HEAD
    size = heads // groups
    copies = []
    for g in range(groups):
        cols = pl.ds(g * size * HEAD, size * HEAD)
        for i, (source, target) in enumerate(
            ((q_hbm, q_ref), (do_hbm, do_ref), (at_hbm, at_ref))
        ):
            copy = pltpu.make_async_copy(
                source.at[:, cols], target.at[:, cols], sems.at[3 * g + i]
            )
            copy.start()
            copies.append(copy)
    wide, signed = row_tables(tables_ref[:HALF, :], tables_ref[HALF:, :])
    norm = lse_ref[...] * LOG2E
    norm_ref[...] = norm
    kv_ref[:, : groups * HEAD] = kr_ref[...]
    kv_ref[:, groups * HEAD :] = v_ref[...]
    chooser = jnp.ones((8, HEAD), BF16)
    for g in range(groups):
        cols = pl.ds(g * HEAD, HEAD)
        dk = dv = None
        for copy in copies[3 * g : 3 * g + 3]:
            copy.wait()
        for h in range(g * size, (g + 1) * size):
            hc = pl.ds(h * HEAD, HEAD)
            grad = do_ref[:, hc]
            query = rotated(q_ref[:, hc].astype(F32), wide, signed).astype(BF16)
            qr_ref[:, hc] = query
            product = grad.astype(F32) * at_ref[:, hc].astype(F32)
            high = product.astype(BF16)
            low = (product - high.astype(F32)).astype(BF16)
            delta = (dot_nt(chooser, high) + dot_nt(chooser, low))[:1]
            delta_ref[h : h + 1, :] = delta
            v_part, k_part, q_part = pair_part(
                kr_ref[:, cols], v_ref[:, cols], query, grad, norm[h : h + 1], delta, True
            )
            dqt_ref[hc, :] = q_part
            dv = v_part if dv is None else dv + v_part
            dk = k_part if dk is None else dk + k_part
        dkv_ref[:, cols] = dk
        dkv_ref[:, pl.ds((groups + g) * HEAD, HEAD)] = dv


def hop_body(
    step, slot_ref, span_ref, k_ref, v_ref, qr_ref, do_ref, norm_ref, delta_ref,
    dqt_in, dqt_ref, dkv_ref,
):
    rows = qr_ref.shape[0]
    half = rows // 2
    heads = qr_ref.shape[1] // HEAD
    groups = k_ref.shape[1] // HEAD
    size = heads // groups
    me = slot_ref[0]
    other = lax.rem(me + step, span_ref.shape[0])
    earlier = span_ref[other] < span_ref[me]
    norm = norm_ref[...]
    delta = delta_ref[...]

    def run(keys, queries):
        for g in range(groups):
            kc = pl.ds(g * HEAD, HEAD)
            vc = pl.ds((groups + g) * HEAD, HEAD)
            dk = dv = None
            for h in range(g * size, (g + 1) * size):
                hc = pl.ds(h * HEAD, HEAD)
                v_part, k_part, q_part = pair_part(
                    k_ref[keys, kc], v_ref[keys, kc], qr_ref[queries, hc], do_ref[queries, hc],
                    norm[h : h + 1, queries.start :], delta[h : h + 1, queries.start :], False,
                )
                if queries.start:
                    dqt_ref[hc, : queries.start] = dqt_in[hc, : queries.start]
                dqt_ref[hc, queries] = dqt_in[hc, queries] + q_part
                dv = v_part if dv is None else dv + v_part
                dk = k_part if dk is None else dk + k_part
            dkv_ref[keys, kc] = dk.astype(BF16)
            dkv_ref[keys, vc] = dv.astype(BF16)
        if keys.stop < rows:
            dkv_ref[keys.stop :, :] = jnp.zeros((rows - keys.stop, dkv_ref.shape[1]), BF16)

    @pl.when(earlier)
    def _():
        run(slice(0, half), slice(0, rows))

    @pl.when(jnp.logical_not(earlier))
    def _():
        run(slice(0, rows), slice(half, rows))


def turned_kernel(
    step, slot_ref, span_ref, kv_ref, qr_ref, do_ref, norm_ref, delta_ref, dqt_in,
    dqt_ref, dkv_ref,
):
    width = kv_ref.shape[1] // 2
    hop_body(
        step, slot_ref, span_ref, kv_ref.at[:, :width], kv_ref.at[:, width:], qr_ref, do_ref,
        norm_ref, delta_ref, dqt_in, dqt_ref, dkv_ref,
    )


def query_kernel(tables_ref, dqt_ref, own_ref, back_ref, out_ref, sum_ref):
    sum_ref[...] = own_ref[...] + back_ref[...].astype(F32)
    cosine_t = tables_ref[:HALF, :] * ROOT_SCALE
    sine_t = tables_ref[HALF:, :] * ROOT_SCALE
    for h in range(out_ref.shape[1] // HEAD):
        y1 = dqt_ref[pl.ds(h * HEAD, HALF), :]
        y2 = dqt_ref[pl.ds(h * HEAD + HALF, HALF), :]
        turned = jnp.concatenate(
            [y1 * cosine_t + y2 * sine_t, y2 * cosine_t - y1 * sine_t], axis=0
        )
        out_ref[:, pl.ds(h * HEAD, HEAD)] = turned.T.astype(BF16)


def add_kernel(a_ref, b_ref, sum_ref):
    sum_ref[...] = (a_ref[...].astype(F32) + b_ref[...].astype(F32)).astype(BF16)


def final_kernel(tables_ref, own_ref, a_ref, dk_ref, dv_ref):
    width = dk_ref.shape[1]
    wide, signed = row_tables(tables_ref[:HALF, :], tables_ref[HALF:, :])
    wide = wide * ROOT_SCALE
    signed = signed * -ROOT_SCALE
    total = own_ref[...] + a_ref[...].astype(F32)
    for g in range(width // HEAD):
        cols = pl.ds(g * HEAD, HEAD)
        dk_ref[:, cols] = rotated(total[:, g * HEAD : (g + 1) * HEAD], wide, signed).astype(BF16)
    dv_ref[...] = total[:, width:].astype(BF16)


SMEM = pl.BlockSpec(memory_space=pltpu.SMEM)
VMEM = pl.BlockSpec(memory_space=pltpu.VMEM)
HBM = pl.BlockSpec(memory_space=pltpu.HBM)


def call(kernel, outs, specs, scratch=(), moved=1):
    return pl.pallas_call(
        kernel,
        out_shape=[jax.ShapeDtypeStruct(shape, dtype) for shape, dtype in outs],
        in_specs=specs,
        out_specs=[VMEM] * len(outs),
        scratch_shapes=list(scratch),
        compiler_params=pltpu.CompilerParams(vmem_limit_bytes=VMEM_LIMIT),
        cost_estimate=pl.CostEstimate(
            flops=1 << 20, bytes_accessed=moved << 20, transcendentals=0
        ),
    )


def shifted(value, steps, axis="ctx"):
    count = lax.axis_size(axis)
    pairs = [(source, (source + steps) % count) for source in range(count)]
    return lax.ppermute(value, axis, pairs)


def shards(q, k, v, do, at, lse, positions, span_map):
    rows = q.shape[0]
    wide_q = q.shape[1]
    wide_k = k.shape[1]
    heads = wide_q // HEAD
    slot = jnp.stack([lax.axis_index("ctx"), lax.axis_index("head")]).astype(jnp.int32)
    q, do, at, k_here, span_map, own = (
        pltpu.with_memory_space_constraint(x, pltpu.HBM)
        for x in (q, do, at, k, span_map, positions)
    )

    pieces = [own] + [shifted(positions, r, "head") for r in (1, 2, 3)]
    v1 = shifted(v, -1)
    kr, tables = call(
        key_kernel,
        [((rows, wide_k), BF16), ((HEAD, rows), F32)],
        [SMEM] + [VMEM] * 5,
        moved=16,
    )(slot, *pieces, k_here)
    k1 = shifted(kr, -1)
    v3 = shifted(v1, -2)
    qr, grad, norm, delta, dqt, dkv, kv = call(
        first_kernel,
        [
            ((rows, wide_q), BF16),
            ((rows, wide_q), BF16),
            ((heads, rows), F32),
            ((heads, rows), F32),
            ((wide_q, rows), F32),
            ((rows, 2 * wide_k), F32),
            ((rows, 2 * wide_k), BF16),
        ],
        [VMEM] * 4 + [HBM] * 3,
        [
            pltpu.VMEM((rows, wide_q), BF16),
            pltpu.VMEM((rows, wide_q), BF16),
            pltpu.SemaphoreType.DMA((3 * (wide_k // HEAD),)),
        ],
        moved=12,
    )(tables, kr, v, lse, q, do, at)
    held, _ = lax.optimization_barrier((k1, delta))
    k3 = shifted(held, -2)
    kv2 = shifted(kv, -2)

    outs = [((wide_q, rows), F32), ((rows, 2 * wide_k), BF16)]
    dqt, part1 = call(
        functools.partial(hop_body, 1), outs, [SMEM] * 2 + [VMEM] * 7, moved=8
    )(slot, span_map, k1, v1, qr, grad, norm, delta, dqt)
    back1 = shifted(part1, 1)
    dqt, part3 = call(
        functools.partial(hop_body, 3), outs, [SMEM] * 2 + [VMEM] * 7, moved=8
    )(slot, span_map, k3, v3, qr, grad, norm, delta, dqt)
    back3 = shifted(part3, 1)
    dqt, part2 = call(
        functools.partial(turned_kernel, 2), outs, [SMEM] * 2 + [VMEM] * 6, moved=8
    )(slot, span_map, kv2, qr, grad, norm, delta, dqt)
    dq, dkv = call(
        query_kernel, [((rows, wide_q), BF16), ((rows, 2 * wide_k), F32)], [VMEM] * 4, moved=4
    )(tables, dqt, dkv, back1)
    part2, _ = lax.optimization_barrier((part2, dkv))
    (part23,) = call(add_kernel, [((rows, 2 * wide_k), BF16)], [VMEM] * 2)(part2, back3)
    back2 = shifted(part23, 2)

    dk, dv = call(
        final_kernel,
        [((rows, wide_k), BF16), ((rows, wide_k), BF16)],
        [VMEM] * 3,
    )(tables, dkv, back2)
    return dq, dk, dv


def solution(mesh):
    placed = (
        P("ctx", "head"),
        P("ctx", "head"),
        P("ctx", "head"),
        P("ctx", "head"),
        P("ctx", "head"),
        P("head", "ctx"),
        P(None, ("ctx", "head")),
        P(),
    )
    return jax.shard_map(
        shards,
        mesh=mesh,
        in_specs=placed,
        out_specs=(P("ctx", "head"), P("ctx", "head"), P("ctx", "head")),
        check_vma=False,
    )
```

```python
import functools
import math

import jax
import jax.numpy as jnp
import numpy as np
from jax import lax
from jax.experimental import pallas as pl
from jax.experimental.pallas import tpu as pltpu
from jax.sharding import PartitionSpec as P

HEAD = 128
HALF = HEAD // 2
WIN = 4
ROPE_BASE = 1000000.0
YARN_FACTOR = 4.0
YARN_INITIAL = 32768.0
BETA_FAST = 32.0
BETA_SLOW = 1.0
YARN_MSCALE = 1.0 + 0.1 * math.log(4.0)
ROOT_SCALE = 1.0 / math.sqrt(HEAD)
LOG2E = math.log2(math.e)
VMEM_LIMIT = 24 * 1024 * 1024

F32 = jnp.float32
BF16 = jnp.bfloat16


def frequencies():
    pair = np.arange(HALF, dtype=np.float64)
    inverse = np.exp(-2.0 * pair / HEAD * math.log(ROPE_BASE))
    ratio = YARN_INITIAL * inverse / (2.0 * math.pi)
    ramp = np.clip((ratio - BETA_SLOW) / (BETA_FAST - BETA_SLOW), 0.0, 1.0)
    return inverse * ((1.0 - ramp) / YARN_FACTOR + ramp)


def frequency_rows(lanes):
    values = frequencies()
    row = lax.broadcasted_iota(jnp.int32, (8, lanes), 0)
    tiles = []
    for first in range(0, HALF, 8):
        tile = jnp.full((8, lanes), float(values[first]), F32)
        for j in range(1, 8):
            tile = jnp.where(row == j, float(values[first + j]), tile)
        tiles.append(tile)
    return jnp.concatenate(tiles, axis=0)


def sine_cosine(angle):
    turns = jnp.floor(angle * (2.0 / math.pi) + 0.5)
    r = angle - turns * 1.5703125
    r = r - turns * 4.837512969970703125e-4
    r = r - turns * 7.54978995489188e-8
    r2 = r * r
    s = r + r * r2 * (-1.6666654611e-1 + r2 * (8.3321608736e-3 - r2 * 1.9515295891e-4))
    c = (
        1.0
        - 0.5 * r2
        + r2
        * r2
        * (4.166664568298827e-2 + r2 * (-1.388731625493765e-3 + r2 * 2.443315711809948e-5))
    )
    quadrant = turns.astype(jnp.int32) & 3
    odd = (quadrant & 1) == 1
    sine = jnp.where(odd, c, s)
    cosine = jnp.where(odd, s, c)
    sine = jnp.where(quadrant >= 2, -sine, sine)
    cosine = jnp.where((quadrant == 1) | (quadrant == 2), -cosine, cosine)
    return sine, cosine


def tables_transposed(place):
    place = place.astype(F32)
    freq = frequency_rows(place.shape[1])
    pair = lax.broadcasted_iota(jnp.int32, freq.shape, 0)
    first = HEAD // 8
    second = first + 3 * HEAD // 16
    chosen = jnp.where(
        pair < first, place[0:1], jnp.where(pair < second, place[1:2], place[2:3])
    )
    sine, cosine = sine_cosine(chosen * freq)
    return cosine * YARN_MSCALE, sine * YARN_MSCALE


def row_tables(cosine_t, sine_t):
    wide = jnp.concatenate([cosine_t, cosine_t], axis=0).T
    signed = jnp.concatenate([-sine_t, sine_t], axis=0).T
    return wide, signed


def rotated(x, wide, signed):
    return x * wide + pltpu.roll(x, HALF, 1) * signed


def dot_nt(a, b):
    return lax.dot_general(a, b, (((1,), (1,)), ((), ())), preferred_element_type=F32)


def dot_nn(a, b):
    return lax.dot_general(a, b, (((1,), (0,)), ((), ())), preferred_element_type=F32)


def dot_tn(a, b):
    return lax.dot_general(a, b, (((0,), (0,)), ((), ())), preferred_element_type=F32)


def pair_part(key, value, query, grad, norm, delta, causal):
    scores = dot_nt(key, query)
    weights = jnp.exp2(scores * (ROOT_SCALE * LOG2E) - norm)
    if causal:
        at_key = lax.broadcasted_iota(jnp.int32, scores.shape, 0)
        at_query = lax.broadcasted_iota(jnp.int32, scores.shape, 1)
        weights = jnp.where(at_key <= at_query, weights, 0.0)
    value_part = dot_nn(weights.astype(BF16), grad)
    score_grad = (weights * (dot_nt(value, grad) - delta)).astype(BF16)
    key_part = dot_nn(score_grad, query)
    query_part = dot_tn(key, score_grad)
    return value_part, key_part, query_part


def key_kernel(slot_ref, own_ref, p1_ref, p2_ref, p3_ref, k_ref, kr_ref, tables_ref):
    pieces = (own_ref[...], p1_ref[...], p2_ref[...], p3_ref[...])
    count = len(pieces)
    head = slot_ref[1]
    parts = []
    for j in range(count):
        back = lax.rem(head - j + count, count)
        part = pieces[0]
        for r in range(1, count):
            part = jnp.where(back == r, pieces[r], part)
        parts.append(part)
    cosine_t, sine_t = tables_transposed(jnp.concatenate(parts, axis=1))
    tables_ref[:HALF, :] = cosine_t
    tables_ref[HALF:, :] = sine_t
    wide, signed = row_tables(cosine_t, sine_t)
    for g in range(k_ref.shape[1] // HEAD):
        cols = pl.ds(g * HEAD, HEAD)
        kr_ref[:, cols] = rotated(k_ref[:, cols].astype(F32), wide, signed).astype(BF16)


def first_kernel(
    tables_ref, kr_ref, v_ref, lse_ref, q_hbm, do_hbm, at_hbm,
    qr_ref, do_ref, norm_ref, delta_ref, dqt_ref, dkv_ref, q_ref, at_ref, sems,
):
    heads = qr_ref.shape[1] // HEAD
    groups = kr_ref.shape[1] // HEAD
    size = heads // groups
    copies = []
    for g in range(groups):
        cols = pl.ds(g * size * HEAD, size * HEAD)
        for i, (source, target) in enumerate(
            ((q_hbm, q_ref), (do_hbm, do_ref), (at_hbm, at_ref))
        ):
            copy = pltpu.make_async_copy(
                source.at[:, cols], target.at[:, cols], sems.at[3 * g + i]
            )
            copy.start()
            copies.append(copy)
    wide, signed = row_tables(tables_ref[:HALF, :], tables_ref[HALF:, :])
    norm = lse_ref[...] * LOG2E
    norm_ref[...] = norm
    chooser = jnp.ones((8, HEAD), BF16)
    for g in range(groups):
        cols = pl.ds(g * HEAD, HEAD)
        dk = dv = None
        for copy in copies[3 * g : 3 * g + 3]:
            copy.wait()
        for h in range(g * size, (g + 1) * size):
            hc = pl.ds(h * HEAD, HEAD)
            grad = do_ref[:, hc]
            query = rotated(q_ref[:, hc].astype(F32), wide, signed).astype(BF16)
            qr_ref[:, hc] = query
            product = grad.astype(F32) * at_ref[:, hc].astype(F32)
            high = product.astype(BF16)
            low = (product - high.astype(F32)).astype(BF16)
            delta = (dot_nt(chooser, high) + dot_nt(chooser, low))[:1]
            delta_ref[h : h + 1, :] = delta
            v_part, k_part, q_part = pair_part(
                kr_ref[:, cols], v_ref[:, cols], query, grad, norm[h : h + 1], delta, True
            )
            dqt_ref[hc, :] = q_part
            dv = v_part if dv is None else dv + v_part
            dk = k_part if dk is None else dk + k_part
        dkv_ref[:, cols] = dk
        dkv_ref[:, pl.ds((groups + g) * HEAD, HEAD)] = dv


def hop_body(
    step, slot_ref, span_ref, k_ref, v_ref, qr_ref, do_ref, norm_ref, delta_ref,
    dqt_in, dqt_ref, dkv_ref,
):
    rows = qr_ref.shape[0]
    half = rows // 2
    heads = qr_ref.shape[1] // HEAD
    groups = k_ref.shape[1] // HEAD
    size = heads // groups
    me = slot_ref[0]
    other = lax.rem(me + step, span_ref.shape[0])
    earlier = span_ref[other] < span_ref[me]
    norm = norm_ref[...]
    delta = delta_ref[...]

    def run(keys, queries):
        for g in range(groups):
            kc = pl.ds(g * HEAD, HEAD)
            vc = pl.ds((groups + g) * HEAD, HEAD)
            dk = dv = None
            for h in range(g * size, (g + 1) * size):
                hc = pl.ds(h * HEAD, HEAD)
                v_part, k_part, q_part = pair_part(
                    k_ref[keys, kc], v_ref[keys, kc], qr_ref[queries, hc], do_ref[queries, hc],
                    norm[h : h + 1, queries.start :], delta[h : h + 1, queries.start :], False,
                )
                if queries.start:
                    dqt_ref[hc, : queries.start] = dqt_in[hc, : queries.start]
                dqt_ref[hc, queries] = dqt_in[hc, queries] + q_part
                dv = v_part if dv is None else dv + v_part
                dk = k_part if dk is None else dk + k_part
            dkv_ref[keys, kc] = dk.astype(BF16)
            dkv_ref[keys, vc] = dv.astype(BF16)
        if keys.stop < rows:
            dkv_ref[keys.stop :, :] = jnp.zeros((rows - keys.stop, dkv_ref.shape[1]), BF16)

    @pl.when(earlier)
    def _():
        run(slice(0, half), slice(0, rows))

    @pl.when(jnp.logical_not(earlier))
    def _():
        run(slice(0, rows), slice(half, rows))


def query_kernel(tables_ref, dqt_ref, own_ref, a_ref, b_ref, out_ref, sum_ref):
    sum_ref[...] = own_ref[...] + a_ref[...].astype(F32) + b_ref[...].astype(F32)
    cosine_t = tables_ref[:HALF, :] * ROOT_SCALE
    sine_t = tables_ref[HALF:, :] * ROOT_SCALE
    for h in range(out_ref.shape[1] // HEAD):
        y1 = dqt_ref[pl.ds(h * HEAD, HALF), :]
        y2 = dqt_ref[pl.ds(h * HEAD + HALF, HALF), :]
        turned = jnp.concatenate(
            [y1 * cosine_t + y2 * sine_t, y2 * cosine_t - y1 * sine_t], axis=0
        )
        out_ref[:, pl.ds(h * HEAD, HEAD)] = turned.T.astype(BF16)


def final_kernel(tables_ref, own_ref, a_ref, dk_ref, dv_ref):
    width = dk_ref.shape[1]
    wide, signed = row_tables(tables_ref[:HALF, :], tables_ref[HALF:, :])
    wide = wide * ROOT_SCALE
    signed = signed * -ROOT_SCALE
    total = own_ref[...] + a_ref[...].astype(F32)
    for g in range(width // HEAD):
        cols = pl.ds(g * HEAD, HEAD)
        dk_ref[:, cols] = rotated(total[:, g * HEAD : (g + 1) * HEAD], wide, signed).astype(BF16)
    dv_ref[...] = total[:, width:].astype(BF16)


SMEM = pl.BlockSpec(memory_space=pltpu.SMEM)
VMEM = pl.BlockSpec(memory_space=pltpu.VMEM)
HBM = pl.BlockSpec(memory_space=pltpu.HBM)


def call(kernel, outs, specs, scratch=()):
    return pl.pallas_call(
        kernel,
        out_shape=[jax.ShapeDtypeStruct(shape, dtype) for shape, dtype in outs],
        in_specs=specs,
        out_specs=[VMEM] * len(outs),
        scratch_shapes=list(scratch),
        compiler_params=pltpu.CompilerParams(vmem_limit_bytes=VMEM_LIMIT),
        cost_estimate=pl.CostEstimate(
            flops=1 << 20, bytes_accessed=1 << 18, transcendentals=0
        ),
    )


def shifted(value, steps, axis="ctx"):
    count = lax.axis_size(axis)
    pairs = [(source, (source + steps) % count) for source in range(count)]
    return lax.ppermute(value, axis, pairs)


def shards(q, k, v, do, at, lse, positions, span_map):
    rows = q.shape[0]
    wide_q = q.shape[1]
    wide_k = k.shape[1]
    heads = wide_q // HEAD
    slot = jnp.stack([lax.axis_index("ctx"), lax.axis_index("head")]).astype(jnp.int32)
    q, do, at, k_here, v_here, lse, span_map, own = (
        pltpu.with_memory_space_constraint(x, pltpu.HBM)
        for x in (q, do, at, k, v, lse, span_map, positions)
    )

    pieces = [own] + [shifted(positions, r, "head") for r in (1, 2, 3)]
    v1 = shifted(v, -1)
    v2 = shifted(v, -2)
    kr, tables = call(
        key_kernel,
        [((rows, wide_k), BF16), ((HEAD, rows), F32)],
        [SMEM] + [VMEM] * 5,
    )(slot, *pieces, k_here)
    kr1, v1 = lax.optimization_barrier((kr, v1))
    k1 = shifted(kr1, -1)
    v3 = shifted(v1, -2)
    kr2, v2 = lax.optimization_barrier((kr, v2))
    k2 = shifted(kr2, -2)
    qr, grad, norm, delta, dqt, dkv = call(
        first_kernel,
        [
            ((rows, wide_q), BF16),
            ((rows, wide_q), BF16),
            ((heads, rows), F32),
            ((heads, rows), F32),
            ((wide_q, rows), F32),
            ((rows, 2 * wide_k), F32),
        ],
        [VMEM] * 4 + [HBM] * 3,
        [
            pltpu.VMEM((rows, wide_q), BF16),
            pltpu.VMEM((rows, wide_q), BF16),
            pltpu.SemaphoreType.DMA((3 * (wide_k // HEAD),)),
        ],
    )(tables, kr, v_here, lse, q, do, at)
    held, _ = lax.optimization_barrier((k1, delta))
    k3 = shifted(held, -2)

    backs = []
    for step, key, value in ((1, k1, v1), (2, k2, v2), (3, k3, v3)):
        dqt, part = call(
            functools.partial(hop_body, step),
            [((wide_q, rows), F32), ((rows, 2 * wide_k), BF16)],
            [SMEM] * 2 + [VMEM] * 7,
        )(slot, span_map, key, value, qr, grad, norm, delta, dqt)
        backs.append(shifted(part, step))
    dq, dkv = call(
        query_kernel, [((rows, wide_q), BF16), ((rows, 2 * wide_k), F32)], [VMEM] * 5
    )(tables, dqt, dkv, backs[1], backs[0])

    dk, dv = call(
        final_kernel,
        [((rows, wide_k), BF16), ((rows, wide_k), BF16)],
        [VMEM] * 3,
    )(tables, dkv, backs[2])
    return dq, dk, dv


def solution(mesh):
    placed = (
        P("ctx", "head"),
        P("ctx", "head"),
        P("ctx", "head"),
        P("ctx", "head"),
        P("ctx", "head"),
        P("head", "ctx"),
        P(None, ("ctx", "head")),
        P(),
    )
    return jax.shard_map(
        shards,
        mesh=mesh,
        in_specs=placed,
        out_specs=(P("ctx", "head"), P("ctx", "head"), P("ctx", "head")),
        check_vma=False,
    )
```

```python
import functools
import math

import jax
import jax.numpy as jnp
import numpy as np
from jax import lax
from jax.experimental import pallas as pl
from jax.experimental.pallas import tpu as pltpu
from jax.sharding import PartitionSpec as P

HEAD = 128
HALF = HEAD // 2
WIN = 4
ROPE_BASE = 1000000.0
YARN_FACTOR = 4.0
YARN_INITIAL = 32768.0
BETA_FAST = 32.0
BETA_SLOW = 1.0
YARN_MSCALE = 1.0 + 0.1 * math.log(4.0)
ROOT_SCALE = 1.0 / math.sqrt(HEAD)
LOG2E = math.log2(math.e)
VMEM_LIMIT = 24 * 1024 * 1024

F32 = jnp.float32
BF16 = jnp.bfloat16


def frequencies():
    pair = np.arange(HALF, dtype=np.float64)
    inverse = np.exp(-2.0 * pair / HEAD * math.log(ROPE_BASE))
    ratio = YARN_INITIAL * inverse / (2.0 * math.pi)
    ramp = np.clip((ratio - BETA_SLOW) / (BETA_FAST - BETA_SLOW), 0.0, 1.0)
    return inverse * ((1.0 - ramp) / YARN_FACTOR + ramp)


def frequency_rows(lanes):
    values = frequencies()
    row = lax.broadcasted_iota(jnp.int32, (8, lanes), 0)
    tiles = []
    for first in range(0, HALF, 8):
        tile = jnp.full((8, lanes), float(values[first]), F32)
        for j in range(1, 8):
            tile = jnp.where(row == j, float(values[first + j]), tile)
        tiles.append(tile)
    return jnp.concatenate(tiles, axis=0)


def sine_cosine(angle):
    turns = jnp.floor(angle * (2.0 / math.pi) + 0.5)
    r = angle - turns * 1.5703125
    r = r - turns * 4.837512969970703125e-4
    r = r - turns * 7.54978995489188e-8
    r2 = r * r
    s = r + r * r2 * (-1.6666654611e-1 + r2 * (8.3321608736e-3 - r2 * 1.9515295891e-4))
    c = (
        1.0
        - 0.5 * r2
        + r2
        * r2
        * (4.166664568298827e-2 + r2 * (-1.388731625493765e-3 + r2 * 2.443315711809948e-5))
    )
    quadrant = turns.astype(jnp.int32) & 3
    odd = (quadrant & 1) == 1
    sine = jnp.where(odd, c, s)
    cosine = jnp.where(odd, s, c)
    sine = jnp.where(quadrant >= 2, -sine, sine)
    cosine = jnp.where((quadrant == 1) | (quadrant == 2), -cosine, cosine)
    return sine, cosine


def tables_transposed(place):
    place = place.astype(F32)
    freq = frequency_rows(place.shape[1])
    pair = lax.broadcasted_iota(jnp.int32, freq.shape, 0)
    first = HEAD // 8
    second = first + 3 * HEAD // 16
    chosen = jnp.where(
        pair < first, place[0:1], jnp.where(pair < second, place[1:2], place[2:3])
    )
    sine, cosine = sine_cosine(chosen * freq)
    return cosine * YARN_MSCALE, sine * YARN_MSCALE


def row_tables(cosine_t, sine_t):
    wide = jnp.concatenate([cosine_t, cosine_t], axis=0).T
    signed = jnp.concatenate([-sine_t, sine_t], axis=0).T
    return wide, signed


def rotated(x, wide, signed):
    return x * wide + pltpu.roll(x, HALF, 1) * signed


def dot_nt(a, b):
    return lax.dot_general(a, b, (((1,), (1,)), ((), ())), preferred_element_type=F32)


def dot_nn(a, b):
    return lax.dot_general(a, b, (((1,), (0,)), ((), ())), preferred_element_type=F32)


def dot_tn(a, b):
    return lax.dot_general(a, b, (((0,), (0,)), ((), ())), preferred_element_type=F32)


def pair_part(key, value, query, grad, norm, delta, causal):
    scores = dot_nt(key, query)
    weights = jnp.exp2(scores * (ROOT_SCALE * LOG2E) - norm)
    if causal:
        at_key = lax.broadcasted_iota(jnp.int32, scores.shape, 0)
        at_query = lax.broadcasted_iota(jnp.int32, scores.shape, 1)
        weights = jnp.where(at_key <= at_query, weights, 0.0)
    value_part = dot_nn(weights.astype(BF16), grad)
    score_grad = (weights * (dot_nt(value, grad) - delta)).astype(BF16)
    key_part = dot_nn(score_grad, query)
    query_part = dot_tn(key, score_grad)
    return value_part, key_part, query_part


def key_kernel(slot_ref, own_ref, p1_ref, p2_ref, p3_ref, k_ref, kr_ref, tables_ref):
    pieces = (own_ref[...], p1_ref[...], p2_ref[...], p3_ref[...])
    count = len(pieces)
    head = slot_ref[1]
    parts = []
    for j in range(count):
        back = lax.rem(head - j + count, count)
        part = pieces[0]
        for r in range(1, count):
            part = jnp.where(back == r, pieces[r], part)
        parts.append(part)
    cosine_t, sine_t = tables_transposed(jnp.concatenate(parts, axis=1))
    tables_ref[:HALF, :] = cosine_t
    tables_ref[HALF:, :] = sine_t
    wide, signed = row_tables(cosine_t, sine_t)
    for g in range(k_ref.shape[1] // HEAD):
        cols = pl.ds(g * HEAD, HEAD)
        kr_ref[:, cols] = rotated(k_ref[:, cols].astype(F32), wide, signed).astype(BF16)


def prep_kernel(
    groups, tables_ref, lse_hbm, q_hbm, do_hbm, at_hbm,
    qr_ref, do_ref, norm_ref, delta_ref, q_ref, at_ref, lse_ref, sems,
):
    heads = qr_ref.shape[1] // HEAD
    size = heads // groups
    copies = []
    for g in range(groups):
        cols = pl.ds(g * size * HEAD, size * HEAD)
        for i, (source, target) in enumerate(
            ((q_hbm, q_ref), (do_hbm, do_ref), (at_hbm, at_ref))
        ):
            copy = pltpu.make_async_copy(
                source.at[:, cols], target.at[:, cols], sems.at[3 * g + i]
            )
            copy.start()
            copies.append(copy)
    lse_copy = pltpu.make_async_copy(lse_hbm, lse_ref, sems.at[3 * groups])
    lse_copy.start()
    wide, signed = row_tables(tables_ref[:HALF, :], tables_ref[HALF:, :])
    chooser = jnp.ones((8, HEAD), BF16)
    for h in range(heads):
        if h % size == 0:
            for copy in copies[3 * (h // size) : 3 * (h // size) + 3]:
                copy.wait()
        hc = pl.ds(h * HEAD, HEAD)
        qr_ref[:, hc] = rotated(q_ref[:, hc].astype(F32), wide, signed).astype(BF16)
        product = do_ref[:, hc].astype(F32) * at_ref[:, hc].astype(F32)
        high = product.astype(BF16)
        low = (product - high.astype(F32)).astype(BF16)
        delta_ref[h : h + 1, :] = (dot_nt(chooser, high) + dot_nt(chooser, low))[:1]
    lse_copy.wait()
    norm_ref[...] = lse_ref[...] * LOG2E


def hop_body(
    step, slot_ref, span_ref, k_ref, v_ref, qr_ref, do_ref, norm_ref, delta_ref, *refs
):
    dqt_ref, dkv_ref = refs[-2:]
    dqt_in = refs[0] if len(refs) > 2 else None
    rows = qr_ref.shape[0]
    half = rows // 2
    heads = qr_ref.shape[1] // HEAD
    groups = k_ref.shape[1] // HEAD
    size = heads // groups
    me = slot_ref[0]
    other = lax.rem(me + step, span_ref.shape[0])
    earlier = span_ref[other] < span_ref[me]
    norm = norm_ref[...]
    delta = delta_ref[...]

    def run(keys, queries):
        for g in range(groups):
            kc = pl.ds(g * HEAD, HEAD)
            vc = pl.ds((groups + g) * HEAD, HEAD)
            dk = dv = None
            for h in range(g * size, (g + 1) * size):
                hc = pl.ds(h * HEAD, HEAD)
                v_part, k_part, q_part = pair_part(
                    k_ref[keys, kc], v_ref[keys, kc], qr_ref[queries, hc], do_ref[queries, hc],
                    norm[h : h + 1, queries.start :], delta[h : h + 1, queries.start :], False,
                )
                if queries.start:
                    before = jnp.zeros((HEAD, queries.start), F32)
                    if dqt_in is not None:
                        before = dqt_in[hc, : queries.start]
                    dqt_ref[hc, : queries.start] = before
                dqt_ref[hc, queries] = q_part if dqt_in is None else dqt_in[hc, queries] + q_part
                dv = v_part if dv is None else dv + v_part
                dk = k_part if dk is None else dk + k_part
            dkv_ref[keys, kc] = dk.astype(BF16)
            dkv_ref[keys, vc] = dv.astype(BF16)
        if keys.stop < rows:
            dkv_ref[keys.stop :, :] = jnp.zeros((rows - keys.stop, dkv_ref.shape[1]), BF16)

    @pl.when(earlier)
    def _():
        run(slice(0, half), slice(0, rows))

    @pl.when(jnp.logical_not(earlier))
    def _():
        run(slice(0, rows), slice(half, rows))


def own_kernel(
    tables_ref, k_ref, v_ref, qr_ref, do_ref, norm_ref, delta_ref, dqt_ref, back_ref,
    out_ref, sum_ref,
):
    heads = qr_ref.shape[1] // HEAD
    groups = k_ref.shape[1] // HEAD
    size = heads // groups
    cosine_t = tables_ref[:HALF, :] * ROOT_SCALE
    sine_t = tables_ref[HALF:, :] * ROOT_SCALE
    norm = norm_ref[...]
    delta = delta_ref[...]
    for g in range(groups):
        kc = pl.ds(g * HEAD, HEAD)
        vc = pl.ds((groups + g) * HEAD, HEAD)
        dk = back_ref[:, kc].astype(F32)
        dv = back_ref[:, vc].astype(F32)
        for h in range(g * size, (g + 1) * size):
            hc = pl.ds(h * HEAD, HEAD)
            v_part, k_part, q_part = pair_part(
                k_ref[:, kc], v_ref[:, kc], qr_ref[:, hc], do_ref[:, hc],
                norm[h : h + 1], delta[h : h + 1], True,
            )
            dk = dk + k_part
            dv = dv + v_part
            total = dqt_ref[hc, :] + q_part
            y1, y2 = total[:HALF], total[HALF:]
            turned = jnp.concatenate(
                [y1 * cosine_t + y2 * sine_t, y2 * cosine_t - y1 * sine_t], axis=0
            )
            out_ref[:, hc] = turned.T.astype(BF16)
        sum_ref[:, kc] = dk
        sum_ref[:, vc] = dv


def final_kernel(tables_ref, own_ref, a_ref, b_ref, dk_ref, dv_ref):
    width = dk_ref.shape[1]
    wide, signed = row_tables(tables_ref[:HALF, :], tables_ref[HALF:, :])
    wide = wide * ROOT_SCALE
    signed = signed * -ROOT_SCALE
    total = own_ref[...] + a_ref[...].astype(F32) + b_ref[...].astype(F32)
    for g in range(width // HEAD):
        cols = pl.ds(g * HEAD, HEAD)
        dk_ref[:, cols] = rotated(total[:, g * HEAD : (g + 1) * HEAD], wide, signed).astype(BF16)
    dv_ref[...] = total[:, width:].astype(BF16)


SMEM = pl.BlockSpec(memory_space=pltpu.SMEM)
VMEM = pl.BlockSpec(memory_space=pltpu.VMEM)
HBM = pl.BlockSpec(memory_space=pltpu.HBM)


def call(kernel, outs, specs, scratch=()):
    return pl.pallas_call(
        kernel,
        out_shape=[jax.ShapeDtypeStruct(shape, dtype) for shape, dtype in outs],
        in_specs=specs,
        out_specs=[VMEM] * len(outs),
        scratch_shapes=list(scratch),
        compiler_params=pltpu.CompilerParams(vmem_limit_bytes=VMEM_LIMIT),
        cost_estimate=pl.CostEstimate(
            flops=1 << 20, bytes_accessed=1 << 18, transcendentals=0
        ),
    )


def shifted(value, steps, axis="ctx"):
    count = lax.axis_size(axis)
    pairs = [(source, (source + steps) % count) for source in range(count)]
    return lax.ppermute(value, axis, pairs)


def shards(q, k, v, do, at, lse, positions, span_map):
    rows = q.shape[0]
    wide_q = q.shape[1]
    wide_k = k.shape[1]
    heads = wide_q // HEAD
    slot = jnp.stack([lax.axis_index("ctx"), lax.axis_index("head")]).astype(jnp.int32)
    q, do, at, k_here, v_here, lse, span_map, own = (
        pltpu.with_memory_space_constraint(x, pltpu.HBM)
        for x in (q, do, at, k, v, lse, span_map, positions)
    )

    pieces = [own] + [shifted(positions, r, "head") for r in (1, 2, 3)]
    v1 = shifted(v, -1)
    v2 = shifted(v, -2)
    kr, tables = call(
        key_kernel,
        [((rows, wide_k), BF16), ((HEAD, rows), F32)],
        [SMEM] + [VMEM] * 5,
    )(slot, *pieces, k_here)
    kr1, v1 = lax.optimization_barrier((kr, v1))
    k1 = shifted(kr1, -1)
    v3 = shifted(v1, -2)
    k2 = shifted(kr, -2)
    turned, v2 = lax.optimization_barrier((tables, v2))
    groups = wide_k // HEAD
    qr, grad, norm, delta = call(
        functools.partial(prep_kernel, groups),
        [((rows, wide_q), BF16)] * 2 + [((heads, rows), F32)] * 2,
        [VMEM] + [HBM] * 4,
        [
            pltpu.VMEM((rows, wide_q), BF16),
            pltpu.VMEM((rows, wide_q), BF16),
            pltpu.VMEM((heads, rows), F32),
            pltpu.SemaphoreType.DMA((3 * groups + 1,)),
        ],
    )(turned, lse, q, do, at)
    held, _ = lax.optimization_barrier((k1, delta))
    k3 = shifted(held, -2)

    dqt = ()
    backs = []
    for step, key, value in ((1, k1, v1), (2, k2, v2), (3, k3, v3)):
        *dqt, part = call(
            functools.partial(hop_body, step),
            [((wide_q, rows), F32), ((rows, 2 * wide_k), BF16)],
            [SMEM] * 2 + [VMEM] * (6 + len(dqt)),
        )(slot, span_map, key, value, qr, grad, norm, delta, *dqt)
        backs.append(shifted(part, step))
    dq, dkv = call(
        own_kernel, [((rows, wide_q), BF16), ((rows, 2 * wide_k), F32)], [VMEM] * 9
    )(tables, kr, v_here, qr, grad, norm, delta, *dqt, backs[0])

    dk, dv = call(
        final_kernel,
        [((rows, wide_k), BF16), ((rows, wide_k), BF16)],
        [VMEM] * 4,
    )(tables, dkv, backs[1], backs[2])
    return dq, dk, dv


def solution(mesh):
    placed = (
        P("ctx", "head"),
        P("ctx", "head"),
        P("ctx", "head"),
        P("ctx", "head"),
        P("ctx", "head"),
        P("head", "ctx"),
        P(None, ("ctx", "head")),
        P(),
    )
    return jax.shard_map(
        shards,
        mesh=mesh,
        in_specs=placed,
        out_specs=(P("ctx", "head"), P("ctx", "head"), P("ctx", "head")),
        check_vma=False,
    )
```

```python
import functools
import math

import jax
import jax.numpy as jnp
import numpy as np
from jax import lax
from jax.experimental import pallas as pl
from jax.experimental.pallas import tpu as pltpu
from jax.sharding import PartitionSpec as P

HEAD = 128
HALF = HEAD // 2
WIN = 4
ROPE_BASE = 1000000.0
YARN_FACTOR = 4.0
YARN_INITIAL = 32768.0
BETA_FAST = 32.0
BETA_SLOW = 1.0
YARN_MSCALE = 1.0 + 0.1 * math.log(4.0)
ROOT_SCALE = 1.0 / math.sqrt(HEAD)
LOG2E = math.log2(math.e)
VMEM_LIMIT = 24 * 1024 * 1024

F32 = jnp.float32
BF16 = jnp.bfloat16


def frequencies():
    pair = np.arange(HALF, dtype=np.float64)
    inverse = np.exp(-2.0 * pair / HEAD * math.log(ROPE_BASE))
    ratio = YARN_INITIAL * inverse / (2.0 * math.pi)
    ramp = np.clip((ratio - BETA_SLOW) / (BETA_FAST - BETA_SLOW), 0.0, 1.0)
    return inverse * ((1.0 - ramp) / YARN_FACTOR + ramp)


def frequency_rows(lanes):
    values = frequencies()
    row = lax.broadcasted_iota(jnp.int32, (8, lanes), 0)
    tiles = []
    for first in range(0, HALF, 8):
        tile = jnp.full((8, lanes), float(values[first]), F32)
        for j in range(1, 8):
            tile = jnp.where(row == j, float(values[first + j]), tile)
        tiles.append(tile)
    return jnp.concatenate(tiles, axis=0)


def sine_cosine(angle):
    turns = jnp.floor(angle * (2.0 / math.pi) + 0.5)
    r = angle - turns * 1.5703125
    r = r - turns * 4.837512969970703125e-4
    r = r - turns * 7.54978995489188e-8
    r2 = r * r
    s = r + r * r2 * (-1.6666654611e-1 + r2 * (8.3321608736e-3 - r2 * 1.9515295891e-4))
    c = (
        1.0
        - 0.5 * r2
        + r2
        * r2
        * (4.166664568298827e-2 + r2 * (-1.388731625493765e-3 + r2 * 2.443315711809948e-5))
    )
    quadrant = turns.astype(jnp.int32) & 3
    odd = (quadrant & 1) == 1
    sine = jnp.where(odd, c, s)
    cosine = jnp.where(odd, s, c)
    sine = jnp.where(quadrant >= 2, -sine, sine)
    cosine = jnp.where((quadrant == 1) | (quadrant == 2), -cosine, cosine)
    return sine, cosine


def tables_transposed(place):
    place = place.astype(F32)
    freq = frequency_rows(place.shape[1])
    pair = lax.broadcasted_iota(jnp.int32, freq.shape, 0)
    first = HEAD // 8
    second = first + 3 * HEAD // 16
    chosen = jnp.where(
        pair < first, place[0:1], jnp.where(pair < second, place[1:2], place[2:3])
    )
    sine, cosine = sine_cosine(chosen * freq)
    return cosine * YARN_MSCALE, sine * YARN_MSCALE


def row_tables(cosine_t, sine_t):
    wide = jnp.concatenate([cosine_t, cosine_t], axis=0).T
    signed = jnp.concatenate([-sine_t, sine_t], axis=0).T
    return wide, signed


def rotated(x, wide, signed):
    return x * wide + pltpu.roll(x, HALF, 1) * signed


def dot_nt(a, b):
    return lax.dot_general(a, b, (((1,), (1,)), ((), ())), preferred_element_type=F32)


def dot_nn(a, b):
    return lax.dot_general(a, b, (((1,), (0,)), ((), ())), preferred_element_type=F32)


def dot_tn(a, b):
    return lax.dot_general(a, b, (((0,), (0,)), ((), ())), preferred_element_type=F32)


def pair_part(key, value, query, grad, norm, delta, causal):
    scores = dot_nt(key, query)
    weights = jnp.exp2(scores * (ROOT_SCALE * LOG2E) - norm)
    if causal:
        at_key = lax.broadcasted_iota(jnp.int32, scores.shape, 0)
        at_query = lax.broadcasted_iota(jnp.int32, scores.shape, 1)
        weights = jnp.where(at_key <= at_query, weights, 0.0)
    value_part = dot_nn(weights.astype(BF16), grad)
    score_grad = (weights * (dot_nt(value, grad) - delta)).astype(BF16)
    key_part = dot_nn(score_grad, query)
    query_part = dot_tn(key, score_grad)
    return value_part, key_part, query_part


def key_kernel(slot_ref, own_ref, p1_ref, p2_ref, p3_ref, k_ref, kr_ref, tables_ref):
    pieces = (own_ref[...], p1_ref[...], p2_ref[...], p3_ref[...])
    count = len(pieces)
    head = slot_ref[1]
    parts = []
    for j in range(count):
        back = lax.rem(head - j + count, count)
        part = pieces[0]
        for r in range(1, count):
            part = jnp.where(back == r, pieces[r], part)
        parts.append(part)
    cosine_t, sine_t = tables_transposed(jnp.concatenate(parts, axis=1))
    tables_ref[:HALF, :] = cosine_t
    tables_ref[HALF:, :] = sine_t
    wide, signed = row_tables(cosine_t, sine_t)
    for g in range(k_ref.shape[1] // HEAD):
        cols = pl.ds(g * HEAD, HEAD)
        kr_ref[:, cols] = rotated(k_ref[:, cols].astype(F32), wide, signed).astype(BF16)


def prep_kernel(
    groups, tables_ref, lse_hbm, q_hbm, do_hbm, at_hbm,
    qr_ref, do_ref, norm_ref, delta_ref, q_ref, at_ref, lse_ref, sems,
):
    heads = qr_ref.shape[1] // HEAD
    size = heads // groups
    copies = []
    for g in range(groups):
        cols = pl.ds(g * size * HEAD, size * HEAD)
        for i, (source, target) in enumerate(
            ((q_hbm, q_ref), (do_hbm, do_ref), (at_hbm, at_ref))
        ):
            copy = pltpu.make_async_copy(
                source.at[:, cols], target.at[:, cols], sems.at[3 * g + i]
            )
            copy.start()
            copies.append(copy)
    lse_copy = pltpu.make_async_copy(lse_hbm, lse_ref, sems.at[3 * groups])
    lse_copy.start()
    wide, signed = row_tables(tables_ref[:HALF, :], tables_ref[HALF:, :])
    chooser = jnp.ones((8, HEAD), BF16)
    for h in range(heads):
        if h % size == 0:
            for copy in copies[3 * (h // size) : 3 * (h // size) + 3]:
                copy.wait()
        hc = pl.ds(h * HEAD, HEAD)
        qr_ref[:, hc] = rotated(q_ref[:, hc].astype(F32), wide, signed).astype(BF16)
        product = do_ref[:, hc].astype(F32) * at_ref[:, hc].astype(F32)
        high = product.astype(BF16)
        low = (product - high.astype(F32)).astype(BF16)
        delta_ref[h : h + 1, :] = (dot_nt(chooser, high) + dot_nt(chooser, low))[:1]
    lse_copy.wait()
    norm_ref[...] = lse_ref[...] * LOG2E


def hop_body(
    step, slot_ref, span_ref, k_ref, v_ref, qr_ref, do_ref, norm_ref, delta_ref, *refs
):
    dqt_ref, dkv_ref = refs[-2:]
    dqt_in = refs[0] if len(refs) > 2 else None
    rows = qr_ref.shape[0]
    half = rows // 2
    heads = qr_ref.shape[1] // HEAD
    groups = k_ref.shape[1] // HEAD
    size = heads // groups
    me = slot_ref[0]
    other = lax.rem(me + step, span_ref.shape[0])
    earlier = span_ref[other] < span_ref[me]
    norm = norm_ref[...]
    delta = delta_ref[...]

    def run(keys, queries):
        for g in range(groups):
            kc = pl.ds(g * HEAD, HEAD)
            vc = pl.ds((groups + g) * HEAD, HEAD)
            dk = dv = None
            for h in range(g * size, (g + 1) * size):
                hc = pl.ds(h * HEAD, HEAD)
                v_part, k_part, q_part = pair_part(
                    k_ref[keys, kc], v_ref[keys, kc], qr_ref[queries, hc], do_ref[queries, hc],
                    norm[h : h + 1, queries.start :], delta[h : h + 1, queries.start :], False,
                )
                if queries.start:
                    before = jnp.zeros((HEAD, queries.start), F32)
                    if dqt_in is not None:
                        before = dqt_in[hc, : queries.start]
                    dqt_ref[hc, : queries.start] = before
                dqt_ref[hc, queries] = q_part if dqt_in is None else dqt_in[hc, queries] + q_part
                dv = v_part if dv is None else dv + v_part
                dk = k_part if dk is None else dk + k_part
            dkv_ref[keys, kc] = dk.astype(BF16)
            dkv_ref[keys, vc] = dv.astype(BF16)
        if keys.stop < rows:
            dkv_ref[keys.stop :, :] = jnp.zeros((rows - keys.stop, dkv_ref.shape[1]), BF16)

    @pl.when(earlier)
    def _():
        run(slice(0, half), slice(0, rows))

    @pl.when(jnp.logical_not(earlier))
    def _():
        run(slice(0, rows), slice(half, rows))


def own_kernel(
    slot_ref, tables_ref, k_ref, v_ref, qr_ref, do_ref, norm_ref, delta_ref, dqt_ref, back_ref,
    out_ref, sum_ref,
):
    odd = (slot_ref[0] & 1) == 1
    heads = qr_ref.shape[1] // HEAD
    groups = k_ref.shape[1] // HEAD
    size = heads // groups
    cosine_t = tables_ref[:HALF, :] * ROOT_SCALE
    sine_t = tables_ref[HALF:, :] * ROOT_SCALE
    norm = norm_ref[...]
    delta = delta_ref[...]
    for g in range(groups):
        kc = pl.ds(g * HEAD, HEAD)
        vc = pl.ds((groups + g) * HEAD, HEAD)
        dk = jnp.where(odd, back_ref[:, kc].astype(F32), 0.0)
        dv = jnp.where(odd, back_ref[:, vc].astype(F32), 0.0)
        for h in range(g * size, (g + 1) * size):
            hc = pl.ds(h * HEAD, HEAD)
            v_part, k_part, q_part = pair_part(
                k_ref[:, kc], v_ref[:, kc], qr_ref[:, hc], do_ref[:, hc],
                norm[h : h + 1], delta[h : h + 1], True,
            )
            dk = dk + k_part
            dv = dv + v_part
            total = dqt_ref[hc, :] + q_part
            y1, y2 = total[:HALF], total[HALF:]
            turned = jnp.concatenate(
                [y1 * cosine_t + y2 * sine_t, y2 * cosine_t - y1 * sine_t], axis=0
            )
            out_ref[:, hc] = turned.T.astype(BF16)
        sum_ref[:, kc] = dk
        sum_ref[:, vc] = dv


def add_kernel(slot_ref, two_ref, three_ref, swapped_ref, sum_ref):
    even = (slot_ref[0] & 1) == 0
    total = two_ref[...].astype(F32) + three_ref[...].astype(F32)
    sum_ref[...] = (total + jnp.where(even, swapped_ref[...].astype(F32), 0.0)).astype(BF16)


def final_kernel(tables_ref, own_ref, a_ref, dk_ref, dv_ref):
    width = dk_ref.shape[1]
    wide, signed = row_tables(tables_ref[:HALF, :], tables_ref[HALF:, :])
    wide = wide * ROOT_SCALE
    signed = signed * -ROOT_SCALE
    total = own_ref[...] + a_ref[...].astype(F32)
    for g in range(width // HEAD):
        cols = pl.ds(g * HEAD, HEAD)
        dk_ref[:, cols] = rotated(total[:, g * HEAD : (g + 1) * HEAD], wide, signed).astype(BF16)
    dv_ref[...] = total[:, width:].astype(BF16)


SMEM = pl.BlockSpec(memory_space=pltpu.SMEM)
VMEM = pl.BlockSpec(memory_space=pltpu.VMEM)
HBM = pl.BlockSpec(memory_space=pltpu.HBM)


def call(kernel, outs, specs, scratch=()):
    return pl.pallas_call(
        kernel,
        out_shape=[jax.ShapeDtypeStruct(shape, dtype) for shape, dtype in outs],
        in_specs=specs,
        out_specs=[VMEM] * len(outs),
        scratch_shapes=list(scratch),
        compiler_params=pltpu.CompilerParams(vmem_limit_bytes=VMEM_LIMIT),
        cost_estimate=pl.CostEstimate(
            flops=1 << 20, bytes_accessed=1 << 18, transcendentals=0
        ),
    )


def shifted(value, steps, axis="ctx"):
    count = lax.axis_size(axis)
    pairs = [(source, (source + steps) % count) for source in range(count)]
    return lax.ppermute(value, axis, pairs)


def exchanged(value):
    count = lax.axis_size("ctx")
    return lax.ppermute(value, "ctx", [(source, source ^ 1) for source in range(count)])


def shards(q, k, v, do, at, lse, positions, span_map):
    rows = q.shape[0]
    wide_q = q.shape[1]
    wide_k = k.shape[1]
    heads = wide_q // HEAD
    slot = jnp.stack([lax.axis_index("ctx"), lax.axis_index("head")]).astype(jnp.int32)
    q, do, at, k_here, v_here, lse, span_map, own = (
        pltpu.with_memory_space_constraint(x, pltpu.HBM)
        for x in (q, do, at, k, v, lse, span_map, positions)
    )

    pieces = [own] + [shifted(positions, r, "head") for r in (1, 2, 3)]
    v1 = shifted(v, -1)
    v2 = shifted(v, -2)
    kr, tables = call(
        key_kernel,
        [((rows, wide_k), BF16), ((HEAD, rows), F32)],
        [SMEM] + [VMEM] * 5,
    )(slot, *pieces, k_here)
    kr1, v1 = lax.optimization_barrier((kr, v1))
    k1 = shifted(kr1, -1)
    v3 = shifted(v1, -2)
    k2 = shifted(kr, -2)
    turned, v2 = lax.optimization_barrier((tables, v2))
    groups = wide_k // HEAD
    qr, grad, norm, delta = call(
        functools.partial(prep_kernel, groups),
        [((rows, wide_q), BF16)] * 2 + [((heads, rows), F32)] * 2,
        [VMEM] + [HBM] * 4,
        [
            pltpu.VMEM((rows, wide_q), BF16),
            pltpu.VMEM((rows, wide_q), BF16),
            pltpu.VMEM((heads, rows), F32),
            pltpu.SemaphoreType.DMA((3 * groups + 1,)),
        ],
    )(turned, lse, q, do, at)
    held, _ = lax.optimization_barrier((k1, delta))
    k3 = shifted(held, -2)

    dqt = ()
    parts = []
    for step, key, value in ((1, k1, v1), (2, k2, v2), (3, k3, v3)):
        *dqt, part = call(
            functools.partial(hop_body, step),
            [((wide_q, rows), F32), ((rows, 2 * wide_k), BF16)],
            [SMEM] * 2 + [VMEM] * (6 + len(dqt)),
        )(slot, span_map, key, value, qr, grad, norm, delta, *dqt)
        parts.append(part)
    swapped = exchanged(parts[0])
    moved = shifted(parts[2], 1)
    dq, dkv = call(
        own_kernel, [((rows, wide_q), BF16), ((rows, 2 * wide_k), F32)], [SMEM] + [VMEM] * 9
    )(slot, tables, kr, v_here, qr, grad, norm, delta, *dqt, swapped)
    part2, _ = lax.optimization_barrier((parts[1], dkv))
    (total,) = call(add_kernel, [((rows, 2 * wide_k), BF16)], [SMEM] + [VMEM] * 3)(
        slot, part2, moved, swapped
    )
    home = shifted(total, 2)

    dk, dv = call(
        final_kernel,
        [((rows, wide_k), BF16), ((rows, wide_k), BF16)],
        [VMEM] * 3,
    )(tables, dkv, home)
    return dq, dk, dv


def solution(mesh):
    placed = (
        P("ctx", "head"),
        P("ctx", "head"),
        P("ctx", "head"),
        P("ctx", "head"),
        P("ctx", "head"),
        P("head", "ctx"),
        P(None, ("ctx", "head")),
        P(),
    )
    return jax.shard_map(
        shards,
        mesh=mesh,
        in_specs=placed,
        out_specs=(P("ctx", "head"), P("ctx", "head"), P("ctx", "head")),
        check_vma=False,
    )
```

```python
import functools
import math

import jax
import jax.numpy as jnp
import numpy as np
from jax import lax
from jax.experimental import pallas as pl
from jax.experimental.pallas import tpu as pltpu
from jax.sharding import PartitionSpec as P

HEAD = 128
HALF = HEAD // 2
WIN = 4
ROPE_BASE = 1000000.0
YARN_FACTOR = 4.0
YARN_INITIAL = 32768.0
BETA_FAST = 32.0
BETA_SLOW = 1.0
YARN_MSCALE = 1.0 + 0.1 * math.log(4.0)
ROOT_SCALE = 1.0 / math.sqrt(HEAD)
LOG2E = math.log2(math.e)
VMEM_LIMIT = 24 * 1024 * 1024

F32 = jnp.float32
BF16 = jnp.bfloat16


def frequencies():
    pair = np.arange(HALF, dtype=np.float64)
    inverse = np.exp(-2.0 * pair / HEAD * math.log(ROPE_BASE))
    ratio = YARN_INITIAL * inverse / (2.0 * math.pi)
    ramp = np.clip((ratio - BETA_SLOW) / (BETA_FAST - BETA_SLOW), 0.0, 1.0)
    return inverse * ((1.0 - ramp) / YARN_FACTOR + ramp)


def frequency_rows(lanes):
    values = frequencies()
    row = lax.broadcasted_iota(jnp.int32, (8, lanes), 0)
    tiles = []
    for first in range(0, HALF, 8):
        tile = jnp.full((8, lanes), float(values[first]), F32)
        for j in range(1, 8):
            tile = jnp.where(row == j, float(values[first + j]), tile)
        tiles.append(tile)
    return jnp.concatenate(tiles, axis=0)


def sine_cosine(angle):
    turns = jnp.floor(angle * (2.0 / math.pi) + 0.5)
    r = angle - turns * 1.5703125
    r = r - turns * 4.837512969970703125e-4
    r = r - turns * 7.54978995489188e-8
    r2 = r * r
    s = r + r * r2 * (-1.6666654611e-1 + r2 * (8.3321608736e-3 - r2 * 1.9515295891e-4))
    c = (
        1.0
        - 0.5 * r2
        + r2
        * r2
        * (4.166664568298827e-2 + r2 * (-1.388731625493765e-3 + r2 * 2.443315711809948e-5))
    )
    quadrant = turns.astype(jnp.int32) & 3
    odd = (quadrant & 1) == 1
    sine = jnp.where(odd, c, s)
    cosine = jnp.where(odd, s, c)
    sine = jnp.where(quadrant >= 2, -sine, sine)
    cosine = jnp.where((quadrant == 1) | (quadrant == 2), -cosine, cosine)
    return sine, cosine


def tables_transposed(place):
    place = place.astype(F32)
    freq = frequency_rows(place.shape[1])
    pair = lax.broadcasted_iota(jnp.int32, freq.shape, 0)
    first = HEAD // 8
    second = first + 3 * HEAD // 16
    chosen = jnp.where(
        pair < first, place[0:1], jnp.where(pair < second, place[1:2], place[2:3])
    )
    sine, cosine = sine_cosine(chosen * freq)
    return cosine * YARN_MSCALE, sine * YARN_MSCALE


def row_tables(cosine_t, sine_t):
    wide = jnp.concatenate([cosine_t, cosine_t], axis=0).T
    signed = jnp.concatenate([-sine_t, sine_t], axis=0).T
    return wide, signed


def rotated(x, wide, signed):
    return x * wide + pltpu.roll(x, HALF, 1) * signed


def dot_nt(a, b):
    return lax.dot_general(a, b, (((1,), (1,)), ((), ())), preferred_element_type=F32)


def dot_nn(a, b):
    return lax.dot_general(a, b, (((1,), (0,)), ((), ())), preferred_element_type=F32)


def dot_tn(a, b):
    return lax.dot_general(a, b, (((0,), (0,)), ((), ())), preferred_element_type=F32)


def pair_part(key, value, query, grad, norm, delta, causal):
    scores = dot_nt(key, query)
    weights = jnp.exp2(scores * (ROOT_SCALE * LOG2E) - norm)
    if causal:
        at_key = lax.broadcasted_iota(jnp.int32, scores.shape, 0)
        at_query = lax.broadcasted_iota(jnp.int32, scores.shape, 1)
        weights = jnp.where(at_key <= at_query, weights, 0.0)
    value_part = dot_nn(weights.astype(BF16), grad)
    score_grad = (weights * (dot_nt(value, grad) - delta)).astype(BF16)
    key_part = dot_nn(score_grad, query)
    query_part = dot_tn(key, score_grad)
    return value_part, key_part, query_part


def key_kernel(slot_ref, own_ref, p1_ref, p2_ref, p3_ref, k_ref, v_ref, kr_ref, kv_ref, tables_ref):
    pieces = (own_ref[...], p1_ref[...], p2_ref[...], p3_ref[...])
    count = len(pieces)
    head = slot_ref[1]
    parts = []
    for j in range(count):
        back = lax.rem(head - j + count, count)
        part = pieces[0]
        for r in range(1, count):
            part = jnp.where(back == r, pieces[r], part)
        parts.append(part)
    cosine_t, sine_t = tables_transposed(jnp.concatenate(parts, axis=1))
    tables_ref[:HALF, :] = cosine_t
    tables_ref[HALF:, :] = sine_t
    wide, signed = row_tables(cosine_t, sine_t)
    for g in range(k_ref.shape[1] // HEAD):
        cols = pl.ds(g * HEAD, HEAD)
        key = rotated(k_ref[:, cols].astype(F32), wide, signed).astype(BF16)
        kr_ref[:, cols] = key
        kv_ref[:, cols] = key
    kv_ref[:, k_ref.shape[1] :] = v_ref[...]


def prep_kernel(
    groups, tables_ref, lse_hbm, q_hbm, do_hbm, at_hbm,
    qr_ref, do_ref, norm_ref, delta_ref, q_ref, at_ref, lse_ref, sems,
):
    heads = qr_ref.shape[1] // HEAD
    size = heads // groups
    copies = []
    for g in range(groups):
        cols = pl.ds(g * size * HEAD, size * HEAD)
        for i, (source, target) in enumerate(
            ((q_hbm, q_ref), (do_hbm, do_ref), (at_hbm, at_ref))
        ):
            copy = pltpu.make_async_copy(
                source.at[:, cols], target.at[:, cols], sems.at[3 * g + i]
            )
            copy.start()
            copies.append(copy)
    lse_copy = pltpu.make_async_copy(lse_hbm, lse_ref, sems.at[3 * groups])
    lse_copy.start()
    wide, signed = row_tables(tables_ref[:HALF, :], tables_ref[HALF:, :])
    chooser = jnp.ones((8, HEAD), BF16)
    for h in range(heads):
        if h % size == 0:
            for copy in copies[3 * (h // size) : 3 * (h // size) + 3]:
                copy.wait()
        hc = pl.ds(h * HEAD, HEAD)
        qr_ref[:, hc] = rotated(q_ref[:, hc].astype(F32), wide, signed).astype(BF16)
        product = do_ref[:, hc].astype(F32) * at_ref[:, hc].astype(F32)
        high = product.astype(BF16)
        low = (product - high.astype(F32)).astype(BF16)
        delta_ref[h : h + 1, :] = (dot_nt(chooser, high) + dot_nt(chooser, low))[:1]
    lse_copy.wait()
    norm_ref[...] = lse_ref[...] * LOG2E


def hop_kernel(step, wanted, started, slot_ref, span_ref, k_ref, v_ref, *refs):
    qr_ref, do_ref, norm_ref, delta_ref = refs[:4]
    count = len(wanted)
    dqt_ins = refs[4 : 4 + count] if started else [None] * count
    dqt_refs, part_ref = refs[-count - 1 : -1], refs[-1]
    rows = qr_ref.shape[0]
    half = rows // 2
    heads = qr_ref.shape[1] // HEAD
    groups = k_ref.shape[1] // HEAD
    size = heads // groups
    me = slot_ref[0]
    other = lax.rem(me + step, span_ref.shape[0])
    earlier = span_ref[other] < span_ref[me]
    norm = norm_ref[...]
    delta = delta_ref[...]

    def run(keys, queries):
        for i, (g, dqt_in, dqt_ref) in enumerate(zip(wanted, dqt_ins, dqt_refs)):
            kc = pl.ds(g * HEAD, HEAD)
            dk = dv = None
            for j in range(size):
                h = g * size + j
                hc = pl.ds(h * HEAD, HEAD)
                to = pl.ds(j * HEAD, HEAD)
                v_part, k_part, q_part = pair_part(
                    k_ref[keys, kc], v_ref[keys, kc], qr_ref[queries, hc], do_ref[queries, hc],
                    norm[h : h + 1, queries.start :], delta[h : h + 1, queries.start :], False,
                )
                if queries.start:
                    before = jnp.zeros((HEAD, queries.start), F32)
                    if dqt_in is not None:
                        before = dqt_in[to, : queries.start]
                    dqt_ref[to, : queries.start] = before
                dqt_ref[to, queries] = q_part if dqt_in is None else dqt_in[to, queries] + q_part
                dv = v_part if dv is None else dv + v_part
                dk = k_part if dk is None else dk + k_part
            part_ref[keys, pl.ds(2 * i * HEAD, HEAD)] = dk.astype(BF16)
            part_ref[keys, pl.ds((2 * i + 1) * HEAD, HEAD)] = dv.astype(BF16)
        if keys.stop < rows:
            part_ref[keys.stop :, :] = jnp.zeros((rows - keys.stop, part_ref.shape[1]), BF16)

    @pl.when(earlier)
    def _():
        run(slice(0, half), slice(0, rows))

    @pl.when(jnp.logical_not(earlier))
    def _():
        run(slice(0, rows), slice(half, rows))


def merged_kernel(step, wanted, started, slot_ref, span_ref, kv_ref, *refs):
    width = kv_ref.shape[1] // 2
    hop_kernel(
        step, wanted, started, slot_ref, span_ref, kv_ref.at[:, :width], kv_ref.at[:, width:],
        *refs,
    )


def own_kernel(groups, k_ref, v_ref, qr_ref, do_ref, norm_ref, delta_ref, *refs):
    dqt_ins, dqt_refs, part_ref = refs[:groups], refs[groups : 2 * groups], refs[2 * groups]
    size = qr_ref.shape[1] // HEAD // groups
    norm = norm_ref[...]
    delta = delta_ref[...]
    for g in range(groups):
        kc = pl.ds(g * HEAD, HEAD)
        dk = dv = None
        for j in range(size):
            h = g * size + j
            hc = pl.ds(h * HEAD, HEAD)
            to = pl.ds(j * HEAD, HEAD)
            v_part, k_part, q_part = pair_part(
                k_ref[:, kc], v_ref[:, kc], qr_ref[:, hc], do_ref[:, hc],
                norm[h : h + 1], delta[h : h + 1], True,
            )
            dqt_refs[g][to, :] = dqt_ins[g][to, :] + q_part
            dv = v_part if dv is None else dv + v_part
            dk = k_part if dk is None else dk + k_part
        part_ref[:, pl.ds(2 * g * HEAD, HEAD)] = dk
        part_ref[:, pl.ds((2 * g + 1) * HEAD, HEAD)] = dv


def query_kernel(groups, slot_ref, tables_ref, own_ref, swapped_ref, *refs):
    dqt_refs, out_ref, sum_ref = refs[:groups], refs[groups], refs[groups + 1]
    odd = (slot_ref[0] & 1) == 1
    sum_ref[...] = own_ref[...] + jnp.where(odd, swapped_ref[...].astype(F32), 0.0)
    cosine_t = tables_ref[:HALF, :] * ROOT_SCALE
    sine_t = tables_ref[HALF:, :] * ROOT_SCALE
    size = dqt_refs[0].shape[0] // HEAD
    for g in range(groups):
        for j in range(size):
            y1 = dqt_refs[g][pl.ds(j * HEAD, HALF), :]
            y2 = dqt_refs[g][pl.ds(j * HEAD + HALF, HALF), :]
            turned = jnp.concatenate(
                [y1 * cosine_t + y2 * sine_t, y2 * cosine_t - y1 * sine_t], axis=0
            )
            out_ref[:, pl.ds((g * size + j) * HEAD, HEAD)] = turned.T.astype(BF16)


def add_kernel(g, slot_ref, two_ref, swapped_ref, three_ref, sum_ref):
    even = (slot_ref[0] & 1) == 0
    cols = pl.ds(2 * g * HEAD, 2 * HEAD)
    total = two_ref[:, cols].astype(F32) + three_ref[...].astype(F32)
    sum_ref[...] = (total + jnp.where(even, swapped_ref[:, cols].astype(F32), 0.0)).astype(BF16)


def final_kernel(groups, tables_ref, own_ref, *refs):
    dk_ref, dv_ref = refs[groups:]
    wide, signed = row_tables(tables_ref[:HALF, :], tables_ref[HALF:, :])
    wide = wide * ROOT_SCALE
    signed = signed * -ROOT_SCALE
    for g in range(groups):
        cols = pl.ds(g * HEAD, HEAD)
        total = own_ref[:, pl.ds(2 * g * HEAD, 2 * HEAD)] + refs[g][...].astype(F32)
        dk_ref[:, cols] = rotated(total[:, :HEAD], wide, signed).astype(BF16)
        dv_ref[:, cols] = total[:, HEAD:].astype(BF16)


SMEM = pl.BlockSpec(memory_space=pltpu.SMEM)
VMEM = pl.BlockSpec(memory_space=pltpu.VMEM)
HBM = pl.BlockSpec(memory_space=pltpu.HBM)


def call(kernel, outs, specs, scratch=()):
    return pl.pallas_call(
        kernel,
        out_shape=[jax.ShapeDtypeStruct(shape, dtype) for shape, dtype in outs],
        in_specs=specs,
        out_specs=[VMEM] * len(outs),
        scratch_shapes=list(scratch),
        compiler_params=pltpu.CompilerParams(vmem_limit_bytes=VMEM_LIMIT),
        cost_estimate=pl.CostEstimate(
            flops=1 << 20, bytes_accessed=1 << 18, transcendentals=0
        ),
    )


def shifted(value, steps, axis="ctx"):
    count = lax.axis_size(axis)
    pairs = [(source, (source + steps) % count) for source in range(count)]
    return lax.ppermute(value, axis, pairs)


def exchanged(value):
    count = lax.axis_size("ctx")
    return lax.ppermute(value, "ctx", [(source, source ^ 1) for source in range(count)])


def shards(q, k, v, do, at, lse, positions, span_map):
    rows = q.shape[0]
    wide_q = q.shape[1]
    wide_k = k.shape[1]
    heads = wide_q // HEAD
    slot = jnp.stack([lax.axis_index("ctx"), lax.axis_index("head")]).astype(jnp.int32)
    q, do, at, k_here, v_here, lse, span_map, own = (
        pltpu.with_memory_space_constraint(x, pltpu.HBM)
        for x in (q, do, at, k, v, lse, span_map, positions)
    )

    pieces = [own] + [shifted(positions, r, "head") for r in (1, 2, 3)]
    groups = wide_k // HEAD
    every = tuple(range(groups))

    v1 = shifted(v, -1)
    kr, kv, tables = call(
        key_kernel,
        [((rows, wide_k), BF16), ((rows, 2 * wide_k), BF16), ((HEAD, rows), F32)],
        [SMEM] + [VMEM] * 6,
    )(slot, *pieces, k_here, v_here)
    k1 = shifted(kr, -1)
    qr, grad, norm, delta = call(
        functools.partial(prep_kernel, groups),
        [((rows, wide_q), BF16)] * 2 + [((heads, rows), F32)] * 2,
        [VMEM] + [HBM] * 4,
        [
            pltpu.VMEM((rows, wide_q), BF16),
            pltpu.VMEM((rows, wide_q), BF16),
            pltpu.VMEM((heads, rows), F32),
            pltpu.SemaphoreType.DMA((3 * groups + 1,)),
        ],
    )(tables, lse, q, do, at)
    held, _ = lax.optimization_barrier((kv, delta))
    kv2 = shifted(held, -2)
    v3 = shifted(v1, -2)

    shared = (qr, grad, norm, delta)
    dqs = [None] * groups

    def hop(kernel, step, wanted, *arrived):
        count = len(wanted)
        started = dqs[wanted[0]] is not None
        before = [dqs[g] for g in wanted] if started else []
        *new, part = call(
            functools.partial(kernel, step, wanted, started),
            [((wide_q // groups, rows), F32)] * count + [((rows, 2 * HEAD * count), BF16)],
            [SMEM] * 2 + [VMEM] * (4 + len(arrived) + len(before)),
        )(slot, span_map, *arrived, *shared, *before)
        for g, dq in zip(wanted, new):
            dqs[g] = dq
        return part

    part1 = hop(hop_kernel, 1, every, k1, v1)
    swapped = exchanged(part1)
    held, _ = lax.optimization_barrier((k1, part1))
    k3 = shifted(held, -2)
    *dqs, own = call(
        functools.partial(own_kernel, groups),
        [((wide_q // groups, rows), F32)] * groups + [((rows, 2 * wide_k), F32)],
        [VMEM] * (6 + groups),
    )(kr, v_here, *shared, *dqs)
    part2 = hop(merged_kernel, 2, every, kv2)
    moved = [shifted(hop(hop_kernel, 3, (g,), k3, v3), 1) for g in every]
    dq, own = call(
        functools.partial(query_kernel, groups),
        [((rows, wide_q), BF16), ((rows, 2 * wide_k), F32)],
        [SMEM] + [VMEM] * (3 + groups),
    )(slot, tables, own, swapped, *dqs)
    part2, _ = lax.optimization_barrier((part2, own))
    home = []
    for g in every:
        (total,) = call(
            functools.partial(add_kernel, g),
            [((rows, 2 * HEAD), BF16)],
            [SMEM] + [VMEM] * 3,
        )(slot, part2, swapped, moved[g])
        home.append(shifted(total, 2))

    dk, dv = call(
        functools.partial(final_kernel, groups),
        [((rows, wide_k), BF16), ((rows, wide_k), BF16)],
        [VMEM] * (2 + groups),
    )(tables, own, *home)
    return dq, dk, dv


def solution(mesh):
    placed = (
        P("ctx", "head"),
        P("ctx", "head"),
        P("ctx", "head"),
        P("ctx", "head"),
        P("ctx", "head"),
        P("head", "ctx"),
        P(None, ("ctx", "head")),
        P(),
    )
    return jax.shard_map(
        shards,
        mesh=mesh,
        in_specs=placed,
        out_specs=(P("ctx", "head"), P("ctx", "head"), P("ctx", "head")),
        check_vma=False,
    )
```

```python
import functools
import math

import jax
import jax.numpy as jnp
import numpy as np
from jax import lax
from jax.experimental import pallas as pl
from jax.experimental.pallas import tpu as pltpu
from jax.sharding import PartitionSpec as P

HEAD = 128
HALF = HEAD // 2
WIN = 4
ROPE_BASE = 1000000.0
YARN_FACTOR = 4.0
YARN_INITIAL = 32768.0
BETA_FAST = 32.0
BETA_SLOW = 1.0
YARN_MSCALE = 1.0 + 0.1 * math.log(4.0)
ROOT_SCALE = 1.0 / math.sqrt(HEAD)
LOG2E = math.log2(math.e)
VMEM_LIMIT = 24 * 1024 * 1024

F32 = jnp.float32
BF16 = jnp.bfloat16


def frequencies():
    pair = np.arange(HALF, dtype=np.float64)
    inverse = np.exp(-2.0 * pair / HEAD * math.log(ROPE_BASE))
    ratio = YARN_INITIAL * inverse / (2.0 * math.pi)
    ramp = np.clip((ratio - BETA_SLOW) / (BETA_FAST - BETA_SLOW), 0.0, 1.0)
    return inverse * ((1.0 - ramp) / YARN_FACTOR + ramp)


def frequency_rows(lanes):
    values = frequencies()
    row = lax.broadcasted_iota(jnp.int32, (8, lanes), 0)
    tiles = []
    for first in range(0, HALF, 8):
        tile = jnp.full((8, lanes), float(values[first]), F32)
        for j in range(1, 8):
            tile = jnp.where(row == j, float(values[first + j]), tile)
        tiles.append(tile)
    return jnp.concatenate(tiles, axis=0)


def sine_cosine(angle):
    turns = jnp.floor(angle * (2.0 / math.pi) + 0.5)
    r = angle - turns * 1.5703125
    r = r - turns * 4.837512969970703125e-4
    r = r - turns * 7.54978995489188e-8
    r2 = r * r
    s = r + r * r2 * (-1.6666654611e-1 + r2 * (8.3321608736e-3 - r2 * 1.9515295891e-4))
    c = (
        1.0
        - 0.5 * r2
        + r2
        * r2
        * (4.166664568298827e-2 + r2 * (-1.388731625493765e-3 + r2 * 2.443315711809948e-5))
    )
    quadrant = turns.astype(jnp.int32) & 3
    odd = (quadrant & 1) == 1
    sine = jnp.where(odd, c, s)
    cosine = jnp.where(odd, s, c)
    sine = jnp.where(quadrant >= 2, -sine, sine)
    cosine = jnp.where((quadrant == 1) | (quadrant == 2), -cosine, cosine)
    return sine, cosine


def tables_transposed(place):
    place = place.astype(F32)
    freq = frequency_rows(place.shape[1])
    pair = lax.broadcasted_iota(jnp.int32, freq.shape, 0)
    first = HEAD // 8
    second = first + 3 * HEAD // 16
    chosen = jnp.where(
        pair < first, place[0:1], jnp.where(pair < second, place[1:2], place[2:3])
    )
    sine, cosine = sine_cosine(chosen * freq)
    return cosine * YARN_MSCALE, sine * YARN_MSCALE


def row_tables(cosine_t, sine_t):
    wide = jnp.concatenate([cosine_t, cosine_t], axis=0).T
    signed = jnp.concatenate([-sine_t, sine_t], axis=0).T
    return wide, signed


def rotated(x, wide, signed):
    return x * wide + pltpu.roll(x, HALF, 1) * signed


def dot_nt(a, b):
    return lax.dot_general(a, b, (((1,), (1,)), ((), ())), preferred_element_type=F32)


def dot_nn(a, b):
    return lax.dot_general(a, b, (((1,), (0,)), ((), ())), preferred_element_type=F32)


def dot_tn(a, b):
    return lax.dot_general(a, b, (((0,), (0,)), ((), ())), preferred_element_type=F32)


def pair_part(key, value, query, grad, norm, delta, causal):
    scores = dot_nt(key, query)
    weights = jnp.exp2(scores * (ROOT_SCALE * LOG2E) - norm)
    if causal:
        at_key = lax.broadcasted_iota(jnp.int32, scores.shape, 0)
        at_query = lax.broadcasted_iota(jnp.int32, scores.shape, 1)
        weights = jnp.where(at_key <= at_query, weights, 0.0)
    value_part = dot_nn(weights.astype(BF16), grad)
    score_grad = (weights * (dot_nt(value, grad) - delta)).astype(BF16)
    key_part = dot_nn(score_grad, query)
    query_part = dot_tn(key, score_grad)
    return value_part, key_part, query_part


def key_kernel(own_ref, p1_ref, p2_ref, p3_ref, k_ref, v_ref, kr_ref, kv_ref, tables_ref):
    pieces = (own_ref[...], p1_ref[...], p2_ref[...], p3_ref[...])
    count = len(pieces)
    head = lax.axis_index("head")
    parts = []
    for j in range(count):
        back = lax.rem(head - j + count, count)
        part = pieces[0]
        for r in range(1, count):
            part = jnp.where(back == r, pieces[r], part)
        parts.append(part)
    cosine_t, sine_t = tables_transposed(jnp.concatenate(parts, axis=1))
    tables_ref[:HALF, :] = cosine_t
    tables_ref[HALF:, :] = sine_t
    wide, signed = row_tables(cosine_t, sine_t)
    for g in range(k_ref.shape[1] // HEAD):
        cols = pl.ds(g * HEAD, HEAD)
        key = rotated(k_ref[:, cols].astype(F32), wide, signed).astype(BF16)
        kr_ref[:, cols] = key
        kv_ref[:, cols] = key
    kv_ref[:, k_ref.shape[1] :] = v_ref[...]


def prep_kernel(
    groups, span_ref, tables_ref, lse_hbm, q_hbm, do_hbm, at_hbm,
    qr_ref, do_ref, norm_ref, delta_ref, flag_ref, q_ref, at_ref, lse_ref, sems,
):
    heads = qr_ref.shape[1] // HEAD
    size = heads // groups
    copies = []
    for g in range(groups):
        cols = pl.ds(g * size * HEAD, size * HEAD)
        for i, (source, target) in enumerate(
            ((q_hbm, q_ref), (do_hbm, do_ref), (at_hbm, at_ref))
        ):
            copy = pltpu.make_async_copy(
                source.at[:, cols], target.at[:, cols], sems.at[3 * g + i]
            )
            copy.start()
            copies.append(copy)
    lse_copy = pltpu.make_async_copy(lse_hbm, lse_ref, sems.at[3 * groups])
    lse_copy.start()
    me = lax.axis_index("ctx")
    step_row = lax.broadcasted_iota(jnp.int32, flag_ref.shape, 0)
    flags = jnp.zeros(flag_ref.shape, jnp.int32)
    for step in range(1, WIN):
        other = lax.rem(me + step, span_ref.shape[0])
        earlier = jnp.where(span_ref[other] < span_ref[me], 1, 0)
        flags = jnp.where(step_row == step, earlier, flags)
    flag_ref[...] = flags
    wide, signed = row_tables(tables_ref[:HALF, :], tables_ref[HALF:, :])
    chooser = jnp.ones((8, HEAD), BF16)
    for h in range(heads):
        if h % size == 0:
            for copy in copies[3 * (h // size) : 3 * (h // size) + 3]:
                copy.wait()
        hc = pl.ds(h * HEAD, HEAD)
        qr_ref[:, hc] = rotated(q_ref[:, hc].astype(F32), wide, signed).astype(BF16)
        product = do_ref[:, hc].astype(F32) * at_ref[:, hc].astype(F32)
        high = product.astype(BF16)
        low = (product - high.astype(F32)).astype(BF16)
        delta_ref[h : h + 1, :] = (dot_nt(chooser, high) + dot_nt(chooser, low))[:1]
    lse_copy.wait()
    norm_ref[...] = lse_ref[...] * LOG2E


def hop_kernel(step, wanted, started, k_ref, v_ref, *refs):
    qr_ref, do_ref, norm_ref, delta_ref, flag_ref = refs[:5]
    count = len(wanted)
    dqt_ins = refs[5 : 5 + count] if started else [None] * count
    dqt_refs, part_ref = refs[-count - 1 : -1], refs[-1]
    rows = qr_ref.shape[0]
    half = rows // 2
    heads = qr_ref.shape[1] // HEAD
    groups = k_ref.shape[1] // HEAD
    size = heads // groups
    earlier = flag_ref[step, 0] == 1
    norm = norm_ref[...]
    delta = delta_ref[...]

    def run(keys, queries):
        for i, (g, dqt_in, dqt_ref) in enumerate(zip(wanted, dqt_ins, dqt_refs)):
            kc = pl.ds(g * HEAD, HEAD)
            dk = dv = None
            for j in range(size):
                h = g * size + j
                hc = pl.ds(h * HEAD, HEAD)
                to = pl.ds(j * HEAD, HEAD)
                v_part, k_part, q_part = pair_part(
                    k_ref[keys, kc], v_ref[keys, kc], qr_ref[queries, hc], do_ref[queries, hc],
                    norm[h : h + 1, queries.start :], delta[h : h + 1, queries.start :], False,
                )
                if queries.start:
                    before = jnp.zeros((HEAD, queries.start), F32)
                    if dqt_in is not None:
                        before = dqt_in[to, : queries.start]
                    dqt_ref[to, : queries.start] = before
                dqt_ref[to, queries] = q_part if dqt_in is None else dqt_in[to, queries] + q_part
                dv = v_part if dv is None else dv + v_part
                dk = k_part if dk is None else dk + k_part
            part_ref[keys, pl.ds(2 * i * HEAD, HEAD)] = dk.astype(BF16)
            part_ref[keys, pl.ds((2 * i + 1) * HEAD, HEAD)] = dv.astype(BF16)
        if keys.stop < rows:
            part_ref[keys.stop :, :] = jnp.zeros((rows - keys.stop, part_ref.shape[1]), BF16)

    @pl.when(earlier)
    def _():
        run(slice(0, half), slice(0, rows))

    @pl.when(jnp.logical_not(earlier))
    def _():
        run(slice(0, rows), slice(half, rows))


def merged_kernel(step, wanted, started, kv_ref, *refs):
    width = kv_ref.shape[1] // 2
    hop_kernel(step, wanted, started, kv_ref.at[:, :width], kv_ref.at[:, width:], *refs)


def own_kernel(groups, k_ref, v_ref, qr_ref, do_ref, norm_ref, delta_ref, *refs):
    dqt_refs, part_ref = refs[:groups], refs[groups]
    size = qr_ref.shape[1] // HEAD // groups
    norm = norm_ref[...]
    delta = delta_ref[...]
    for g in range(groups):
        kc = pl.ds(g * HEAD, HEAD)
        dk = dv = None
        for j in range(size):
            h = g * size + j
            hc = pl.ds(h * HEAD, HEAD)
            to = pl.ds(j * HEAD, HEAD)
            v_part, k_part, q_part = pair_part(
                k_ref[:, kc], v_ref[:, kc], qr_ref[:, hc], do_ref[:, hc],
                norm[h : h + 1], delta[h : h + 1], True,
            )
            dqt_refs[g][to, :] = q_part
            dv = v_part if dv is None else dv + v_part
            dk = k_part if dk is None else dk + k_part
        part_ref[:, pl.ds(2 * g * HEAD, HEAD)] = dk
        part_ref[:, pl.ds((2 * g + 1) * HEAD, HEAD)] = dv


def query_kernel(groups, tables_ref, own_ref, swapped_ref, *refs):
    dqt_refs, out_ref, sum_ref = refs[:groups], refs[groups], refs[groups + 1]
    odd = (lax.axis_index("ctx") & 1) == 1
    sum_ref[...] = own_ref[...] + jnp.where(odd, swapped_ref[...].astype(F32), 0.0)
    cosine_t = tables_ref[:HALF, :] * ROOT_SCALE
    sine_t = tables_ref[HALF:, :] * ROOT_SCALE
    size = dqt_refs[0].shape[0] // HEAD
    for g in range(groups):
        for j in range(size):
            y1 = dqt_refs[g][pl.ds(j * HEAD, HALF), :]
            y2 = dqt_refs[g][pl.ds(j * HEAD + HALF, HALF), :]
            turned = jnp.concatenate(
                [y1 * cosine_t + y2 * sine_t, y2 * cosine_t - y1 * sine_t], axis=0
            )
            out_ref[:, pl.ds((g * size + j) * HEAD, HEAD)] = turned.T.astype(BF16)


def add_kernel(g, two_ref, swapped_ref, three_ref, sum_ref):
    even = (lax.axis_index("ctx") & 1) == 0
    cols = pl.ds(2 * g * HEAD, 2 * HEAD)
    total = two_ref[:, cols].astype(F32) + three_ref[...].astype(F32)
    sum_ref[...] = (total + jnp.where(even, swapped_ref[:, cols].astype(F32), 0.0)).astype(BF16)


def final_kernel(groups, tables_ref, own_ref, *refs):
    dk_ref, dv_ref = refs[groups:]
    wide, signed = row_tables(tables_ref[:HALF, :], tables_ref[HALF:, :])
    wide = wide * ROOT_SCALE
    signed = signed * -ROOT_SCALE
    for g in range(groups):
        cols = pl.ds(g * HEAD, HEAD)
        total = own_ref[:, pl.ds(2 * g * HEAD, 2 * HEAD)] + refs[g][...].astype(F32)
        dk_ref[:, cols] = rotated(total[:, :HEAD], wide, signed).astype(BF16)
        dv_ref[:, cols] = total[:, HEAD:].astype(BF16)


SMEM = pl.BlockSpec(memory_space=pltpu.SMEM)
VMEM = pl.BlockSpec(memory_space=pltpu.VMEM)
HBM = pl.BlockSpec(memory_space=pltpu.HBM)


def call(kernel, outs, specs, scratch=(), micros=1):
    return pl.pallas_call(
        kernel,
        out_shape=[jax.ShapeDtypeStruct(shape, dtype) for shape, dtype in outs],
        in_specs=specs,
        out_specs=[VMEM] * len(outs),
        scratch_shapes=list(scratch),
        compiler_params=pltpu.CompilerParams(vmem_limit_bytes=VMEM_LIMIT),
        cost_estimate=pl.CostEstimate(
            flops=1 << 20, bytes_accessed=micros * 3690000, transcendentals=0
        ),
    )


def shifted(value, steps, axis="ctx"):
    count = lax.axis_size(axis)
    pairs = [(source, (source + steps) % count) for source in range(count)]
    return lax.ppermute(value, axis, pairs)


def exchanged(value):
    count = lax.axis_size("ctx")
    return lax.ppermute(value, "ctx", [(source, source ^ 1) for source in range(count)])


def shards(q, k, v, do, at, lse, positions, span_map):
    rows = q.shape[0]
    wide_q = q.shape[1]
    wide_k = k.shape[1]
    heads = wide_q // HEAD
    q, do, at, k_here, v_here, lse, span_map, own = (
        pltpu.with_memory_space_constraint(x, pltpu.HBM)
        for x in (q, do, at, k, v, lse, span_map, positions)
    )

    pieces = [own] + [shifted(positions, r, "head") for r in (1, 2, 3)]
    groups = wide_k // HEAD
    every = tuple(range(groups))

    groups = wide_k // HEAD
    every = tuple(range(groups))

    v1 = shifted(v, -1)
    kr, kv, tables = call(
        key_kernel,
        [((rows, wide_k), BF16), ((rows, 2 * wide_k), BF16), ((HEAD, rows), F32)],
        [VMEM] * 6,
    )(*pieces, k_here, v_here)
    k1 = shifted(kr, -1)
    shared = call(
        functools.partial(prep_kernel, groups),
        [((rows, wide_q), BF16)] * 2 + [((heads, rows), F32)] * 2 + [((8, HEAD), jnp.int32)],
        [SMEM, VMEM] + [HBM] * 4,
        [
            pltpu.VMEM((rows, wide_q), BF16),
            pltpu.VMEM((rows, wide_q), BF16),
            pltpu.VMEM((heads, rows), F32),
            pltpu.SemaphoreType.DMA((3 * groups + 1,)),
        ],
        micros=2,
    )(span_map, tables, lse, q, do, at)
    *dqs, own = call(
        functools.partial(own_kernel, groups),
        [((wide_q // groups, rows), F32)] * groups + [((rows, 2 * wide_k), F32)],
        [VMEM] * 6,
        micros=3,
    )(kr, v_here, *shared[:4])

    def hop(kernel, step, wanted, *arrived):
        count = len(wanted)
        before = [dqs[g] for g in wanted]
        *new, part = call(
            functools.partial(kernel, step, wanted, True),
            [((wide_q // groups, rows), F32)] * count + [((rows, 2 * HEAD * count), BF16)],
            [VMEM] * (5 + len(arrived) + count),
            micros=count,
        )(*arrived, *shared, *before)
        for g, dq in zip(wanted, new):
            dqs[g] = dq
        return part

    v1, k1, _ = lax.optimization_barrier((v1, k1, own))
    v3 = shifted(v1, -2)
    k3 = shifted(k1, -2)
    part1 = hop(hop_kernel, 1, every, k1, v1)
    held, _ = lax.optimization_barrier((kv, part1))
    kv2 = shifted(held, -2)
    part1, k3, v3 = lax.optimization_barrier((part1, k3, v3))
    swapped = exchanged(part1)
    moved = [shifted(hop(hop_kernel, 3, (g,), k3, v3), 1) for g in every]
    part2 = hop(merged_kernel, 2, every, kv2)
    dq, own = call(
        functools.partial(query_kernel, groups),
        [((rows, wide_q), BF16), ((rows, 2 * wide_k), F32)],
        [VMEM] * (3 + groups),
    )(tables, own, swapped, *dqs)
    part2, _ = lax.optimization_barrier((part2, own))
    home = []
    for g in every:
        (total,) = call(
            functools.partial(add_kernel, g), [((rows, 2 * HEAD), BF16)], [VMEM] * 3
        )(part2, swapped, moved[g])
        home.append(shifted(total, 2))

    dk, dv = call(
        functools.partial(final_kernel, groups),
        [((rows, wide_k), BF16), ((rows, wide_k), BF16)],
        [VMEM] * (2 + groups),
    )(tables, own, *home)
    return dq, dk, dv


def solution(mesh):
    placed = (
        P("ctx", "head"),
        P("ctx", "head"),
        P("ctx", "head"),
        P("ctx", "head"),
        P("ctx", "head"),
        P("head", "ctx"),
        P(None, ("ctx", "head")),
        P(),
    )
    return jax.shard_map(
        shards,
        mesh=mesh,
        in_specs=placed,
        out_specs=(P("ctx", "head"), P("ctx", "head"), P("ctx", "head")),
        check_vma=False,
    )
```

```python
import functools
import math

import jax
import jax.numpy as jnp
import numpy as np
from jax import lax
from jax.experimental import pallas as pl
from jax.experimental.pallas import tpu as pltpu
from jax.sharding import PartitionSpec as P

HEAD = 128
HALF = HEAD // 2
WIN = 4
ROPE_BASE = 1000000.0
YARN_FACTOR = 4.0
YARN_INITIAL = 32768.0
BETA_FAST = 32.0
BETA_SLOW = 1.0
YARN_MSCALE = 1.0 + 0.1 * math.log(4.0)
ROOT_SCALE = 1.0 / math.sqrt(HEAD)
LOG2E = math.log2(math.e)
VMEM_LIMIT = 24 * 1024 * 1024

F32 = jnp.float32
BF16 = jnp.bfloat16


def frequencies():
    pair = np.arange(HALF, dtype=np.float64)
    inverse = np.exp(-2.0 * pair / HEAD * math.log(ROPE_BASE))
    ratio = YARN_INITIAL * inverse / (2.0 * math.pi)
    ramp = np.clip((ratio - BETA_SLOW) / (BETA_FAST - BETA_SLOW), 0.0, 1.0)
    return inverse * ((1.0 - ramp) / YARN_FACTOR + ramp)


def frequency_rows(lanes):
    values = frequencies()
    row = lax.broadcasted_iota(jnp.int32, (8, lanes), 0)
    tiles = []
    for first in range(0, HALF, 8):
        tile = jnp.full((8, lanes), float(values[first]), F32)
        for j in range(1, 8):
            tile = jnp.where(row == j, float(values[first + j]), tile)
        tiles.append(tile)
    return jnp.concatenate(tiles, axis=0)


def sine_cosine(angle):
    turns = jnp.floor(angle * (2.0 / math.pi) + 0.5)
    r = angle - turns * 1.5703125
    r = r - turns * 4.837512969970703125e-4
    r = r - turns * 7.54978995489188e-8
    r2 = r * r
    s = r + r * r2 * (-1.6666654611e-1 + r2 * (8.3321608736e-3 - r2 * 1.9515295891e-4))
    c = (
        1.0
        - 0.5 * r2
        + r2
        * r2
        * (4.166664568298827e-2 + r2 * (-1.388731625493765e-3 + r2 * 2.443315711809948e-5))
    )
    quadrant = turns.astype(jnp.int32) & 3
    odd = (quadrant & 1) == 1
    sine = jnp.where(odd, c, s)
    cosine = jnp.where(odd, s, c)
    sine = jnp.where(quadrant >= 2, -sine, sine)
    cosine = jnp.where((quadrant == 1) | (quadrant == 2), -cosine, cosine)
    return sine, cosine


def tables_transposed(place):
    place = place.astype(F32)
    freq = frequency_rows(place.shape[1])
    pair = lax.broadcasted_iota(jnp.int32, freq.shape, 0)
    first = HEAD // 8
    second = first + 3 * HEAD // 16
    chosen = jnp.where(
        pair < first, place[0:1], jnp.where(pair < second, place[1:2], place[2:3])
    )
    sine, cosine = sine_cosine(chosen * freq)
    return cosine * YARN_MSCALE, sine * YARN_MSCALE


def row_tables(cosine_t, sine_t):
    wide = jnp.concatenate([cosine_t, cosine_t], axis=0).T
    signed = jnp.concatenate([-sine_t, sine_t], axis=0).T
    return wide, signed


def rotated(x, wide, signed):
    return x * wide + pltpu.roll(x, HALF, 1) * signed


def dot_nt(a, b):
    return lax.dot_general(a, b, (((1,), (1,)), ((), ())), preferred_element_type=F32)


def dot_nn(a, b):
    return lax.dot_general(a, b, (((1,), (0,)), ((), ())), preferred_element_type=F32)


def dot_tn(a, b):
    return lax.dot_general(a, b, (((0,), (0,)), ((), ())), preferred_element_type=F32)


def pair_part(key, value, query, grad, norm, delta, causal):
    scores = dot_nt(key, query)
    weights = jnp.exp2(scores * (ROOT_SCALE * LOG2E) - norm)
    if causal:
        at_key = lax.broadcasted_iota(jnp.int32, scores.shape, 0)
        at_query = lax.broadcasted_iota(jnp.int32, scores.shape, 1)
        weights = jnp.where(at_key <= at_query, weights, 0.0)
    value_part = dot_nn(weights.astype(BF16), grad)
    score_grad = (weights * (dot_nt(value, grad) - delta)).astype(BF16)
    key_part = dot_nn(score_grad, query)
    query_part = dot_tn(key, score_grad)
    return value_part, key_part, query_part


def key_kernel(own_ref, p1_ref, p2_ref, p3_ref, k_ref, v_ref, kr_ref, kv_ref, tables_ref):
    pieces = (own_ref[...], p1_ref[...], p2_ref[...], p3_ref[...])
    count = len(pieces)
    head = lax.axis_index("head")
    parts = []
    for j in range(count):
        back = lax.rem(head - j + count, count)
        part = pieces[0]
        for r in range(1, count):
            part = jnp.where(back == r, pieces[r], part)
        parts.append(part)
    cosine_t, sine_t = tables_transposed(jnp.concatenate(parts, axis=1))
    tables_ref[:HALF, :] = cosine_t
    tables_ref[HALF:, :] = sine_t
    wide, signed = row_tables(cosine_t, sine_t)
    for g in range(k_ref.shape[1] // HEAD):
        cols = pl.ds(g * HEAD, HEAD)
        key = rotated(k_ref[:, cols].astype(F32), wide, signed).astype(BF16)
        kr_ref[:, cols] = key
        kv_ref[:, cols] = key
    kv_ref[:, k_ref.shape[1] :] = v_ref[...]


def prep_kernel(
    groups, span_ref, tables_ref, lse_hbm, q_hbm, do_hbm, at_hbm,
    qr_ref, do_ref, norm_ref, delta_ref, flag_ref, q_ref, at_ref, lse_ref, sems,
):
    heads = qr_ref.shape[1] // HEAD
    size = heads // groups
    copies = []
    for g in range(groups):
        cols = pl.ds(g * size * HEAD, size * HEAD)
        for i, (source, target) in enumerate(
            ((q_hbm, q_ref), (do_hbm, do_ref), (at_hbm, at_ref))
        ):
            copy = pltpu.make_async_copy(
                source.at[:, cols], target.at[:, cols], sems.at[3 * g + i]
            )
            copy.start()
            copies.append(copy)
    lse_copy = pltpu.make_async_copy(lse_hbm, lse_ref, sems.at[3 * groups])
    lse_copy.start()
    me = lax.axis_index("ctx")
    step_row = lax.broadcasted_iota(jnp.int32, flag_ref.shape, 0)
    flags = jnp.zeros(flag_ref.shape, jnp.int32)
    for step in range(1, WIN):
        other = lax.rem(me + step, span_ref.shape[0])
        earlier = jnp.where(span_ref[other] < span_ref[me], 1, 0)
        flags = jnp.where(step_row == step, earlier, flags)
    flag_ref[...] = flags
    wide, signed = row_tables(tables_ref[:HALF, :], tables_ref[HALF:, :])
    chooser = jnp.ones((8, HEAD), BF16)
    for h in range(heads):
        if h % size == 0:
            for copy in copies[3 * (h // size) : 3 * (h // size) + 3]:
                copy.wait()
        hc = pl.ds(h * HEAD, HEAD)
        qr_ref[:, hc] = rotated(q_ref[:, hc].astype(F32), wide, signed).astype(BF16)
        product = do_ref[:, hc].astype(F32) * at_ref[:, hc].astype(F32)
        high = product.astype(BF16)
        low = (product - high.astype(F32)).astype(BF16)
        delta_ref[h : h + 1, :] = (dot_nt(chooser, high) + dot_nt(chooser, low))[:1]
    lse_copy.wait()
    norm_ref[...] = lse_ref[...] * LOG2E


def hop_kernel(step, wanted, *refs):
    count = len(wanted)
    dqt_ins, dqt_refs, part_ref = refs[:count], refs[-count - 1 : -1], refs[-1]
    k_ref, v_ref, qr_ref, do_ref, norm_ref, delta_ref, flag_ref = refs[count : -count - 1]
    rows = qr_ref.shape[0]
    half = rows // 2
    heads = qr_ref.shape[1] // HEAD
    groups = k_ref.shape[1] // HEAD
    size = heads // groups
    earlier = flag_ref[step, 0] == 1
    norm = norm_ref[...]
    delta = delta_ref[...]

    def run(keys, queries):
        for i, (g, dqt_in, dqt_ref) in enumerate(zip(wanted, dqt_ins, dqt_refs)):
            kc = pl.ds(g * HEAD, HEAD)
            dk = dv = None
            for j in range(size):
                h = g * size + j
                hc = pl.ds(h * HEAD, HEAD)
                to = pl.ds(j * HEAD, HEAD)
                v_part, k_part, q_part = pair_part(
                    k_ref[keys, kc], v_ref[keys, kc], qr_ref[queries, hc], do_ref[queries, hc],
                    norm[h : h + 1, queries.start :], delta[h : h + 1, queries.start :], False,
                )
                if queries.start:
                    dqt_ref[to, : queries.start] = dqt_in[to, : queries.start]
                dqt_ref[to, queries] = dqt_in[to, queries] + q_part
                dv = v_part if dv is None else dv + v_part
                dk = k_part if dk is None else dk + k_part
            part_ref[keys, pl.ds(2 * i * HEAD, HEAD)] = dk.astype(BF16)
            part_ref[keys, pl.ds((2 * i + 1) * HEAD, HEAD)] = dv.astype(BF16)
        if keys.stop < rows:
            part_ref[keys.stop :, :] = jnp.zeros((rows - keys.stop, part_ref.shape[1]), BF16)

    @pl.when(earlier)
    def _():
        run(slice(0, half), slice(0, rows))

    @pl.when(jnp.logical_not(earlier))
    def _():
        run(slice(0, rows), slice(half, rows))


def merged_kernel(step, wanted, *refs):
    count = len(wanted)
    kv_ref = refs[count]
    width = kv_ref.shape[1] // 2
    hop_kernel(
        step, wanted, *refs[:count], kv_ref.at[:, :width], kv_ref.at[:, width:], *refs[count + 1 :]
    )


def beside_kernel(k_ref, v_ref, kv_ref):
    width = k_ref.shape[1]
    kv_ref[:, :width] = k_ref[...]
    kv_ref[:, width:] = v_ref[...]


def own_kernel(groups, k_ref, v_ref, qr_ref, do_ref, norm_ref, delta_ref, *refs):
    dqt_refs, part_ref = refs[:groups], refs[groups]
    size = qr_ref.shape[1] // HEAD // groups
    norm = norm_ref[...]
    delta = delta_ref[...]
    for g in range(groups):
        kc = pl.ds(g * HEAD, HEAD)
        dk = dv = None
        for j in range(size):
            h = g * size + j
            hc = pl.ds(h * HEAD, HEAD)
            to = pl.ds(j * HEAD, HEAD)
            v_part, k_part, q_part = pair_part(
                k_ref[:, kc], v_ref[:, kc], qr_ref[:, hc], do_ref[:, hc],
                norm[h : h + 1], delta[h : h + 1], True,
            )
            dqt_refs[g][to, :] = q_part
            dv = v_part if dv is None else dv + v_part
            dk = k_part if dk is None else dk + k_part
        part_ref[:, pl.ds(2 * g * HEAD, HEAD)] = dk
        part_ref[:, pl.ds((2 * g + 1) * HEAD, HEAD)] = dv


def query_kernel(groups, tables_ref, *refs):
    dqt_refs = refs[:groups]
    own_ref, swapped_ref, out_ref, sum_ref = refs[groups:]
    odd = (lax.axis_index("ctx") & 1) == 1
    sum_ref[...] = own_ref[...] + jnp.where(odd, swapped_ref[...].astype(F32), 0.0)
    cosine_t = tables_ref[:HALF, :] * ROOT_SCALE
    sine_t = tables_ref[HALF:, :] * ROOT_SCALE
    size = dqt_refs[0].shape[0] // HEAD
    for g in range(groups):
        for j in range(size):
            y1 = dqt_refs[g][pl.ds(j * HEAD, HALF), :]
            y2 = dqt_refs[g][pl.ds(j * HEAD + HALF, HALF), :]
            turned = jnp.concatenate(
                [y1 * cosine_t + y2 * sine_t, y2 * cosine_t - y1 * sine_t], axis=0
            )
            out_ref[:, pl.ds((g * size + j) * HEAD, HEAD)] = turned.T.astype(BF16)


def add_kernel(g, two_ref, swapped_ref, three_ref, sum_ref):
    even = (lax.axis_index("ctx") & 1) == 0
    cols = pl.ds(2 * g * HEAD, 2 * HEAD)
    total = two_ref[:, cols].astype(F32) + three_ref[...].astype(F32)
    sum_ref[...] = (total + jnp.where(even, swapped_ref[:, cols].astype(F32), 0.0)).astype(BF16)


def final_kernel(groups, tables_ref, own_ref, *refs):
    dk_ref, dv_ref = refs[groups:]
    wide, signed = row_tables(tables_ref[:HALF, :], tables_ref[HALF:, :])
    wide = wide * ROOT_SCALE
    signed = signed * -ROOT_SCALE
    for g in range(groups):
        cols = pl.ds(g * HEAD, HEAD)
        total = own_ref[:, pl.ds(2 * g * HEAD, 2 * HEAD)] + refs[g][...].astype(F32)
        dk_ref[:, cols] = rotated(total[:, :HEAD], wide, signed).astype(BF16)
        dv_ref[:, cols] = total[:, HEAD:].astype(BF16)


SMEM = pl.BlockSpec(memory_space=pltpu.SMEM)
VMEM = pl.BlockSpec(memory_space=pltpu.VMEM)
HBM = pl.BlockSpec(memory_space=pltpu.HBM)


def call(kernel, outs, specs, scratch=(), micros=1):
    return pl.pallas_call(
        kernel,
        out_shape=[jax.ShapeDtypeStruct(shape, dtype) for shape, dtype in outs],
        in_specs=specs,
        out_specs=[VMEM] * len(outs),
        scratch_shapes=list(scratch),
        compiler_params=pltpu.CompilerParams(vmem_limit_bytes=VMEM_LIMIT),
        cost_estimate=pl.CostEstimate(
            flops=1 << 20, bytes_accessed=micros * 3690000, transcendentals=0
        ),
    )


def shifted(value, steps, axis="ctx"):
    count = lax.axis_size(axis)
    pairs = [(source, (source + steps) % count) for source in range(count)]
    return lax.ppermute(value, axis, pairs)


def exchanged(value):
    count = lax.axis_size("ctx")
    return lax.ppermute(value, "ctx", [(source, source ^ 1) for source in range(count)])


def shards(q, k, v, do, at, lse, positions, span_map):
    rows = q.shape[0]
    wide_q = q.shape[1]
    wide_k = k.shape[1]
    heads = wide_q // HEAD
    q, do, at, k_here, v_here, lse, span_map, own = (
        pltpu.with_memory_space_constraint(x, pltpu.HBM)
        for x in (q, do, at, k, v, lse, span_map, positions)
    )

    pieces = [own] + [shifted(positions, r, "head") for r in (1, 2, 3)]
    groups = wide_k // HEAD
    every = tuple(range(groups))

    groups = wide_k // HEAD
    every = tuple(range(groups))

    v1 = shifted(v, -1)
    kr, kv, tables = call(
        key_kernel,
        [((rows, wide_k), BF16), ((rows, 2 * wide_k), BF16), ((HEAD, rows), F32)],
        [VMEM] * 6,
    )(*pieces, k_here, v_here)
    k1 = shifted(kr, -1)
    shared = call(
        functools.partial(prep_kernel, groups),
        [((rows, wide_q), BF16)] * 2 + [((heads, rows), F32)] * 2 + [((8, HEAD), jnp.int32)],
        [SMEM, VMEM] + [HBM] * 4,
        [
            pltpu.VMEM((rows, wide_q), BF16),
            pltpu.VMEM((rows, wide_q), BF16),
            pltpu.VMEM((heads, rows), F32),
            pltpu.SemaphoreType.DMA((3 * groups + 1,)),
        ],
        micros=2,
    )(span_map, tables, lse, q, do, at)
    *dqs, own = call(
        functools.partial(own_kernel, groups),
        [((wide_q // groups, rows), F32)] * groups + [((rows, 2 * wide_k), F32)],
        [VMEM] * 6,
        micros=3,
    )(kr, v_here, *shared[:4])

    def hop(kernel, step, wanted, *arrived):
        count = len(wanted)
        before = [dqs[g] for g in wanted]
        *new, part = call(
            functools.partial(kernel, step, wanted),
            [((wide_q // groups, rows), F32)] * count + [((rows, 2 * HEAD * count), BF16)],
            [VMEM] * (5 + len(arrived) + count),
            micros=count,
        )(*before, *arrived, *shared)
        for g, dq in zip(wanted, new):
            dqs[g] = dq
        return part

    k1, _ = lax.optimization_barrier((k1, own))
    (kv1,) = call(beside_kernel, [((rows, 2 * wide_k), BF16)], [VMEM] * 2)(k1, v1)
    kv3 = shifted(kv1, -2)
    part1 = hop(merged_kernel, 1, every, kv1)
    held, _ = lax.optimization_barrier((kv, part1))
    kv2 = shifted(held, -2)
    swapped = exchanged(part1)
    moved = [shifted(hop(merged_kernel, 3, (g,), kv3), 1) for g in every]
    part2 = hop(merged_kernel, 2, every, kv2)
    dq, own = call(
        functools.partial(query_kernel, groups),
        [((rows, wide_q), BF16), ((rows, 2 * wide_k), F32)],
        [VMEM] * (3 + groups),
    )(tables, *dqs, own, swapped)
    part2, _ = lax.optimization_barrier((part2, own))
    home = []
    for g in every:
        (total,) = call(
            functools.partial(add_kernel, g), [((rows, 2 * HEAD), BF16)], [VMEM] * 3
        )(part2, swapped, moved[g])
        home.append(shifted(total, 2))

    dk, dv = call(
        functools.partial(final_kernel, groups),
        [((rows, wide_k), BF16), ((rows, wide_k), BF16)],
        [VMEM] * (2 + groups),
    )(tables, own, *home)
    return dq, dk, dv


def solution(mesh):
    placed = (
        P("ctx", "head"),
        P("ctx", "head"),
        P("ctx", "head"),
        P("ctx", "head"),
        P("ctx", "head"),
        P("head", "ctx"),
        P(None, ("ctx", "head")),
        P(),
    )
    return jax.shard_map(
        shards,
        mesh=mesh,
        in_specs=placed,
        out_specs=(P("ctx", "head"), P("ctx", "head"), P("ctx", "head")),
        check_vma=False,
    )
```

```python
import functools
import math

import jax
import jax.numpy as jnp
import numpy as np
from jax import lax
from jax.experimental import pallas as pl
from jax.experimental.pallas import tpu as pltpu
from jax.sharding import PartitionSpec as P

HEAD = 128
HALF = HEAD // 2
WIN = 4
ROPE_BASE = 1000000.0
YARN_FACTOR = 4.0
YARN_INITIAL = 32768.0
BETA_FAST = 32.0
BETA_SLOW = 1.0
YARN_MSCALE = 1.0 + 0.1 * math.log(4.0)
ROOT_SCALE = 1.0 / math.sqrt(HEAD)
LOG2E = math.log2(math.e)
VMEM_LIMIT = 24 * 1024 * 1024

F32 = jnp.float32
BF16 = jnp.bfloat16


def frequencies():
    pair = np.arange(HALF, dtype=np.float64)
    inverse = np.exp(-2.0 * pair / HEAD * math.log(ROPE_BASE))
    ratio = YARN_INITIAL * inverse / (2.0 * math.pi)
    ramp = np.clip((ratio - BETA_SLOW) / (BETA_FAST - BETA_SLOW), 0.0, 1.0)
    return inverse * ((1.0 - ramp) / YARN_FACTOR + ramp)


def frequency_rows(lanes):
    values = frequencies()
    row = lax.broadcasted_iota(jnp.int32, (8, lanes), 0)
    tiles = []
    for first in range(0, HALF, 8):
        tile = jnp.full((8, lanes), float(values[first]), F32)
        for j in range(1, 8):
            tile = jnp.where(row == j, float(values[first + j]), tile)
        tiles.append(tile)
    return jnp.concatenate(tiles, axis=0)


def sine_cosine(angle):
    turns = jnp.floor(angle * (2.0 / math.pi) + 0.5)
    r = angle - turns * 1.5703125
    r = r - turns * 4.837512969970703125e-4
    r = r - turns * 7.54978995489188e-8
    r2 = r * r
    s = r + r * r2 * (-1.6666654611e-1 + r2 * (8.3321608736e-3 - r2 * 1.9515295891e-4))
    c = (
        1.0
        - 0.5 * r2
        + r2
        * r2
        * (4.166664568298827e-2 + r2 * (-1.388731625493765e-3 + r2 * 2.443315711809948e-5))
    )
    quadrant = turns.astype(jnp.int32) & 3
    odd = (quadrant & 1) == 1
    sine = jnp.where(odd, c, s)
    cosine = jnp.where(odd, s, c)
    sine = jnp.where(quadrant >= 2, -sine, sine)
    cosine = jnp.where((quadrant == 1) | (quadrant == 2), -cosine, cosine)
    return sine, cosine


def tables_transposed(place):
    place = place.astype(F32)
    freq = frequency_rows(place.shape[1])
    pair = lax.broadcasted_iota(jnp.int32, freq.shape, 0)
    first = HEAD // 8
    second = first + 3 * HEAD // 16
    chosen = jnp.where(
        pair < first, place[0:1], jnp.where(pair < second, place[1:2], place[2:3])
    )
    sine, cosine = sine_cosine(chosen * freq)
    return cosine * YARN_MSCALE, sine * YARN_MSCALE


def row_tables(cosine_t, sine_t):
    wide = jnp.concatenate([cosine_t, cosine_t], axis=0).T
    signed = jnp.concatenate([-sine_t, sine_t], axis=0).T
    return wide, signed


def rotated(x, wide, signed):
    return x * wide + pltpu.roll(x, HALF, 1) * signed


def dot_nt(a, b):
    return lax.dot_general(a, b, (((1,), (1,)), ((), ())), preferred_element_type=F32)


def dot_nn(a, b):
    return lax.dot_general(a, b, (((1,), (0,)), ((), ())), preferred_element_type=F32)


def dot_tn(a, b):
    return lax.dot_general(a, b, (((0,), (0,)), ((), ())), preferred_element_type=F32)


def pair_part(key, value, query, grad, norm, delta, causal):
    scores = dot_nt(key, query)
    weights = jnp.exp2(scores * (ROOT_SCALE * LOG2E) - norm)
    if causal:
        at_key = lax.broadcasted_iota(jnp.int32, scores.shape, 0)
        at_query = lax.broadcasted_iota(jnp.int32, scores.shape, 1)
        weights = jnp.where(at_key <= at_query, weights, 0.0)
    value_part = dot_nn(weights.astype(BF16), grad)
    score_grad = (weights * (dot_nt(value, grad) - delta)).astype(BF16)
    key_part = dot_nn(score_grad, query)
    query_part = dot_tn(key, score_grad)
    return value_part, key_part, query_part


def key_kernel(
    own_ref, p1_ref, p2_ref, p3_ref, k_ref, v_ref, kr_ref, kv_ref, tables_ref, packed_ref
):
    pieces = (own_ref[...], p1_ref[...], p2_ref[...], p3_ref[...])
    count = len(pieces)
    head = lax.axis_index("head")
    parts = []
    for j in range(count):
        back = lax.rem(head - j + count, count)
        part = pieces[0]
        for r in range(1, count):
            part = jnp.where(back == r, pieces[r], part)
        parts.append(part)
    place = jnp.concatenate(parts, axis=1)
    spare = jnp.zeros((packed_ref.shape[0] - 6, place.shape[1]), F32)
    packed_ref[...] = jnp.concatenate(
        [(place >> 6).astype(F32), (place & 63).astype(F32), spare], axis=0
    ).astype(BF16)
    cosine_t, sine_t = tables_transposed(place.astype(F32))
    tables_ref[:HALF, :] = cosine_t
    tables_ref[HALF:, :] = sine_t
    wide, signed = row_tables(cosine_t, sine_t)
    for g in range(k_ref.shape[1] // HEAD):
        cols = pl.ds(g * HEAD, HEAD)
        key = rotated(k_ref[:, cols].astype(F32), wide, signed).astype(BF16)
        kr_ref[:, cols] = key
        kv_ref[:, cols] = key
    kv_ref[:, k_ref.shape[1] :] = v_ref[...]


def prep_kernel(
    groups, span_ref, tables_ref, lse_hbm, q_hbm, do_hbm, at_hbm,
    qr_ref, do_ref, norm_ref, delta_ref, flag_ref, q_ref, at_ref, lse_ref, sems,
):
    heads = qr_ref.shape[1] // HEAD
    size = heads // groups
    copies = []
    for g in range(groups):
        cols = pl.ds(g * size * HEAD, size * HEAD)
        for i, (source, target) in enumerate(
            ((q_hbm, q_ref), (do_hbm, do_ref), (at_hbm, at_ref))
        ):
            copy = pltpu.make_async_copy(
                source.at[:, cols], target.at[:, cols], sems.at[3 * g + i]
            )
            copy.start()
            copies.append(copy)
    lse_copy = pltpu.make_async_copy(lse_hbm, lse_ref, sems.at[3 * groups])
    lse_copy.start()
    me = lax.axis_index("ctx")
    step_row = lax.broadcasted_iota(jnp.int32, flag_ref.shape, 0)
    flags = jnp.zeros(flag_ref.shape, jnp.int32)
    for step in range(1, WIN):
        other = lax.rem(me + step, span_ref.shape[0])
        earlier = jnp.where(span_ref[other] < span_ref[me], 1, 0)
        flags = jnp.where(step_row == step, earlier, flags)
    flag_ref[...] = flags
    wide, signed = row_tables(tables_ref[:HALF, :], tables_ref[HALF:, :])
    chooser = jnp.ones((8, HEAD), BF16)
    for h in range(heads):
        if h % size == 0:
            for copy in copies[3 * (h // size) : 3 * (h // size) + 3]:
                copy.wait()
        hc = pl.ds(h * HEAD, HEAD)
        qr_ref[:, hc] = rotated(q_ref[:, hc].astype(F32), wide, signed).astype(BF16)
        product = do_ref[:, hc].astype(F32) * at_ref[:, hc].astype(F32)
        high = product.astype(BF16)
        low = (product - high.astype(F32)).astype(BF16)
        delta_ref[h : h + 1, :] = (dot_nt(chooser, high) + dot_nt(chooser, low))[:1]
    lse_copy.wait()
    norm_ref[...] = lse_ref[...] * LOG2E


def hop_kernel(step, wanted, *refs):
    count = len(wanted)
    dqt_ins, dqt_refs, part_ref = refs[:count], refs[-count - 1 : -1], refs[-1]
    k_ref, v_ref, qr_ref, do_ref, norm_ref, delta_ref, flag_ref = refs[count : -count - 1]
    rows = qr_ref.shape[0]
    half = rows // 2
    heads = qr_ref.shape[1] // HEAD
    groups = k_ref.shape[1] // HEAD
    size = heads // groups
    earlier = flag_ref[step, 0] == 1
    norm = norm_ref[...]
    delta = delta_ref[...]

    def run(keys, queries):
        for i, (g, dqt_in, dqt_ref) in enumerate(zip(wanted, dqt_ins, dqt_refs)):
            kc = pl.ds(g * HEAD, HEAD)
            dk = dv = None
            for j in range(size):
                h = g * size + j
                hc = pl.ds(h * HEAD, HEAD)
                to = pl.ds(j * HEAD, HEAD)
                v_part, k_part, q_part = pair_part(
                    k_ref[keys, kc], v_ref[keys, kc], qr_ref[queries, hc], do_ref[queries, hc],
                    norm[h : h + 1, queries.start :], delta[h : h + 1, queries.start :], False,
                )
                if queries.start:
                    dqt_ref[to, : queries.start] = dqt_in[to, : queries.start]
                dqt_ref[to, queries] = dqt_in[to, queries] + q_part
                dv = v_part if dv is None else dv + v_part
                dk = k_part if dk is None else dk + k_part
            part_ref[keys, pl.ds(2 * i * HEAD, HEAD)] = dk.astype(BF16)
            part_ref[keys, pl.ds((2 * i + 1) * HEAD, HEAD)] = dv.astype(BF16)
        if keys.stop < rows:
            part_ref[keys.stop :, :] = jnp.zeros((rows - keys.stop, part_ref.shape[1]), BF16)

    @pl.when(earlier)
    def _():
        run(slice(0, half), slice(0, rows))

    @pl.when(jnp.logical_not(earlier))
    def _():
        run(slice(0, rows), slice(half, rows))


def merged_kernel(step, wanted, *refs):
    count = len(wanted)
    kv_ref = refs[count]
    width = kv_ref.shape[1] // 2
    hop_kernel(
        step, wanted, *refs[:count], kv_ref.at[:, :width], kv_ref.at[:, width:], *refs[count + 1 :]
    )


def raw_kernel(step, wanted, *refs):
    *refs, key_ref = refs
    count = len(wanted)
    kv_ref, packed_ref = refs[count : count + 2]
    width = kv_ref.shape[1] // 2
    place = packed_ref[...].astype(F32)
    wide, signed = row_tables(*tables_transposed(place[0:3] * 64.0 + place[3:6]))
    for g in wanted:
        cols = pl.ds(g * HEAD, HEAD)
        key_ref[:, cols] = rotated(kv_ref[:, cols].astype(F32), wide, signed).astype(BF16)
    hop_kernel(
        step, wanted, *refs[:count], key_ref, kv_ref.at[:, width:], *refs[count + 2 :]
    )


def beside_kernel(k_ref, v_ref, kv_ref):
    width = k_ref.shape[1]
    kv_ref[:, :width] = k_ref[...]
    kv_ref[:, width:] = v_ref[...]


def own_kernel(groups, k_ref, v_ref, qr_ref, do_ref, norm_ref, delta_ref, *refs):
    dqt_refs, part_ref = refs[:groups], refs[groups]
    size = qr_ref.shape[1] // HEAD // groups
    norm = norm_ref[...]
    delta = delta_ref[...]
    for g in range(groups):
        kc = pl.ds(g * HEAD, HEAD)
        dk = dv = None
        for j in range(size):
            h = g * size + j
            hc = pl.ds(h * HEAD, HEAD)
            to = pl.ds(j * HEAD, HEAD)
            v_part, k_part, q_part = pair_part(
                k_ref[:, kc], v_ref[:, kc], qr_ref[:, hc], do_ref[:, hc],
                norm[h : h + 1], delta[h : h + 1], True,
            )
            dqt_refs[g][to, :] = q_part
            dv = v_part if dv is None else dv + v_part
            dk = k_part if dk is None else dk + k_part
        part_ref[:, pl.ds(2 * g * HEAD, HEAD)] = dk
        part_ref[:, pl.ds((2 * g + 1) * HEAD, HEAD)] = dv


def query_kernel(groups, tables_ref, *refs):
    dqt_refs = refs[:groups]
    own_ref, swapped_ref, out_ref, sum_ref = refs[groups:]
    odd = (lax.axis_index("ctx") & 1) == 1
    sum_ref[...] = own_ref[...] + jnp.where(odd, swapped_ref[...].astype(F32), 0.0)
    cosine_t = tables_ref[:HALF, :] * ROOT_SCALE
    sine_t = tables_ref[HALF:, :] * ROOT_SCALE
    size = dqt_refs[0].shape[0] // HEAD
    for g in range(groups):
        for j in range(size):
            y1 = dqt_refs[g][pl.ds(j * HEAD, HALF), :]
            y2 = dqt_refs[g][pl.ds(j * HEAD + HALF, HALF), :]
            turned = jnp.concatenate(
                [y1 * cosine_t + y2 * sine_t, y2 * cosine_t - y1 * sine_t], axis=0
            )
            out_ref[:, pl.ds((g * size + j) * HEAD, HEAD)] = turned.T.astype(BF16)


def add_kernel(g, two_ref, swapped_ref, three_ref, sum_ref):
    even = (lax.axis_index("ctx") & 1) == 0
    cols = pl.ds(2 * g * HEAD, 2 * HEAD)
    total = two_ref[:, cols].astype(F32) + three_ref[...].astype(F32)
    sum_ref[...] = (total + jnp.where(even, swapped_ref[:, cols].astype(F32), 0.0)).astype(BF16)


def final_kernel(groups, tables_ref, own_ref, *refs):
    dk_ref, dv_ref = refs[groups:]
    wide, signed = row_tables(tables_ref[:HALF, :], tables_ref[HALF:, :])
    wide = wide * ROOT_SCALE
    signed = signed * -ROOT_SCALE
    for g in range(groups):
        cols = pl.ds(g * HEAD, HEAD)
        total = own_ref[:, pl.ds(2 * g * HEAD, 2 * HEAD)] + refs[g][...].astype(F32)
        dk_ref[:, cols] = rotated(total[:, :HEAD], wide, signed).astype(BF16)
        dv_ref[:, cols] = total[:, HEAD:].astype(BF16)


SMEM = pl.BlockSpec(memory_space=pltpu.SMEM)
VMEM = pl.BlockSpec(memory_space=pltpu.VMEM)
HBM = pl.BlockSpec(memory_space=pltpu.HBM)


def call(kernel, outs, specs, scratch=(), micros=1):
    return pl.pallas_call(
        kernel,
        out_shape=[jax.ShapeDtypeStruct(shape, dtype) for shape, dtype in outs],
        in_specs=specs,
        out_specs=[VMEM] * len(outs),
        scratch_shapes=list(scratch),
        compiler_params=pltpu.CompilerParams(vmem_limit_bytes=VMEM_LIMIT),
        cost_estimate=pl.CostEstimate(
            flops=1 << 20, bytes_accessed=micros * 3690000, transcendentals=0
        ),
    )


def shifted(value, steps, axis="ctx"):
    count = lax.axis_size(axis)
    pairs = [(source, (source + steps) % count) for source in range(count)]
    return lax.ppermute(value, axis, pairs)


def exchanged(value):
    count = lax.axis_size("ctx")
    return lax.ppermute(value, "ctx", [(source, source ^ 1) for source in range(count)])


def shards(q, k, v, do, at, lse, positions, span_map):
    rows = q.shape[0]
    wide_q = q.shape[1]
    wide_k = k.shape[1]
    heads = wide_q // HEAD
    q, do, at, k_here, v_here, lse, span_map, own = (
        pltpu.with_memory_space_constraint(x, pltpu.HBM)
        for x in (q, do, at, k, v, lse, span_map, positions)
    )

    pieces = [own] + [shifted(positions, r, "head") for r in (1, 2, 3)]
    groups = wide_k // HEAD
    every = tuple(range(groups))

    groups = wide_k // HEAD
    every = tuple(range(groups))

    k1 = shifted(k, -1)
    v1 = shifted(v, -1)
    kr, kv, tables, packed = call(
        key_kernel,
        [
            ((rows, wide_k), BF16),
            ((rows, 2 * wide_k), BF16),
            ((HEAD, rows), F32),
            ((16, rows), BF16),
        ],
        [VMEM] * 6,
    )(*pieces, k_here, v_here)
    packed1 = shifted(packed, -1)
    packed3 = shifted(packed, -3)
    turned, k1, v1, packed1, packed3 = lax.optimization_barrier(
        (tables, k1, v1, packed1, packed3)
    )
    (kv1,) = call(beside_kernel, [((rows, 2 * wide_k), BF16)], [VMEM] * 2)(k1, v1)
    kv3 = shifted(kv1, -2)
    shared = call(
        functools.partial(prep_kernel, groups),
        [((rows, wide_q), BF16)] * 2 + [((heads, rows), F32)] * 2 + [((8, HEAD), jnp.int32)],
        [SMEM, VMEM] + [HBM] * 4,
        [
            pltpu.VMEM((rows, wide_q), BF16),
            pltpu.VMEM((rows, wide_q), BF16),
            pltpu.VMEM((heads, rows), F32),
            pltpu.SemaphoreType.DMA((3 * groups + 1,)),
        ],
        micros=2,
    )(span_map, turned, lse, q, do, at)
    *dqs, own = call(
        functools.partial(own_kernel, groups),
        [((wide_q // groups, rows), F32)] * groups + [((rows, 2 * wide_k), F32)],
        [VMEM] * 6,
        micros=3,
    )(kr, v_here, *shared[:4])

    def hop(kernel, step, wanted, arrived, scratch=()):
        count = len(wanted)
        before = [dqs[g] for g in wanted]
        *new, part = call(
            functools.partial(kernel, step, wanted),
            [((wide_q // groups, rows), F32)] * count + [((rows, 2 * HEAD * count), BF16)],
            [VMEM] * (5 + len(arrived) + count),
            scratch,
            micros=count,
        )(*before, *arrived, *shared)
        for g, dq in zip(wanted, new):
            dqs[g] = dq
        return part

    held, _ = lax.optimization_barrier((kv, own))
    kv2 = shifted(held, -2)
    turned_key = [pltpu.VMEM((rows, wide_k), BF16)]
    part1 = hop(raw_kernel, 1, every, (kv1, packed1), turned_key)
    swapped = exchanged(part1)
    moved = [shifted(hop(raw_kernel, 3, (g,), (kv3, packed3), turned_key), 1) for g in every]
    part2 = hop(merged_kernel, 2, every, (kv2,))
    dq, own = call(
        functools.partial(query_kernel, groups),
        [((rows, wide_q), BF16), ((rows, 2 * wide_k), F32)],
        [VMEM] * (3 + groups),
    )(tables, *dqs, own, swapped)
    part2, _ = lax.optimization_barrier((part2, own))
    home = []
    for g in every:
        (total,) = call(
            functools.partial(add_kernel, g), [((rows, 2 * HEAD), BF16)], [VMEM] * 3
        )(part2, swapped, moved[g])
        home.append(shifted(total, 2))

    dk, dv = call(
        functools.partial(final_kernel, groups),
        [((rows, wide_k), BF16), ((rows, wide_k), BF16)],
        [VMEM] * (2 + groups),
    )(tables, own, *home)
    return dq, dk, dv


def solution(mesh):
    placed = (
        P("ctx", "head"),
        P("ctx", "head"),
        P("ctx", "head"),
        P("ctx", "head"),
        P("ctx", "head"),
        P("head", "ctx"),
        P(None, ("ctx", "head")),
        P(),
    )
    return jax.shard_map(
        shards,
        mesh=mesh,
        in_specs=placed,
        out_specs=(P("ctx", "head"), P("ctx", "head"), P("ctx", "head")),
        check_vma=False,
    )
```

```python
import functools
import math

import jax
import jax.numpy as jnp
import numpy as np
from jax import lax
from jax.experimental import pallas as pl
from jax.experimental.pallas import tpu as pltpu
from jax.sharding import PartitionSpec as P

HEAD = 128
HALF = HEAD // 2
WIN = 4
ROPE_BASE = 1000000.0
YARN_FACTOR = 4.0
YARN_INITIAL = 32768.0
BETA_FAST = 32.0
BETA_SLOW = 1.0
YARN_MSCALE = 1.0 + 0.1 * math.log(4.0)
ROOT_SCALE = 1.0 / math.sqrt(HEAD)
LOG2E = math.log2(math.e)
VMEM_LIMIT = 24 * 1024 * 1024

F32 = jnp.float32
BF16 = jnp.bfloat16


def frequencies():
    pair = np.arange(HALF, dtype=np.float64)
    inverse = np.exp(-2.0 * pair / HEAD * math.log(ROPE_BASE))
    ratio = YARN_INITIAL * inverse / (2.0 * math.pi)
    ramp = np.clip((ratio - BETA_SLOW) / (BETA_FAST - BETA_SLOW), 0.0, 1.0)
    return inverse * ((1.0 - ramp) / YARN_FACTOR + ramp)


def frequency_rows(lanes):
    values = frequencies()
    row = lax.broadcasted_iota(jnp.int32, (8, lanes), 0)
    tiles = []
    for first in range(0, HALF, 8):
        tile = jnp.full((8, lanes), float(values[first]), F32)
        for j in range(1, 8):
            tile = jnp.where(row == j, float(values[first + j]), tile)
        tiles.append(tile)
    return jnp.concatenate(tiles, axis=0)


def sine_cosine(angle):
    turns = jnp.floor(angle * (2.0 / math.pi) + 0.5)
    r = angle - turns * 1.5703125
    r = r - turns * 4.837512969970703125e-4
    r = r - turns * 7.54978995489188e-8
    r2 = r * r
    s = r + r * r2 * (-1.6666654611e-1 + r2 * (8.3321608736e-3 - r2 * 1.9515295891e-4))
    c = (
        1.0
        - 0.5 * r2
        + r2
        * r2
        * (4.166664568298827e-2 + r2 * (-1.388731625493765e-3 + r2 * 2.443315711809948e-5))
    )
    quadrant = turns.astype(jnp.int32) & 3
    odd = (quadrant & 1) == 1
    sine = jnp.where(odd, c, s)
    cosine = jnp.where(odd, s, c)
    sine = jnp.where(quadrant >= 2, -sine, sine)
    cosine = jnp.where((quadrant == 1) | (quadrant == 2), -cosine, cosine)
    return sine, cosine


def tables_transposed(place):
    place = place.astype(F32)
    freq = frequency_rows(place.shape[1])
    pair = lax.broadcasted_iota(jnp.int32, freq.shape, 0)
    first = HEAD // 8
    second = first + 3 * HEAD // 16
    chosen = jnp.where(
        pair < first, place[0:1], jnp.where(pair < second, place[1:2], place[2:3])
    )
    sine, cosine = sine_cosine(chosen * freq)
    return cosine * YARN_MSCALE, sine * YARN_MSCALE


def row_tables(cosine_t, sine_t):
    wide = jnp.concatenate([cosine_t, cosine_t], axis=0).T
    signed = jnp.concatenate([-sine_t, sine_t], axis=0).T
    return wide, signed


def rotated(x, wide, signed):
    return x * wide + pltpu.roll(x, HALF, 1) * signed


def dot_nt(a, b):
    return lax.dot_general(a, b, (((1,), (1,)), ((), ())), preferred_element_type=F32)


def dot_nn(a, b):
    return lax.dot_general(a, b, (((1,), (0,)), ((), ())), preferred_element_type=F32)


def dot_tn(a, b):
    return lax.dot_general(a, b, (((0,), (0,)), ((), ())), preferred_element_type=F32)


def pair_part(key, value, query, grad, norm, delta, causal):
    scores = dot_nt(key, query)
    weights = jnp.exp2(scores * (ROOT_SCALE * LOG2E) - norm)
    if causal:
        at_key = lax.broadcasted_iota(jnp.int32, scores.shape, 0)
        at_query = lax.broadcasted_iota(jnp.int32, scores.shape, 1)
        weights = jnp.where(at_key <= at_query, weights, 0.0)
    value_part = dot_nn(weights.astype(BF16), grad)
    score_grad = (weights * (dot_nt(value, grad) - delta)).astype(BF16)
    key_part = dot_nn(score_grad, query)
    query_part = dot_tn(key, score_grad)
    return value_part, key_part, query_part


def key_kernel(
    own_ref, p1_ref, p2_ref, p3_ref, k_ref, v_ref, kr_ref, kv_ref, tables_ref, packed_ref
):
    pieces = (own_ref[...], p1_ref[...], p2_ref[...], p3_ref[...])
    count = len(pieces)
    head = lax.axis_index("head")
    parts = []
    for j in range(count):
        back = lax.rem(head - j + count, count)
        part = pieces[0]
        for r in range(1, count):
            part = jnp.where(back == r, pieces[r], part)
        parts.append(part)
    place = jnp.concatenate(parts, axis=1)
    spare = jnp.zeros((packed_ref.shape[0] - 6, place.shape[1]), F32)
    packed_ref[...] = jnp.concatenate(
        [(place >> 6).astype(F32), (place & 63).astype(F32), spare], axis=0
    ).astype(BF16)
    cosine_t, sine_t = tables_transposed(place.astype(F32))
    tables_ref[:HALF, :] = cosine_t
    tables_ref[HALF:, :] = sine_t
    wide, signed = row_tables(cosine_t, sine_t)
    for g in range(k_ref.shape[1] // HEAD):
        cols = pl.ds(g * HEAD, HEAD)
        key = rotated(k_ref[:, cols].astype(F32), wide, signed).astype(BF16)
        kr_ref[:, cols] = key
        kv_ref[:, cols] = key
    kv_ref[:, k_ref.shape[1] :] = v_ref[...]


def prep_kernel(
    groups, span_ref, tables_ref, lse_hbm, q_hbm, do_hbm, at_hbm,
    qr_ref, do_ref, norm_ref, delta_ref, flag_ref, q_ref, at_ref, lse_ref, sems,
):
    heads = qr_ref.shape[1] // HEAD
    size = heads // groups
    copies = []
    for g in range(groups):
        cols = pl.ds(g * size * HEAD, size * HEAD)
        for i, (source, target) in enumerate(
            ((q_hbm, q_ref), (do_hbm, do_ref), (at_hbm, at_ref))
        ):
            copy = pltpu.make_async_copy(
                source.at[:, cols], target.at[:, cols], sems.at[3 * g + i]
            )
            copy.start()
            copies.append(copy)
    lse_copy = pltpu.make_async_copy(lse_hbm, lse_ref, sems.at[3 * groups])
    lse_copy.start()
    me = lax.axis_index("ctx")
    step_row = lax.broadcasted_iota(jnp.int32, flag_ref.shape, 0)
    flags = jnp.zeros(flag_ref.shape, jnp.int32)
    for step in range(1, WIN):
        other = lax.rem(me + step, span_ref.shape[0])
        earlier = jnp.where(span_ref[other] < span_ref[me], 1, 0)
        flags = jnp.where(step_row == step, earlier, flags)
    flag_ref[...] = flags
    wide, signed = row_tables(tables_ref[:HALF, :], tables_ref[HALF:, :])
    chooser = jnp.ones((8, HEAD), BF16)
    for h in range(heads):
        if h % size == 0:
            for copy in copies[3 * (h // size) : 3 * (h // size) + 3]:
                copy.wait()
        hc = pl.ds(h * HEAD, HEAD)
        qr_ref[:, hc] = rotated(q_ref[:, hc].astype(F32), wide, signed).astype(BF16)
        product = do_ref[:, hc].astype(F32) * at_ref[:, hc].astype(F32)
        high = product.astype(BF16)
        low = (product - high.astype(F32)).astype(BF16)
        delta_ref[h : h + 1, :] = (dot_nt(chooser, high) + dot_nt(chooser, low))[:1]
    lse_copy.wait()
    norm_ref[...] = lse_ref[...] * LOG2E


def hop_kernel(step, wanted, started, *refs):
    count = len(wanted)
    dqt_ins, dqt_refs, part_ref = refs[:count], refs[-count - 1 : -1], refs[-1]
    k_ref, v_ref, qr_ref, do_ref, norm_ref, delta_ref, flag_ref = refs[count * started : -count - 1]
    rows = qr_ref.shape[0]
    half = rows // 2
    heads = qr_ref.shape[1] // HEAD
    groups = k_ref.shape[1] // HEAD
    size = heads // groups
    earlier = flag_ref[step, 0] == 1
    norm = norm_ref[...]
    delta = delta_ref[...]

    def run(keys, queries):
        for i, (g, dqt_in, dqt_ref) in enumerate(zip(wanted, dqt_ins, dqt_refs)):
            kc = pl.ds(g * HEAD, HEAD)
            dk = dv = None
            for j in range(size):
                h = g * size + j
                hc = pl.ds(h * HEAD, HEAD)
                to = pl.ds(j * HEAD, HEAD)
                v_part, k_part, q_part = pair_part(
                    k_ref[keys, kc], v_ref[keys, kc], qr_ref[queries, hc], do_ref[queries, hc],
                    norm[h : h + 1, queries.start :], delta[h : h + 1, queries.start :], False,
                )
                if queries.start:
                    zeros = jnp.zeros((HEAD, queries.start), F32)
                    dqt_ref[to, : queries.start] = (
                        dqt_in[to, : queries.start] if started else zeros
                    )
                dqt_ref[to, queries] = dqt_in[to, queries] + q_part if started else q_part
                dv = v_part if dv is None else dv + v_part
                dk = k_part if dk is None else dk + k_part
            part_ref[keys, pl.ds(2 * i * HEAD, HEAD)] = dk.astype(BF16)
            part_ref[keys, pl.ds((2 * i + 1) * HEAD, HEAD)] = dv.astype(BF16)
        if keys.stop < rows:
            part_ref[keys.stop :, :] = jnp.zeros((rows - keys.stop, part_ref.shape[1]), BF16)

    @pl.when(earlier)
    def _():
        run(slice(0, half), slice(0, rows))

    @pl.when(jnp.logical_not(earlier))
    def _():
        run(slice(0, rows), slice(half, rows))


def merged_kernel(step, wanted, started, *refs):
    count = len(wanted) * started
    kv_ref = refs[count]
    width = kv_ref.shape[1] // 2
    hop_kernel(
        step, wanted, started, *refs[:count], kv_ref.at[:, :width], kv_ref.at[:, width:],
        *refs[count + 1 :],
    )


def raw_kernel(step, wanted, started, *refs):
    *refs, key_ref = refs
    count = len(wanted) * started
    kv_ref, packed_ref = refs[count : count + 2]
    width = kv_ref.shape[1] // 2
    place = packed_ref[...].astype(F32)
    wide, signed = row_tables(*tables_transposed(place[0:3] * 64.0 + place[3:6]))
    for g in wanted:
        cols = pl.ds(g * HEAD, HEAD)
        key_ref[:, cols] = rotated(kv_ref[:, cols].astype(F32), wide, signed).astype(BF16)
    hop_kernel(
        step, wanted, started, *refs[:count], key_ref, kv_ref.at[:, width:], *refs[count + 2 :]
    )


def beside_kernel(k_ref, v_ref, kv_ref):
    width = k_ref.shape[1]
    kv_ref[:, :width] = k_ref[...]
    kv_ref[:, width:] = v_ref[...]


def own_kernel(groups, k_ref, v_ref, qr_ref, do_ref, norm_ref, delta_ref, *refs):
    dqt_ins, dqt_refs, part_ref = refs[:groups], refs[groups : 2 * groups], refs[2 * groups]
    size = qr_ref.shape[1] // HEAD // groups
    norm = norm_ref[...]
    delta = delta_ref[...]
    for g in range(groups):
        kc = pl.ds(g * HEAD, HEAD)
        dk = dv = None
        for j in range(size):
            h = g * size + j
            hc = pl.ds(h * HEAD, HEAD)
            to = pl.ds(j * HEAD, HEAD)
            v_part, k_part, q_part = pair_part(
                k_ref[:, kc], v_ref[:, kc], qr_ref[:, hc], do_ref[:, hc],
                norm[h : h + 1], delta[h : h + 1], True,
            )
            dqt_refs[g][to, :] = dqt_ins[g][to, :] + q_part
            dv = v_part if dv is None else dv + v_part
            dk = k_part if dk is None else dk + k_part
        part_ref[:, pl.ds(2 * g * HEAD, HEAD)] = dk
        part_ref[:, pl.ds((2 * g + 1) * HEAD, HEAD)] = dv


def query_kernel(groups, tables_ref, *refs):
    dqt_refs = refs[:groups]
    own_ref, swapped_ref, out_ref, sum_ref = refs[groups:]
    odd = (lax.axis_index("ctx") & 1) == 1
    sum_ref[...] = own_ref[...] + jnp.where(odd, swapped_ref[...].astype(F32), 0.0)
    cosine_t = tables_ref[:HALF, :] * ROOT_SCALE
    sine_t = tables_ref[HALF:, :] * ROOT_SCALE
    size = dqt_refs[0].shape[0] // HEAD
    for g in range(groups):
        for j in range(size):
            y1 = dqt_refs[g][pl.ds(j * HEAD, HALF), :]
            y2 = dqt_refs[g][pl.ds(j * HEAD + HALF, HALF), :]
            turned = jnp.concatenate(
                [y1 * cosine_t + y2 * sine_t, y2 * cosine_t - y1 * sine_t], axis=0
            )
            out_ref[:, pl.ds((g * size + j) * HEAD, HEAD)] = turned.T.astype(BF16)


def add_kernel(g, two_ref, swapped_ref, three_ref, sum_ref):
    even = (lax.axis_index("ctx") & 1) == 0
    cols = pl.ds(2 * g * HEAD, 2 * HEAD)
    total = two_ref[:, cols].astype(F32) + three_ref[...].astype(F32)
    sum_ref[...] = (total + jnp.where(even, swapped_ref[:, cols].astype(F32), 0.0)).astype(BF16)


def final_kernel(groups, tables_ref, own_ref, *refs):
    dk_ref, dv_ref = refs[groups:]
    wide, signed = row_tables(tables_ref[:HALF, :], tables_ref[HALF:, :])
    wide = wide * ROOT_SCALE
    signed = signed * -ROOT_SCALE
    for g in range(groups):
        cols = pl.ds(g * HEAD, HEAD)
        total = own_ref[:, pl.ds(2 * g * HEAD, 2 * HEAD)] + refs[g][...].astype(F32)
        dk_ref[:, cols] = rotated(total[:, :HEAD], wide, signed).astype(BF16)
        dv_ref[:, cols] = total[:, HEAD:].astype(BF16)


SMEM = pl.BlockSpec(memory_space=pltpu.SMEM)
VMEM = pl.BlockSpec(memory_space=pltpu.VMEM)
HBM = pl.BlockSpec(memory_space=pltpu.HBM)


def call(kernel, outs, specs, scratch=(), micros=1):
    return pl.pallas_call(
        kernel,
        out_shape=[jax.ShapeDtypeStruct(shape, dtype) for shape, dtype in outs],
        in_specs=specs,
        out_specs=[VMEM] * len(outs),
        scratch_shapes=list(scratch),
        compiler_params=pltpu.CompilerParams(vmem_limit_bytes=VMEM_LIMIT),
        cost_estimate=pl.CostEstimate(
            flops=1 << 20, bytes_accessed=micros * 3690000, transcendentals=0
        ),
    )


def shifted(value, steps, axis="ctx"):
    count = lax.axis_size(axis)
    pairs = [(source, (source + steps) % count) for source in range(count)]
    return lax.ppermute(value, axis, pairs)


def exchanged(value):
    count = lax.axis_size("ctx")
    return lax.ppermute(value, "ctx", [(source, source ^ 1) for source in range(count)])


def shards(q, k, v, do, at, lse, positions, span_map):
    rows = q.shape[0]
    wide_q = q.shape[1]
    wide_k = k.shape[1]
    heads = wide_q // HEAD
    q, do, at, k_here, v_here, lse, span_map, own = (
        pltpu.with_memory_space_constraint(x, pltpu.HBM)
        for x in (q, do, at, k, v, lse, span_map, positions)
    )

    pieces = [own] + [shifted(positions, r, "head") for r in (1, 2, 3)]
    groups = wide_k // HEAD
    every = tuple(range(groups))

    groups = wide_k // HEAD
    every = tuple(range(groups))

    k1 = shifted(k, -1)
    v1 = shifted(v, -1)
    kr, kv, tables, packed = call(
        key_kernel,
        [
            ((rows, wide_k), BF16),
            ((rows, 2 * wide_k), BF16),
            ((HEAD, rows), F32),
            ((16, rows), BF16),
        ],
        [VMEM] * 6,
    )(*pieces, k_here, v_here)
    packed1 = shifted(packed, -1)
    packed3 = shifted(packed, -3)
    turned, k1, v1 = lax.optimization_barrier((tables, k1, v1))
    (kv1,) = call(beside_kernel, [((rows, 2 * wide_k), BF16)], [VMEM] * 2)(k1, v1)
    kv3 = shifted(kv1, -2)
    shared = call(
        functools.partial(prep_kernel, groups),
        [((rows, wide_q), BF16)] * 2 + [((heads, rows), F32)] * 2 + [((8, HEAD), jnp.int32)],
        [SMEM, VMEM] + [HBM] * 4,
        [
            pltpu.VMEM((rows, wide_q), BF16),
            pltpu.VMEM((rows, wide_q), BF16),
            pltpu.VMEM((heads, rows), F32),
            pltpu.SemaphoreType.DMA((3 * groups + 1,)),
        ],
        micros=2,
    )(span_map, turned, lse, q, do, at)
    dqs = []

    def hop(kernel, step, wanted, arrived, scratch=()):
        count = len(wanted)
        started = len(dqs) > 0
        before = [dqs[g] for g in wanted] if started else []
        *new, part = call(
            functools.partial(kernel, step, wanted, started),
            [((wide_q // groups, rows), F32)] * count + [((rows, 2 * HEAD * count), BF16)],
            [VMEM] * (5 + len(arrived) + len(before)),
            scratch,
            micros=count,
        )(*before, *arrived, *shared)
        if not started:
            dqs.extend(new)
        for g, dq in zip(wanted, new):
            dqs[g] = dq
        return part

    turned_key = [pltpu.VMEM((rows, wide_k), BF16)]
    part1 = hop(raw_kernel, 1, every, (kv1, packed1), turned_key)
    swapped = exchanged(part1)
    held, _ = lax.optimization_barrier((kv, part1))
    kv2 = shifted(held, -2)
    *dqs, own = call(
        functools.partial(own_kernel, groups),
        [((wide_q // groups, rows), F32)] * groups + [((rows, 2 * wide_k), F32)],
        [VMEM] * (6 + groups),
        micros=3,
    )(kr, v_here, *shared[:4], *dqs)

    moved = [shifted(hop(raw_kernel, 3, (g,), (kv3, packed3), turned_key), 1) for g in every]
    part2 = hop(merged_kernel, 2, every, (kv2,))
    dq, own = call(
        functools.partial(query_kernel, groups),
        [((rows, wide_q), BF16), ((rows, 2 * wide_k), F32)],
        [VMEM] * (3 + groups),
    )(tables, *dqs, own, swapped)
    part2, _ = lax.optimization_barrier((part2, own))
    home = []
    for g in every:
        (total,) = call(
            functools.partial(add_kernel, g), [((rows, 2 * HEAD), BF16)], [VMEM] * 3
        )(part2, swapped, moved[g])
        home.append(shifted(total, 2))

    dk, dv = call(
        functools.partial(final_kernel, groups),
        [((rows, wide_k), BF16), ((rows, wide_k), BF16)],
        [VMEM] * (2 + groups),
    )(tables, own, *home)
    return dq, dk, dv


def solution(mesh):
    placed = (
        P("ctx", "head"),
        P("ctx", "head"),
        P("ctx", "head"),
        P("ctx", "head"),
        P("ctx", "head"),
        P("head", "ctx"),
        P(None, ("ctx", "head")),
        P(),
    )
    return jax.shard_map(
        shards,
        mesh=mesh,
        in_specs=placed,
        out_specs=(P("ctx", "head"), P("ctx", "head"), P("ctx", "head")),
        check_vma=False,
    )
```

```python
import functools
import math

import jax
import jax.numpy as jnp
import numpy as np
from jax import lax
from jax.experimental import pallas as pl
from jax.experimental.pallas import tpu as pltpu
from jax.sharding import PartitionSpec as P

HEAD = 128
HALF = HEAD // 2
WIN = 4
ROPE_BASE = 1000000.0
YARN_FACTOR = 4.0
YARN_INITIAL = 32768.0
BETA_FAST = 32.0
BETA_SLOW = 1.0
YARN_MSCALE = 1.0 + 0.1 * math.log(4.0)
ROOT_SCALE = 1.0 / math.sqrt(HEAD)
LOG2E = math.log2(math.e)
VMEM_LIMIT = 24 * 1024 * 1024

F32 = jnp.float32
BF16 = jnp.bfloat16


def frequencies():
    pair = np.arange(HALF, dtype=np.float64)
    inverse = np.exp(-2.0 * pair / HEAD * math.log(ROPE_BASE))
    ratio = YARN_INITIAL * inverse / (2.0 * math.pi)
    ramp = np.clip((ratio - BETA_SLOW) / (BETA_FAST - BETA_SLOW), 0.0, 1.0)
    return inverse * ((1.0 - ramp) / YARN_FACTOR + ramp)


def frequency_rows(lanes):
    values = frequencies()
    row = lax.broadcasted_iota(jnp.int32, (8, lanes), 0)
    tiles = []
    for first in range(0, HALF, 8):
        tile = jnp.full((8, lanes), float(values[first]), F32)
        for j in range(1, 8):
            tile = jnp.where(row == j, float(values[first + j]), tile)
        tiles.append(tile)
    return jnp.concatenate(tiles, axis=0)


def sine_cosine(angle):
    turns = jnp.floor(angle * (2.0 / math.pi) + 0.5)
    r = angle - turns * 1.5703125
    r = r - turns * 4.837512969970703125e-4
    r = r - turns * 7.54978995489188e-8
    r2 = r * r
    s = r + r * r2 * (-1.6666654611e-1 + r2 * (8.3321608736e-3 - r2 * 1.9515295891e-4))
    c = (
        1.0
        - 0.5 * r2
        + r2
        * r2
        * (4.166664568298827e-2 + r2 * (-1.388731625493765e-3 + r2 * 2.443315711809948e-5))
    )
    quadrant = turns.astype(jnp.int32) & 3
    odd = (quadrant & 1) == 1
    sine = jnp.where(odd, c, s)
    cosine = jnp.where(odd, s, c)
    sine = jnp.where(quadrant >= 2, -sine, sine)
    cosine = jnp.where((quadrant == 1) | (quadrant == 2), -cosine, cosine)
    return sine, cosine


def tables_transposed(place):
    place = place.astype(F32)
    freq = frequency_rows(place.shape[1])
    pair = lax.broadcasted_iota(jnp.int32, freq.shape, 0)
    first = HEAD // 8
    second = first + 3 * HEAD // 16
    chosen = jnp.where(
        pair < first, place[0:1], jnp.where(pair < second, place[1:2], place[2:3])
    )
    sine, cosine = sine_cosine(chosen * freq)
    return cosine * YARN_MSCALE, sine * YARN_MSCALE


def row_tables(cosine_t, sine_t):
    wide = jnp.concatenate([cosine_t, cosine_t], axis=0).T
    signed = jnp.concatenate([-sine_t, sine_t], axis=0).T
    return wide, signed


def rotated(x, wide, signed):
    return x * wide + pltpu.roll(x, HALF, 1) * signed


def dot_nt(a, b):
    return lax.dot_general(a, b, (((1,), (1,)), ((), ())), preferred_element_type=F32)


def dot_nn(a, b):
    return lax.dot_general(a, b, (((1,), (0,)), ((), ())), preferred_element_type=F32)


def dot_tn(a, b):
    return lax.dot_general(a, b, (((0,), (0,)), ((), ())), preferred_element_type=F32)


def pair_part(key, value, query, grad, norm, delta, causal):
    scores = dot_nt(key, query)
    weights = jnp.exp2(scores * (ROOT_SCALE * LOG2E) - norm)
    if causal:
        at_key = lax.broadcasted_iota(jnp.int32, scores.shape, 0)
        at_query = lax.broadcasted_iota(jnp.int32, scores.shape, 1)
        weights = jnp.where(at_key <= at_query, weights, 0.0)
    value_part = dot_nn(weights.astype(BF16), grad)
    score_grad = (weights * (dot_nt(value, grad) - delta)).astype(BF16)
    key_part = dot_nn(score_grad, query)
    query_part = dot_tn(key, score_grad)
    return value_part, key_part, query_part


def key_kernel(own_ref, p1_ref, p2_ref, p3_ref, k_ref, v_ref, kr_ref, kv_ref, tables_ref):
    pieces = (own_ref[...], p1_ref[...], p2_ref[...], p3_ref[...])
    count = len(pieces)
    head = lax.axis_index("head")
    parts = []
    for j in range(count):
        back = lax.rem(head - j + count, count)
        part = pieces[0]
        for r in range(1, count):
            part = jnp.where(back == r, pieces[r], part)
        parts.append(part)
    cosine_t, sine_t = tables_transposed(jnp.concatenate(parts, axis=1))
    tables_ref[:HALF, :] = cosine_t
    tables_ref[HALF:, :] = sine_t
    wide, signed = row_tables(cosine_t, sine_t)
    for g in range(k_ref.shape[1] // HEAD):
        cols = pl.ds(g * HEAD, HEAD)
        key = rotated(k_ref[:, cols].astype(F32), wide, signed).astype(BF16)
        kr_ref[:, cols] = key
        kv_ref[:, cols] = key
    kv_ref[:, k_ref.shape[1] :] = v_ref[...]


def prep_kernel(
    groups, span_ref, tables_ref, lse_hbm, q_hbm, do_hbm, at_hbm,
    qr_ref, do_ref, norm_ref, delta_ref, flag_ref, q_ref, at_ref, lse_ref, sems,
):
    heads = qr_ref.shape[1] // HEAD
    size = heads // groups
    copies = []
    for g in range(groups):
        cols = pl.ds(g * size * HEAD, size * HEAD)
        for i, (source, target) in enumerate(
            ((q_hbm, q_ref), (do_hbm, do_ref), (at_hbm, at_ref))
        ):
            copy = pltpu.make_async_copy(
                source.at[:, cols], target.at[:, cols], sems.at[3 * g + i]
            )
            copy.start()
            copies.append(copy)
    lse_copy = pltpu.make_async_copy(lse_hbm, lse_ref, sems.at[3 * groups])
    lse_copy.start()
    me = lax.axis_index("ctx")
    step_row = lax.broadcasted_iota(jnp.int32, flag_ref.shape, 0)
    flags = jnp.zeros(flag_ref.shape, jnp.int32)
    for step in range(1, WIN):
        other = lax.rem(me + step, span_ref.shape[0])
        earlier = jnp.where(span_ref[other] < span_ref[me], 1, 0)
        flags = jnp.where(step_row == step, earlier, flags)
    flag_ref[...] = flags
    wide, signed = row_tables(tables_ref[:HALF, :], tables_ref[HALF:, :])
    chooser = jnp.ones((8, HEAD), BF16)
    for h in range(heads):
        if h % size == 0:
            for copy in copies[3 * (h // size) : 3 * (h // size) + 3]:
                copy.wait()
        hc = pl.ds(h * HEAD, HEAD)
        qr_ref[:, hc] = rotated(q_ref[:, hc].astype(F32), wide, signed).astype(BF16)
        product = do_ref[:, hc].astype(F32) * at_ref[:, hc].astype(F32)
        high = product.astype(BF16)
        low = (product - high.astype(F32)).astype(BF16)
        delta_ref[h : h + 1, :] = (dot_nt(chooser, high) + dot_nt(chooser, low))[:1]
    lse_copy.wait()
    norm_ref[...] = lse_ref[...] * LOG2E


def hop_kernel(step, wanted, started, *refs):
    count = len(wanted)
    dqt_ins, dqt_refs, part_ref = refs[:count], refs[-count - 1 : -1], refs[-1]
    k_ref, v_ref, qr_ref, do_ref, norm_ref, delta_ref, flag_ref = refs[count * started : -count - 1]
    rows = qr_ref.shape[0]
    half = rows // 2
    heads = qr_ref.shape[1] // HEAD
    groups = k_ref.shape[1] // HEAD
    size = heads // groups
    earlier = flag_ref[step, 0] == 1
    norm = norm_ref[...]
    delta = delta_ref[...]

    def run(keys, queries):
        for i, (g, dqt_in, dqt_ref) in enumerate(zip(wanted, dqt_ins, dqt_refs)):
            kc = pl.ds(g * HEAD, HEAD)
            dk = dv = None
            for j in range(size):
                h = g * size + j
                hc = pl.ds(h * HEAD, HEAD)
                to = pl.ds(j * HEAD, HEAD)
                v_part, k_part, q_part = pair_part(
                    k_ref[keys, kc], v_ref[keys, kc], qr_ref[queries, hc], do_ref[queries, hc],
                    norm[h : h + 1, queries.start :], delta[h : h + 1, queries.start :], False,
                )
                if queries.start:
                    zeros = jnp.zeros((HEAD, queries.start), F32)
                    dqt_ref[to, : queries.start] = (
                        dqt_in[to, : queries.start] if started else zeros
                    )
                dqt_ref[to, queries] = dqt_in[to, queries] + q_part if started else q_part
                dv = v_part if dv is None else dv + v_part
                dk = k_part if dk is None else dk + k_part
            part_ref[keys, pl.ds(2 * i * HEAD, HEAD)] = dk.astype(BF16)
            part_ref[keys, pl.ds((2 * i + 1) * HEAD, HEAD)] = dv.astype(BF16)
        if keys.stop < rows:
            part_ref[keys.stop :, :] = jnp.zeros((rows - keys.stop, part_ref.shape[1]), BF16)

    @pl.when(earlier)
    def _():
        run(slice(0, half), slice(0, rows))

    @pl.when(jnp.logical_not(earlier))
    def _():
        run(slice(0, rows), slice(half, rows))


def merged_kernel(step, wanted, started, *refs):
    count = len(wanted) * started
    kv_ref = refs[count]
    width = kv_ref.shape[1] // 2
    hop_kernel(
        step, wanted, started, *refs[:count], kv_ref.at[:, :width], kv_ref.at[:, width:],
        *refs[count + 1 :],
    )


def beside_kernel(k_ref, v_ref, kv_ref):
    width = k_ref.shape[1]
    kv_ref[:, :width] = k_ref[...]
    kv_ref[:, width:] = v_ref[...]


def own_kernel(groups, k_ref, v_ref, qr_ref, do_ref, norm_ref, delta_ref, *refs):
    dqt_ins, dqt_refs, part_ref = refs[:groups], refs[groups : 2 * groups], refs[2 * groups]
    size = qr_ref.shape[1] // HEAD // groups
    norm = norm_ref[...]
    delta = delta_ref[...]
    for g in range(groups):
        kc = pl.ds(g * HEAD, HEAD)
        dk = dv = None
        for j in range(size):
            h = g * size + j
            hc = pl.ds(h * HEAD, HEAD)
            to = pl.ds(j * HEAD, HEAD)
            v_part, k_part, q_part = pair_part(
                k_ref[:, kc], v_ref[:, kc], qr_ref[:, hc], do_ref[:, hc],
                norm[h : h + 1], delta[h : h + 1], True,
            )
            dqt_refs[g][to, :] = dqt_ins[g][to, :] + q_part
            dv = v_part if dv is None else dv + v_part
            dk = k_part if dk is None else dk + k_part
        part_ref[:, pl.ds(2 * g * HEAD, HEAD)] = dk
        part_ref[:, pl.ds((2 * g + 1) * HEAD, HEAD)] = dv


def query_kernel(groups, tables_ref, *refs):
    dqt_refs = refs[:groups]
    own_ref, swapped_ref, out_ref, sum_ref = refs[groups:]
    odd = (lax.axis_index("ctx") & 1) == 1
    sum_ref[...] = own_ref[...] + jnp.where(odd, swapped_ref[...].astype(F32), 0.0)
    cosine_t = tables_ref[:HALF, :] * ROOT_SCALE
    sine_t = tables_ref[HALF:, :] * ROOT_SCALE
    size = dqt_refs[0].shape[0] // HEAD
    for g in range(groups):
        for j in range(size):
            y1 = dqt_refs[g][pl.ds(j * HEAD, HALF), :]
            y2 = dqt_refs[g][pl.ds(j * HEAD + HALF, HALF), :]
            turned = jnp.concatenate(
                [y1 * cosine_t + y2 * sine_t, y2 * cosine_t - y1 * sine_t], axis=0
            )
            out_ref[:, pl.ds((g * size + j) * HEAD, HEAD)] = turned.T.astype(BF16)


def add_kernel(g, two_ref, swapped_ref, three_ref, sum_ref):
    even = (lax.axis_index("ctx") & 1) == 0
    cols = pl.ds(2 * g * HEAD, 2 * HEAD)
    total = two_ref[:, cols].astype(F32) + three_ref[...].astype(F32)
    sum_ref[...] = (total + jnp.where(even, swapped_ref[:, cols].astype(F32), 0.0)).astype(BF16)


def final_kernel(groups, tables_ref, own_ref, *refs):
    dk_ref, dv_ref = refs[groups:]
    wide, signed = row_tables(tables_ref[:HALF, :], tables_ref[HALF:, :])
    wide = wide * ROOT_SCALE
    signed = signed * -ROOT_SCALE
    for g in range(groups):
        cols = pl.ds(g * HEAD, HEAD)
        total = own_ref[:, pl.ds(2 * g * HEAD, 2 * HEAD)] + refs[g][...].astype(F32)
        dk_ref[:, cols] = rotated(total[:, :HEAD], wide, signed).astype(BF16)
        dv_ref[:, cols] = total[:, HEAD:].astype(BF16)


SMEM = pl.BlockSpec(memory_space=pltpu.SMEM)
VMEM = pl.BlockSpec(memory_space=pltpu.VMEM)
HBM = pl.BlockSpec(memory_space=pltpu.HBM)


def call(kernel, outs, specs, scratch=(), micros=1):
    return pl.pallas_call(
        kernel,
        out_shape=[jax.ShapeDtypeStruct(shape, dtype) for shape, dtype in outs],
        in_specs=specs,
        out_specs=[VMEM] * len(outs),
        scratch_shapes=list(scratch),
        compiler_params=pltpu.CompilerParams(vmem_limit_bytes=VMEM_LIMIT),
        cost_estimate=pl.CostEstimate(
            flops=1 << 20, bytes_accessed=micros * 3690000, transcendentals=0
        ),
    )


def shifted(value, steps, axis="ctx"):
    count = lax.axis_size(axis)
    pairs = [(source, (source + steps) % count) for source in range(count)]
    return lax.ppermute(value, axis, pairs)


def exchanged(value):
    count = lax.axis_size("ctx")
    return lax.ppermute(value, "ctx", [(source, source ^ 1) for source in range(count)])


def shards(q, k, v, do, at, lse, positions, span_map):
    rows = q.shape[0]
    wide_q = q.shape[1]
    wide_k = k.shape[1]
    heads = wide_q // HEAD
    q, do, at, k_here, v_here, lse, span_map, own = (
        pltpu.with_memory_space_constraint(x, pltpu.HBM)
        for x in (q, do, at, k, v, lse, span_map, positions)
    )

    pieces = [own] + [shifted(positions, r, "head") for r in (1, 2, 3)]
    groups = wide_k // HEAD
    every = tuple(range(groups))

    groups = wide_k // HEAD
    every = tuple(range(groups))

    v1 = shifted(v, -1)
    kr, kv, tables = call(
        key_kernel,
        [((rows, wide_k), BF16), ((rows, 2 * wide_k), BF16), ((HEAD, rows), F32)],
        [VMEM] * 6,
    )(*pieces, k_here, v_here)
    k1 = shifted(kr, -1)
    shared = call(
        functools.partial(prep_kernel, groups),
        [((rows, wide_q), BF16)] * 2 + [((heads, rows), F32)] * 2 + [((8, HEAD), jnp.int32)],
        [SMEM, VMEM] + [HBM] * 4,
        [
            pltpu.VMEM((rows, wide_q), BF16),
            pltpu.VMEM((rows, wide_q), BF16),
            pltpu.VMEM((heads, rows), F32),
            pltpu.SemaphoreType.DMA((3 * groups + 1,)),
        ],
        micros=2,
    )(span_map, tables, lse, q, do, at)
    held, _, v1 = lax.optimization_barrier((kv, shared[3], v1))
    kv2 = shifted(held, -2)
    (kv1,) = call(beside_kernel, [((rows, 2 * wide_k), BF16)], [VMEM] * 2)(k1, v1)
    kv3 = shifted(kv1, -2)
    dqs = []

    def hop(step, wanted, arrived):
        count = len(wanted)
        started = len(dqs) > 0
        before = [dqs[g] for g in wanted] if started else []
        *new, part = call(
            functools.partial(merged_kernel, step, wanted, started),
            [((wide_q // groups, rows), F32)] * count + [((rows, 2 * HEAD * count), BF16)],
            [VMEM] * (6 + len(before)),
            micros=count,
        )(*before, arrived, *shared)
        if not started:
            dqs.extend(new)
        for g, dq in zip(wanted, new):
            dqs[g] = dq
        return part

    part1 = hop(1, every, kv1)
    swapped = exchanged(part1)
    kr, kv2 = lax.optimization_barrier((kr, kv2))
    *dqs, own = call(
        functools.partial(own_kernel, groups),
        [((wide_q // groups, rows), F32)] * groups + [((rows, 2 * wide_k), F32)],
        [VMEM] * (6 + groups),
        micros=3,
    )(kr, v_here, *shared[:4], *dqs)

    moved = [shifted(hop(3, (g,), kv3), 1) for g in every]
    part2 = hop(2, every, kv2)
    dq, own = call(
        functools.partial(query_kernel, groups),
        [((rows, wide_q), BF16), ((rows, 2 * wide_k), F32)],
        [VMEM] * (3 + groups),
    )(tables, *dqs, own, swapped)
    part2, _ = lax.optimization_barrier((part2, own))
    home = []
    for g in every:
        (total,) = call(
            functools.partial(add_kernel, g), [((rows, 2 * HEAD), BF16)], [VMEM] * 3
        )(part2, swapped, moved[g])
        home.append(shifted(total, 2))

    dk, dv = call(
        functools.partial(final_kernel, groups),
        [((rows, wide_k), BF16), ((rows, wide_k), BF16)],
        [VMEM] * (2 + groups),
    )(tables, own, *home)
    return dq, dk, dv


def solution(mesh):
    placed = (
        P("ctx", "head"),
        P("ctx", "head"),
        P("ctx", "head"),
        P("ctx", "head"),
        P("ctx", "head"),
        P("head", "ctx"),
        P(None, ("ctx", "head")),
        P(),
    )
    return jax.shard_map(
        shards,
        mesh=mesh,
        in_specs=placed,
        out_specs=(P("ctx", "head"), P("ctx", "head"), P("ctx", "head")),
        check_vma=False,
    )
```

```python
import functools
import math

import jax
import jax.numpy as jnp
import numpy as np
from jax import lax
from jax.experimental import pallas as pl
from jax.experimental.pallas import tpu as pltpu
from jax.sharding import PartitionSpec as P

HEAD = 128
HALF = HEAD // 2
WIN = 4
ROPE_BASE = 1000000.0
YARN_FACTOR = 4.0
YARN_INITIAL = 32768.0
BETA_FAST = 32.0
BETA_SLOW = 1.0
YARN_MSCALE = 1.0 + 0.1 * math.log(4.0)
ROOT_SCALE = 1.0 / math.sqrt(HEAD)
LOG2E = math.log2(math.e)
VMEM_LIMIT = 24 * 1024 * 1024

F32 = jnp.float32
BF16 = jnp.bfloat16


def frequencies():
    pair = np.arange(HALF, dtype=np.float64)
    inverse = np.exp(-2.0 * pair / HEAD * math.log(ROPE_BASE))
    ratio = YARN_INITIAL * inverse / (2.0 * math.pi)
    ramp = np.clip((ratio - BETA_SLOW) / (BETA_FAST - BETA_SLOW), 0.0, 1.0)
    return inverse * ((1.0 - ramp) / YARN_FACTOR + ramp)


def frequency_rows(lanes):
    values = frequencies()
    row = lax.broadcasted_iota(jnp.int32, (8, lanes), 0)
    tiles = []
    for first in range(0, HALF, 8):
        tile = jnp.full((8, lanes), float(values[first]), F32)
        for j in range(1, 8):
            tile = jnp.where(row == j, float(values[first + j]), tile)
        tiles.append(tile)
    return jnp.concatenate(tiles, axis=0)


def sine_cosine(angle):
    turns = jnp.floor(angle * (2.0 / math.pi) + 0.5)
    r = angle - turns * 1.5703125
    r = r - turns * 4.837512969970703125e-4
    r = r - turns * 7.54978995489188e-8
    r2 = r * r
    s = r + r * r2 * (-1.6666654611e-1 + r2 * (8.3321608736e-3 - r2 * 1.9515295891e-4))
    c = (
        1.0
        - 0.5 * r2
        + r2
        * r2
        * (4.166664568298827e-2 + r2 * (-1.388731625493765e-3 + r2 * 2.443315711809948e-5))
    )
    quadrant = turns.astype(jnp.int32) & 3
    odd = (quadrant & 1) == 1
    sine = jnp.where(odd, c, s)
    cosine = jnp.where(odd, s, c)
    sine = jnp.where(quadrant >= 2, -sine, sine)
    cosine = jnp.where((quadrant == 1) | (quadrant == 2), -cosine, cosine)
    return sine, cosine


def tables_transposed(place):
    place = place.astype(F32)
    freq = frequency_rows(place.shape[1])
    pair = lax.broadcasted_iota(jnp.int32, freq.shape, 0)
    first = HEAD // 8
    second = first + 3 * HEAD // 16
    chosen = jnp.where(
        pair < first, place[0:1], jnp.where(pair < second, place[1:2], place[2:3])
    )
    sine, cosine = sine_cosine(chosen * freq)
    return cosine * YARN_MSCALE, sine * YARN_MSCALE


def row_tables(cosine_t, sine_t):
    wide = jnp.concatenate([cosine_t, cosine_t], axis=0).T
    signed = jnp.concatenate([-sine_t, sine_t], axis=0).T
    return wide, signed


def rotated(x, wide, signed):
    return x * wide + pltpu.roll(x, HALF, 1) * signed


def dot_nt(a, b):
    return lax.dot_general(a, b, (((1,), (1,)), ((), ())), preferred_element_type=F32)


def dot_nn(a, b):
    return lax.dot_general(a, b, (((1,), (0,)), ((), ())), preferred_element_type=F32)


def dot_tn(a, b):
    return lax.dot_general(a, b, (((0,), (0,)), ((), ())), preferred_element_type=F32)


def pair_part(key, value, query, grad, norm, delta, causal):
    scores = dot_nt(key, query)
    weights = jnp.exp2(scores * (ROOT_SCALE * LOG2E) - norm)
    if causal:
        at_key = lax.broadcasted_iota(jnp.int32, scores.shape, 0)
        at_query = lax.broadcasted_iota(jnp.int32, scores.shape, 1)
        weights = jnp.where(at_key <= at_query, weights, 0.0)
    value_part = dot_nn(weights.astype(BF16), grad)
    score_grad = (weights * (dot_nt(value, grad) - delta)).astype(BF16)
    key_part = dot_nn(score_grad, query)
    query_part = dot_tn(key, score_grad)
    return value_part, key_part, query_part


def key_kernel(own_ref, p1_ref, p2_ref, p3_ref, k_ref, v_ref, kr_ref, kv_ref, tables_ref):
    pieces = (own_ref[...], p1_ref[...], p2_ref[...], p3_ref[...])
    count = len(pieces)
    head = lax.axis_index("head")
    parts = []
    for j in range(count):
        back = lax.rem(head - j + count, count)
        part = pieces[0]
        for r in range(1, count):
            part = jnp.where(back == r, pieces[r], part)
        parts.append(part)
    cosine_t, sine_t = tables_transposed(jnp.concatenate(parts, axis=1))
    tables_ref[:HALF, :] = cosine_t
    tables_ref[HALF:, :] = sine_t
    wide, signed = row_tables(cosine_t, sine_t)
    for g in range(k_ref.shape[1] // HEAD):
        cols = pl.ds(g * HEAD, HEAD)
        key = rotated(k_ref[:, cols].astype(F32), wide, signed).astype(BF16)
        kr_ref[:, cols] = key
        kv_ref[:, cols] = key
    kv_ref[:, k_ref.shape[1] :] = v_ref[...]


def prep_kernel(
    groups, span_ref, tables_ref, lse_hbm, q_hbm, do_hbm, at_hbm,
    qr_ref, do_ref, norm_ref, delta_ref, flag_ref, q_ref, at_ref, lse_ref, sems,
):
    heads = qr_ref.shape[1] // HEAD
    size = heads // groups
    copies = []
    for g in range(groups):
        cols = pl.ds(g * size * HEAD, size * HEAD)
        for i, (source, target) in enumerate(
            ((q_hbm, q_ref), (do_hbm, do_ref), (at_hbm, at_ref))
        ):
            copy = pltpu.make_async_copy(
                source.at[:, cols], target.at[:, cols], sems.at[3 * g + i]
            )
            copy.start()
            copies.append(copy)
    lse_copy = pltpu.make_async_copy(lse_hbm, lse_ref, sems.at[3 * groups])
    lse_copy.start()
    me = lax.axis_index("ctx")
    step_row = lax.broadcasted_iota(jnp.int32, flag_ref.shape, 0)
    flags = jnp.zeros(flag_ref.shape, jnp.int32)
    for step in range(1, WIN):
        other = lax.rem(me + step, span_ref.shape[0])
        earlier = jnp.where(span_ref[other] < span_ref[me], 1, 0)
        flags = jnp.where(step_row == step, earlier, flags)
    flag_ref[...] = flags
    wide, signed = row_tables(tables_ref[:HALF, :], tables_ref[HALF:, :])
    chooser = jnp.ones((8, HEAD), BF16)
    for h in range(heads):
        if h % size == 0:
            for copy in copies[3 * (h // size) : 3 * (h // size) + 3]:
                copy.wait()
        hc = pl.ds(h * HEAD, HEAD)
        qr_ref[:, hc] = rotated(q_ref[:, hc].astype(F32), wide, signed).astype(BF16)
        product = do_ref[:, hc].astype(F32) * at_ref[:, hc].astype(F32)
        high = product.astype(BF16)
        low = (product - high.astype(F32)).astype(BF16)
        delta_ref[h : h + 1, :] = (dot_nt(chooser, high) + dot_nt(chooser, low))[:1]
    lse_copy.wait()
    norm_ref[...] = lse_ref[...] * LOG2E


def hop_kernel(step, wanted, started, *refs):
    count = len(wanted)
    dqt_ins, dqt_refs, part_ref = refs[:count], refs[-count - 1 : -1], refs[-1]
    k_ref, v_ref, qr_ref, do_ref, norm_ref, delta_ref, flag_ref = refs[count * started : -count - 1]
    rows = qr_ref.shape[0]
    half = rows // 2
    heads = qr_ref.shape[1] // HEAD
    groups = k_ref.shape[1] // HEAD
    size = heads // groups
    earlier = flag_ref[step, 0] == 1
    norm = norm_ref[...]
    delta = delta_ref[...]

    def run(keys, queries):
        for i, (g, dqt_in, dqt_ref) in enumerate(zip(wanted, dqt_ins, dqt_refs)):
            kc = pl.ds(g * HEAD, HEAD)
            dk = dv = None
            for j in range(size):
                h = g * size + j
                hc = pl.ds(h * HEAD, HEAD)
                to = pl.ds(j * HEAD, HEAD)
                v_part, k_part, q_part = pair_part(
                    k_ref[keys, kc], v_ref[keys, kc], qr_ref[queries, hc], do_ref[queries, hc],
                    norm[h : h + 1, queries.start :], delta[h : h + 1, queries.start :], False,
                )
                if queries.start:
                    zeros = jnp.zeros((HEAD, queries.start), F32)
                    dqt_ref[to, : queries.start] = (
                        dqt_in[to, : queries.start] if started else zeros
                    )
                dqt_ref[to, queries] = dqt_in[to, queries] + q_part if started else q_part
                dv = v_part if dv is None else dv + v_part
                dk = k_part if dk is None else dk + k_part
            part_ref[keys, pl.ds(2 * i * HEAD, HEAD)] = dk.astype(BF16)
            part_ref[keys, pl.ds((2 * i + 1) * HEAD, HEAD)] = dv.astype(BF16)
        if keys.stop < rows:
            part_ref[keys.stop :, :] = jnp.zeros((rows - keys.stop, part_ref.shape[1]), BF16)

    @pl.when(earlier)
    def _():
        run(slice(0, half), slice(0, rows))

    @pl.when(jnp.logical_not(earlier))
    def _():
        run(slice(0, rows), slice(half, rows))


def merged_kernel(step, wanted, started, *refs):
    count = len(wanted) * started
    kv_ref = refs[count]
    width = kv_ref.shape[1] // 2
    hop_kernel(
        step, wanted, started, *refs[:count], kv_ref.at[:, :width], kv_ref.at[:, width:],
        *refs[count + 1 :],
    )


def beside_kernel(k_ref, v_ref, kv_ref):
    width = k_ref.shape[1]
    kv_ref[:, :width] = k_ref[...]
    kv_ref[:, width:] = v_ref[...]


def own_kernel(groups, k_ref, v_ref, qr_ref, do_ref, norm_ref, delta_ref, *refs):
    dqt_ins, dqt_refs, part_ref = refs[:groups], refs[groups : 2 * groups], refs[2 * groups]
    size = qr_ref.shape[1] // HEAD // groups
    norm = norm_ref[...]
    delta = delta_ref[...]
    for g in range(groups):
        kc = pl.ds(g * HEAD, HEAD)
        dk = dv = None
        for j in range(size):
            h = g * size + j
            hc = pl.ds(h * HEAD, HEAD)
            to = pl.ds(j * HEAD, HEAD)
            v_part, k_part, q_part = pair_part(
                k_ref[:, kc], v_ref[:, kc], qr_ref[:, hc], do_ref[:, hc],
                norm[h : h + 1], delta[h : h + 1], True,
            )
            dqt_refs[g][to, :] = dqt_ins[g][to, :] + q_part
            dv = v_part if dv is None else dv + v_part
            dk = k_part if dk is None else dk + k_part
        part_ref[:, pl.ds(2 * g * HEAD, HEAD)] = dk
        part_ref[:, pl.ds((2 * g + 1) * HEAD, HEAD)] = dv


def query_kernel(groups, tables_ref, *refs):
    dqt_refs = refs[:groups]
    own_ref, swapped_ref, out_ref, sum_ref = refs[groups:]
    odd = (lax.axis_index("ctx") & 1) == 1
    sum_ref[...] = own_ref[...] + jnp.where(odd, swapped_ref[...].astype(F32), 0.0)
    cosine_t = tables_ref[:HALF, :] * ROOT_SCALE
    sine_t = tables_ref[HALF:, :] * ROOT_SCALE
    size = dqt_refs[0].shape[0] // HEAD
    for g in range(groups):
        for j in range(size):
            y1 = dqt_refs[g][pl.ds(j * HEAD, HALF), :]
            y2 = dqt_refs[g][pl.ds(j * HEAD + HALF, HALF), :]
            turned = jnp.concatenate(
                [y1 * cosine_t + y2 * sine_t, y2 * cosine_t - y1 * sine_t], axis=0
            )
            out_ref[:, pl.ds((g * size + j) * HEAD, HEAD)] = turned.T.astype(BF16)


def add_kernel(g, two_ref, swapped_ref, three_ref, sum_ref):
    even = (lax.axis_index("ctx") & 1) == 0
    cols = pl.ds(2 * g * HEAD, 2 * HEAD)
    total = two_ref[:, cols].astype(F32) + three_ref[...].astype(F32)
    sum_ref[...] = (total + jnp.where(even, swapped_ref[:, cols].astype(F32), 0.0)).astype(BF16)


def final_kernel(groups, tables_ref, own_ref, *refs):
    dk_ref, dv_ref = refs[groups:]
    wide, signed = row_tables(tables_ref[:HALF, :], tables_ref[HALF:, :])
    wide = wide * ROOT_SCALE
    signed = signed * -ROOT_SCALE
    for g in range(groups):
        cols = pl.ds(g * HEAD, HEAD)
        total = own_ref[:, pl.ds(2 * g * HEAD, 2 * HEAD)] + refs[g][...].astype(F32)
        dk_ref[:, cols] = rotated(total[:, :HEAD], wide, signed).astype(BF16)
        dv_ref[:, cols] = total[:, HEAD:].astype(BF16)


SMEM = pl.BlockSpec(memory_space=pltpu.SMEM)
VMEM = pl.BlockSpec(memory_space=pltpu.VMEM)
HBM = pl.BlockSpec(memory_space=pltpu.HBM)


def call(kernel, outs, specs, scratch=(), micros=1):
    return pl.pallas_call(
        kernel,
        out_shape=[jax.ShapeDtypeStruct(shape, dtype) for shape, dtype in outs],
        in_specs=specs,
        out_specs=[VMEM] * len(outs),
        scratch_shapes=list(scratch),
        compiler_params=pltpu.CompilerParams(vmem_limit_bytes=VMEM_LIMIT),
        cost_estimate=pl.CostEstimate(
            flops=1 << 20, bytes_accessed=micros * 3690000, transcendentals=0
        ),
    )


def shifted(value, steps, axis="ctx"):
    count = lax.axis_size(axis)
    pairs = [(source, (source + steps) % count) for source in range(count)]
    return lax.ppermute(value, axis, pairs)


def exchanged(value):
    count = lax.axis_size("ctx")
    return lax.ppermute(value, "ctx", [(source, source ^ 1) for source in range(count)])


def shards(q, k, v, do, at, lse, positions, span_map):
    rows = q.shape[0]
    wide_q = q.shape[1]
    wide_k = k.shape[1]
    heads = wide_q // HEAD
    q, do, at, k_here, v_here, lse, span_map, own = (
        pltpu.with_memory_space_constraint(x, pltpu.HBM)
        for x in (q, do, at, k, v, lse, span_map, positions)
    )

    pieces = [own] + [shifted(positions, r, "head") for r in (1, 2, 3)]
    groups = wide_k // HEAD
    every = tuple(range(groups))

    groups = wide_k // HEAD
    every = tuple(range(groups))

    v1 = shifted(v, -1)
    kr, kv, tables = call(
        key_kernel,
        [((rows, wide_k), BF16), ((rows, 2 * wide_k), BF16), ((HEAD, rows), F32)],
        [VMEM] * 6,
    )(*pieces, k_here, v_here)
    k1 = shifted(kr, -1)
    shared = call(
        functools.partial(prep_kernel, groups),
        [((rows, wide_q), BF16)] * 2 + [((heads, rows), F32)] * 2 + [((8, HEAD), jnp.int32)],
        [SMEM, VMEM] + [HBM] * 4,
        [
            pltpu.VMEM((rows, wide_q), BF16),
            pltpu.VMEM((rows, wide_q), BF16),
            pltpu.VMEM((heads, rows), F32),
            pltpu.SemaphoreType.DMA((3 * groups + 1,)),
        ],
        micros=2,
    )(span_map, tables, lse, q, do, at)
    k1, _, v1 = lax.optimization_barrier((k1, shared[3], v1))
    (kv1,) = call(beside_kernel, [((rows, 2 * wide_k), BF16)], [VMEM] * 2)(k1, v1)
    kv3 = shifted(kv1, -2)
    dqs = []

    def hop(step, wanted, arrived):
        count = len(wanted)
        started = len(dqs) > 0
        before = [dqs[g] for g in wanted] if started else []
        *new, part = call(
            functools.partial(merged_kernel, step, wanted, started),
            [((wide_q // groups, rows), F32)] * count + [((rows, 2 * HEAD * count), BF16)],
            [VMEM] * (6 + len(before)),
            micros=count,
        )(*before, arrived, *shared)
        if not started:
            dqs.extend(new)
        for g, dq in zip(wanted, new):
            dqs[g] = dq
        return part

    part1 = hop(1, every, kv1)
    swapped = exchanged(part1)
    held, _ = lax.optimization_barrier((kv, part1))
    kv2 = shifted(held, -2)
    *dqs, own = call(
        functools.partial(own_kernel, groups),
        [((wide_q // groups, rows), F32)] * groups + [((rows, 2 * wide_k), F32)],
        [VMEM] * (6 + groups),
        micros=3,
    )(kr, v_here, *shared[:4], *dqs)

    moved = [shifted(hop(3, (g,), kv3), 1) for g in every]
    part2 = hop(2, every, kv2)
    dq, own = call(
        functools.partial(query_kernel, groups),
        [((rows, wide_q), BF16), ((rows, 2 * wide_k), F32)],
        [VMEM] * (3 + groups),
    )(tables, *dqs, own, swapped)
    part2, _ = lax.optimization_barrier((part2, own))
    home = []
    for g in every:
        (total,) = call(
            functools.partial(add_kernel, g), [((rows, 2 * HEAD), BF16)], [VMEM] * 3
        )(part2, swapped, moved[g])
        home.append(shifted(total, 2))

    dk, dv = call(
        functools.partial(final_kernel, groups),
        [((rows, wide_k), BF16), ((rows, wide_k), BF16)],
        [VMEM] * (2 + groups),
    )(tables, own, *home)
    return dq, dk, dv


def solution(mesh):
    placed = (
        P("ctx", "head"),
        P("ctx", "head"),
        P("ctx", "head"),
        P("ctx", "head"),
        P("ctx", "head"),
        P("head", "ctx"),
        P(None, ("ctx", "head")),
        P(),
    )
    return jax.shard_map(
        shards,
        mesh=mesh,
        in_specs=placed,
        out_specs=(P("ctx", "head"), P("ctx", "head"), P("ctx", "head")),
        check_vma=False,
    )
```

```python
import functools
import math

import jax
import jax.numpy as jnp
import numpy as np
from jax import lax
from jax.experimental import pallas as pl
from jax.experimental.pallas import tpu as pltpu
from jax.sharding import PartitionSpec as P

HEAD = 128
HALF = HEAD // 2
WIN = 4
ROPE_BASE = 1000000.0
YARN_FACTOR = 4.0
YARN_INITIAL = 32768.0
BETA_FAST = 32.0
BETA_SLOW = 1.0
YARN_MSCALE = 1.0 + 0.1 * math.log(4.0)
ROOT_SCALE = 1.0 / math.sqrt(HEAD)
LOG2E = math.log2(math.e)
VMEM_LIMIT = 24 * 1024 * 1024

F32 = jnp.float32
BF16 = jnp.bfloat16


def frequencies():
    pair = np.arange(HALF, dtype=np.float64)
    inverse = np.exp(-2.0 * pair / HEAD * math.log(ROPE_BASE))
    ratio = YARN_INITIAL * inverse / (2.0 * math.pi)
    ramp = np.clip((ratio - BETA_SLOW) / (BETA_FAST - BETA_SLOW), 0.0, 1.0)
    return inverse * ((1.0 - ramp) / YARN_FACTOR + ramp)


def frequency_rows(lanes):
    values = frequencies()
    row = lax.broadcasted_iota(jnp.int32, (8, lanes), 0)
    tiles = []
    for first in range(0, HALF, 8):
        tile = jnp.full((8, lanes), float(values[first]), F32)
        for j in range(1, 8):
            tile = jnp.where(row == j, float(values[first + j]), tile)
        tiles.append(tile)
    return jnp.concatenate(tiles, axis=0)


def sine_cosine(angle):
    turns = jnp.floor(angle * (2.0 / math.pi) + 0.5)
    r = angle - turns * 1.5703125
    r = r - turns * 4.837512969970703125e-4
    r = r - turns * 7.54978995489188e-8
    r2 = r * r
    s = r + r * r2 * (-1.6666654611e-1 + r2 * (8.3321608736e-3 - r2 * 1.9515295891e-4))
    c = (
        1.0
        - 0.5 * r2
        + r2
        * r2
        * (4.166664568298827e-2 + r2 * (-1.388731625493765e-3 + r2 * 2.443315711809948e-5))
    )
    quadrant = turns.astype(jnp.int32) & 3
    odd = (quadrant & 1) == 1
    sine = jnp.where(odd, c, s)
    cosine = jnp.where(odd, s, c)
    sine = jnp.where(quadrant >= 2, -sine, sine)
    cosine = jnp.where((quadrant == 1) | (quadrant == 2), -cosine, cosine)
    return sine, cosine


def tables_transposed(place):
    place = place.astype(F32)
    freq = frequency_rows(place.shape[1])
    pair = lax.broadcasted_iota(jnp.int32, freq.shape, 0)
    first = HEAD // 8
    second = first + 3 * HEAD // 16
    chosen = jnp.where(
        pair < first, place[0:1], jnp.where(pair < second, place[1:2], place[2:3])
    )
    sine, cosine = sine_cosine(chosen * freq)
    return cosine * YARN_MSCALE, sine * YARN_MSCALE


def row_tables(cosine_t, sine_t):
    wide = jnp.concatenate([cosine_t, cosine_t], axis=0).T
    signed = jnp.concatenate([-sine_t, sine_t], axis=0).T
    return wide, signed


def rotated(x, wide, signed):
    return x * wide + pltpu.roll(x, HALF, 1) * signed


def dot_nt(a, b):
    return lax.dot_general(a, b, (((1,), (1,)), ((), ())), preferred_element_type=F32)


def dot_nn(a, b):
    return lax.dot_general(a, b, (((1,), (0,)), ((), ())), preferred_element_type=F32)


def dot_tn(a, b):
    return lax.dot_general(a, b, (((0,), (0,)), ((), ())), preferred_element_type=F32)


def pair_part(key, value, query, grad, norm, delta, causal):
    scores = dot_nt(key, query)
    weights = jnp.exp2(scores * (ROOT_SCALE * LOG2E) - norm)
    if causal:
        at_key = lax.broadcasted_iota(jnp.int32, scores.shape, 0)
        at_query = lax.broadcasted_iota(jnp.int32, scores.shape, 1)
        weights = jnp.where(at_key <= at_query, weights, 0.0)
    value_part = dot_nn(weights.astype(BF16), grad)
    score_grad = (weights * (dot_nt(value, grad) - delta)).astype(BF16)
    key_part = dot_nn(score_grad, query)
    query_part = dot_tn(key, score_grad)
    return value_part, key_part, query_part


def key_kernel(own_ref, p1_ref, p2_ref, p3_ref, k_ref, kr_ref, tables_ref):
    pieces = (own_ref[...], p1_ref[...], p2_ref[...], p3_ref[...])
    count = len(pieces)
    head = lax.axis_index("head")
    parts = []
    for j in range(count):
        back = lax.rem(head - j + count, count)
        part = pieces[0]
        for r in range(1, count):
            part = jnp.where(back == r, pieces[r], part)
        parts.append(part)
    cosine_t, sine_t = tables_transposed(jnp.concatenate(parts, axis=1))
    tables_ref[:HALF, :] = cosine_t
    tables_ref[HALF:, :] = sine_t
    wide, signed = row_tables(cosine_t, sine_t)
    for g in range(k_ref.shape[1] // HEAD):
        cols = pl.ds(g * HEAD, HEAD)
        kr_ref[:, cols] = rotated(k_ref[:, cols].astype(F32), wide, signed).astype(BF16)


def prep_kernel(
    groups, span_ref, tables_ref, lse_hbm, q_hbm, do_hbm, at_hbm,
    qr_ref, do_ref, norm_ref, delta_ref, flag_ref, q_ref, at_ref, lse_ref, sems,
):
    heads = qr_ref.shape[1] // HEAD
    size = heads // groups
    copies = []
    for g in range(groups):
        cols = pl.ds(g * size * HEAD, size * HEAD)
        for i, (source, target) in enumerate(
            ((q_hbm, q_ref), (do_hbm, do_ref), (at_hbm, at_ref))
        ):
            copy = pltpu.make_async_copy(
                source.at[:, cols], target.at[:, cols], sems.at[3 * g + i]
            )
            copy.start()
            copies.append(copy)
    lse_copy = pltpu.make_async_copy(lse_hbm, lse_ref, sems.at[3 * groups])
    lse_copy.start()
    me = lax.axis_index("ctx")
    step_row = lax.broadcasted_iota(jnp.int32, flag_ref.shape, 0)
    flags = jnp.zeros(flag_ref.shape, jnp.int32)
    for step in range(1, WIN):
        other = lax.rem(me + step, span_ref.shape[0])
        earlier = jnp.where(span_ref[other] < span_ref[me], 1, 0)
        flags = jnp.where(step_row == step, earlier, flags)
    flag_ref[...] = flags
    wide, signed = row_tables(tables_ref[:HALF, :], tables_ref[HALF:, :])
    chooser = jnp.ones((8, HEAD), BF16)
    for h in range(heads):
        if h % size == 0:
            for copy in copies[3 * (h // size) : 3 * (h // size) + 3]:
                copy.wait()
        hc = pl.ds(h * HEAD, HEAD)
        qr_ref[:, hc] = rotated(q_ref[:, hc].astype(F32), wide, signed).astype(BF16)
        product = do_ref[:, hc].astype(F32) * at_ref[:, hc].astype(F32)
        high = product.astype(BF16)
        low = (product - high.astype(F32)).astype(BF16)
        delta_ref[h : h + 1, :] = (dot_nt(chooser, high) + dot_nt(chooser, low))[:1]
    lse_copy.wait()
    norm_ref[...] = lse_ref[...] * LOG2E


def hop_kernel(step, wanted, started, *refs):
    count = len(wanted)
    dqt_ins, dqt_refs, part_refs = refs[:count], refs[-2 * count : -count], refs[-count:]
    k_ref, v_ref, qr_ref, do_ref, norm_ref, delta_ref, flag_ref = refs[
        count * started : -2 * count
    ]
    rows = qr_ref.shape[0]
    half = rows // 2
    heads = qr_ref.shape[1] // HEAD
    groups = k_ref.shape[1] // HEAD
    size = heads // groups
    earlier = flag_ref[step, 0] == 1
    norm = norm_ref[...]
    delta = delta_ref[...]

    def run(keys, queries):
        for g, dqt_in, dqt_ref, part_ref in zip(wanted, dqt_ins, dqt_refs, part_refs):
            kc = pl.ds(g * HEAD, HEAD)
            dk = dv = None
            for j in range(size):
                h = g * size + j
                hc = pl.ds(h * HEAD, HEAD)
                to = pl.ds(j * HEAD, HEAD)
                v_part, k_part, q_part = pair_part(
                    k_ref[keys, kc], v_ref[keys, kc], qr_ref[queries, hc], do_ref[queries, hc],
                    norm[h : h + 1, queries.start :], delta[h : h + 1, queries.start :], False,
                )
                if queries.start:
                    zeros = jnp.zeros((HEAD, queries.start), F32)
                    dqt_ref[to, : queries.start] = (
                        dqt_in[to, : queries.start] if started else zeros
                    )
                dqt_ref[to, queries] = dqt_in[to, queries] + q_part if started else q_part
                dv = v_part if dv is None else dv + v_part
                dk = k_part if dk is None else dk + k_part
            part_ref[keys, :HEAD] = dk.astype(BF16)
            part_ref[keys, HEAD:] = dv.astype(BF16)
            if keys.stop < rows:
                part_ref[keys.stop :, :] = jnp.zeros((rows - keys.stop, 2 * HEAD), BF16)

    @pl.when(earlier)
    def _():
        run(slice(0, half), slice(0, rows))

    @pl.when(jnp.logical_not(earlier))
    def _():
        run(slice(0, rows), slice(half, rows))


def own_kernel(groups, k_ref, v_ref, qr_ref, do_ref, norm_ref, delta_ref, *refs):
    dqt_ins, dqt_refs, part_refs = refs[:groups], refs[groups : 2 * groups], refs[2 * groups :]
    size = qr_ref.shape[1] // HEAD // groups
    norm = norm_ref[...]
    delta = delta_ref[...]
    for g in range(groups):
        kc = pl.ds(g * HEAD, HEAD)
        dk = dv = None
        for j in range(size):
            h = g * size + j
            hc = pl.ds(h * HEAD, HEAD)
            to = pl.ds(j * HEAD, HEAD)
            v_part, k_part, q_part = pair_part(
                k_ref[:, kc], v_ref[:, kc], qr_ref[:, hc], do_ref[:, hc],
                norm[h : h + 1], delta[h : h + 1], True,
            )
            dqt_refs[g][to, :] = dqt_ins[g][to, :] + q_part
            dv = v_part if dv is None else dv + v_part
            dk = k_part if dk is None else dk + k_part
        part_refs[g][:, :HEAD] = dk
        part_refs[g][:, HEAD:] = dv


def query_kernel(groups, tables_ref, *refs):
    dqt_refs, own_refs = refs[:groups], refs[groups : 2 * groups]
    swapped_refs, out_ref = refs[2 * groups : 3 * groups], refs[3 * groups]
    sum_refs = refs[3 * groups + 1 :]
    odd = (lax.axis_index("ctx") & 1) == 1
    for g in range(groups):
        sum_refs[g][...] = own_refs[g][...] + jnp.where(
            odd, swapped_refs[g][...].astype(F32), 0.0
        )
    cosine_t = tables_ref[:HALF, :] * ROOT_SCALE
    sine_t = tables_ref[HALF:, :] * ROOT_SCALE
    size = dqt_refs[0].shape[0] // HEAD
    for g in range(groups):
        for j in range(size):
            y1 = dqt_refs[g][pl.ds(j * HEAD, HALF), :]
            y2 = dqt_refs[g][pl.ds(j * HEAD + HALF, HALF), :]
            turned = jnp.concatenate(
                [y1 * cosine_t + y2 * sine_t, y2 * cosine_t - y1 * sine_t], axis=0
            )
            out_ref[:, pl.ds((g * size + j) * HEAD, HEAD)] = turned.T.astype(BF16)


def add_kernel(two_ref, swapped_ref, three_ref, sum_ref):
    even = (lax.axis_index("ctx") & 1) == 0
    total = two_ref[...].astype(F32) + three_ref[...].astype(F32)
    sum_ref[...] = (total + jnp.where(even, swapped_ref[...].astype(F32), 0.0)).astype(BF16)


def final_kernel(groups, tables_ref, *refs):
    own_refs, home_refs, (dk_ref, dv_ref) = refs[:groups], refs[groups : 2 * groups], refs[-2:]
    wide, signed = row_tables(tables_ref[:HALF, :], tables_ref[HALF:, :])
    wide = wide * ROOT_SCALE
    signed = signed * -ROOT_SCALE
    for g in range(groups):
        cols = pl.ds(g * HEAD, HEAD)
        total = own_refs[g][...] + home_refs[g][...].astype(F32)
        dk_ref[:, cols] = rotated(total[:, :HEAD], wide, signed).astype(BF16)
        dv_ref[:, cols] = total[:, HEAD:].astype(BF16)


SMEM = pl.BlockSpec(memory_space=pltpu.SMEM)
VMEM = pl.BlockSpec(memory_space=pltpu.VMEM)
HBM = pl.BlockSpec(memory_space=pltpu.HBM)


def call(kernel, outs, specs, scratch=(), micros=1):
    return pl.pallas_call(
        kernel,
        out_shape=[jax.ShapeDtypeStruct(shape, dtype) for shape, dtype in outs],
        in_specs=specs,
        out_specs=[VMEM] * len(outs),
        scratch_shapes=list(scratch),
        compiler_params=pltpu.CompilerParams(vmem_limit_bytes=VMEM_LIMIT),
        cost_estimate=pl.CostEstimate(
            flops=1 << 20, bytes_accessed=micros * 3690000, transcendentals=0
        ),
    )


def shifted(value, steps, axis="ctx"):
    count = lax.axis_size(axis)
    pairs = [(source, (source + steps) % count) for source in range(count)]
    return lax.ppermute(value, axis, pairs)


def exchanged(value):
    count = lax.axis_size("ctx")
    return lax.ppermute(value, "ctx", [(source, source ^ 1) for source in range(count)])


def shards(q, k, v, do, at, lse, positions, span_map):
    rows = q.shape[0]
    wide_q = q.shape[1]
    wide_k = k.shape[1]
    heads = wide_q // HEAD
    q, do, at, k_here, v_here, lse, span_map, own = (
        pltpu.with_memory_space_constraint(x, pltpu.HBM)
        for x in (q, do, at, k, v, lse, span_map, positions)
    )

    pieces = [own] + [shifted(positions, r, "head") for r in (1, 2, 3)]
    groups = wide_k // HEAD
    every = tuple(range(groups))

    groups = wide_k // HEAD
    every = tuple(range(groups))

    v1 = shifted(v, -1)
    kr, tables = call(
        key_kernel, [((rows, wide_k), BF16), ((HEAD, rows), F32)], [VMEM] * 5
    )(*pieces, k_here)
    k1 = shifted(kr, -1)
    shared = call(
        functools.partial(prep_kernel, groups),
        [((rows, wide_q), BF16)] * 2 + [((heads, rows), F32)] * 2 + [((8, HEAD), jnp.int32)],
        [SMEM, VMEM] + [HBM] * 4,
        [
            pltpu.VMEM((rows, wide_q), BF16),
            pltpu.VMEM((rows, wide_q), BF16),
            pltpu.VMEM((heads, rows), F32),
            pltpu.SemaphoreType.DMA((3 * groups + 1,)),
        ],
        micros=2,
    )(span_map, tables, lse, q, do, at)
    v1, _ = lax.optimization_barrier((v1, shared[3]))
    v3 = shifted(v1, -2)
    k3 = shifted(k1, -2)
    dqs = []
    dq_out = ((wide_q // groups, rows), F32)
    part_out = ((rows, 2 * HEAD), BF16)

    def hop(step, wanted, key, value):
        count = len(wanted)
        started = len(dqs) > 0
        before = [dqs[g] for g in wanted] if started else []
        results = call(
            functools.partial(hop_kernel, step, wanted, started),
            [dq_out] * count + [part_out] * count,
            [VMEM] * (7 + len(before)),
            micros=count,
        )(*before, key, value, *shared)
        if not started:
            dqs.extend(results[:count])
        for i, g in enumerate(wanted):
            dqs[g] = results[i]
        return results[count:]

    parts1 = hop(1, every, k1, v1)
    swapped = [exchanged(part) for part in parts1]
    kr2, v_far, _ = lax.optimization_barrier((kr, v, parts1[0]))
    k2 = shifted(kr2, -2)
    v2 = shifted(v_far, -2)
    moved = [shifted(*hop(3, (g,), k3, v3), 1) for g in every]
    results = call(
        functools.partial(own_kernel, groups),
        [dq_out] * groups + [((rows, 2 * HEAD), F32)] * groups,
        [VMEM] * (6 + groups),
        micros=3,
    )(kr, v_here, *shared[:4], *dqs)
    dqs, owns = list(results[:groups]), results[groups:]
    parts2 = hop(2, every, k2, v2)
    dq, *owns = call(
        functools.partial(query_kernel, groups),
        [((rows, wide_q), BF16)] + [((rows, 2 * HEAD), F32)] * groups,
        [VMEM] * (1 + 3 * groups),
    )(tables, *dqs, *owns, *swapped)
    *parts2, _ = lax.optimization_barrier((*parts2, owns[0]))
    home = []
    for g in every:
        (total,) = call(add_kernel, [part_out], [VMEM] * 3)(parts2[g], swapped[g], moved[g])
        home.append(shifted(total, 2))

    dk, dv = call(
        functools.partial(final_kernel, groups),
        [((rows, wide_k), BF16), ((rows, wide_k), BF16)],
        [VMEM] * (1 + 2 * groups),
    )(tables, *owns, *home)
    return dq, dk, dv


def solution(mesh):
    placed = (
        P("ctx", "head"),
        P("ctx", "head"),
        P("ctx", "head"),
        P("ctx", "head"),
        P("ctx", "head"),
        P("head", "ctx"),
        P(None, ("ctx", "head")),
        P(),
    )
    return jax.shard_map(
        shards,
        mesh=mesh,
        in_specs=placed,
        out_specs=(P("ctx", "head"), P("ctx", "head"), P("ctx", "head")),
        check_vma=False,
    )
```

```python
import functools
import math

import jax
import jax.numpy as jnp
import numpy as np
from jax import lax
from jax.experimental import pallas as pl
from jax.experimental.pallas import tpu as pltpu
from jax.sharding import PartitionSpec as P

HEAD = 128
HALF = HEAD // 2
WIN = 4
ROPE_BASE = 1000000.0
YARN_FACTOR = 4.0
YARN_INITIAL = 32768.0
BETA_FAST = 32.0
BETA_SLOW = 1.0
YARN_MSCALE = 1.0 + 0.1 * math.log(4.0)
ROOT_SCALE = 1.0 / math.sqrt(HEAD)
LOG2E = math.log2(math.e)
VMEM_LIMIT = 24 * 1024 * 1024

F32 = jnp.float32
BF16 = jnp.bfloat16


def frequencies():
    pair = np.arange(HALF, dtype=np.float64)
    inverse = np.exp(-2.0 * pair / HEAD * math.log(ROPE_BASE))
    ratio = YARN_INITIAL * inverse / (2.0 * math.pi)
    ramp = np.clip((ratio - BETA_SLOW) / (BETA_FAST - BETA_SLOW), 0.0, 1.0)
    return inverse * ((1.0 - ramp) / YARN_FACTOR + ramp)


def frequency_rows(lanes):
    values = frequencies()
    row = lax.broadcasted_iota(jnp.int32, (8, lanes), 0)
    tiles = []
    for first in range(0, HALF, 8):
        tile = jnp.full((8, lanes), float(values[first]), F32)
        for j in range(1, 8):
            tile = jnp.where(row == j, float(values[first + j]), tile)
        tiles.append(tile)
    return jnp.concatenate(tiles, axis=0)


def sine_cosine(angle):
    turns = jnp.floor(angle * (2.0 / math.pi) + 0.5)
    r = angle - turns * 1.5703125
    r = r - turns * 4.837512969970703125e-4
    r = r - turns * 7.54978995489188e-8
    r2 = r * r
    s = r + r * r2 * (-1.6666654611e-1 + r2 * (8.3321608736e-3 - r2 * 1.9515295891e-4))
    c = (
        1.0
        - 0.5 * r2
        + r2
        * r2
        * (4.166664568298827e-2 + r2 * (-1.388731625493765e-3 + r2 * 2.443315711809948e-5))
    )
    quadrant = turns.astype(jnp.int32) & 3
    odd = (quadrant & 1) == 1
    sine = jnp.where(odd, c, s)
    cosine = jnp.where(odd, s, c)
    sine = jnp.where(quadrant >= 2, -sine, sine)
    cosine = jnp.where((quadrant == 1) | (quadrant == 2), -cosine, cosine)
    return sine, cosine


def tables_transposed(place):
    place = place.astype(F32)
    freq = frequency_rows(place.shape[1])
    pair = lax.broadcasted_iota(jnp.int32, freq.shape, 0)
    first = HEAD // 8
    second = first + 3 * HEAD // 16
    chosen = jnp.where(
        pair < first, place[0:1], jnp.where(pair < second, place[1:2], place[2:3])
    )
    sine, cosine = sine_cosine(chosen * freq)
    return cosine * YARN_MSCALE, sine * YARN_MSCALE


def row_tables(cosine_t, sine_t):
    wide = jnp.concatenate([cosine_t, cosine_t], axis=0).T
    signed = jnp.concatenate([-sine_t, sine_t], axis=0).T
    return wide, signed


def rotated(x, wide, signed):
    return x * wide + pltpu.roll(x, HALF, 1) * signed


def dot_nt(a, b):
    return lax.dot_general(a, b, (((1,), (1,)), ((), ())), preferred_element_type=F32)


def dot_nn(a, b):
    return lax.dot_general(a, b, (((1,), (0,)), ((), ())), preferred_element_type=F32)


def dot_tn(a, b):
    return lax.dot_general(a, b, (((0,), (0,)), ((), ())), preferred_element_type=F32)


def pair_part(key, value, query, grad, norm, delta, causal):
    scores = dot_nt(key, query)
    weights = jnp.exp2(scores * (ROOT_SCALE * LOG2E) - norm)
    if causal:
        at_key = lax.broadcasted_iota(jnp.int32, scores.shape, 0)
        at_query = lax.broadcasted_iota(jnp.int32, scores.shape, 1)
        weights = jnp.where(at_key <= at_query, weights, 0.0)
    value_part = dot_nn(weights.astype(BF16), grad)
    score_grad = (weights * (dot_nt(value, grad) - delta)).astype(BF16)
    key_part = dot_nn(score_grad, query)
    query_part = dot_tn(key, score_grad)
    return value_part, key_part, query_part


def key_kernel(own_ref, p1_ref, p2_ref, p3_ref, k_ref, kr_ref, tables_ref):
    pieces = (own_ref[...], p1_ref[...], p2_ref[...], p3_ref[...])
    count = len(pieces)
    head = lax.axis_index("head")
    parts = []
    for j in range(count):
        back = lax.rem(head - j + count, count)
        part = pieces[0]
        for r in range(1, count):
            part = jnp.where(back == r, pieces[r], part)
        parts.append(part)
    cosine_t, sine_t = tables_transposed(jnp.concatenate(parts, axis=1))
    tables_ref[:HALF, :] = cosine_t
    tables_ref[HALF:, :] = sine_t
    wide, signed = row_tables(cosine_t, sine_t)
    for g in range(k_ref.shape[1] // HEAD):
        cols = pl.ds(g * HEAD, HEAD)
        kr_ref[:, cols] = rotated(k_ref[:, cols].astype(F32), wide, signed).astype(BF16)


def prep_kernel(
    groups, span_ref, tables_ref, lse_hbm, q_hbm, do_hbm, at_hbm,
    qr_ref, do_ref, norm_ref, delta_ref, flag_ref, q_ref, at_ref, lse_ref, sems,
):
    heads = qr_ref.shape[1] // HEAD
    size = heads // groups
    copies = []
    for g in range(groups):
        cols = pl.ds(g * size * HEAD, size * HEAD)
        for i, (source, target) in enumerate(
            ((q_hbm, q_ref), (do_hbm, do_ref), (at_hbm, at_ref))
        ):
            copy = pltpu.make_async_copy(
                source.at[:, cols], target.at[:, cols], sems.at[3 * g + i]
            )
            copy.start()
            copies.append(copy)
    lse_copy = pltpu.make_async_copy(lse_hbm, lse_ref, sems.at[3 * groups])
    lse_copy.start()
    me = lax.axis_index("ctx")
    step_row = lax.broadcasted_iota(jnp.int32, flag_ref.shape, 0)
    flags = jnp.zeros(flag_ref.shape, jnp.int32)
    for step in range(1, WIN):
        other = lax.rem(me + step, span_ref.shape[0])
        earlier = jnp.where(span_ref[other] < span_ref[me], 1, 0)
        flags = jnp.where(step_row == step, earlier, flags)
    flag_ref[...] = flags
    wide, signed = row_tables(tables_ref[:HALF, :], tables_ref[HALF:, :])
    chooser = jnp.ones((8, HEAD), BF16)
    for h in range(heads):
        if h % size == 0:
            for copy in copies[3 * (h // size) : 3 * (h // size) + 3]:
                copy.wait()
        hc = pl.ds(h * HEAD, HEAD)
        qr_ref[:, hc] = rotated(q_ref[:, hc].astype(F32), wide, signed).astype(BF16)
        product = do_ref[:, hc].astype(F32) * at_ref[:, hc].astype(F32)
        high = product.astype(BF16)
        low = (product - high.astype(F32)).astype(BF16)
        delta_ref[h : h + 1, :] = (dot_nt(chooser, high) + dot_nt(chooser, low))[:1]
    lse_copy.wait()
    norm_ref[...] = lse_ref[...] * LOG2E


def hop_kernel(step, wanted, started, *refs):
    count = len(wanted)
    dqt_ins, dqt_refs, part_refs = refs[:count], refs[-2 * count : -count], refs[-count:]
    k_ref, v_ref, qr_ref, do_ref, norm_ref, delta_ref, flag_ref = refs[
        count * started : -2 * count
    ]
    rows = qr_ref.shape[0]
    half = rows // 2
    heads = qr_ref.shape[1] // HEAD
    groups = k_ref.shape[1] // HEAD
    size = heads // groups
    earlier = flag_ref[step, 0] == 1
    norm = norm_ref[...]
    delta = delta_ref[...]

    def run(keys, queries):
        for g, dqt_in, dqt_ref, part_ref in zip(wanted, dqt_ins, dqt_refs, part_refs):
            kc = pl.ds(g * HEAD, HEAD)
            dk = dv = None
            for j in range(size):
                h = g * size + j
                hc = pl.ds(h * HEAD, HEAD)
                to = pl.ds(j * HEAD, HEAD)
                v_part, k_part, q_part = pair_part(
                    k_ref[keys, kc], v_ref[keys, kc], qr_ref[queries, hc], do_ref[queries, hc],
                    norm[h : h + 1, queries.start :], delta[h : h + 1, queries.start :], False,
                )
                if queries.start:
                    zeros = jnp.zeros((HEAD, queries.start), F32)
                    dqt_ref[to, : queries.start] = (
                        dqt_in[to, : queries.start] if started else zeros
                    )
                dqt_ref[to, queries] = dqt_in[to, queries] + q_part if started else q_part
                dv = v_part if dv is None else dv + v_part
                dk = k_part if dk is None else dk + k_part
            part_ref[keys, :HEAD] = dk.astype(BF16)
            part_ref[keys, HEAD:] = dv.astype(BF16)
            if keys.stop < rows:
                part_ref[keys.stop :, :] = jnp.zeros((rows - keys.stop, 2 * HEAD), BF16)

    @pl.when(earlier)
    def _():
        run(slice(0, half), slice(0, rows))

    @pl.when(jnp.logical_not(earlier))
    def _():
        run(slice(0, rows), slice(half, rows))


def own_kernel(groups, k_ref, v_ref, qr_ref, do_ref, norm_ref, delta_ref, *refs):
    dqt_ins, dqt_refs, part_refs = refs[:groups], refs[groups : 2 * groups], refs[2 * groups :]
    size = qr_ref.shape[1] // HEAD // groups
    norm = norm_ref[...]
    delta = delta_ref[...]
    for g in range(groups):
        kc = pl.ds(g * HEAD, HEAD)
        dk = dv = None
        for j in range(size):
            h = g * size + j
            hc = pl.ds(h * HEAD, HEAD)
            to = pl.ds(j * HEAD, HEAD)
            v_part, k_part, q_part = pair_part(
                k_ref[:, kc], v_ref[:, kc], qr_ref[:, hc], do_ref[:, hc],
                norm[h : h + 1], delta[h : h + 1], True,
            )
            dqt_refs[g][to, :] = dqt_ins[g][to, :] + q_part
            dv = v_part if dv is None else dv + v_part
            dk = k_part if dk is None else dk + k_part
        part_refs[g][:, :HEAD] = dk
        part_refs[g][:, HEAD:] = dv


def query_kernel(groups, tables_ref, *refs):
    dqt_refs, own_refs = refs[:groups], refs[groups : 2 * groups]
    swapped_refs, out_ref = refs[2 * groups : 3 * groups], refs[3 * groups]
    sum_refs = refs[3 * groups + 1 :]
    odd = (lax.axis_index("ctx") & 1) == 1
    for g in range(groups):
        sum_refs[g][...] = own_refs[g][...] + jnp.where(
            odd, swapped_refs[g][...].astype(F32), 0.0
        )
    cosine_t = tables_ref[:HALF, :] * ROOT_SCALE
    sine_t = tables_ref[HALF:, :] * ROOT_SCALE
    size = dqt_refs[0].shape[0] // HEAD
    for g in range(groups):
        for j in range(size):
            y1 = dqt_refs[g][pl.ds(j * HEAD, HALF), :]
            y2 = dqt_refs[g][pl.ds(j * HEAD + HALF, HALF), :]
            turned = jnp.concatenate(
                [y1 * cosine_t + y2 * sine_t, y2 * cosine_t - y1 * sine_t], axis=0
            )
            out_ref[:, pl.ds((g * size + j) * HEAD, HEAD)] = turned.T.astype(BF16)


def add_kernel(two_ref, swapped_ref, three_ref, sum_ref):
    even = (lax.axis_index("ctx") & 1) == 0
    total = two_ref[...].astype(F32) + three_ref[...].astype(F32)
    sum_ref[...] = (total + jnp.where(even, swapped_ref[...].astype(F32), 0.0)).astype(BF16)


def final_kernel(groups, tables_ref, *refs):
    own_refs, home_refs, (dk_ref, dv_ref) = refs[:groups], refs[groups : 2 * groups], refs[-2:]
    wide, signed = row_tables(tables_ref[:HALF, :], tables_ref[HALF:, :])
    wide = wide * ROOT_SCALE
    signed = signed * -ROOT_SCALE
    for g in range(groups):
        cols = pl.ds(g * HEAD, HEAD)
        total = own_refs[g][...] + home_refs[g][...].astype(F32)
        dk_ref[:, cols] = rotated(total[:, :HEAD], wide, signed).astype(BF16)
        dv_ref[:, cols] = total[:, HEAD:].astype(BF16)


SMEM = pl.BlockSpec(memory_space=pltpu.SMEM)
VMEM = pl.BlockSpec(memory_space=pltpu.VMEM)
HBM = pl.BlockSpec(memory_space=pltpu.HBM)


def call(kernel, outs, specs, scratch=(), micros=1):
    return pl.pallas_call(
        kernel,
        out_shape=[jax.ShapeDtypeStruct(shape, dtype) for shape, dtype in outs],
        in_specs=specs,
        out_specs=[VMEM] * len(outs),
        scratch_shapes=list(scratch),
        compiler_params=pltpu.CompilerParams(vmem_limit_bytes=VMEM_LIMIT),
        cost_estimate=pl.CostEstimate(
            flops=1 << 20, bytes_accessed=micros * 3690000, transcendentals=0
        ),
    )


def shifted(value, steps, axis="ctx"):
    count = lax.axis_size(axis)
    pairs = [(source, (source + steps) % count) for source in range(count)]
    return lax.ppermute(value, axis, pairs)


def exchanged(value):
    count = lax.axis_size("ctx")
    return lax.ppermute(value, "ctx", [(source, source ^ 1) for source in range(count)])


def shards(q, k, v, do, at, lse, positions, span_map):
    rows = q.shape[0]
    wide_q = q.shape[1]
    wide_k = k.shape[1]
    heads = wide_q // HEAD
    q, do, at, k_here, v_here, lse, span_map, own = (
        pltpu.with_memory_space_constraint(x, pltpu.HBM)
        for x in (q, do, at, k, v, lse, span_map, positions)
    )

    pieces = [own] + [shifted(positions, r, "head") for r in (1, 2, 3)]
    groups = wide_k // HEAD
    every = tuple(range(groups))

    groups = wide_k // HEAD
    every = tuple(range(groups))

    v1 = shifted(v, -1)
    kr, tables = call(
        key_kernel, [((rows, wide_k), BF16), ((HEAD, rows), F32)], [VMEM] * 5
    )(*pieces, k_here)
    k1 = shifted(kr, -1)
    shared = call(
        functools.partial(prep_kernel, groups),
        [((rows, wide_q), BF16)] * 2 + [((heads, rows), F32)] * 2 + [((8, HEAD), jnp.int32)],
        [SMEM, VMEM] + [HBM] * 4,
        [
            pltpu.VMEM((rows, wide_q), BF16),
            pltpu.VMEM((rows, wide_q), BF16),
            pltpu.VMEM((heads, rows), F32),
            pltpu.SemaphoreType.DMA((3 * groups + 1,)),
        ],
        micros=2,
    )(span_map, tables, lse, q, do, at)
    v1, _ = lax.optimization_barrier((v1, shared[3]))
    v3 = shifted(v1, -2)
    v_far, _ = lax.optimization_barrier((v, shared[3]))
    v2 = shifted(v_far, -2)
    k3 = shifted(k1, -2)
    dqs = []
    dq_out = ((wide_q // groups, rows), F32)
    part_out = ((rows, 2 * HEAD), BF16)

    def hop(step, wanted, key, value):
        count = len(wanted)
        started = len(dqs) > 0
        before = [dqs[g] for g in wanted] if started else []
        results = call(
            functools.partial(hop_kernel, step, wanted, started),
            [dq_out] * count + [part_out] * count,
            [VMEM] * (7 + len(before)),
            micros=count,
        )(*before, key, value, *shared)
        if not started:
            dqs.extend(results[:count])
        for i, g in enumerate(wanted):
            dqs[g] = results[i]
        return results[count:]

    parts1 = hop(1, every, k1, v1)
    swapped = [exchanged(part) for part in parts1]
    kr2, _ = lax.optimization_barrier((kr, parts1[0]))
    k2 = shifted(kr2, -2)
    moved = [shifted(*hop(3, (g,), k3, v3), 1) for g in every]
    parts2 = hop(2, every, k2, v2)
    results = call(
        functools.partial(own_kernel, groups),
        [dq_out] * groups + [((rows, 2 * HEAD), F32)] * groups,
        [VMEM] * (6 + groups),
        micros=3,
    )(kr, v_here, *shared[:4], *dqs)
    dqs, owns = list(results[:groups]), results[groups:]
    dq, *owns = call(
        functools.partial(query_kernel, groups),
        [((rows, wide_q), BF16)] + [((rows, 2 * HEAD), F32)] * groups,
        [VMEM] * (1 + 3 * groups),
    )(tables, *dqs, *owns, *swapped)
    home = []
    for g in every:
        (total,) = call(add_kernel, [part_out], [VMEM] * 3)(parts2[g], swapped[g], moved[g])
        home.append(shifted(total, 2))

    dk, dv = call(
        functools.partial(final_kernel, groups),
        [((rows, wide_k), BF16), ((rows, wide_k), BF16)],
        [VMEM] * (1 + 2 * groups),
    )(tables, *owns, *home)
    return dq, dk, dv


def solution(mesh):
    placed = (
        P("ctx", "head"),
        P("ctx", "head"),
        P("ctx", "head"),
        P("ctx", "head"),
        P("ctx", "head"),
        P("head", "ctx"),
        P(None, ("ctx", "head")),
        P(),
    )
    return jax.shard_map(
        shards,
        mesh=mesh,
        in_specs=placed,
        out_specs=(P("ctx", "head"), P("ctx", "head"), P("ctx", "head")),
        check_vma=False,
    )
```

```python
import functools
import math

import jax
import jax.numpy as jnp
import numpy as np
from jax import lax
from jax.experimental import pallas as pl
from jax.experimental.pallas import tpu as pltpu
from jax.sharding import PartitionSpec as P

HEAD = 128
HALF = HEAD // 2
WIN = 4
ROPE_BASE = 1000000.0
YARN_FACTOR = 4.0
YARN_INITIAL = 32768.0
BETA_FAST = 32.0
BETA_SLOW = 1.0
YARN_MSCALE = 1.0 + 0.1 * math.log(4.0)
ROOT_SCALE = 1.0 / math.sqrt(HEAD)
LOG2E = math.log2(math.e)
VMEM_LIMIT = 24 * 1024 * 1024

F32 = jnp.float32
BF16 = jnp.bfloat16


def frequencies():
    pair = np.arange(HALF, dtype=np.float64)
    inverse = np.exp(-2.0 * pair / HEAD * math.log(ROPE_BASE))
    ratio = YARN_INITIAL * inverse / (2.0 * math.pi)
    ramp = np.clip((ratio - BETA_SLOW) / (BETA_FAST - BETA_SLOW), 0.0, 1.0)
    return inverse * ((1.0 - ramp) / YARN_FACTOR + ramp)


def frequency_rows(lanes):
    values = frequencies()
    row = lax.broadcasted_iota(jnp.int32, (8, lanes), 0)
    tiles = []
    for first in range(0, HALF, 8):
        tile = jnp.full((8, lanes), float(values[first]), F32)
        for j in range(1, 8):
            tile = jnp.where(row == j, float(values[first + j]), tile)
        tiles.append(tile)
    return jnp.concatenate(tiles, axis=0)


def sine_cosine(angle):
    turns = jnp.floor(angle * (2.0 / math.pi) + 0.5)
    r = angle - turns * 1.5703125
    r = r - turns * 4.837512969970703125e-4
    r = r - turns * 7.54978995489188e-8
    r2 = r * r
    s = r + r * r2 * (-1.6666654611e-1 + r2 * (8.3321608736e-3 - r2 * 1.9515295891e-4))
    c = (
        1.0
        - 0.5 * r2
        + r2
        * r2
        * (4.166664568298827e-2 + r2 * (-1.388731625493765e-3 + r2 * 2.443315711809948e-5))
    )
    quadrant = turns.astype(jnp.int32) & 3
    odd = (quadrant & 1) == 1
    sine = jnp.where(odd, c, s)
    cosine = jnp.where(odd, s, c)
    sine = jnp.where(quadrant >= 2, -sine, sine)
    cosine = jnp.where((quadrant == 1) | (quadrant == 2), -cosine, cosine)
    return sine, cosine


def tables_transposed(place):
    place = place.astype(F32)
    freq = frequency_rows(place.shape[1])
    pair = lax.broadcasted_iota(jnp.int32, freq.shape, 0)
    first = HEAD // 8
    second = first + 3 * HEAD // 16
    chosen = jnp.where(
        pair < first, place[0:1], jnp.where(pair < second, place[1:2], place[2:3])
    )
    sine, cosine = sine_cosine(chosen * freq)
    return cosine * YARN_MSCALE, sine * YARN_MSCALE


def row_tables(cosine_t, sine_t):
    wide = jnp.concatenate([cosine_t, cosine_t], axis=0).T
    signed = jnp.concatenate([-sine_t, sine_t], axis=0).T
    return wide, signed


def rotated(x, wide, signed):
    return x * wide + pltpu.roll(x, HALF, 1) * signed


def dot_nt(a, b):
    return lax.dot_general(a, b, (((1,), (1,)), ((), ())), preferred_element_type=F32)


def dot_nn(a, b):
    return lax.dot_general(a, b, (((1,), (0,)), ((), ())), preferred_element_type=F32)


def dot_tn(a, b):
    return lax.dot_general(a, b, (((0,), (0,)), ((), ())), preferred_element_type=F32)


def pair_part(key, value, query, grad, norm, delta, causal):
    scores = dot_nt(key, query)
    weights = jnp.exp2(scores * (ROOT_SCALE * LOG2E) - norm)
    if causal:
        at_key = lax.broadcasted_iota(jnp.int32, scores.shape, 0)
        at_query = lax.broadcasted_iota(jnp.int32, scores.shape, 1)
        weights = jnp.where(at_key <= at_query, weights, 0.0)
    value_part = dot_nn(weights.astype(BF16), grad)
    score_grad = (weights * (dot_nt(value, grad) - delta)).astype(BF16)
    key_part = dot_nn(score_grad, query)
    query_part = dot_tn(key, score_grad)
    return value_part, key_part, query_part


def key_kernel(own_ref, p1_ref, p2_ref, p3_ref, k_ref, kr_ref, tables_ref):
    pieces = (own_ref[...], p1_ref[...], p2_ref[...], p3_ref[...])
    count = len(pieces)
    head = lax.axis_index("head")
    parts = []
    for j in range(count):
        back = lax.rem(head - j + count, count)
        part = pieces[0]
        for r in range(1, count):
            part = jnp.where(back == r, pieces[r], part)
        parts.append(part)
    cosine_t, sine_t = tables_transposed(jnp.concatenate(parts, axis=1))
    tables_ref[:HALF, :] = cosine_t
    tables_ref[HALF:, :] = sine_t
    wide, signed = row_tables(cosine_t, sine_t)
    for g in range(k_ref.shape[1] // HEAD):
        cols = pl.ds(g * HEAD, HEAD)
        kr_ref[:, cols] = rotated(k_ref[:, cols].astype(F32), wide, signed).astype(BF16)


def prep_kernel(
    groups, span_ref, tables_ref, lse_hbm, q_hbm, do_hbm, at_hbm,
    qr_ref, do_ref, norm_ref, delta_ref, flag_ref, q_ref, at_ref, lse_ref, sems,
):
    heads = qr_ref.shape[1] // HEAD
    size = heads // groups
    copies = []
    for g in range(groups):
        cols = pl.ds(g * size * HEAD, size * HEAD)
        for i, (source, target) in enumerate(
            ((q_hbm, q_ref), (do_hbm, do_ref), (at_hbm, at_ref))
        ):
            copy = pltpu.make_async_copy(
                source.at[:, cols], target.at[:, cols], sems.at[3 * g + i]
            )
            copy.start()
            copies.append(copy)
    lse_copy = pltpu.make_async_copy(lse_hbm, lse_ref, sems.at[3 * groups])
    lse_copy.start()
    me = lax.axis_index("ctx")
    step_row = lax.broadcasted_iota(jnp.int32, flag_ref.shape, 0)
    flags = jnp.zeros(flag_ref.shape, jnp.int32)
    for step in range(1, WIN):
        other = lax.rem(me + step, span_ref.shape[0])
        earlier = jnp.where(span_ref[other] < span_ref[me], 1, 0)
        flags = jnp.where(step_row == step, earlier, flags)
    flag_ref[...] = flags
    wide, signed = row_tables(tables_ref[:HALF, :], tables_ref[HALF:, :])
    chooser = jnp.ones((8, HEAD), BF16)
    for h in range(heads):
        if h % size == 0:
            for copy in copies[3 * (h // size) : 3 * (h // size) + 3]:
                copy.wait()
        hc = pl.ds(h * HEAD, HEAD)
        qr_ref[:, hc] = rotated(q_ref[:, hc].astype(F32), wide, signed).astype(BF16)
        product = do_ref[:, hc].astype(F32) * at_ref[:, hc].astype(F32)
        high = product.astype(BF16)
        low = (product - high.astype(F32)).astype(BF16)
        delta_ref[h : h + 1, :] = (dot_nt(chooser, high) + dot_nt(chooser, low))[:1]
    lse_copy.wait()
    norm_ref[...] = lse_ref[...] * LOG2E


def hop_kernel(step, wanted, started, joined, *refs):
    count = len(wanted)
    if joined:
        *refs, part_ref = refs
        refs += [part_ref.at[:, 2 * HEAD * i : 2 * HEAD * (i + 1)] for i in range(count)]
    dqt_ins, dqt_refs, part_refs = refs[:count], refs[-2 * count : -count], refs[-count:]
    k_ref, v_ref, qr_ref, do_ref, norm_ref, delta_ref, flag_ref = refs[
        count * started : -2 * count
    ]
    rows = qr_ref.shape[0]
    half = rows // 2
    heads = qr_ref.shape[1] // HEAD
    groups = k_ref.shape[1] // HEAD
    size = heads // groups
    earlier = flag_ref[step, 0] == 1
    norm = norm_ref[...]
    delta = delta_ref[...]

    def run(keys, queries):
        for g, dqt_in, dqt_ref, part_ref in zip(wanted, dqt_ins, dqt_refs, part_refs):
            kc = pl.ds(g * HEAD, HEAD)
            dk = dv = None
            for j in range(size):
                h = g * size + j
                hc = pl.ds(h * HEAD, HEAD)
                to = pl.ds(j * HEAD, HEAD)
                v_part, k_part, q_part = pair_part(
                    k_ref[keys, kc], v_ref[keys, kc], qr_ref[queries, hc], do_ref[queries, hc],
                    norm[h : h + 1, queries.start :], delta[h : h + 1, queries.start :], False,
                )
                if queries.start:
                    zeros = jnp.zeros((HEAD, queries.start), F32)
                    dqt_ref[to, : queries.start] = (
                        dqt_in[to, : queries.start] if started else zeros
                    )
                dqt_ref[to, queries] = dqt_in[to, queries] + q_part if started else q_part
                dv = v_part if dv is None else dv + v_part
                dk = k_part if dk is None else dk + k_part
            part_ref[keys, :HEAD] = dk.astype(BF16)
            part_ref[keys, HEAD:] = dv.astype(BF16)
            if keys.stop < rows:
                part_ref[keys.stop :, :] = jnp.zeros((rows - keys.stop, 2 * HEAD), BF16)

    @pl.when(earlier)
    def _():
        run(slice(0, half), slice(0, rows))

    @pl.when(jnp.logical_not(earlier))
    def _():
        run(slice(0, rows), slice(half, rows))


def own_kernel(groups, k_ref, v_ref, qr_ref, do_ref, norm_ref, delta_ref, *refs):
    dqt_ins, dqt_refs, part_refs = refs[:groups], refs[groups : 2 * groups], refs[2 * groups :]
    size = qr_ref.shape[1] // HEAD // groups
    norm = norm_ref[...]
    delta = delta_ref[...]
    for g in range(groups):
        kc = pl.ds(g * HEAD, HEAD)
        dk = dv = None
        for j in range(size):
            h = g * size + j
            hc = pl.ds(h * HEAD, HEAD)
            to = pl.ds(j * HEAD, HEAD)
            v_part, k_part, q_part = pair_part(
                k_ref[:, kc], v_ref[:, kc], qr_ref[:, hc], do_ref[:, hc],
                norm[h : h + 1], delta[h : h + 1], True,
            )
            dqt_refs[g][to, :] = dqt_ins[g][to, :] + q_part
            dv = v_part if dv is None else dv + v_part
            dk = k_part if dk is None else dk + k_part
        part_refs[g][:, :HEAD] = dk
        part_refs[g][:, HEAD:] = dv


def query_kernel(groups, tables_ref, *refs):
    dqt_refs, own_refs = refs[:groups], refs[groups : 2 * groups]
    swapped_ref, out_ref, *sum_refs = refs[2 * groups :]
    odd = (lax.axis_index("ctx") & 1) == 1
    for g in range(groups):
        sum_refs[g][...] = own_refs[g][...] + jnp.where(
            odd, swapped_ref[:, 2 * HEAD * g : 2 * HEAD * (g + 1)].astype(F32), 0.0
        )
    cosine_t = tables_ref[:HALF, :] * ROOT_SCALE
    sine_t = tables_ref[HALF:, :] * ROOT_SCALE
    size = dqt_refs[0].shape[0] // HEAD
    for g in range(groups):
        for j in range(size):
            y1 = dqt_refs[g][pl.ds(j * HEAD, HALF), :]
            y2 = dqt_refs[g][pl.ds(j * HEAD + HALF, HALF), :]
            turned = jnp.concatenate(
                [y1 * cosine_t + y2 * sine_t, y2 * cosine_t - y1 * sine_t], axis=0
            )
            out_ref[:, pl.ds((g * size + j) * HEAD, HEAD)] = turned.T.astype(BF16)


def add_kernel(g, two_ref, swapped_ref, three_ref, sum_ref):
    even = (lax.axis_index("ctx") & 1) == 0
    total = two_ref[...].astype(F32) + three_ref[...].astype(F32)
    swapped = swapped_ref[:, 2 * HEAD * g : 2 * HEAD * (g + 1)].astype(F32)
    sum_ref[...] = (total + jnp.where(even, swapped, 0.0)).astype(BF16)


def final_kernel(groups, tables_ref, *refs):
    own_refs, home_refs, (dk_ref, dv_ref) = refs[:groups], refs[groups : 2 * groups], refs[-2:]
    wide, signed = row_tables(tables_ref[:HALF, :], tables_ref[HALF:, :])
    wide = wide * ROOT_SCALE
    signed = signed * -ROOT_SCALE
    for g in range(groups):
        cols = pl.ds(g * HEAD, HEAD)
        total = own_refs[g][...] + home_refs[g][...].astype(F32)
        dk_ref[:, cols] = rotated(total[:, :HEAD], wide, signed).astype(BF16)
        dv_ref[:, cols] = total[:, HEAD:].astype(BF16)


SMEM = pl.BlockSpec(memory_space=pltpu.SMEM)
VMEM = pl.BlockSpec(memory_space=pltpu.VMEM)
HBM = pl.BlockSpec(memory_space=pltpu.HBM)


def call(kernel, outs, specs, scratch=(), micros=1):
    return pl.pallas_call(
        kernel,
        out_shape=[jax.ShapeDtypeStruct(shape, dtype) for shape, dtype in outs],
        in_specs=specs,
        out_specs=[VMEM] * len(outs),
        scratch_shapes=list(scratch),
        compiler_params=pltpu.CompilerParams(vmem_limit_bytes=VMEM_LIMIT),
        cost_estimate=pl.CostEstimate(
            flops=1 << 20, bytes_accessed=micros * 3690000, transcendentals=0
        ),
    )


def shifted(value, steps, axis="ctx"):
    count = lax.axis_size(axis)
    pairs = [(source, (source + steps) % count) for source in range(count)]
    return lax.ppermute(value, axis, pairs)


def exchanged(value):
    count = lax.axis_size("ctx")
    return lax.ppermute(value, "ctx", [(source, source ^ 1) for source in range(count)])


def shards(q, k, v, do, at, lse, positions, span_map):
    rows = q.shape[0]
    wide_q = q.shape[1]
    wide_k = k.shape[1]
    heads = wide_q // HEAD
    q, do, at, k_here, v_here, lse, span_map, own = (
        pltpu.with_memory_space_constraint(x, pltpu.HBM)
        for x in (q, do, at, k, v, lse, span_map, positions)
    )

    pieces = [own] + [shifted(positions, r, "head") for r in (1, 2, 3)]
    groups = wide_k // HEAD
    every = tuple(range(groups))

    groups = wide_k // HEAD
    every = tuple(range(groups))

    v1 = shifted(v, -1)
    kr, tables = call(
        key_kernel, [((rows, wide_k), BF16), ((HEAD, rows), F32)], [VMEM] * 5
    )(*pieces, k_here)
    k1 = shifted(kr, -1)
    shared = call(
        functools.partial(prep_kernel, groups),
        [((rows, wide_q), BF16)] * 2 + [((heads, rows), F32)] * 2 + [((8, HEAD), jnp.int32)],
        [SMEM, VMEM] + [HBM] * 4,
        [
            pltpu.VMEM((rows, wide_q), BF16),
            pltpu.VMEM((rows, wide_q), BF16),
            pltpu.VMEM((heads, rows), F32),
            pltpu.SemaphoreType.DMA((3 * groups + 1,)),
        ],
        micros=2,
    )(span_map, tables, lse, q, do, at)
    v1, _ = lax.optimization_barrier((v1, shared[3]))
    v3 = shifted(v1, -2)
    dqs = []
    dq_out = ((wide_q // groups, rows), F32)
    part_out = ((rows, 2 * HEAD), BF16)

    def hop(step, wanted, key, value, joined=False):
        count = len(wanted)
        started = len(dqs) > 0
        before = [dqs[g] for g in wanted] if started else []
        results = call(
            functools.partial(hop_kernel, step, wanted, started, joined),
            [dq_out] * count
            + ([((rows, 2 * HEAD * count), BF16)] if joined else [part_out] * count),
            [VMEM] * (7 + len(before)),
            micros=count,
        )(*before, key, value, *shared)
        if not started:
            dqs.extend(results[:count])
        for i, g in enumerate(wanted):
            dqs[g] = results[i]
        return results[count:]

    (part1,) = hop(1, every, k1, v1, joined=True)
    swapped = exchanged(part1)
    held, kr2, v_far, _ = lax.optimization_barrier((k1, kr, v, part1))
    k3 = shifted(held, -2)
    k2 = shifted(kr2, -2)
    v2 = shifted(v_far, -2)
    moved = [shifted(*hop(3, (g,), k3, v3), 1) for g in every]
    k2, swapped = lax.optimization_barrier((k2, swapped))
    parts2 = hop(2, every, k2, v2)
    results = call(
        functools.partial(own_kernel, groups),
        [dq_out] * groups + [((rows, 2 * HEAD), F32)] * groups,
        [VMEM] * (6 + groups),
        micros=3,
    )(kr, v_here, *shared[:4], *dqs)
    dqs, owns = list(results[:groups]), results[groups:]
    dq, *owns = call(
        functools.partial(query_kernel, groups),
        [((rows, wide_q), BF16)] + [((rows, 2 * HEAD), F32)] * groups,
        [VMEM] * (2 + 2 * groups),
    )(tables, *dqs, *owns, swapped)
    home = []
    for g in every:
        (total,) = call(functools.partial(add_kernel, g), [part_out], [VMEM] * 3)(
            parts2[g], swapped, moved[g]
        )
        home.append(shifted(total, 2))

    dk, dv = call(
        functools.partial(final_kernel, groups),
        [((rows, wide_k), BF16), ((rows, wide_k), BF16)],
        [VMEM] * (1 + 2 * groups),
    )(tables, *owns, *home)
    return dq, dk, dv


def solution(mesh):
    placed = (
        P("ctx", "head"),
        P("ctx", "head"),
        P("ctx", "head"),
        P("ctx", "head"),
        P("ctx", "head"),
        P("head", "ctx"),
        P(None, ("ctx", "head")),
        P(),
    )
    return jax.shard_map(
        shards,
        mesh=mesh,
        in_specs=placed,
        out_specs=(P("ctx", "head"), P("ctx", "head"), P("ctx", "head")),
        check_vma=False,
    )
```

```python
import functools
import math

import jax
import jax.numpy as jnp
import numpy as np
from jax import lax
from jax.experimental import pallas as pl
from jax.experimental.pallas import tpu as pltpu
from jax.sharding import PartitionSpec as P

HEAD = 128
HALF = HEAD // 2
WIN = 4
ROPE_BASE = 1000000.0
YARN_FACTOR = 4.0
YARN_INITIAL = 32768.0
BETA_FAST = 32.0
BETA_SLOW = 1.0
YARN_MSCALE = 1.0 + 0.1 * math.log(4.0)
ROOT_SCALE = 1.0 / math.sqrt(HEAD)
LOG2E = math.log2(math.e)
VMEM_LIMIT = 24 * 1024 * 1024

F32 = jnp.float32
BF16 = jnp.bfloat16


def frequencies():
    pair = np.arange(HALF, dtype=np.float64)
    inverse = np.exp(-2.0 * pair / HEAD * math.log(ROPE_BASE))
    ratio = YARN_INITIAL * inverse / (2.0 * math.pi)
    ramp = np.clip((ratio - BETA_SLOW) / (BETA_FAST - BETA_SLOW), 0.0, 1.0)
    return inverse * ((1.0 - ramp) / YARN_FACTOR + ramp)


def frequency_rows(lanes):
    values = frequencies()
    row = lax.broadcasted_iota(jnp.int32, (8, lanes), 0)
    tiles = []
    for first in range(0, HALF, 8):
        tile = jnp.full((8, lanes), float(values[first]), F32)
        for j in range(1, 8):
            tile = jnp.where(row == j, float(values[first + j]), tile)
        tiles.append(tile)
    return jnp.concatenate(tiles, axis=0)


def sine_cosine(angle):
    turns = jnp.floor(angle * (2.0 / math.pi) + 0.5)
    r = angle - turns * 1.5703125
    r = r - turns * 4.837512969970703125e-4
    r = r - turns * 7.54978995489188e-8
    r2 = r * r
    s = r + r * r2 * (-1.6666654611e-1 + r2 * (8.3321608736e-3 - r2 * 1.9515295891e-4))
    c = (
        1.0
        - 0.5 * r2
        + r2
        * r2
        * (4.166664568298827e-2 + r2 * (-1.388731625493765e-3 + r2 * 2.443315711809948e-5))
    )
    quadrant = turns.astype(jnp.int32) & 3
    odd = (quadrant & 1) == 1
    sine = jnp.where(odd, c, s)
    cosine = jnp.where(odd, s, c)
    sine = jnp.where(quadrant >= 2, -sine, sine)
    cosine = jnp.where((quadrant == 1) | (quadrant == 2), -cosine, cosine)
    return sine, cosine


def tables_transposed(place):
    place = place.astype(F32)
    freq = frequency_rows(place.shape[1])
    pair = lax.broadcasted_iota(jnp.int32, freq.shape, 0)
    first = HEAD // 8
    second = first + 3 * HEAD // 16
    chosen = jnp.where(
        pair < first, place[0:1], jnp.where(pair < second, place[1:2], place[2:3])
    )
    sine, cosine = sine_cosine(chosen * freq)
    return cosine * YARN_MSCALE, sine * YARN_MSCALE


def row_tables(cosine_t, sine_t):
    wide = jnp.concatenate([cosine_t, cosine_t], axis=0).T
    signed = jnp.concatenate([-sine_t, sine_t], axis=0).T
    return wide, signed


def rotated(x, wide, signed):
    return x * wide + pltpu.roll(x, HALF, 1) * signed


def dot_nt(a, b):
    return lax.dot_general(a, b, (((1,), (1,)), ((), ())), preferred_element_type=F32)


def dot_nn(a, b):
    return lax.dot_general(a, b, (((1,), (0,)), ((), ())), preferred_element_type=F32)


def dot_tn(a, b):
    return lax.dot_general(a, b, (((0,), (0,)), ((), ())), preferred_element_type=F32)


def pair_part(key, value, query, grad, norm, delta, causal):
    scores = dot_nt(key, query)
    weights = jnp.exp2(scores * (ROOT_SCALE * LOG2E) - norm)
    if causal:
        at_key = lax.broadcasted_iota(jnp.int32, scores.shape, 0)
        at_query = lax.broadcasted_iota(jnp.int32, scores.shape, 1)
        weights = jnp.where(at_key <= at_query, weights, 0.0)
    value_part = dot_nn(weights.astype(BF16), grad)
    score_grad = (weights * (dot_nt(value, grad) - delta)).astype(BF16)
    key_part = dot_nn(score_grad, query)
    query_part = dot_tn(key, score_grad)
    return value_part, key_part, query_part


def key_kernel(own_ref, p1_ref, p2_ref, p3_ref, k_ref, kr_ref, tables_ref):
    pieces = (own_ref[...], p1_ref[...], p2_ref[...], p3_ref[...])
    count = len(pieces)
    head = lax.axis_index("head")
    parts = []
    for j in range(count):
        back = lax.rem(head - j + count, count)
        part = pieces[0]
        for r in range(1, count):
            part = jnp.where(back == r, pieces[r], part)
        parts.append(part)
    cosine_t, sine_t = tables_transposed(jnp.concatenate(parts, axis=1))
    tables_ref[:HALF, :] = cosine_t
    tables_ref[HALF:, :] = sine_t
    wide, signed = row_tables(cosine_t, sine_t)
    for g in range(k_ref.shape[1] // HEAD):
        cols = pl.ds(g * HEAD, HEAD)
        kr_ref[:, cols] = rotated(k_ref[:, cols].astype(F32), wide, signed).astype(BF16)


def prep_kernel(
    groups, span_ref, tables_ref, lse_hbm, q_hbm, do_hbm, at_hbm,
    qr_ref, do_ref, norm_ref, delta_ref, flag_ref, q_ref, at_ref, lse_ref, sems,
):
    heads = qr_ref.shape[1] // HEAD
    size = heads // groups
    copies = []
    for g in range(groups):
        cols = pl.ds(g * size * HEAD, size * HEAD)
        for i, (source, target) in enumerate(
            ((q_hbm, q_ref), (do_hbm, do_ref), (at_hbm, at_ref))
        ):
            copy = pltpu.make_async_copy(
                source.at[:, cols], target.at[:, cols], sems.at[3 * g + i]
            )
            copy.start()
            copies.append(copy)
    lse_copy = pltpu.make_async_copy(lse_hbm, lse_ref, sems.at[3 * groups])
    lse_copy.start()
    me = lax.axis_index("ctx")
    step_row = lax.broadcasted_iota(jnp.int32, flag_ref.shape, 0)
    flags = jnp.zeros(flag_ref.shape, jnp.int32)
    for step in range(1, WIN):
        other = lax.rem(me + step, span_ref.shape[0])
        earlier = jnp.where(span_ref[other] < span_ref[me], 1, 0)
        flags = jnp.where(step_row == step, earlier, flags)
    flag_ref[...] = flags
    wide, signed = row_tables(tables_ref[:HALF, :], tables_ref[HALF:, :])
    chooser = jnp.ones((8, HEAD), BF16)
    for h in range(heads):
        if h % size == 0:
            for copy in copies[3 * (h // size) : 3 * (h // size) + 3]:
                copy.wait()
        hc = pl.ds(h * HEAD, HEAD)
        qr_ref[:, hc] = rotated(q_ref[:, hc].astype(F32), wide, signed).astype(BF16)
        product = do_ref[:, hc].astype(F32) * at_ref[:, hc].astype(F32)
        high = product.astype(BF16)
        low = (product - high.astype(F32)).astype(BF16)
        delta_ref[h : h + 1, :] = (dot_nt(chooser, high) + dot_nt(chooser, low))[:1]
    lse_copy.wait()
    norm_ref[...] = lse_ref[...] * LOG2E


def hop_kernel(step, wanted, started, joined, *refs):
    count = len(wanted)
    if joined:
        *refs, part_ref = refs
        refs += [part_ref.at[:, 2 * HEAD * i : 2 * HEAD * (i + 1)] for i in range(count)]
    dqt_ins, dqt_refs, part_refs = refs[:count], refs[-2 * count : -count], refs[-count:]
    k_ref, v_ref, qr_ref, do_ref, norm_ref, delta_ref, flag_ref = refs[
        count * started : -2 * count
    ]
    rows = qr_ref.shape[0]
    half = rows // 2
    heads = qr_ref.shape[1] // HEAD
    groups = k_ref.shape[1] // HEAD
    size = heads // groups
    earlier = flag_ref[step, 0] == 1
    norm = norm_ref[...]
    delta = delta_ref[...]

    def run(keys, queries):
        for g, dqt_in, dqt_ref, part_ref in zip(wanted, dqt_ins, dqt_refs, part_refs):
            kc = pl.ds(g * HEAD, HEAD)
            dk = dv = None
            for j in range(size):
                h = g * size + j
                hc = pl.ds(h * HEAD, HEAD)
                to = pl.ds(j * HEAD, HEAD)
                v_part, k_part, q_part = pair_part(
                    k_ref[keys, kc], v_ref[keys, kc], qr_ref[queries, hc], do_ref[queries, hc],
                    norm[h : h + 1, queries.start :], delta[h : h + 1, queries.start :], False,
                )
                if queries.start:
                    zeros = jnp.zeros((HEAD, queries.start), F32)
                    dqt_ref[to, : queries.start] = (
                        dqt_in[to, : queries.start] if started else zeros
                    )
                dqt_ref[to, queries] = dqt_in[to, queries] + q_part if started else q_part
                dv = v_part if dv is None else dv + v_part
                dk = k_part if dk is None else dk + k_part
            part_ref[keys, :HEAD] = dk.astype(BF16)
            part_ref[keys, HEAD:] = dv.astype(BF16)
            if keys.stop < rows:
                part_ref[keys.stop :, :] = jnp.zeros((rows - keys.stop, 2 * HEAD), BF16)

    @pl.when(earlier)
    def _():
        run(slice(0, half), slice(0, rows))

    @pl.when(jnp.logical_not(earlier))
    def _():
        run(slice(0, rows), slice(half, rows))


def own_kernel(groups, k_ref, v_ref, qr_ref, do_ref, norm_ref, delta_ref, *refs):
    dqt_ins, dqt_refs, part_refs = refs[:groups], refs[groups : 2 * groups], refs[2 * groups :]
    size = qr_ref.shape[1] // HEAD // groups
    norm = norm_ref[...]
    delta = delta_ref[...]
    for g in range(groups):
        kc = pl.ds(g * HEAD, HEAD)
        dk = dv = None
        for j in range(size):
            h = g * size + j
            hc = pl.ds(h * HEAD, HEAD)
            to = pl.ds(j * HEAD, HEAD)
            v_part, k_part, q_part = pair_part(
                k_ref[:, kc], v_ref[:, kc], qr_ref[:, hc], do_ref[:, hc],
                norm[h : h + 1], delta[h : h + 1], True,
            )
            dqt_refs[g][to, :] = dqt_ins[g][to, :] + q_part
            dv = v_part if dv is None else dv + v_part
            dk = k_part if dk is None else dk + k_part
        part_refs[g][:, :HEAD] = dk
        part_refs[g][:, HEAD:] = dv


def query_kernel(groups, tables_ref, *refs):
    dqt_refs, own_refs = refs[:groups], refs[groups : 2 * groups]
    swapped_ref, out_ref, *sum_refs = refs[2 * groups :]
    odd = (lax.axis_index("ctx") & 1) == 1
    for g in range(groups):
        sum_refs[g][...] = own_refs[g][...] + jnp.where(
            odd, swapped_ref[:, 2 * HEAD * g : 2 * HEAD * (g + 1)].astype(F32), 0.0
        )
    cosine_t = tables_ref[:HALF, :] * ROOT_SCALE
    sine_t = tables_ref[HALF:, :] * ROOT_SCALE
    size = dqt_refs[0].shape[0] // HEAD
    for g in range(groups):
        for j in range(size):
            y1 = dqt_refs[g][pl.ds(j * HEAD, HALF), :]
            y2 = dqt_refs[g][pl.ds(j * HEAD + HALF, HALF), :]
            turned = jnp.concatenate(
                [y1 * cosine_t + y2 * sine_t, y2 * cosine_t - y1 * sine_t], axis=0
            )
            out_ref[:, pl.ds((g * size + j) * HEAD, HEAD)] = turned.T.astype(BF16)


def add_kernel(g, two_ref, swapped_ref, three_ref, sum_ref):
    even = (lax.axis_index("ctx") & 1) == 0
    total = two_ref[...].astype(F32) + three_ref[...].astype(F32)
    swapped = swapped_ref[:, 2 * HEAD * g : 2 * HEAD * (g + 1)].astype(F32)
    sum_ref[...] = (total + jnp.where(even, swapped, 0.0)).astype(BF16)


def final_kernel(groups, tables_ref, *refs):
    own_refs, home_refs, (dk_ref, dv_ref) = refs[:groups], refs[groups : 2 * groups], refs[-2:]
    wide, signed = row_tables(tables_ref[:HALF, :], tables_ref[HALF:, :])
    wide = wide * ROOT_SCALE
    signed = signed * -ROOT_SCALE
    for g in range(groups):
        cols = pl.ds(g * HEAD, HEAD)
        total = own_refs[g][...] + home_refs[g][...].astype(F32)
        dk_ref[:, cols] = rotated(total[:, :HEAD], wide, signed).astype(BF16)
        dv_ref[:, cols] = total[:, HEAD:].astype(BF16)


SMEM = pl.BlockSpec(memory_space=pltpu.SMEM)
VMEM = pl.BlockSpec(memory_space=pltpu.VMEM)
HBM = pl.BlockSpec(memory_space=pltpu.HBM)


def call(kernel, outs, specs, scratch=(), micros=1):
    return pl.pallas_call(
        kernel,
        out_shape=[jax.ShapeDtypeStruct(shape, dtype) for shape, dtype in outs],
        in_specs=specs,
        out_specs=[VMEM] * len(outs),
        scratch_shapes=list(scratch),
        compiler_params=pltpu.CompilerParams(vmem_limit_bytes=VMEM_LIMIT),
        cost_estimate=pl.CostEstimate(
            flops=1 << 20, bytes_accessed=micros * 3690000, transcendentals=0
        ),
    )


def shifted(value, steps, axis="ctx"):
    count = lax.axis_size(axis)
    pairs = [(source, (source + steps) % count) for source in range(count)]
    return lax.ppermute(value, axis, pairs)


def exchanged(value):
    count = lax.axis_size("ctx")
    return lax.ppermute(value, "ctx", [(source, source ^ 1) for source in range(count)])


def shards(q, k, v, do, at, lse, positions, span_map):
    rows = q.shape[0]
    wide_q = q.shape[1]
    wide_k = k.shape[1]
    heads = wide_q // HEAD
    q, do, at, k_here, v_here, lse, span_map, own = (
        pltpu.with_memory_space_constraint(x, pltpu.HBM)
        for x in (q, do, at, k, v, lse, span_map, positions)
    )

    pieces = [own] + [shifted(positions, r, "head") for r in (1, 2, 3)]
    groups = wide_k // HEAD
    every = tuple(range(groups))

    groups = wide_k // HEAD
    every = tuple(range(groups))

    v1 = shifted(v, -1)
    kr, tables = call(
        key_kernel, [((rows, wide_k), BF16), ((HEAD, rows), F32)], [VMEM] * 5
    )(*pieces, k_here)
    k1 = shifted(kr, -1)
    shared = call(
        functools.partial(prep_kernel, groups),
        [((rows, wide_q), BF16)] * 2 + [((heads, rows), F32)] * 2 + [((8, HEAD), jnp.int32)],
        [SMEM, VMEM] + [HBM] * 4,
        [
            pltpu.VMEM((rows, wide_q), BF16),
            pltpu.VMEM((rows, wide_q), BF16),
            pltpu.VMEM((heads, rows), F32),
            pltpu.SemaphoreType.DMA((3 * groups + 1,)),
        ],
        micros=2,
    )(span_map, tables, lse, q, do, at)
    v1, _ = lax.optimization_barrier((v1, shared[3]))
    v3 = shifted(v1, -2)
    k3 = shifted(k1, -2)
    dqs = []
    dq_out = ((wide_q // groups, rows), F32)
    part_out = ((rows, 2 * HEAD), BF16)

    def hop(step, wanted, key, value, joined=False):
        count = len(wanted)
        started = len(dqs) > 0
        before = [dqs[g] for g in wanted] if started else []
        results = call(
            functools.partial(hop_kernel, step, wanted, started, joined),
            [dq_out] * count
            + ([((rows, 2 * HEAD * count), BF16)] if joined else [part_out] * count),
            [VMEM] * (7 + len(before)),
            micros=count,
        )(*before, key, value, *shared)
        if not started:
            dqs.extend(results[:count])
        for i, g in enumerate(wanted):
            dqs[g] = results[i]
        return results[count:]

    (part1,) = hop(1, every, k1, v1, joined=True)
    swapped = exchanged(part1)
    kr2, v_far, _ = lax.optimization_barrier((kr, v, part1))
    k2 = shifted(kr2, -2)
    v2 = shifted(v_far, -2)
    moved = [shifted(*hop(3, (g,), k3, v3), 1) for g in every]
    parts2 = hop(2, every, k2, v2)
    results = call(
        functools.partial(own_kernel, groups),
        [dq_out] * groups + [((rows, 2 * HEAD), F32)] * groups,
        [VMEM] * (6 + groups),
        micros=3,
    )(kr, v_here, *shared[:4], *dqs)
    dqs, owns = list(results[:groups]), results[groups:]
    dq, *owns = call(
        functools.partial(query_kernel, groups),
        [((rows, wide_q), BF16)] + [((rows, 2 * HEAD), F32)] * groups,
        [VMEM] * (2 + 2 * groups),
    )(tables, *dqs, *owns, swapped)
    home = []
    for g in every:
        (total,) = call(functools.partial(add_kernel, g), [part_out], [VMEM] * 3)(
            parts2[g], swapped, moved[g]
        )
        home.append(shifted(total, 2))

    dk, dv = call(
        functools.partial(final_kernel, groups),
        [((rows, wide_k), BF16), ((rows, wide_k), BF16)],
        [VMEM] * (1 + 2 * groups),
    )(tables, *owns, *home)
    return dq, dk, dv


def solution(mesh):
    placed = (
        P("ctx", "head"),
        P("ctx", "head"),
        P("ctx", "head"),
        P("ctx", "head"),
        P("ctx", "head"),
        P("head", "ctx"),
        P(None, ("ctx", "head")),
        P(),
    )
    return jax.shard_map(
        shards,
        mesh=mesh,
        in_specs=placed,
        out_specs=(P("ctx", "head"), P("ctx", "head"), P("ctx", "head")),
        check_vma=False,
    )
```

```python
import functools
import math

import jax
import jax.numpy as jnp
import numpy as np
from jax import lax
from jax.experimental import pallas as pl
from jax.experimental.pallas import tpu as pltpu
from jax.sharding import PartitionSpec as P

HEAD = 128
HALF = HEAD // 2
WIN = 4
ROPE_BASE = 1000000.0
YARN_FACTOR = 4.0
YARN_INITIAL = 32768.0
BETA_FAST = 32.0
BETA_SLOW = 1.0
YARN_MSCALE = 1.0 + 0.1 * math.log(4.0)
ROOT_SCALE = 1.0 / math.sqrt(HEAD)
LOG2E = math.log2(math.e)
VMEM_LIMIT = 24 * 1024 * 1024

F32 = jnp.float32
BF16 = jnp.bfloat16


def frequencies():
    pair = np.arange(HALF, dtype=np.float64)
    inverse = np.exp(-2.0 * pair / HEAD * math.log(ROPE_BASE))
    ratio = YARN_INITIAL * inverse / (2.0 * math.pi)
    ramp = np.clip((ratio - BETA_SLOW) / (BETA_FAST - BETA_SLOW), 0.0, 1.0)
    return inverse * ((1.0 - ramp) / YARN_FACTOR + ramp)


def frequency_rows(lanes):
    values = frequencies()
    row = lax.broadcasted_iota(jnp.int32, (8, lanes), 0)
    tiles = []
    for first in range(0, HALF, 8):
        tile = jnp.full((8, lanes), float(values[first]), F32)
        for j in range(1, 8):
            tile = jnp.where(row == j, float(values[first + j]), tile)
        tiles.append(tile)
    return jnp.concatenate(tiles, axis=0)


def sine_cosine(angle):
    turns = jnp.floor(angle * (2.0 / math.pi) + 0.5)
    r = angle - turns * 1.5703125
    r = r - turns * 4.837512969970703125e-4
    r = r - turns * 7.54978995489188e-8
    r2 = r * r
    s = r + r * r2 * (-1.6666654611e-1 + r2 * (8.3321608736e-3 - r2 * 1.9515295891e-4))
    c = (
        1.0
        - 0.5 * r2
        + r2
        * r2
        * (4.166664568298827e-2 + r2 * (-1.388731625493765e-3 + r2 * 2.443315711809948e-5))
    )
    quadrant = turns.astype(jnp.int32) & 3
    odd = (quadrant & 1) == 1
    sine = jnp.where(odd, c, s)
    cosine = jnp.where(odd, s, c)
    sine = jnp.where(quadrant >= 2, -sine, sine)
    cosine = jnp.where((quadrant == 1) | (quadrant == 2), -cosine, cosine)
    return sine, cosine


def tables_transposed(place):
    place = place.astype(F32)
    freq = frequency_rows(place.shape[1])
    pair = lax.broadcasted_iota(jnp.int32, freq.shape, 0)
    first = HEAD // 8
    second = first + 3 * HEAD // 16
    chosen = jnp.where(
        pair < first, place[0:1], jnp.where(pair < second, place[1:2], place[2:3])
    )
    sine, cosine = sine_cosine(chosen * freq)
    return cosine * YARN_MSCALE, sine * YARN_MSCALE


def row_tables(cosine_t, sine_t):
    wide = jnp.concatenate([cosine_t, cosine_t], axis=0).T
    signed = jnp.concatenate([-sine_t, sine_t], axis=0).T
    return wide, signed


def rotated(x, wide, signed):
    return x * wide + pltpu.roll(x, HALF, 1) * signed


def dot_nt(a, b):
    return lax.dot_general(a, b, (((1,), (1,)), ((), ())), preferred_element_type=F32)


def dot_nn(a, b):
    return lax.dot_general(a, b, (((1,), (0,)), ((), ())), preferred_element_type=F32)


def dot_tn(a, b):
    return lax.dot_general(a, b, (((0,), (0,)), ((), ())), preferred_element_type=F32)


def pair_part(key, value, query, grad, norm, delta, causal):
    scores = dot_nt(key, query)
    weights = jnp.exp2(scores * (ROOT_SCALE * LOG2E) - norm)
    if causal:
        at_key = lax.broadcasted_iota(jnp.int32, scores.shape, 0)
        at_query = lax.broadcasted_iota(jnp.int32, scores.shape, 1)
        weights = jnp.where(at_key <= at_query, weights, 0.0)
    value_part = dot_nn(weights.astype(BF16), grad)
    score_grad = (weights * (dot_nt(value, grad) - delta)).astype(BF16)
    key_part = dot_nn(score_grad, query)
    query_part = dot_tn(key, score_grad)
    return value_part, key_part, query_part


def key_kernel(own_ref, p1_ref, p2_ref, p3_ref, k_ref, kr_ref, tables_ref):
    pieces = (own_ref[...], p1_ref[...], p2_ref[...], p3_ref[...])
    count = len(pieces)
    head = lax.axis_index("head")
    parts = []
    for j in range(count):
        back = lax.rem(head - j + count, count)
        part = pieces[0]
        for r in range(1, count):
            part = jnp.where(back == r, pieces[r], part)
        parts.append(part)
    cosine_t, sine_t = tables_transposed(jnp.concatenate(parts, axis=1))
    tables_ref[:HALF, :] = cosine_t
    tables_ref[HALF:, :] = sine_t
    wide, signed = row_tables(cosine_t, sine_t)
    for g in range(k_ref.shape[1] // HEAD):
        cols = pl.ds(g * HEAD, HEAD)
        kr_ref[:, cols] = rotated(k_ref[:, cols].astype(F32), wide, signed).astype(BF16)


def prep_kernel(
    groups, span_ref, tables_ref, lse_hbm, q_hbm, do_hbm, at_hbm,
    qr_ref, do_ref, norm_ref, delta_ref, flag_ref, q_ref, at_ref, lse_ref, sems,
):
    heads = qr_ref.shape[1] // HEAD
    size = heads // groups
    copies = []
    for g in range(groups):
        cols = pl.ds(g * size * HEAD, size * HEAD)
        for i, (source, target) in enumerate(
            ((q_hbm, q_ref), (do_hbm, do_ref), (at_hbm, at_ref))
        ):
            copy = pltpu.make_async_copy(
                source.at[:, cols], target.at[:, cols], sems.at[3 * g + i]
            )
            copy.start()
            copies.append(copy)
    lse_copy = pltpu.make_async_copy(lse_hbm, lse_ref, sems.at[3 * groups])
    lse_copy.start()
    me = lax.axis_index("ctx")
    step_row = lax.broadcasted_iota(jnp.int32, flag_ref.shape, 0)
    flags = jnp.zeros(flag_ref.shape, jnp.int32)
    for step in range(1, WIN):
        other = lax.rem(me + step, span_ref.shape[0])
        earlier = jnp.where(span_ref[other] < span_ref[me], 1, 0)
        flags = jnp.where(step_row == step, earlier, flags)
    flag_ref[...] = flags
    wide, signed = row_tables(tables_ref[:HALF, :], tables_ref[HALF:, :])
    chooser = jnp.ones((8, HEAD), BF16)
    for h in range(heads):
        if h % size == 0:
            for copy in copies[3 * (h // size) : 3 * (h // size) + 3]:
                copy.wait()
        hc = pl.ds(h * HEAD, HEAD)
        qr_ref[:, hc] = rotated(q_ref[:, hc].astype(F32), wide, signed).astype(BF16)
        product = do_ref[:, hc].astype(F32) * at_ref[:, hc].astype(F32)
        high = product.astype(BF16)
        low = (product - high.astype(F32)).astype(BF16)
        delta_ref[h : h + 1, :] = (dot_nt(chooser, high) + dot_nt(chooser, low))[:1]
    lse_copy.wait()
    norm_ref[...] = lse_ref[...] * LOG2E


def hop_kernel(step, wanted, started, joined, *refs):
    count = len(wanted)
    if joined:
        *refs, part_ref = refs
        refs += [part_ref.at[:, 2 * HEAD * i : 2 * HEAD * (i + 1)] for i in range(count)]
    dqt_ins, dqt_refs, part_refs = refs[:count], refs[-2 * count : -count], refs[-count:]
    k_ref, v_ref, qr_ref, do_ref, norm_ref, delta_ref, flag_ref = refs[
        count * started : -2 * count
    ]
    rows = qr_ref.shape[0]
    half = rows // 2
    heads = qr_ref.shape[1] // HEAD
    groups = k_ref.shape[1] // HEAD
    size = heads // groups
    earlier = flag_ref[step, 0] == 1
    norm = norm_ref[...]
    delta = delta_ref[...]

    def run(keys, queries):
        for g, dqt_in, dqt_ref, part_ref in zip(wanted, dqt_ins, dqt_refs, part_refs):
            kc = pl.ds(g * HEAD, HEAD)
            dk = dv = None
            for j in range(size):
                h = g * size + j
                hc = pl.ds(h * HEAD, HEAD)
                to = pl.ds(j * HEAD, HEAD)
                v_part, k_part, q_part = pair_part(
                    k_ref[keys, kc], v_ref[keys, kc], qr_ref[queries, hc], do_ref[queries, hc],
                    norm[h : h + 1, queries.start :], delta[h : h + 1, queries.start :], False,
                )
                if queries.start:
                    zeros = jnp.zeros((HEAD, queries.start), F32)
                    dqt_ref[to, : queries.start] = (
                        dqt_in[to, : queries.start] if started else zeros
                    )
                dqt_ref[to, queries] = dqt_in[to, queries] + q_part if started else q_part
                dv = v_part if dv is None else dv + v_part
                dk = k_part if dk is None else dk + k_part
            part_ref[keys, :HEAD] = dk.astype(BF16)
            part_ref[keys, HEAD:] = dv.astype(BF16)
            if keys.stop < rows:
                part_ref[keys.stop :, :] = jnp.zeros((rows - keys.stop, 2 * HEAD), BF16)

    @pl.when(earlier)
    def _():
        run(slice(0, half), slice(0, rows))

    @pl.when(jnp.logical_not(earlier))
    def _():
        run(slice(0, rows), slice(half, rows))


def own_kernel(groups, k_ref, v_ref, qr_ref, do_ref, norm_ref, delta_ref, *refs):
    dqt_ins, dqt_refs, part_refs = refs[:groups], refs[groups : 2 * groups], refs[2 * groups :]
    size = qr_ref.shape[1] // HEAD // groups
    norm = norm_ref[...]
    delta = delta_ref[...]
    for g in range(groups):
        kc = pl.ds(g * HEAD, HEAD)
        dk = dv = None
        for j in range(size):
            h = g * size + j
            hc = pl.ds(h * HEAD, HEAD)
            to = pl.ds(j * HEAD, HEAD)
            v_part, k_part, q_part = pair_part(
                k_ref[:, kc], v_ref[:, kc], qr_ref[:, hc], do_ref[:, hc],
                norm[h : h + 1], delta[h : h + 1], True,
            )
            dqt_refs[g][to, :] = dqt_ins[g][to, :] + q_part
            dv = v_part if dv is None else dv + v_part
            dk = k_part if dk is None else dk + k_part
        part_refs[g][:, :HEAD] = dk
        part_refs[g][:, HEAD:] = dv


def query_kernel(groups, tables_ref, *refs):
    dqt_refs, own_refs = refs[:groups], refs[groups : 2 * groups]
    swapped_ref, out_ref, *sum_refs = refs[2 * groups :]
    odd = (lax.axis_index("ctx") & 1) == 1
    for g in range(groups):
        sum_refs[g][...] = own_refs[g][...] + jnp.where(
            odd, swapped_ref[:, 2 * HEAD * g : 2 * HEAD * (g + 1)].astype(F32), 0.0
        )
    cosine_t = tables_ref[:HALF, :] * ROOT_SCALE
    sine_t = tables_ref[HALF:, :] * ROOT_SCALE
    size = dqt_refs[0].shape[0] // HEAD
    for g in range(groups):
        for j in range(size):
            y1 = dqt_refs[g][pl.ds(j * HEAD, HALF), :]
            y2 = dqt_refs[g][pl.ds(j * HEAD + HALF, HALF), :]
            turned = jnp.concatenate(
                [y1 * cosine_t + y2 * sine_t, y2 * cosine_t - y1 * sine_t], axis=0
            )
            out_ref[:, pl.ds((g * size + j) * HEAD, HEAD)] = turned.T.astype(BF16)


def add_kernel(g, two_ref, swapped_ref, three_ref, sum_ref):
    even = (lax.axis_index("ctx") & 1) == 0
    total = two_ref[...].astype(F32) + three_ref[...].astype(F32)
    swapped = swapped_ref[:, 2 * HEAD * g : 2 * HEAD * (g + 1)].astype(F32)
    sum_ref[...] = (total + jnp.where(even, swapped, 0.0)).astype(BF16)


def final_kernel(groups, tables_ref, *refs):
    own_refs, home_refs, (dk_ref, dv_ref) = refs[:groups], refs[groups : 2 * groups], refs[-2:]
    wide, signed = row_tables(tables_ref[:HALF, :], tables_ref[HALF:, :])
    wide = wide * ROOT_SCALE
    signed = signed * -ROOT_SCALE
    for g in range(groups):
        cols = pl.ds(g * HEAD, HEAD)
        total = own_refs[g][...] + home_refs[g][...].astype(F32)
        dk_ref[:, cols] = rotated(total[:, :HEAD], wide, signed).astype(BF16)
        dv_ref[:, cols] = total[:, HEAD:].astype(BF16)


SMEM = pl.BlockSpec(memory_space=pltpu.SMEM)
VMEM = pl.BlockSpec(memory_space=pltpu.VMEM)
HBM = pl.BlockSpec(memory_space=pltpu.HBM)


def call(kernel, outs, specs, scratch=(), micros=1):
    return pl.pallas_call(
        kernel,
        out_shape=[jax.ShapeDtypeStruct(shape, dtype) for shape, dtype in outs],
        in_specs=specs,
        out_specs=[VMEM] * len(outs),
        scratch_shapes=list(scratch),
        compiler_params=pltpu.CompilerParams(vmem_limit_bytes=VMEM_LIMIT),
        cost_estimate=pl.CostEstimate(
            flops=1 << 20, bytes_accessed=micros * 3690000, transcendentals=0
        ),
    )


def shifted(value, steps, axis="ctx"):
    count = lax.axis_size(axis)
    pairs = [(source, (source + steps) % count) for source in range(count)]
    return lax.ppermute(value, axis, pairs)


def exchanged(value):
    count = lax.axis_size("ctx")
    return lax.ppermute(value, "ctx", [(source, source ^ 1) for source in range(count)])


def shards(q, k, v, do, at, lse, positions, span_map):
    rows = q.shape[0]
    wide_q = q.shape[1]
    wide_k = k.shape[1]
    heads = wide_q // HEAD
    q, do, at, k_here, v_here, lse, span_map, own = (
        pltpu.with_memory_space_constraint(x, pltpu.HBM)
        for x in (q, do, at, k, v, lse, span_map, positions)
    )

    pieces = [own] + [shifted(positions, r, "head") for r in (1, 2, 3)]
    groups = wide_k // HEAD
    every = tuple(range(groups))

    groups = wide_k // HEAD
    every = tuple(range(groups))

    v1 = shifted(v, -1)
    kr, tables = call(
        key_kernel, [((rows, wide_k), BF16), ((HEAD, rows), F32)], [VMEM] * 5
    )(*pieces, k_here)
    k1 = shifted(kr, -1)
    shared = call(
        functools.partial(prep_kernel, groups),
        [((rows, wide_q), BF16)] * 2 + [((heads, rows), F32)] * 2 + [((8, HEAD), jnp.int32)],
        [SMEM, VMEM] + [HBM] * 4,
        [
            pltpu.VMEM((rows, wide_q), BF16),
            pltpu.VMEM((rows, wide_q), BF16),
            pltpu.VMEM((heads, rows), F32),
            pltpu.SemaphoreType.DMA((3 * groups + 1,)),
        ],
        micros=2,
    )(span_map, tables, lse, q, do, at)
    v1, _ = lax.optimization_barrier((v1, shared[3]))
    v3 = shifted(v1, -2)
    k3 = shifted(kr, -3)
    dqs = []
    dq_out = ((wide_q // groups, rows), F32)
    part_out = ((rows, 2 * HEAD), BF16)

    def hop(step, wanted, key, value, joined=False):
        count = len(wanted)
        started = len(dqs) > 0
        before = [dqs[g] for g in wanted] if started else []
        results = call(
            functools.partial(hop_kernel, step, wanted, started, joined),
            [dq_out] * count
            + ([((rows, 2 * HEAD * count), BF16)] if joined else [part_out] * count),
            [VMEM] * (7 + len(before)),
            micros=count,
        )(*before, key, value, *shared)
        if not started:
            dqs.extend(results[:count])
        for i, g in enumerate(wanted):
            dqs[g] = results[i]
        return results[count:]

    (part1,) = hop(1, every, k1, v1, joined=True)
    swapped = exchanged(part1)
    kr2, v_far, _ = lax.optimization_barrier((kr, v, part1))
    k2 = shifted(kr2, -2)
    v2 = shifted(v_far, -2)
    moved = [shifted(*hop(3, (g,), k3, v3), 1) for g in every]
    parts2 = hop(2, every, k2, v2)
    results = call(
        functools.partial(own_kernel, groups),
        [dq_out] * groups + [((rows, 2 * HEAD), F32)] * groups,
        [VMEM] * (6 + groups),
        micros=3,
    )(kr, v_here, *shared[:4], *dqs)
    dqs, owns = list(results[:groups]), results[groups:]
    dq, *owns = call(
        functools.partial(query_kernel, groups),
        [((rows, wide_q), BF16)] + [((rows, 2 * HEAD), F32)] * groups,
        [VMEM] * (2 + 2 * groups),
    )(tables, *dqs, *owns, swapped)
    home = []
    for g in every:
        (total,) = call(functools.partial(add_kernel, g), [part_out], [VMEM] * 3)(
            parts2[g], swapped, moved[g]
        )
        home.append(shifted(total, 2))

    dk, dv = call(
        functools.partial(final_kernel, groups),
        [((rows, wide_k), BF16), ((rows, wide_k), BF16)],
        [VMEM] * (1 + 2 * groups),
    )(tables, *owns, *home)
    return dq, dk, dv


def solution(mesh):
    placed = (
        P("ctx", "head"),
        P("ctx", "head"),
        P("ctx", "head"),
        P("ctx", "head"),
        P("ctx", "head"),
        P("head", "ctx"),
        P(None, ("ctx", "head")),
        P(),
    )
    return jax.shard_map(
        shards,
        mesh=mesh,
        in_specs=placed,
        out_specs=(P("ctx", "head"), P("ctx", "head"), P("ctx", "head")),
        check_vma=False,
    )
```

```python
import functools
import math

import jax
import jax.numpy as jnp
import numpy as np
from jax import lax
from jax.experimental import pallas as pl
from jax.experimental.pallas import tpu as pltpu
from jax.sharding import PartitionSpec as P

HEAD = 128
HALF = HEAD // 2
WIN = 4
ROPE_BASE = 1000000.0
YARN_FACTOR = 4.0
YARN_INITIAL = 32768.0
BETA_FAST = 32.0
BETA_SLOW = 1.0
YARN_MSCALE = 1.0 + 0.1 * math.log(4.0)
ROOT_SCALE = 1.0 / math.sqrt(HEAD)
LOG2E = math.log2(math.e)
VMEM_LIMIT = 24 * 1024 * 1024

F32 = jnp.float32
BF16 = jnp.bfloat16


def frequencies():
    pair = np.arange(HALF, dtype=np.float64)
    inverse = np.exp(-2.0 * pair / HEAD * math.log(ROPE_BASE))
    ratio = YARN_INITIAL * inverse / (2.0 * math.pi)
    ramp = np.clip((ratio - BETA_SLOW) / (BETA_FAST - BETA_SLOW), 0.0, 1.0)
    return inverse * ((1.0 - ramp) / YARN_FACTOR + ramp)


def frequency_rows(lanes):
    values = frequencies()
    row = lax.broadcasted_iota(jnp.int32, (8, lanes), 0)
    tiles = []
    for first in range(0, HALF, 8):
        tile = jnp.full((8, lanes), float(values[first]), F32)
        for j in range(1, 8):
            tile = jnp.where(row == j, float(values[first + j]), tile)
        tiles.append(tile)
    return jnp.concatenate(tiles, axis=0)


def sine_cosine(angle):
    turns = jnp.floor(angle * (2.0 / math.pi) + 0.5)
    r = angle - turns * 1.5703125
    r = r - turns * 4.837512969970703125e-4
    r = r - turns * 7.54978995489188e-8
    r2 = r * r
    s = r + r * r2 * (-1.6666654611e-1 + r2 * (8.3321608736e-3 - r2 * 1.9515295891e-4))
    c = (
        1.0
        - 0.5 * r2
        + r2
        * r2
        * (4.166664568298827e-2 + r2 * (-1.388731625493765e-3 + r2 * 2.443315711809948e-5))
    )
    quadrant = turns.astype(jnp.int32) & 3
    odd = (quadrant & 1) == 1
    sine = jnp.where(odd, c, s)
    cosine = jnp.where(odd, s, c)
    sine = jnp.where(quadrant >= 2, -sine, sine)
    cosine = jnp.where((quadrant == 1) | (quadrant == 2), -cosine, cosine)
    return sine, cosine


def tables_transposed(place):
    place = place.astype(F32)
    freq = frequency_rows(place.shape[1])
    pair = lax.broadcasted_iota(jnp.int32, freq.shape, 0)
    first = HEAD // 8
    second = first + 3 * HEAD // 16
    chosen = jnp.where(
        pair < first, place[0:1], jnp.where(pair < second, place[1:2], place[2:3])
    )
    sine, cosine = sine_cosine(chosen * freq)
    return cosine * YARN_MSCALE, sine * YARN_MSCALE


def row_tables(cosine_t, sine_t):
    wide = jnp.concatenate([cosine_t, cosine_t], axis=0).T
    signed = jnp.concatenate([-sine_t, sine_t], axis=0).T
    return wide, signed


def rotated(x, wide, signed):
    return x * wide + pltpu.roll(x, HALF, 1) * signed


def dot_nt(a, b):
    return lax.dot_general(a, b, (((1,), (1,)), ((), ())), preferred_element_type=F32)


def dot_nn(a, b):
    return lax.dot_general(a, b, (((1,), (0,)), ((), ())), preferred_element_type=F32)


def dot_tn(a, b):
    return lax.dot_general(a, b, (((0,), (0,)), ((), ())), preferred_element_type=F32)


def pair_part(key, value, query, grad, norm, delta, causal):
    scores = dot_nt(key, query)
    weights = jnp.exp2(scores * (ROOT_SCALE * LOG2E) - norm)
    if causal:
        at_key = lax.broadcasted_iota(jnp.int32, scores.shape, 0)
        at_query = lax.broadcasted_iota(jnp.int32, scores.shape, 1)
        weights = jnp.where(at_key <= at_query, weights, 0.0)
    value_part = dot_nn(weights.astype(BF16), grad)
    score_grad = (weights * (dot_nt(value, grad) - delta)).astype(BF16)
    key_part = dot_nn(score_grad, query)
    query_part = dot_tn(key, score_grad)
    return value_part, key_part, query_part


def key_kernel(own_ref, p1_ref, p2_ref, p3_ref, k_ref, kr_ref, tables_ref):
    pieces = (own_ref[...], p1_ref[...], p2_ref[...], p3_ref[...])
    count = len(pieces)
    head = lax.axis_index("head")
    parts = []
    for j in range(count):
        back = lax.rem(head - j + count, count)
        part = pieces[0]
        for r in range(1, count):
            part = jnp.where(back == r, pieces[r], part)
        parts.append(part)
    cosine_t, sine_t = tables_transposed(jnp.concatenate(parts, axis=1))
    tables_ref[:HALF, :] = cosine_t
    tables_ref[HALF:, :] = sine_t
    wide, signed = row_tables(cosine_t, sine_t)
    for g in range(k_ref.shape[1] // HEAD):
        cols = pl.ds(g * HEAD, HEAD)
        kr_ref[:, cols] = rotated(k_ref[:, cols].astype(F32), wide, signed).astype(BF16)


def prep_kernel(
    groups, span_ref, tables_ref, lse_hbm, q_hbm, do_hbm, at_hbm,
    qr_ref, do_ref, norm_ref, delta_ref, flag_ref, q_ref, at_ref, lse_ref, sems,
):
    heads = qr_ref.shape[1] // HEAD
    size = heads // groups
    copies = []
    for g in range(groups):
        cols = pl.ds(g * size * HEAD, size * HEAD)
        for i, (source, target) in enumerate(
            ((q_hbm, q_ref), (do_hbm, do_ref), (at_hbm, at_ref))
        ):
            copy = pltpu.make_async_copy(
                source.at[:, cols], target.at[:, cols], sems.at[3 * g + i]
            )
            copy.start()
            copies.append(copy)
    lse_copy = pltpu.make_async_copy(lse_hbm, lse_ref, sems.at[3 * groups])
    lse_copy.start()
    me = lax.axis_index("ctx")
    step_row = lax.broadcasted_iota(jnp.int32, flag_ref.shape, 0)
    flags = jnp.zeros(flag_ref.shape, jnp.int32)
    for step in range(1, WIN):
        other = lax.rem(me + step, span_ref.shape[0])
        earlier = jnp.where(span_ref[other] < span_ref[me], 1, 0)
        flags = jnp.where(step_row == step, earlier, flags)
    flag_ref[...] = flags
    wide, signed = row_tables(tables_ref[:HALF, :], tables_ref[HALF:, :])
    chooser = jnp.ones((8, HEAD), BF16)
    for h in range(heads):
        if h % size == 0:
            for copy in copies[3 * (h // size) : 3 * (h // size) + 3]:
                copy.wait()
        hc = pl.ds(h * HEAD, HEAD)
        qr_ref[:, hc] = rotated(q_ref[:, hc].astype(F32), wide, signed).astype(BF16)
        product = do_ref[:, hc].astype(F32) * at_ref[:, hc].astype(F32)
        high = product.astype(BF16)
        low = (product - high.astype(F32)).astype(BF16)
        delta_ref[h : h + 1, :] = (dot_nt(chooser, high) + dot_nt(chooser, low))[:1]
    lse_copy.wait()
    norm_ref[...] = lse_ref[...] * LOG2E


def hop_kernel(step, wanted, started, joined, *refs):
    count = len(wanted)
    if joined:
        *refs, part_ref = refs
        refs += [part_ref.at[:, 2 * HEAD * i : 2 * HEAD * (i + 1)] for i in range(count)]
    dqt_ins, dqt_refs, part_refs = refs[:count], refs[-2 * count : -count], refs[-count:]
    k_ref, v_ref, qr_ref, do_ref, norm_ref, delta_ref, flag_ref = refs[
        count * started : -2 * count
    ]
    rows = qr_ref.shape[0]
    half = rows // 2
    heads = qr_ref.shape[1] // HEAD
    groups = k_ref.shape[1] // HEAD
    size = heads // groups
    earlier = flag_ref[step, 0] == 1
    norm = norm_ref[...]
    delta = delta_ref[...]

    def run(keys, queries):
        for g, dqt_in, dqt_ref, part_ref in zip(wanted, dqt_ins, dqt_refs, part_refs):
            kc = pl.ds(g * HEAD, HEAD)
            dk = dv = None
            for j in range(size):
                h = g * size + j
                hc = pl.ds(h * HEAD, HEAD)
                to = pl.ds(j * HEAD, HEAD)
                v_part, k_part, q_part = pair_part(
                    k_ref[keys, kc], v_ref[keys, kc], qr_ref[queries, hc], do_ref[queries, hc],
                    norm[h : h + 1, queries.start :], delta[h : h + 1, queries.start :], False,
                )
                if queries.start:
                    zeros = jnp.zeros((HEAD, queries.start), F32)
                    dqt_ref[to, : queries.start] = (
                        dqt_in[to, : queries.start] if started else zeros
                    )
                dqt_ref[to, queries] = dqt_in[to, queries] + q_part if started else q_part
                dv = v_part if dv is None else dv + v_part
                dk = k_part if dk is None else dk + k_part
            part_ref[keys, :HEAD] = dk.astype(BF16)
            part_ref[keys, HEAD:] = dv.astype(BF16)
            if keys.stop < rows:
                part_ref[keys.stop :, :] = jnp.zeros((rows - keys.stop, 2 * HEAD), BF16)

    @pl.when(earlier)
    def _():
        run(slice(0, half), slice(0, rows))

    @pl.when(jnp.logical_not(earlier))
    def _():
        run(slice(0, rows), slice(half, rows))


def own_kernel(groups, k_ref, v_ref, qr_ref, do_ref, norm_ref, delta_ref, *refs):
    dqt_ins, dqt_refs, part_refs = refs[:groups], refs[groups : 2 * groups], refs[2 * groups :]
    size = qr_ref.shape[1] // HEAD // groups
    norm = norm_ref[...]
    delta = delta_ref[...]
    for g in range(groups):
        kc = pl.ds(g * HEAD, HEAD)
        dk = dv = None
        for j in range(size):
            h = g * size + j
            hc = pl.ds(h * HEAD, HEAD)
            to = pl.ds(j * HEAD, HEAD)
            v_part, k_part, q_part = pair_part(
                k_ref[:, kc], v_ref[:, kc], qr_ref[:, hc], do_ref[:, hc],
                norm[h : h + 1], delta[h : h + 1], True,
            )
            dqt_refs[g][to, :] = dqt_ins[g][to, :] + q_part
            dv = v_part if dv is None else dv + v_part
            dk = k_part if dk is None else dk + k_part
        part_refs[g][:, :HEAD] = dk
        part_refs[g][:, HEAD:] = dv


def query_kernel(groups, tables_ref, *refs):
    dqt_refs, own_refs = refs[:groups], refs[groups : 2 * groups]
    back_refs, (out_ref, *sum_refs) = refs[2 * groups : 3 * groups], refs[3 * groups :]
    for g in range(groups):
        sum_refs[g][...] = own_refs[g][...] + back_refs[g][...].astype(F32)
    cosine_t = tables_ref[:HALF, :] * ROOT_SCALE
    sine_t = tables_ref[HALF:, :] * ROOT_SCALE
    size = dqt_refs[0].shape[0] // HEAD
    for g in range(groups):
        for j in range(size):
            y1 = dqt_refs[g][pl.ds(j * HEAD, HALF), :]
            y2 = dqt_refs[g][pl.ds(j * HEAD + HALF, HALF), :]
            turned = jnp.concatenate(
                [y1 * cosine_t + y2 * sine_t, y2 * cosine_t - y1 * sine_t], axis=0
            )
            out_ref[:, pl.ds((g * size + j) * HEAD, HEAD)] = turned.T.astype(BF16)


def add_kernel(a_ref, b_ref, sum_ref):
    sum_ref[...] = (a_ref[...].astype(F32) + b_ref[...].astype(F32)).astype(BF16)


def final_kernel(groups, tables_ref, *refs):
    own_refs, home_refs, (dk_ref, dv_ref) = refs[:groups], refs[groups : 2 * groups], refs[-2:]
    wide, signed = row_tables(tables_ref[:HALF, :], tables_ref[HALF:, :])
    wide = wide * ROOT_SCALE
    signed = signed * -ROOT_SCALE
    for g in range(groups):
        cols = pl.ds(g * HEAD, HEAD)
        total = own_refs[g][...] + home_refs[g][...].astype(F32)
        dk_ref[:, cols] = rotated(total[:, :HEAD], wide, signed).astype(BF16)
        dv_ref[:, cols] = total[:, HEAD:].astype(BF16)


SMEM = pl.BlockSpec(memory_space=pltpu.SMEM)
VMEM = pl.BlockSpec(memory_space=pltpu.VMEM)
HBM = pl.BlockSpec(memory_space=pltpu.HBM)


def call(kernel, outs, specs, scratch=(), micros=1):
    return pl.pallas_call(
        kernel,
        out_shape=[jax.ShapeDtypeStruct(shape, dtype) for shape, dtype in outs],
        in_specs=specs,
        out_specs=[VMEM] * len(outs),
        scratch_shapes=list(scratch),
        compiler_params=pltpu.CompilerParams(vmem_limit_bytes=VMEM_LIMIT),
        cost_estimate=pl.CostEstimate(
            flops=1 << 20, bytes_accessed=micros * 3690000, transcendentals=0
        ),
    )


def shifted(value, steps, axis="ctx"):
    count = lax.axis_size(axis)
    pairs = [(source, (source + steps) % count) for source in range(count)]
    return lax.ppermute(value, axis, pairs)


def shards(q, k, v, do, at, lse, positions, span_map):
    rows = q.shape[0]
    wide_q = q.shape[1]
    wide_k = k.shape[1]
    heads = wide_q // HEAD
    q, do, at, k_here, v_here, lse, span_map, own = (
        pltpu.with_memory_space_constraint(x, pltpu.HBM)
        for x in (q, do, at, k, v, lse, span_map, positions)
    )

    pieces = [own] + [shifted(positions, r, "head") for r in (1, 2, 3)]
    groups = wide_k // HEAD
    every = tuple(range(groups))

    groups = wide_k // HEAD
    every = tuple(range(groups))

    v1 = shifted(v, -1)
    kr, tables = call(
        key_kernel, [((rows, wide_k), BF16), ((HEAD, rows), F32)], [VMEM] * 5
    )(*pieces, k_here)
    k1 = shifted(kr, -1)
    shared = call(
        functools.partial(prep_kernel, groups),
        [((rows, wide_q), BF16)] * 2 + [((heads, rows), F32)] * 2 + [((8, HEAD), jnp.int32)],
        [SMEM, VMEM] + [HBM] * 4,
        [
            pltpu.VMEM((rows, wide_q), BF16),
            pltpu.VMEM((rows, wide_q), BF16),
            pltpu.VMEM((heads, rows), F32),
            pltpu.SemaphoreType.DMA((3 * groups + 1,)),
        ],
        micros=2,
    )(span_map, tables, lse, q, do, at)
    v1, _ = lax.optimization_barrier((v1, shared[3]))
    v3 = shifted(v1, -2)
    k3 = shifted(k1, -2)
    dqs = []
    dq_out = ((wide_q // groups, rows), F32)
    part_out = ((rows, 2 * HEAD), BF16)

    def hop(step, wanted, key, value, joined=False):
        count = len(wanted)
        started = len(dqs) > 0
        before = [dqs[g] for g in wanted] if started else []
        results = call(
            functools.partial(hop_kernel, step, wanted, started, joined),
            [dq_out] * count
            + ([((rows, 2 * HEAD * count), BF16)] if joined else [part_out] * count),
            [VMEM] * (7 + len(before)),
            micros=count,
        )(*before, key, value, *shared)
        if not started:
            dqs.extend(results[:count])
        for i, g in enumerate(wanted):
            dqs[g] = results[i]
        return results[count:]

    parts1 = hop(1, every, k1, v1)
    kr2, v_far, _ = lax.optimization_barrier((kr, v, parts1[0]))
    k2 = shifted(kr2, -2)
    v2 = shifted(v_far, -2)
    moved = [shifted(*hop(3, (g,), k3, v3), 2) for g in every]
    back2 = [shifted(part, 2) for part in hop(2, every, k2, v2)]
    results = call(
        functools.partial(own_kernel, groups),
        [dq_out] * groups + [((rows, 2 * HEAD), F32)] * groups,
        [VMEM] * (6 + groups),
        micros=3,
    )(kr, v_here, *shared[:4], *dqs)
    dqs, owns = list(results[:groups]), results[groups:]
    dq, *owns = call(
        functools.partial(query_kernel, groups),
        [((rows, wide_q), BF16)] + [((rows, 2 * HEAD), F32)] * groups,
        [VMEM] * (1 + 3 * groups),
    )(tables, *dqs, *owns, *back2)
    home = []
    for g in every:
        (total,) = call(add_kernel, [part_out], [VMEM] * 2)(parts1[g], moved[g])
        home.append(shifted(total, 1))

    dk, dv = call(
        functools.partial(final_kernel, groups),
        [((rows, wide_k), BF16), ((rows, wide_k), BF16)],
        [VMEM] * (1 + 2 * groups),
    )(tables, *owns, *home)
    return dq, dk, dv


def solution(mesh):
    placed = (
        P("ctx", "head"),
        P("ctx", "head"),
        P("ctx", "head"),
        P("ctx", "head"),
        P("ctx", "head"),
        P("head", "ctx"),
        P(None, ("ctx", "head")),
        P(),
    )
    return jax.shard_map(
        shards,
        mesh=mesh,
        in_specs=placed,
        out_specs=(P("ctx", "head"), P("ctx", "head"), P("ctx", "head")),
        check_vma=False,
    )
```

```python
import functools
import math

import jax
import jax.numpy as jnp
import numpy as np
from jax import lax
from jax.experimental import pallas as pl
from jax.experimental.pallas import tpu as pltpu
from jax.sharding import PartitionSpec as P

HEAD = 128
HALF = HEAD // 2
WIN = 4
ROPE_BASE = 1000000.0
YARN_FACTOR = 4.0
YARN_INITIAL = 32768.0
BETA_FAST = 32.0
BETA_SLOW = 1.0
YARN_MSCALE = 1.0 + 0.1 * math.log(4.0)
ROOT_SCALE = 1.0 / math.sqrt(HEAD)
LOG2E = math.log2(math.e)
VMEM_LIMIT = 24 * 1024 * 1024

F32 = jnp.float32
BF16 = jnp.bfloat16


def frequencies():
    pair = np.arange(HALF, dtype=np.float64)
    inverse = np.exp(-2.0 * pair / HEAD * math.log(ROPE_BASE))
    ratio = YARN_INITIAL * inverse / (2.0 * math.pi)
    ramp = np.clip((ratio - BETA_SLOW) / (BETA_FAST - BETA_SLOW), 0.0, 1.0)
    return inverse * ((1.0 - ramp) / YARN_FACTOR + ramp)


def frequency_rows(lanes):
    values = frequencies()
    row = lax.broadcasted_iota(jnp.int32, (8, lanes), 0)
    tiles = []
    for first in range(0, HALF, 8):
        tile = jnp.full((8, lanes), float(values[first]), F32)
        for j in range(1, 8):
            tile = jnp.where(row == j, float(values[first + j]), tile)
        tiles.append(tile)
    return jnp.concatenate(tiles, axis=0)


def sine_cosine(angle):
    turns = jnp.floor(angle * (2.0 / math.pi) + 0.5)
    r = angle - turns * 1.5703125
    r = r - turns * 4.837512969970703125e-4
    r = r - turns * 7.54978995489188e-8
    r2 = r * r
    s = r + r * r2 * (-1.6666654611e-1 + r2 * (8.3321608736e-3 - r2 * 1.9515295891e-4))
    c = (
        1.0
        - 0.5 * r2
        + r2
        * r2
        * (4.166664568298827e-2 + r2 * (-1.388731625493765e-3 + r2 * 2.443315711809948e-5))
    )
    quadrant = turns.astype(jnp.int32) & 3
    odd = (quadrant & 1) == 1
    sine = jnp.where(odd, c, s)
    cosine = jnp.where(odd, s, c)
    sine = jnp.where(quadrant >= 2, -sine, sine)
    cosine = jnp.where((quadrant == 1) | (quadrant == 2), -cosine, cosine)
    return sine, cosine


def tables_transposed(place):
    place = place.astype(F32)
    freq = frequency_rows(place.shape[1])
    pair = lax.broadcasted_iota(jnp.int32, freq.shape, 0)
    first = HEAD // 8
    second = first + 3 * HEAD // 16
    chosen = jnp.where(
        pair < first, place[0:1], jnp.where(pair < second, place[1:2], place[2:3])
    )
    sine, cosine = sine_cosine(chosen * freq)
    return cosine * YARN_MSCALE, sine * YARN_MSCALE


def row_tables(cosine_t, sine_t):
    wide = jnp.concatenate([cosine_t, cosine_t], axis=0).T
    signed = jnp.concatenate([-sine_t, sine_t], axis=0).T
    return wide, signed


def rotated(x, wide, signed):
    return x * wide + pltpu.roll(x, HALF, 1) * signed


def dot_nt(a, b):
    return lax.dot_general(a, b, (((1,), (1,)), ((), ())), preferred_element_type=F32)


def dot_nn(a, b):
    return lax.dot_general(a, b, (((1,), (0,)), ((), ())), preferred_element_type=F32)


def dot_tn(a, b):
    return lax.dot_general(a, b, (((0,), (0,)), ((), ())), preferred_element_type=F32)


def pair_part(key, value, query, grad, norm, delta, causal):
    scores = dot_nt(key, query)
    weights = jnp.exp2(scores * (ROOT_SCALE * LOG2E) - norm)
    if causal:
        at_key = lax.broadcasted_iota(jnp.int32, scores.shape, 0)
        at_query = lax.broadcasted_iota(jnp.int32, scores.shape, 1)
        weights = jnp.where(at_key <= at_query, weights, 0.0)
    value_part = dot_nn(weights.astype(BF16), grad)
    score_grad = (weights * (dot_nt(value, grad) - delta)).astype(BF16)
    key_part = dot_nn(score_grad, query)
    query_part = dot_tn(key, score_grad)
    return value_part, key_part, query_part


def key_kernel(own_ref, p1_ref, p2_ref, p3_ref, k_ref, kr_ref, tables_ref):
    pieces = (own_ref[...], p1_ref[...], p2_ref[...], p3_ref[...])
    count = len(pieces)
    head = lax.axis_index("head")
    parts = []
    for j in range(count):
        back = lax.rem(head - j + count, count)
        part = pieces[0]
        for r in range(1, count):
            part = jnp.where(back == r, pieces[r], part)
        parts.append(part)
    cosine_t, sine_t = tables_transposed(jnp.concatenate(parts, axis=1))
    tables_ref[:HALF, :] = cosine_t
    tables_ref[HALF:, :] = sine_t
    wide, signed = row_tables(cosine_t, sine_t)
    for g in range(k_ref.shape[1] // HEAD):
        cols = pl.ds(g * HEAD, HEAD)
        kr_ref[:, cols] = rotated(k_ref[:, cols].astype(F32), wide, signed).astype(BF16)


def prep_kernel(
    groups, span_ref, tables_ref, lse_hbm, q_hbm, do_hbm, at_hbm,
    qr_ref, do_ref, norm_ref, delta_ref, flag_ref, q_ref, at_ref, lse_ref, sems,
):
    heads = qr_ref.shape[1] // HEAD
    size = heads // groups
    copies = []
    for g in range(groups):
        cols = pl.ds(g * size * HEAD, size * HEAD)
        for i, (source, target) in enumerate(
            ((q_hbm, q_ref), (do_hbm, do_ref), (at_hbm, at_ref))
        ):
            copy = pltpu.make_async_copy(
                source.at[:, cols], target.at[:, cols], sems.at[3 * g + i]
            )
            copy.start()
            copies.append(copy)
    lse_copy = pltpu.make_async_copy(lse_hbm, lse_ref, sems.at[3 * groups])
    lse_copy.start()
    me = lax.axis_index("ctx")
    step_row = lax.broadcasted_iota(jnp.int32, flag_ref.shape, 0)
    flags = jnp.zeros(flag_ref.shape, jnp.int32)
    for step in range(1, WIN):
        other = lax.rem(me + step, span_ref.shape[0])
        earlier = jnp.where(span_ref[other] < span_ref[me], 1, 0)
        flags = jnp.where(step_row == step, earlier, flags)
    flag_ref[...] = flags
    wide, signed = row_tables(tables_ref[:HALF, :], tables_ref[HALF:, :])
    chooser = jnp.ones((8, HEAD), BF16)
    for h in range(heads):
        if h % size == 0:
            for copy in copies[3 * (h // size) : 3 * (h // size) + 3]:
                copy.wait()
        hc = pl.ds(h * HEAD, HEAD)
        qr_ref[:, hc] = rotated(q_ref[:, hc].astype(F32), wide, signed).astype(BF16)
        product = do_ref[:, hc].astype(F32) * at_ref[:, hc].astype(F32)
        high = product.astype(BF16)
        low = (product - high.astype(F32)).astype(BF16)
        delta_ref[h : h + 1, :] = (dot_nt(chooser, high) + dot_nt(chooser, low))[:1]
    lse_copy.wait()
    norm_ref[...] = lse_ref[...] * LOG2E


def hop_kernel(step, wanted, started, joined, *refs):
    count = len(wanted)
    if joined:
        *refs, part_ref = refs
        refs += [part_ref.at[:, 2 * HEAD * i : 2 * HEAD * (i + 1)] for i in range(count)]
    dqt_ins, dqt_refs, part_refs = refs[:count], refs[-2 * count : -count], refs[-count:]
    k_ref, v_ref, qr_ref, do_ref, norm_ref, delta_ref, flag_ref = refs[
        count * started : -2 * count
    ]
    rows = qr_ref.shape[0]
    half = rows // 2
    heads = qr_ref.shape[1] // HEAD
    groups = k_ref.shape[1] // HEAD
    size = heads // groups
    earlier = flag_ref[step, 0] == 1
    norm = norm_ref[...]
    delta = delta_ref[...]

    def run(keys, queries):
        for g, dqt_in, dqt_ref, part_ref in zip(wanted, dqt_ins, dqt_refs, part_refs):
            kc = pl.ds(g * HEAD, HEAD)
            dk = dv = None
            for j in range(size):
                h = g * size + j
                hc = pl.ds(h * HEAD, HEAD)
                to = pl.ds(j * HEAD, HEAD)
                v_part, k_part, q_part = pair_part(
                    k_ref[keys, kc], v_ref[keys, kc], qr_ref[queries, hc], do_ref[queries, hc],
                    norm[h : h + 1, queries.start :], delta[h : h + 1, queries.start :], False,
                )
                if queries.start:
                    zeros = jnp.zeros((HEAD, queries.start), F32)
                    dqt_ref[to, : queries.start] = (
                        dqt_in[to, : queries.start] if started else zeros
                    )
                dqt_ref[to, queries] = dqt_in[to, queries] + q_part if started else q_part
                dv = v_part if dv is None else dv + v_part
                dk = k_part if dk is None else dk + k_part
            part_ref[keys, :HEAD] = dk.astype(BF16)
            part_ref[keys, HEAD:] = dv.astype(BF16)
            if keys.stop < rows:
                part_ref[keys.stop :, :] = jnp.zeros((rows - keys.stop, 2 * HEAD), BF16)

    @pl.when(earlier)
    def _():
        run(slice(0, half), slice(0, rows))

    @pl.when(jnp.logical_not(earlier))
    def _():
        run(slice(0, rows), slice(half, rows))


def own_kernel(groups, k_ref, v_ref, qr_ref, do_ref, norm_ref, delta_ref, *refs):
    dqt_ins, dqt_refs, part_refs = refs[:groups], refs[groups : 2 * groups], refs[2 * groups :]
    size = qr_ref.shape[1] // HEAD // groups
    norm = norm_ref[...]
    delta = delta_ref[...]
    for g in range(groups):
        kc = pl.ds(g * HEAD, HEAD)
        dk = dv = None
        for j in range(size):
            h = g * size + j
            hc = pl.ds(h * HEAD, HEAD)
            to = pl.ds(j * HEAD, HEAD)
            v_part, k_part, q_part = pair_part(
                k_ref[:, kc], v_ref[:, kc], qr_ref[:, hc], do_ref[:, hc],
                norm[h : h + 1], delta[h : h + 1], True,
            )
            dqt_refs[g][to, :] = dqt_ins[g][to, :] + q_part
            dv = v_part if dv is None else dv + v_part
            dk = k_part if dk is None else dk + k_part
        part_refs[g][:, :HEAD] = dk
        part_refs[g][:, HEAD:] = dv


def query_kernel(groups, tables_ref, *refs):
    dqt_refs, own_refs = refs[:groups], refs[groups : 2 * groups]
    back_refs, (out_ref, *sum_refs) = refs[2 * groups : 3 * groups], refs[3 * groups :]
    for g in range(groups):
        sum_refs[g][...] = own_refs[g][...] + back_refs[g][...].astype(F32)
    cosine_t = tables_ref[:HALF, :] * ROOT_SCALE
    sine_t = tables_ref[HALF:, :] * ROOT_SCALE
    size = dqt_refs[0].shape[0] // HEAD
    for g in range(groups):
        for j in range(size):
            y1 = dqt_refs[g][pl.ds(j * HEAD, HALF), :]
            y2 = dqt_refs[g][pl.ds(j * HEAD + HALF, HALF), :]
            turned = jnp.concatenate(
                [y1 * cosine_t + y2 * sine_t, y2 * cosine_t - y1 * sine_t], axis=0
            )
            out_ref[:, pl.ds((g * size + j) * HEAD, HEAD)] = turned.T.astype(BF16)


def add_kernel(a_ref, b_ref, sum_ref):
    sum_ref[...] = (a_ref[...].astype(F32) + b_ref[...].astype(F32)).astype(BF16)


def final_kernel(groups, tables_ref, *refs):
    own_refs, home_refs, (dk_ref, dv_ref) = refs[:groups], refs[groups : 2 * groups], refs[-2:]
    wide, signed = row_tables(tables_ref[:HALF, :], tables_ref[HALF:, :])
    wide = wide * ROOT_SCALE
    signed = signed * -ROOT_SCALE
    for g in range(groups):
        cols = pl.ds(g * HEAD, HEAD)
        total = own_refs[g][...] + home_refs[g][...].astype(F32)
        dk_ref[:, cols] = rotated(total[:, :HEAD], wide, signed).astype(BF16)
        dv_ref[:, cols] = total[:, HEAD:].astype(BF16)


SMEM = pl.BlockSpec(memory_space=pltpu.SMEM)
VMEM = pl.BlockSpec(memory_space=pltpu.VMEM)
HBM = pl.BlockSpec(memory_space=pltpu.HBM)


def call(kernel, outs, specs, scratch=(), micros=1):
    return pl.pallas_call(
        kernel,
        out_shape=[jax.ShapeDtypeStruct(shape, dtype) for shape, dtype in outs],
        in_specs=specs,
        out_specs=[VMEM] * len(outs),
        scratch_shapes=list(scratch),
        compiler_params=pltpu.CompilerParams(vmem_limit_bytes=VMEM_LIMIT),
        cost_estimate=pl.CostEstimate(
            flops=1 << 20, bytes_accessed=micros * 3690000, transcendentals=0
        ),
    )


def shifted(value, steps, axis="ctx"):
    count = lax.axis_size(axis)
    pairs = [(source, (source + steps) % count) for source in range(count)]
    return lax.ppermute(value, axis, pairs)


def shards(q, k, v, do, at, lse, positions, span_map):
    rows = q.shape[0]
    wide_q = q.shape[1]
    wide_k = k.shape[1]
    heads = wide_q // HEAD
    q, do, at, k_here, v_here, lse, span_map, own = (
        pltpu.with_memory_space_constraint(x, pltpu.HBM)
        for x in (q, do, at, k, v, lse, span_map, positions)
    )

    pieces = [own] + [shifted(positions, r, "head") for r in (1, 2, 3)]
    groups = wide_k // HEAD
    every = tuple(range(groups))

    groups = wide_k // HEAD
    every = tuple(range(groups))

    v1 = shifted(v, -1)
    kr, tables = call(
        key_kernel, [((rows, wide_k), BF16), ((HEAD, rows), F32)], [VMEM] * 5
    )(*pieces, k_here)
    k1 = shifted(kr, -1)
    shared = call(
        functools.partial(prep_kernel, groups),
        [((rows, wide_q), BF16)] * 2 + [((heads, rows), F32)] * 2 + [((8, HEAD), jnp.int32)],
        [SMEM, VMEM] + [HBM] * 4,
        [
            pltpu.VMEM((rows, wide_q), BF16),
            pltpu.VMEM((rows, wide_q), BF16),
            pltpu.VMEM((heads, rows), F32),
            pltpu.SemaphoreType.DMA((3 * groups + 1,)),
        ],
        micros=2,
    )(span_map, tables, lse, q, do, at)
    v1, _ = lax.optimization_barrier((v1, shared[3]))
    v3 = shifted(v1, -2)
    v_far, _ = lax.optimization_barrier((v, shared[3]))
    v2 = shifted(v_far, -2)
    k3 = shifted(k1, -2)
    dqs = []
    dq_out = ((wide_q // groups, rows), F32)
    part_out = ((rows, 2 * HEAD), BF16)

    def hop(step, wanted, key, value, joined=False):
        count = len(wanted)
        started = len(dqs) > 0
        before = [dqs[g] for g in wanted] if started else []
        results = call(
            functools.partial(hop_kernel, step, wanted, started, joined),
            [dq_out] * count
            + ([((rows, 2 * HEAD * count), BF16)] if joined else [part_out] * count),
            [VMEM] * (7 + len(before)),
            micros=count,
        )(*before, key, value, *shared)
        if not started:
            dqs.extend(results[:count])
        for i, g in enumerate(wanted):
            dqs[g] = results[i]
        return results[count:]

    parts1 = hop(1, every, k1, v1)
    kr2, _ = lax.optimization_barrier((kr, parts1[0]))
    k2 = shifted(kr2, -2)
    moved = [shifted(*hop(3, (g,), k3, v3), 2) for g in every]
    back2 = [shifted(part, 2) for part in hop(2, every, k2, v2)]
    results = call(
        functools.partial(own_kernel, groups),
        [dq_out] * groups + [((rows, 2 * HEAD), F32)] * groups,
        [VMEM] * (6 + groups),
        micros=3,
    )(kr, v_here, *shared[:4], *dqs)
    dqs, owns = list(results[:groups]), results[groups:]
    dq, *owns = call(
        functools.partial(query_kernel, groups),
        [((rows, wide_q), BF16)] + [((rows, 2 * HEAD), F32)] * groups,
        [VMEM] * (1 + 3 * groups),
    )(tables, *dqs, *owns, *back2)
    home = []
    for g in every:
        (total,) = call(add_kernel, [part_out], [VMEM] * 2)(parts1[g], moved[g])
        home.append(shifted(total, 1))

    dk, dv = call(
        functools.partial(final_kernel, groups),
        [((rows, wide_k), BF16), ((rows, wide_k), BF16)],
        [VMEM] * (1 + 2 * groups),
    )(tables, *owns, *home)
    return dq, dk, dv


def solution(mesh):
    placed = (
        P("ctx", "head"),
        P("ctx", "head"),
        P("ctx", "head"),
        P("ctx", "head"),
        P("ctx", "head"),
        P("head", "ctx"),
        P(None, ("ctx", "head")),
        P(),
    )
    return jax.shard_map(
        shards,
        mesh=mesh,
        in_specs=placed,
        out_specs=(P("ctx", "head"), P("ctx", "head"), P("ctx", "head")),
        check_vma=False,
    )
```

```python
import functools
import math

import jax
import jax.numpy as jnp
import numpy as np
from jax import lax
from jax.experimental import pallas as pl
from jax.experimental.pallas import tpu as pltpu
from jax.sharding import PartitionSpec as P

HEAD = 128
HALF = HEAD // 2
WIN = 4
ROPE_BASE = 1000000.0
YARN_FACTOR = 4.0
YARN_INITIAL = 32768.0
BETA_FAST = 32.0
BETA_SLOW = 1.0
YARN_MSCALE = 1.0 + 0.1 * math.log(4.0)
ROOT_SCALE = 1.0 / math.sqrt(HEAD)
LOG2E = math.log2(math.e)
VMEM_LIMIT = 24 * 1024 * 1024

F32 = jnp.float32
BF16 = jnp.bfloat16


def frequencies():
    pair = np.arange(HALF, dtype=np.float64)
    inverse = np.exp(-2.0 * pair / HEAD * math.log(ROPE_BASE))
    ratio = YARN_INITIAL * inverse / (2.0 * math.pi)
    ramp = np.clip((ratio - BETA_SLOW) / (BETA_FAST - BETA_SLOW), 0.0, 1.0)
    return inverse * ((1.0 - ramp) / YARN_FACTOR + ramp)


def frequency_rows(lanes):
    values = frequencies()
    row = lax.broadcasted_iota(jnp.int32, (8, lanes), 0)
    tiles = []
    for first in range(0, HALF, 8):
        tile = jnp.full((8, lanes), float(values[first]), F32)
        for j in range(1, 8):
            tile = jnp.where(row == j, float(values[first + j]), tile)
        tiles.append(tile)
    return jnp.concatenate(tiles, axis=0)


def sine_cosine(angle):
    turns = jnp.floor(angle * (2.0 / math.pi) + 0.5)
    r = angle - turns * 1.5703125
    r = r - turns * 4.837512969970703125e-4
    r = r - turns * 7.54978995489188e-8
    r2 = r * r
    s = r + r * r2 * (-1.6666654611e-1 + r2 * (8.3321608736e-3 - r2 * 1.9515295891e-4))
    c = (
        1.0
        - 0.5 * r2
        + r2
        * r2
        * (4.166664568298827e-2 + r2 * (-1.388731625493765e-3 + r2 * 2.443315711809948e-5))
    )
    quadrant = turns.astype(jnp.int32) & 3
    odd = (quadrant & 1) == 1
    sine = jnp.where(odd, c, s)
    cosine = jnp.where(odd, s, c)
    sine = jnp.where(quadrant >= 2, -sine, sine)
    cosine = jnp.where((quadrant == 1) | (quadrant == 2), -cosine, cosine)
    return sine, cosine


def tables_transposed(place):
    place = place.astype(F32)
    freq = frequency_rows(place.shape[1])
    pair = lax.broadcasted_iota(jnp.int32, freq.shape, 0)
    first = HEAD // 8
    second = first + 3 * HEAD // 16
    chosen = jnp.where(
        pair < first, place[0:1], jnp.where(pair < second, place[1:2], place[2:3])
    )
    sine, cosine = sine_cosine(chosen * freq)
    return cosine * YARN_MSCALE, sine * YARN_MSCALE


def row_tables(cosine_t, sine_t):
    wide = jnp.concatenate([cosine_t, cosine_t], axis=0).T
    signed = jnp.concatenate([-sine_t, sine_t], axis=0).T
    return wide, signed


def rotated(x, wide, signed):
    return x * wide + pltpu.roll(x, HALF, 1) * signed


def dot_nt(a, b):
    return lax.dot_general(a, b, (((1,), (1,)), ((), ())), preferred_element_type=F32)


def dot_nn(a, b):
    return lax.dot_general(a, b, (((1,), (0,)), ((), ())), preferred_element_type=F32)


def dot_tn(a, b):
    return lax.dot_general(a, b, (((0,), (0,)), ((), ())), preferred_element_type=F32)


def pair_part(key, value, query, grad, norm, delta, causal):
    scores = dot_nt(key, query)
    weights = jnp.exp2(scores * (ROOT_SCALE * LOG2E) - norm)
    if causal:
        at_key = lax.broadcasted_iota(jnp.int32, scores.shape, 0)
        at_query = lax.broadcasted_iota(jnp.int32, scores.shape, 1)
        weights = jnp.where(at_key <= at_query, weights, 0.0)
    value_part = dot_nn(weights.astype(BF16), grad)
    score_grad = (weights * (dot_nt(value, grad) - delta)).astype(BF16)
    key_part = dot_nn(score_grad, query)
    query_part = dot_tn(key, score_grad)
    return value_part, key_part, query_part


def key_kernel(own_ref, p1_ref, p2_ref, p3_ref, k_ref, kr_ref, tables_ref):
    pieces = (own_ref[...], p1_ref[...], p2_ref[...], p3_ref[...])
    count = len(pieces)
    head = lax.axis_index("head")
    parts = []
    for j in range(count):
        back = lax.rem(head - j + count, count)
        part = pieces[0]
        for r in range(1, count):
            part = jnp.where(back == r, pieces[r], part)
        parts.append(part)
    cosine_t, sine_t = tables_transposed(jnp.concatenate(parts, axis=1))
    tables_ref[:HALF, :] = cosine_t
    tables_ref[HALF:, :] = sine_t
    wide, signed = row_tables(cosine_t, sine_t)
    for g in range(k_ref.shape[1] // HEAD):
        cols = pl.ds(g * HEAD, HEAD)
        kr_ref[:, cols] = rotated(k_ref[:, cols].astype(F32), wide, signed).astype(BF16)


def prep_kernel(
    groups, span_ref, tables_ref, lse_hbm, q_hbm, do_hbm, at_hbm,
    qr_ref, do_ref, norm_ref, delta_ref, flag_ref, q_ref, at_ref, lse_ref, sems,
):
    heads = qr_ref.shape[1] // HEAD
    size = heads // groups
    copies = []
    for g in range(groups):
        cols = pl.ds(g * size * HEAD, size * HEAD)
        for i, (source, target) in enumerate(
            ((q_hbm, q_ref), (do_hbm, do_ref), (at_hbm, at_ref))
        ):
            copy = pltpu.make_async_copy(
                source.at[:, cols], target.at[:, cols], sems.at[3 * g + i]
            )
            copy.start()
            copies.append(copy)
    lse_copy = pltpu.make_async_copy(lse_hbm, lse_ref, sems.at[3 * groups])
    lse_copy.start()
    me = lax.axis_index("ctx")
    step_row = lax.broadcasted_iota(jnp.int32, flag_ref.shape, 0)
    flags = jnp.zeros(flag_ref.shape, jnp.int32)
    for step in range(1, WIN):
        other = lax.rem(me + step, span_ref.shape[0])
        earlier = jnp.where(span_ref[other] < span_ref[me], 1, 0)
        flags = jnp.where(step_row == step, earlier, flags)
    flag_ref[...] = flags
    wide, signed = row_tables(tables_ref[:HALF, :], tables_ref[HALF:, :])
    chooser = jnp.ones((8, HEAD), BF16)
    for h in range(heads):
        if h % size == 0:
            for copy in copies[3 * (h // size) : 3 * (h // size) + 3]:
                copy.wait()
        hc = pl.ds(h * HEAD, HEAD)
        qr_ref[:, hc] = rotated(q_ref[:, hc].astype(F32), wide, signed).astype(BF16)
        product = do_ref[:, hc].astype(F32) * at_ref[:, hc].astype(F32)
        high = product.astype(BF16)
        low = (product - high.astype(F32)).astype(BF16)
        delta_ref[h : h + 1, :] = (dot_nt(chooser, high) + dot_nt(chooser, low))[:1]
    lse_copy.wait()
    norm_ref[...] = lse_ref[...] * LOG2E


def hop_kernel(step, wanted, started, joined, *refs):
    count = len(wanted)
    if joined:
        *refs, part_ref = refs
        refs += [part_ref.at[:, 2 * HEAD * i : 2 * HEAD * (i + 1)] for i in range(count)]
    dqt_ins, dqt_refs, part_refs = refs[:count], refs[-2 * count : -count], refs[-count:]
    k_ref, v_ref, qr_ref, do_ref, norm_ref, delta_ref, flag_ref = refs[
        count * started : -2 * count
    ]
    rows = qr_ref.shape[0]
    half = rows // 2
    heads = qr_ref.shape[1] // HEAD
    groups = k_ref.shape[1] // HEAD
    size = heads // groups
    earlier = flag_ref[step, 0] == 1
    norm = norm_ref[...]
    delta = delta_ref[...]

    def run(keys, queries):
        for g, dqt_in, dqt_ref, part_ref in zip(wanted, dqt_ins, dqt_refs, part_refs):
            kc = pl.ds(g * HEAD, HEAD)
            dk = dv = None
            for j in range(size):
                h = g * size + j
                hc = pl.ds(h * HEAD, HEAD)
                to = pl.ds(j * HEAD, HEAD)
                v_part, k_part, q_part = pair_part(
                    k_ref[keys, kc], v_ref[keys, kc], qr_ref[queries, hc], do_ref[queries, hc],
                    norm[h : h + 1, queries.start :], delta[h : h + 1, queries.start :], False,
                )
                if queries.start:
                    zeros = jnp.zeros((HEAD, queries.start), F32)
                    dqt_ref[to, : queries.start] = (
                        dqt_in[to, : queries.start] if started else zeros
                    )
                dqt_ref[to, queries] = dqt_in[to, queries] + q_part if started else q_part
                dv = v_part if dv is None else dv + v_part
                dk = k_part if dk is None else dk + k_part
            part_ref[keys, :HEAD] = dk.astype(BF16)
            part_ref[keys, HEAD:] = dv.astype(BF16)
            if keys.stop < rows:
                part_ref[keys.stop :, :] = jnp.zeros((rows - keys.stop, 2 * HEAD), BF16)

    @pl.when(earlier)
    def _():
        run(slice(0, half), slice(0, rows))

    @pl.when(jnp.logical_not(earlier))
    def _():
        run(slice(0, rows), slice(half, rows))


def own_kernel(groups, k_ref, v_ref, qr_ref, do_ref, norm_ref, delta_ref, *refs):
    dqt_ins, dqt_refs, part_refs = refs[:groups], refs[groups : 2 * groups], refs[2 * groups :]
    size = qr_ref.shape[1] // HEAD // groups
    norm = norm_ref[...]
    delta = delta_ref[...]
    for g in range(groups):
        kc = pl.ds(g * HEAD, HEAD)
        dk = dv = None
        for j in range(size):
            h = g * size + j
            hc = pl.ds(h * HEAD, HEAD)
            to = pl.ds(j * HEAD, HEAD)
            v_part, k_part, q_part = pair_part(
                k_ref[:, kc], v_ref[:, kc], qr_ref[:, hc], do_ref[:, hc],
                norm[h : h + 1], delta[h : h + 1], True,
            )
            dqt_refs[g][to, :] = dqt_ins[g][to, :] + q_part
            dv = v_part if dv is None else dv + v_part
            dk = k_part if dk is None else dk + k_part
        part_refs[g][:, :HEAD] = dk
        part_refs[g][:, HEAD:] = dv


def query_kernel(groups, tables_ref, *refs):
    dqt_refs, own_refs = refs[:groups], refs[groups : 2 * groups]
    back_refs, (out_ref, *sum_refs) = refs[2 * groups : 3 * groups], refs[3 * groups :]
    for g in range(groups):
        sum_refs[g][...] = own_refs[g][...] + back_refs[g][...].astype(F32)
    cosine_t = tables_ref[:HALF, :] * ROOT_SCALE
    sine_t = tables_ref[HALF:, :] * ROOT_SCALE
    size = dqt_refs[0].shape[0] // HEAD
    for g in range(groups):
        for j in range(size):
            y1 = dqt_refs[g][pl.ds(j * HEAD, HALF), :]
            y2 = dqt_refs[g][pl.ds(j * HEAD + HALF, HALF), :]
            turned = jnp.concatenate(
                [y1 * cosine_t + y2 * sine_t, y2 * cosine_t - y1 * sine_t], axis=0
            )
            out_ref[:, pl.ds((g * size + j) * HEAD, HEAD)] = turned.T.astype(BF16)


def add_kernel(a_ref, b_ref, sum_ref):
    sum_ref[...] = (a_ref[...].astype(F32) + b_ref[...].astype(F32)).astype(BF16)


def final_kernel(groups, tables_ref, *refs):
    own_refs, home_refs, (dk_ref, dv_ref) = refs[:groups], refs[groups : 2 * groups], refs[-2:]
    wide, signed = row_tables(tables_ref[:HALF, :], tables_ref[HALF:, :])
    wide = wide * ROOT_SCALE
    signed = signed * -ROOT_SCALE
    for g in range(groups):
        cols = pl.ds(g * HEAD, HEAD)
        total = own_refs[g][...] + home_refs[g][...].astype(F32)
        dk_ref[:, cols] = rotated(total[:, :HEAD], wide, signed).astype(BF16)
        dv_ref[:, cols] = total[:, HEAD:].astype(BF16)


SMEM = pl.BlockSpec(memory_space=pltpu.SMEM)
VMEM = pl.BlockSpec(memory_space=pltpu.VMEM)
HBM = pl.BlockSpec(memory_space=pltpu.HBM)


def call(kernel, outs, specs, scratch=(), micros=1):
    return pl.pallas_call(
        kernel,
        out_shape=[jax.ShapeDtypeStruct(shape, dtype) for shape, dtype in outs],
        in_specs=specs,
        out_specs=[VMEM] * len(outs),
        scratch_shapes=list(scratch),
        compiler_params=pltpu.CompilerParams(vmem_limit_bytes=VMEM_LIMIT),
        cost_estimate=pl.CostEstimate(
            flops=1 << 20, bytes_accessed=micros * 3690000, transcendentals=0
        ),
    )


def shifted(value, steps, axis="ctx"):
    count = lax.axis_size(axis)
    pairs = [(source, (source + steps) % count) for source in range(count)]
    return lax.ppermute(value, axis, pairs)


def shards(q, k, v, do, at, lse, positions, span_map):
    rows = q.shape[0]
    wide_q = q.shape[1]
    wide_k = k.shape[1]
    heads = wide_q // HEAD
    q, do, at, k_here, v_here, lse, span_map, own = (
        pltpu.with_memory_space_constraint(x, pltpu.HBM)
        for x in (q, do, at, k, v, lse, span_map, positions)
    )

    pieces = [own] + [shifted(positions, r, "head") for r in (1, 2, 3)]
    groups = wide_k // HEAD
    every = tuple(range(groups))

    groups = wide_k // HEAD
    every = tuple(range(groups))

    v1 = shifted(v, -1)
    kr, tables = call(
        key_kernel, [((rows, wide_k), BF16), ((HEAD, rows), F32)], [VMEM] * 5
    )(*pieces, k_here)
    k1 = shifted(kr, -1)
    shared = call(
        functools.partial(prep_kernel, groups),
        [((rows, wide_q), BF16)] * 2 + [((heads, rows), F32)] * 2 + [((8, HEAD), jnp.int32)],
        [SMEM, VMEM] + [HBM] * 4,
        [
            pltpu.VMEM((rows, wide_q), BF16),
            pltpu.VMEM((rows, wide_q), BF16),
            pltpu.VMEM((heads, rows), F32),
            pltpu.SemaphoreType.DMA((3 * groups + 1,)),
        ],
        micros=2,
    )(span_map, tables, lse, q, do, at)
    v1, _ = lax.optimization_barrier((v1, shared[3]))
    v3 = shifted(v1, -2)
    v_far, kr_far, _ = lax.optimization_barrier((v, kr, shared[3]))
    v2 = shifted(v_far, -2)
    k2 = shifted(kr_far, -2)
    k3 = shifted(k1, -2)
    dqs = []
    dq_out = ((wide_q // groups, rows), F32)
    part_out = ((rows, 2 * HEAD), BF16)

    def hop(step, wanted, key, value, joined=False):
        count = len(wanted)
        started = len(dqs) > 0
        before = [dqs[g] for g in wanted] if started else []
        results = call(
            functools.partial(hop_kernel, step, wanted, started, joined),
            [dq_out] * count
            + ([((rows, 2 * HEAD * count), BF16)] if joined else [part_out] * count),
            [VMEM] * (7 + len(before)),
            micros=count,
        )(*before, key, value, *shared)
        if not started:
            dqs.extend(results[:count])
        for i, g in enumerate(wanted):
            dqs[g] = results[i]
        return results[count:]

    parts1 = hop(1, every, k1, v1)
    moved = [shifted(*hop(3, (g,), k3, v3), 2) for g in every]
    back2 = [shifted(part, 2) for part in hop(2, every, k2, v2)]
    results = call(
        functools.partial(own_kernel, groups),
        [dq_out] * groups + [((rows, 2 * HEAD), F32)] * groups,
        [VMEM] * (6 + groups),
        micros=3,
    )(kr, v_here, *shared[:4], *dqs)
    dqs, owns = list(results[:groups]), results[groups:]
    dq, *owns = call(
        functools.partial(query_kernel, groups),
        [((rows, wide_q), BF16)] + [((rows, 2 * HEAD), F32)] * groups,
        [VMEM] * (1 + 3 * groups),
    )(tables, *dqs, *owns, *back2)
    home = []
    for g in every:
        (total,) = call(add_kernel, [part_out], [VMEM] * 2)(parts1[g], moved[g])
        home.append(shifted(total, 1))

    dk, dv = call(
        functools.partial(final_kernel, groups),
        [((rows, wide_k), BF16), ((rows, wide_k), BF16)],
        [VMEM] * (1 + 2 * groups),
    )(tables, *owns, *home)
    return dq, dk, dv


def solution(mesh):
    placed = (
        P("ctx", "head"),
        P("ctx", "head"),
        P("ctx", "head"),
        P("ctx", "head"),
        P("ctx", "head"),
        P("head", "ctx"),
        P(None, ("ctx", "head")),
        P(),
    )
    return jax.shard_map(
        shards,
        mesh=mesh,
        in_specs=placed,
        out_specs=(P("ctx", "head"), P("ctx", "head"), P("ctx", "head")),
        check_vma=False,
    )
```

```python
import functools
import math

import jax
import jax.numpy as jnp
import numpy as np
from jax import lax
from jax.experimental import pallas as pl
from jax.experimental.pallas import tpu as pltpu
from jax.sharding import PartitionSpec as P

HEAD = 128
HALF = HEAD // 2
WIN = 4
ROPE_BASE = 1000000.0
YARN_FACTOR = 4.0
YARN_INITIAL = 32768.0
BETA_FAST = 32.0
BETA_SLOW = 1.0
YARN_MSCALE = 1.0 + 0.1 * math.log(4.0)
ROOT_SCALE = 1.0 / math.sqrt(HEAD)
LOG2E = math.log2(math.e)
VMEM_LIMIT = 24 * 1024 * 1024

F32 = jnp.float32
BF16 = jnp.bfloat16


def frequencies():
    pair = np.arange(HALF, dtype=np.float64)
    inverse = np.exp(-2.0 * pair / HEAD * math.log(ROPE_BASE))
    ratio = YARN_INITIAL * inverse / (2.0 * math.pi)
    ramp = np.clip((ratio - BETA_SLOW) / (BETA_FAST - BETA_SLOW), 0.0, 1.0)
    return inverse * ((1.0 - ramp) / YARN_FACTOR + ramp)


def frequency_rows(lanes):
    values = frequencies()
    row = lax.broadcasted_iota(jnp.int32, (8, lanes), 0)
    tiles = []
    for first in range(0, HALF, 8):
        tile = jnp.full((8, lanes), float(values[first]), F32)
        for j in range(1, 8):
            tile = jnp.where(row == j, float(values[first + j]), tile)
        tiles.append(tile)
    return jnp.concatenate(tiles, axis=0)


def sine_cosine(angle):
    turns = jnp.floor(angle * (2.0 / math.pi) + 0.5)
    r = angle - turns * 1.5703125
    r = r - turns * 4.837512969970703125e-4
    r = r - turns * 7.54978995489188e-8
    r2 = r * r
    s = r + r * r2 * (-1.6666654611e-1 + r2 * (8.3321608736e-3 - r2 * 1.9515295891e-4))
    c = (
        1.0
        - 0.5 * r2
        + r2
        * r2
        * (4.166664568298827e-2 + r2 * (-1.388731625493765e-3 + r2 * 2.443315711809948e-5))
    )
    quadrant = turns.astype(jnp.int32) & 3
    odd = (quadrant & 1) == 1
    sine = jnp.where(odd, c, s)
    cosine = jnp.where(odd, s, c)
    sine = jnp.where(quadrant >= 2, -sine, sine)
    cosine = jnp.where((quadrant == 1) | (quadrant == 2), -cosine, cosine)
    return sine, cosine


def tables_transposed(place):
    place = place.astype(F32)
    freq = frequency_rows(place.shape[1])
    pair = lax.broadcasted_iota(jnp.int32, freq.shape, 0)
    first = HEAD // 8
    second = first + 3 * HEAD // 16
    chosen = jnp.where(
        pair < first, place[0:1], jnp.where(pair < second, place[1:2], place[2:3])
    )
    sine, cosine = sine_cosine(chosen * freq)
    return cosine * YARN_MSCALE, sine * YARN_MSCALE


def row_tables(cosine_t, sine_t):
    wide = jnp.concatenate([cosine_t, cosine_t], axis=0).T
    signed = jnp.concatenate([-sine_t, sine_t], axis=0).T
    return wide, signed


def rotated(x, wide, signed):
    return x * wide + pltpu.roll(x, HALF, 1) * signed


def dot_nt(a, b):
    return lax.dot_general(a, b, (((1,), (1,)), ((), ())), preferred_element_type=F32)


def dot_nn(a, b):
    return lax.dot_general(a, b, (((1,), (0,)), ((), ())), preferred_element_type=F32)


def dot_tn(a, b):
    return lax.dot_general(a, b, (((0,), (0,)), ((), ())), preferred_element_type=F32)


def pair_part(key, value, query, grad, norm, delta, causal):
    scores = dot_nt(key, query)
    weights = jnp.exp2(scores * (ROOT_SCALE * LOG2E) - norm)
    if causal:
        at_key = lax.broadcasted_iota(jnp.int32, scores.shape, 0)
        at_query = lax.broadcasted_iota(jnp.int32, scores.shape, 1)
        weights = jnp.where(at_key <= at_query, weights, 0.0)
    value_part = dot_nn(weights.astype(BF16), grad)
    score_grad = (weights * (dot_nt(value, grad) - delta)).astype(BF16)
    key_part = dot_nn(score_grad, query)
    query_part = dot_tn(key, score_grad)
    return value_part, key_part, query_part


def key_kernel(own_ref, p1_ref, p2_ref, p3_ref, k_ref, kr_ref, tables_ref):
    pieces = (own_ref[...], p1_ref[...], p2_ref[...], p3_ref[...])
    count = len(pieces)
    head = lax.axis_index("head")
    parts = []
    for j in range(count):
        back = lax.rem(head - j + count, count)
        part = pieces[0]
        for r in range(1, count):
            part = jnp.where(back == r, pieces[r], part)
        parts.append(part)
    cosine_t, sine_t = tables_transposed(jnp.concatenate(parts, axis=1))
    tables_ref[:HALF, :] = cosine_t
    tables_ref[HALF:, :] = sine_t
    wide, signed = row_tables(cosine_t, sine_t)
    for g in range(k_ref.shape[1] // HEAD):
        cols = pl.ds(g * HEAD, HEAD)
        kr_ref[:, cols] = rotated(k_ref[:, cols].astype(F32), wide, signed).astype(BF16)


def prep_kernel(
    groups, span_ref, tables_ref, lse_hbm, q_hbm, do_hbm, at_hbm,
    qr_ref, do_ref, norm_ref, delta_ref, flag_ref, q_ref, at_ref, lse_ref, sems,
):
    heads = qr_ref.shape[1] // HEAD
    size = heads // groups
    copies = []
    for g in range(groups):
        cols = pl.ds(g * size * HEAD, size * HEAD)
        for i, (source, target) in enumerate(
            ((q_hbm, q_ref), (do_hbm, do_ref), (at_hbm, at_ref))
        ):
            copy = pltpu.make_async_copy(
                source.at[:, cols], target.at[:, cols], sems.at[3 * g + i]
            )
            copy.start()
            copies.append(copy)
    lse_copy = pltpu.make_async_copy(lse_hbm, lse_ref, sems.at[3 * groups])
    lse_copy.start()
    me = lax.axis_index("ctx")
    step_row = lax.broadcasted_iota(jnp.int32, flag_ref.shape, 0)
    flags = jnp.zeros(flag_ref.shape, jnp.int32)
    for step in range(1, WIN):
        other = lax.rem(me + step, span_ref.shape[0])
        earlier = jnp.where(span_ref[other] < span_ref[me], 1, 0)
        flags = jnp.where(step_row == step, earlier, flags)
    flag_ref[...] = flags
    wide, signed = row_tables(tables_ref[:HALF, :], tables_ref[HALF:, :])
    chooser = jnp.ones((8, HEAD), BF16)
    for h in range(heads):
        if h % size == 0:
            for copy in copies[3 * (h // size) : 3 * (h // size) + 3]:
                copy.wait()
        hc = pl.ds(h * HEAD, HEAD)
        qr_ref[:, hc] = rotated(q_ref[:, hc].astype(F32), wide, signed).astype(BF16)
        product = do_ref[:, hc].astype(F32) * at_ref[:, hc].astype(F32)
        high = product.astype(BF16)
        low = (product - high.astype(F32)).astype(BF16)
        delta_ref[h : h + 1, :] = (dot_nt(chooser, high) + dot_nt(chooser, low))[:1]
    lse_copy.wait()
    norm_ref[...] = lse_ref[...] * LOG2E


def hop_kernel(step, wanted, started, joined, *refs):
    count = len(wanted)
    if joined:
        *refs, part_ref = refs
        refs += [part_ref.at[:, 2 * HEAD * i : 2 * HEAD * (i + 1)] for i in range(count)]
    dqt_ins, dqt_refs, part_refs = refs[:count], refs[-2 * count : -count], refs[-count:]
    k_ref, v_ref, qr_ref, do_ref, norm_ref, delta_ref, flag_ref = refs[
        count * started : -2 * count
    ]
    rows = qr_ref.shape[0]
    half = rows // 2
    heads = qr_ref.shape[1] // HEAD
    groups = k_ref.shape[1] // HEAD
    size = heads // groups
    earlier = flag_ref[step, 0] == 1
    norm = norm_ref[...]
    delta = delta_ref[...]

    def run(keys, queries):
        for g, dqt_in, dqt_ref, part_ref in zip(wanted, dqt_ins, dqt_refs, part_refs):
            kc = pl.ds(g * HEAD, HEAD)
            dk = dv = None
            for j in range(size):
                h = g * size + j
                hc = pl.ds(h * HEAD, HEAD)
                to = pl.ds(j * HEAD, HEAD)
                v_part, k_part, q_part = pair_part(
                    k_ref[keys, kc], v_ref[keys, kc], qr_ref[queries, hc], do_ref[queries, hc],
                    norm[h : h + 1, queries.start :], delta[h : h + 1, queries.start :], False,
                )
                if queries.start:
                    zeros = jnp.zeros((HEAD, queries.start), F32)
                    dqt_ref[to, : queries.start] = (
                        dqt_in[to, : queries.start] if started else zeros
                    )
                dqt_ref[to, queries] = dqt_in[to, queries] + q_part if started else q_part
                dv = v_part if dv is None else dv + v_part
                dk = k_part if dk is None else dk + k_part
            part_ref[keys, :HEAD] = dk.astype(BF16)
            part_ref[keys, HEAD:] = dv.astype(BF16)
            if keys.stop < rows:
                part_ref[keys.stop :, :] = jnp.zeros((rows - keys.stop, 2 * HEAD), BF16)

    @pl.when(earlier)
    def _():
        run(slice(0, half), slice(0, rows))

    @pl.when(jnp.logical_not(earlier))
    def _():
        run(slice(0, rows), slice(half, rows))


def own_kernel(groups, k_ref, v_ref, qr_ref, do_ref, norm_ref, delta_ref, *refs):
    dqt_ins, dqt_refs, part_refs = refs[:groups], refs[groups : 2 * groups], refs[2 * groups :]
    size = qr_ref.shape[1] // HEAD // groups
    norm = norm_ref[...]
    delta = delta_ref[...]
    for g in range(groups):
        kc = pl.ds(g * HEAD, HEAD)
        dk = dv = None
        for j in range(size):
            h = g * size + j
            hc = pl.ds(h * HEAD, HEAD)
            to = pl.ds(j * HEAD, HEAD)
            v_part, k_part, q_part = pair_part(
                k_ref[:, kc], v_ref[:, kc], qr_ref[:, hc], do_ref[:, hc],
                norm[h : h + 1], delta[h : h + 1], True,
            )
            dqt_refs[g][to, :] = dqt_ins[g][to, :] + q_part
            dv = v_part if dv is None else dv + v_part
            dk = k_part if dk is None else dk + k_part
        part_refs[g][:, :HEAD] = dk
        part_refs[g][:, HEAD:] = dv


def query_kernel(groups, tables_ref, *refs):
    dqt_refs, own_refs = refs[:groups], refs[groups : 2 * groups]
    swapped_ref, out_ref, *sum_refs = refs[2 * groups :]
    odd = (lax.axis_index("ctx") & 1) == 1
    for g in range(groups):
        sum_refs[g][...] = own_refs[g][...] + jnp.where(
            odd, swapped_ref[:, 2 * HEAD * g : 2 * HEAD * (g + 1)].astype(F32), 0.0
        )
    cosine_t = tables_ref[:HALF, :] * ROOT_SCALE
    sine_t = tables_ref[HALF:, :] * ROOT_SCALE
    size = dqt_refs[0].shape[0] // HEAD
    for g in range(groups):
        for j in range(size):
            y1 = dqt_refs[g][pl.ds(j * HEAD, HALF), :]
            y2 = dqt_refs[g][pl.ds(j * HEAD + HALF, HALF), :]
            turned = jnp.concatenate(
                [y1 * cosine_t + y2 * sine_t, y2 * cosine_t - y1 * sine_t], axis=0
            )
            out_ref[:, pl.ds((g * size + j) * HEAD, HEAD)] = turned.T.astype(BF16)


def add_kernel(g, two_ref, swapped_ref, three_ref, sum_ref):
    even = (lax.axis_index("ctx") & 1) == 0
    total = two_ref[...].astype(F32) + three_ref[...].astype(F32)
    swapped = swapped_ref[:, 2 * HEAD * g : 2 * HEAD * (g + 1)].astype(F32)
    sum_ref[...] = (total + jnp.where(even, swapped, 0.0)).astype(BF16)


def final_kernel(groups, tables_ref, *refs):
    own_refs, home_refs, (dk_ref, dv_ref) = refs[:groups], refs[groups : 2 * groups], refs[-2:]
    wide, signed = row_tables(tables_ref[:HALF, :], tables_ref[HALF:, :])
    wide = wide * ROOT_SCALE
    signed = signed * -ROOT_SCALE
    for g in range(groups):
        cols = pl.ds(g * HEAD, HEAD)
        total = own_refs[g][...] + home_refs[g][...].astype(F32)
        dk_ref[:, cols] = rotated(total[:, :HEAD], wide, signed).astype(BF16)
        dv_ref[:, cols] = total[:, HEAD:].astype(BF16)


SMEM = pl.BlockSpec(memory_space=pltpu.SMEM)
VMEM = pl.BlockSpec(memory_space=pltpu.VMEM)
HBM = pl.BlockSpec(memory_space=pltpu.HBM)


def call(kernel, outs, specs, scratch=(), micros=1):
    return pl.pallas_call(
        kernel,
        out_shape=[jax.ShapeDtypeStruct(shape, dtype) for shape, dtype in outs],
        in_specs=specs,
        out_specs=[VMEM] * len(outs),
        scratch_shapes=list(scratch),
        compiler_params=pltpu.CompilerParams(vmem_limit_bytes=VMEM_LIMIT),
        cost_estimate=pl.CostEstimate(
            flops=1 << 20, bytes_accessed=micros * 3690000, transcendentals=0
        ),
    )


def shifted(value, steps, axis="ctx"):
    count = lax.axis_size(axis)
    pairs = [(source, (source + steps) % count) for source in range(count)]
    return lax.ppermute(value, axis, pairs)


def exchanged(value):
    count = lax.axis_size("ctx")
    return lax.ppermute(value, "ctx", [(source, source ^ 1) for source in range(count)])


def shards(q, k, v, do, at, lse, positions, span_map):
    rows = q.shape[0]
    wide_q = q.shape[1]
    wide_k = k.shape[1]
    heads = wide_q // HEAD
    q, do, at, k_here, v_here, lse, span_map, own = (
        pltpu.with_memory_space_constraint(x, pltpu.HBM)
        for x in (q, do, at, k, v, lse, span_map, positions)
    )

    pieces = [own] + [shifted(positions, r, "head") for r in (1, 2, 3)]
    groups = wide_k // HEAD
    every = tuple(range(groups))

    groups = wide_k // HEAD
    every = tuple(range(groups))

    v1 = shifted(v, -1)
    kr, tables = call(
        key_kernel, [((rows, wide_k), BF16), ((HEAD, rows), F32)], [VMEM] * 5
    )(*pieces, k_here)
    k1 = shifted(kr, -1)
    shared = call(
        functools.partial(prep_kernel, groups),
        [((rows, wide_q), BF16)] * 2 + [((heads, rows), F32)] * 2 + [((8, HEAD), jnp.int32)],
        [SMEM, VMEM] + [HBM] * 4,
        [
            pltpu.VMEM((rows, wide_q), BF16),
            pltpu.VMEM((rows, wide_q), BF16),
            pltpu.VMEM((heads, rows), F32),
            pltpu.SemaphoreType.DMA((3 * groups + 1,)),
        ],
        micros=2,
    )(span_map, tables, lse, q, do, at)
    v1, _ = lax.optimization_barrier((v1, shared[3]))
    v3 = shifted(v1, -2)
    v_far, _ = lax.optimization_barrier((v, shared[3]))
    v2 = shifted(v_far, -2)
    k3 = shifted(k1, -2)
    dqs = []
    dq_out = ((wide_q // groups, rows), F32)
    part_out = ((rows, 2 * HEAD), BF16)

    def hop(step, wanted, key, value, joined=False):
        count = len(wanted)
        started = len(dqs) > 0
        before = [dqs[g] for g in wanted] if started else []
        results = call(
            functools.partial(hop_kernel, step, wanted, started, joined),
            [dq_out] * count
            + ([((rows, 2 * HEAD * count), BF16)] if joined else [part_out] * count),
            [VMEM] * (7 + len(before)),
            micros=count,
        )(*before, key, value, *shared)
        if not started:
            dqs.extend(results[:count])
        for i, g in enumerate(wanted):
            dqs[g] = results[i]
        return results[count:]

    (part1,) = hop(1, every, k1, v1, joined=True)
    swapped = exchanged(part1)
    kr2, _ = lax.optimization_barrier((kr, part1))
    k2 = shifted(kr2, -2)
    moved = [shifted(*hop(3, (g,), k3, v3), 1) for g in every]
    parts2 = hop(2, every, k2, v2)
    results = call(
        functools.partial(own_kernel, groups),
        [dq_out] * groups + [((rows, 2 * HEAD), F32)] * groups,
        [VMEM] * (6 + groups),
        micros=3,
    )(kr, v_here, *shared[:4], *dqs)
    dqs, owns = list(results[:groups]), results[groups:]
    dq, *owns = call(
        functools.partial(query_kernel, groups),
        [((rows, wide_q), BF16)] + [((rows, 2 * HEAD), F32)] * groups,
        [VMEM] * (2 + 2 * groups),
    )(tables, *dqs, *owns, swapped)
    home = []
    for g in every:
        (total,) = call(functools.partial(add_kernel, g), [part_out], [VMEM] * 3)(
            parts2[g], swapped, moved[g]
        )
        home.append(shifted(total, 2))

    dk, dv = call(
        functools.partial(final_kernel, groups),
        [((rows, wide_k), BF16), ((rows, wide_k), BF16)],
        [VMEM] * (1 + 2 * groups),
    )(tables, *owns, *home)
    return dq, dk, dv


def solution(mesh):
    placed = (
        P("ctx", "head"),
        P("ctx", "head"),
        P("ctx", "head"),
        P("ctx", "head"),
        P("ctx", "head"),
        P("head", "ctx"),
        P(None, ("ctx", "head")),
        P(),
    )
    return jax.shard_map(
        shards,
        mesh=mesh,
        in_specs=placed,
        out_specs=(P("ctx", "head"), P("ctx", "head"), P("ctx", "head")),
        check_vma=False,
    )
```
